32 devices in a mesh: dp: 8 (over z, y), section: 4 (over x, core).
Axes of the slice: x: 2, y: 2, z: 4, core: 2. Of those that a mesh axis runs over, the one named last changes fastest.
Arguments:
- field_inputs: float32 [4096, 8, 256], P('dp', 'section'), may hold values from -6 to 6
- field_weight: float32 [8], P('section'), may hold values from 0.2 to 2
- norm_gain: float32 [256], replicated, may hold values from 0.1 to 1.9
- gate_weight: float32 [2, 256, 80], replicated, may hold values from -0.375 to 0.375
- expert_in: float32 [32, 256, 256], P('section'), may hold values from -0.375 to 0.375
- expert_out: float32 [32, 256, 256], P('section'), may hold values from -2 to 2
- tower_in: float32 [4, 256, 128], P('section'), may hold values from -0.375 to 0.375
- tower_out: float32 [4, 128], P('section'), may hold values from -0.5 to 0.5
- tower_bias: float32 [4], P('section'), may hold values from -4 to 4
- labels: float32 [4096, 4], P('dp', 'section'), may hold values from 0 to 1
- source_ids: int32 [4096], P('dp'), may hold values from 0 to 31, as said below
- task_table: int32 [32, 4], P(None, 'section'), may hold values from 0 to 1, as said below
Outputs:
- predictions: float32 [4096, 4], P('dp', 'section')
- inputs_grad: float32 [4096, 8, 256], P('dp', 'section')
- field_weight_grad: float32 [8], P('section')
- norm_gain_grad: float32 [256], replicated
- gate_weight_grad: float32 [2, 256, 80], replicated
- expert_in_grad: float32 [32, 256, 256], P('section')
- expert_out_grad: float32 [32, 256, 256], P('section')
- tower_in_grad: float32 [4, 256, 128], P('section')
- tower_out_grad: float32 [4, 128], P('section')
- tower_bias_grad: float32 [4], P('section')
The draws below stay inside these ranges and needn't reach their ends.
Inputs may be any that keep to these rules, and one draw needn't show every extreme that they name: `source_ids`: row 0 has source 0 and the last row source 32 - 1. `task_table`: source s labels exactly 1 + (s mod 4) of the 4 tasks.
All inputs are finite; a program needn't handle non-finite values.
Results may differ from the reference program's by a relative error of at most 0.0003.
Values sent between devices are 32-bit elements; how exact they have to be, the bound alone decides.
A program may use at most 256 MiB of HBM per device.

```python
import math
import jax
import jax.numpy as jnp
from jax import lax

D = 256
H = 256
E = 16
TASKS = 4
SEL = 4
BITS = 4
GATE = 80
TOWER = 128
FIELDS = 8
SOURCES = 32
ROWS_DEV = 512
ROWS = 4096


def draw_task_table(key, part):
    key = jax.random.fold_in(key, 11)
    scores = jax.random.randint(key, (SOURCES, TASKS), 0, 1 << 20) * TASKS + jnp.arange(TASKS)[None, :]
    ranks = jnp.argsort(jnp.argsort(scores, axis=1), axis=1)
    active = 1 + jnp.arange(SOURCES) % TASKS
    return (ranks < active[:, None]).astype(jnp.int32)


def draw_source_ids(key, part):
    key = jax.random.fold_in(key, 23)
    keys = jax.random.split(key, 4)
    block_index = jnp.arange(ROWS) // ROWS_DEV
    block_total = ROWS // ROWS_DEV
    fewer = (jax.random.randint(keys[0], (ROWS,), 0, 4) == 0).astype(jnp.int32)
    larger = 3 - (jax.random.randint(keys[1], (ROWS,), 0, 4) == 0).astype(jnp.int32)
    choose_many = jax.random.randint(keys[2], (ROWS,), 0, max(block_total - 1, 1)) < block_index
    classes = jnp.where(choose_many, larger, fewer)
    groups = jax.random.randint(keys[3], (ROWS,), 0, SOURCES // TASKS)
    source_values = groups * TASKS + classes
    source_values = source_values.at[0].set(0).at[ROWS - 1].set(SOURCES - 1)
    return source_values.astype(jnp.int32)


def block_scale(stream_key, dims, cuts, smallest, top_value):
    loudness, own = 1.0, jax.random.fold_in(stream_key, 6)
    for dim, shards_of in cuts:
        steps = jnp.exp(jax.random.uniform(jax.random.fold_in(own, dim), (shards_of,), jnp.float32, smallest / len(cuts), top_value / len(cuts)))
        loudness = loudness * jnp.repeat(steps, dims[dim] // shards_of).reshape([-1 if axis == dim else 1 for axis in range(len(dims))])
    return loudness


def gaussian(rng, shape, width, limit, cuts=(), dtype=jnp.bfloat16):
    level = block_scale(rng, shape, cuts, -0.22, 0.18) if cuts else 1.0
    array = jax.random.normal(rng, shape, jnp.float32) * width * level
    return jnp.minimum(jnp.maximum(array, -limit), limit).astype(dtype)


def setup_inputs(seed: int = 0) -> dict:
    streams_of = jax.random.split(jax.random.key(seed), 13)
    field_inputs = gaussian(streams_of[0], (ROWS, FIELDS, D), 1.0, 6.0, ((0, 8), (1, 4)), jnp.float32)
    field_weight = jnp.clip(jnp.exp(math.log(2.0) - 2.3025851 * jax.random.uniform(streams_of[1], (FIELDS,), jnp.float32) ** block_scale(streams_of[1], (FIELDS,), ((0, 4),), -0.2, 0.2)), 0.2, 2.0)
    norm_gain = jnp.clip(1.0 + 0.18 * jax.random.normal(streams_of[2], (D,), jnp.float32), 0.1, 1.9)
    gate_weight = gaussian(streams_of[3], (2, D, GATE), D ** -0.5, 0.375, (), jnp.float32)
    expert_in = gaussian(streams_of[4], (2 * E, D, H), D ** -0.5, 0.375, ((0, 4),), jnp.float32)
    expert_out = gaussian(streams_of[5], (2 * E, H, D), (H // 32) ** -0.5, 2.0, ((0, 4),), jnp.float32)
    tower_in = gaussian(streams_of[6], (TASKS, D, TOWER), D ** -0.5, 0.375, ((0, 4),), jnp.float32)
    tower_out = gaussian(streams_of[7], (TASKS, TOWER), TOWER ** -0.5, 0.5, ((0, 4),), jnp.float32)
    tower_bias = gaussian(streams_of[8], (TASKS,), 1.0, 4.0, ((0, 4),), jnp.float32)
    labels = jnp.clip(1.0 * jax.random.uniform(streams_of[9], (ROWS, TASKS), jnp.float32) ** block_scale(streams_of[9], (ROWS, TASKS), ((0, 8), (1, 4)), -0.2, 0.2), 0.0, 1.0)
    source_ids = draw_source_ids(jax.random.fold_in(streams_of[12], 71), 0)
    task_table = draw_task_table(jax.random.fold_in(streams_of[12], 71), 0)
    return {"field_inputs": field_inputs, "field_weight": field_weight, "norm_gain": norm_gain, "gate_weight": gate_weight, "expert_in": expert_in, "expert_out": expert_out, "tower_in": tower_in, "tower_out": tower_out, "tower_bias": tower_bias, "labels": labels, "source_ids": source_ids, "task_table": task_table}


@jax.custom_vjp
def low(v):
    return lax.optimization_barrier(v.astype(jnp.bfloat16)).astype(jnp.float32)

@jax.custom_vjp
def low_back(v):
    return v

def low_keep(v):
    return (low(v), None)

def low_pass(kept, grad):
    return (grad,)

def back_keep(v):
    return (v, None)

def back_low(kept, grad):
    return (low(grad),)
low.defvjp(low_keep, low_pass)
low_back.defvjp(back_keep, back_low)
STEP_SLOPE = 0.6
ENTROPY_WEIGHT = 0.05
NORM_EPS = 1e-05
PRECISE = lax.Precision.HIGHEST

def gelu_tanh(values):
    return jax.nn.gelu(values, approximate=True)

def bit_rows():
    expert_index = jnp.arange(E)
    levels = jnp.arange(BITS)
    return (expert_index[None, :] >> levels[:, None] & 1).astype(jnp.float32)

def selectors(logits):
    step_logits = logits[..., :BITS] * STEP_SLOPE
    alpha_logits = logits[..., BITS]
    bits_on = bit_rows()
    log_upper = jax.nn.log_sigmoid(step_logits)
    log_lower = jax.nn.log_sigmoid(-step_logits)
    log_r = jnp.einsum('rtsb,be->rtse', log_upper, bits_on, precision=PRECISE) + jnp.einsum('rtsb,be->rtse', log_lower, 1.0 - bits_on, precision=PRECISE)
    select_probs = jnp.exp(log_r)
    entropy = -jnp.sum(select_probs * log_r)
    mixing = jax.nn.softmax(alpha_logits, axis=-1)
    gate_values = jnp.einsum('rts,rtse->rte', mixing, select_probs, precision=PRECISE)
    return (gate_values, entropy)

def block_loss(field_rows, label_rows, mask_rows, field_weight, norm_gain, gate_weight, expert_in, expert_out, tower_in, tower_out, tower_bias):
    row_total = field_rows.shape[0]
    pre_norm = jnp.einsum('rfd,f->rd', field_rows, field_weight, precision=PRECISE)
    pooled = pre_norm * lax.rsqrt(lax.optimization_barrier(jnp.mean(pre_norm * pre_norm, axis=-1, keepdims=True)) + NORM_EPS) * norm_gain
    gate_first = gate_weight[0].reshape(D, TASKS, SEL * (BITS + 1))
    logits = jnp.einsum('rd,dtk->rtk', pooled, gate_first, precision=PRECISE).reshape(row_total, TASKS, SEL, BITS + 1)
    gate_values, entropy_first = selectors(logits)
    hidden = gelu_tanh(jnp.einsum('rd,edh->reh', pooled, expert_in[:E], precision=PRECISE))
    expert_outs = jnp.einsum('reh,ehd->red', hidden, expert_out[:E], precision=PRECISE)
    first_streams = pooled[:, None, :] + jnp.einsum('rte,red->rtd', gate_values, expert_outs, precision=PRECISE)
    gate_second = gate_weight[1].reshape(D, TASKS, SEL * (BITS + 1))
    logits = jnp.einsum('rtd,dtk->rtk', first_streams, gate_second, precision=PRECISE).reshape(row_total, TASKS, SEL, BITS + 1)
    gate_values, entropy_second = selectors(logits)
    hidden = gelu_tanh(jnp.einsum('rtd,edh->rteh', first_streams, expert_in[E:], precision=PRECISE))
    second = first_streams + jnp.einsum('rteh,ehd->rtd', gate_values[..., None] * hidden, expert_out[E:], precision=PRECISE)
    tower_hidden = gelu_tanh(jnp.einsum('rtd,tdk->rtk', second, tower_in, precision=PRECISE))
    logit_values = jnp.einsum('rtk,tk->rt', tower_hidden, tower_out, precision=PRECISE) + tower_bias
    cross_entropy = jnp.sum(mask_rows * (jax.nn.softplus(logit_values) - label_rows * logit_values))
    return (cross_entropy + ENTROPY_WEIGHT * (entropy_first + entropy_second), jax.nn.sigmoid(logit_values))

def reference(field_inputs, field_weight, norm_gain, gate_weight, expert_in, expert_out, tower_in, tower_out, tower_bias, labels, source_ids, task_table):
    label_mask = task_table[source_ids].astype(jnp.float32)
    label_count = jnp.sum(label_mask)
    loss_scale = ROWS / label_count
    block_rows = math.gcd(ROWS, 512)
    blocks = ROWS // block_rows
    weights = (field_weight, norm_gain, gate_weight, expert_in, expert_out, tower_in, tower_out, tower_bias)

    def total_loss(inputs_all, params):

        def scan_step(running, block_items):
            part_loss, part_pred = jax.checkpoint(block_loss)(*block_items, *params)
            return (running + part_loss, part_pred)
        block_items = (inputs_all.reshape(blocks, block_rows, FIELDS, D), labels.reshape(blocks, block_rows, TASKS), label_mask.reshape(blocks, block_rows, TASKS))
        running, block_preds = lax.scan(scan_step, jnp.zeros((), jnp.float32), block_items)
        return (loss_scale * running, block_preds.reshape(ROWS, TASKS))
    loss_value, pull_back, predictions = jax.vjp(total_loss, field_inputs, weights, has_aux=True)
    inputs_grad, weight_grads = pull_back(jnp.ones((), jnp.float32))
    return (predictions, inputs_grad, weight_grads[0], weight_grads[1], weight_grads[2], weight_grads[3], weight_grads[4], weight_grads[5], weight_grads[6], weight_grads[7])
```

```python
from functools import partial

import jax
import jax.numpy as jnp
from jax import lax
from jax.experimental import pallas as pl
from jax.experimental.pallas import tpu as pltpu
from jax.sharding import PartitionSpec as P

D = 256
H = 256
E = 16
TASKS = 4
SEL = 4
BITS = 4
TOWER = 128
SOURCES = 32
HALF = E // 2
GROWS = 32

STEP_SLOPE = 0.6
ENTROPY_WEIGHT = 0.05
NORM_EPS = 1e-05
GELU_A = 0.7978845608028654
GELU_B = 0.044715

F32 = jnp.float32
BF16 = jnp.bfloat16
MESH = pl.DeviceIdType.MESH

K_W, K_P, K_SM, K_TI, K_UP, K_DOWN, K_TW, K_DX, K_DG, K_DP, K_GO = 0, 2, 4, 8, 12, 16, 20, 24, 26, 27, 30
K_COUNT = 34

GATE_AT = HALF * H
MISC_AT = GATE_AT + 2 * GROWS
SMALL = 2 * GROWS + 8


def split(x):
    hi = x.astype(BF16)
    return hi, (x - hi.astype(F32)).astype(BF16)


def wide(x):
    hi, lo = split(x)
    return jnp.concatenate([hi, lo, hi], axis=1)


def tall(x):
    hi, lo = split(x)
    return jnp.concatenate([hi, hi, lo], axis=0)


def mm(a, b):
    return jnp.dot(a, b, preferred_element_type=F32)


def pair(x):
    k = x.shape[1] // 2
    return jnp.concatenate([x, x[:, :k]], axis=1)


def gelu_pair(x):
    x2 = x * x
    h = 0.5 + 0.5 * jnp.tanh(x * (GELU_A + (GELU_A * GELU_B) * x2))
    g = x * h
    slope = h + g * (1.0 - h) * (2.0 * GELU_A + (6.0 * GELU_A * GELU_B) * x2)
    return g, slope


def rows8(x):
    return jnp.sum(x.reshape(x.shape[0] // 8, 8, x.shape[1]), axis=0)


def gate_state(c):
    zs = [c[SEL * b : SEL * b + SEL] * STEP_SLOPE for b in range(BITS)]
    alpha = c[SEL * BITS : SEL * BITS + SEL]
    ups, downs, sig_p, sig_n = [], [], [], []
    for z in zs:
        e = jnp.exp(-jnp.abs(z))
        tail = jnp.log1p(e)
        ups.append(jnp.minimum(z, 0.0) - tail)
        downs.append(jnp.minimum(-z, 0.0) - tail)
        big = 1.0 / (1.0 + e)
        small = e * big
        sig_p.append(jnp.where(z >= 0.0, big, small))
        sig_n.append(jnp.where(z >= 0.0, small, big))
    low = [(ups[0] if k & 1 else downs[0]) + (ups[1] if k & 2 else downs[1]) for k in range(4)]
    high = [(ups[2] if k & 1 else downs[2]) + (ups[3] if k & 2 else downs[3]) for k in range(4)]
    log_r = [low[j & 3] + high[j >> 2] for j in range(E)]
    r = [jnp.exp(v) for v in log_r]
    top = jnp.exp(alpha - jnp.max(alpha, axis=0, keepdims=True))
    mix = top / jnp.sum(top, axis=0, keepdims=True)
    return log_r, r, mix, sig_p, sig_n


def gate_forward(c):
    _, r, mix, _, _ = gate_state(c)
    return [jnp.sum(mix * v, axis=0, keepdims=True) for v in r]


def gate_backward(c, dgate):
    log_r, r, mix, sig_p, sig_n = gate_state(c)
    total = jnp.zeros_like(mix)
    on = [jnp.zeros_like(mix) for _ in range(BITS)]
    off = [jnp.zeros_like(mix) for _ in range(BITS)]
    for j in range(E):
        total = total + dgate[j] * r[j]
        dlog = r[j] * (mix * dgate[j] - ENTROPY_WEIGHT * (log_r[j] + 1.0))
        for b in range(BITS):
            if j >> b & 1:
                on[b] = on[b] + dlog
            else:
                off[b] = off[b] + dlog
    dalpha = mix * (total - jnp.sum(mix * total, axis=0, keepdims=True))
    dz = [STEP_SLOPE * (on[b] * sig_n[b] - off[b] * sig_p[b]) for b in range(BITS)]
    pad = jnp.zeros((GROWS - SEL * (BITS + 1), c.shape[1]), F32)
    return jnp.concatenate(dz + [dalpha, pad], axis=0)


def t_dot(a, b):
    ah, al = split(a)
    left = jnp.concatenate([ah, al, ah], axis=0)
    return lax.dot_general(left, tall(b), (((0,), (0,)), ((), ())), preferred_element_type=F32)


def kernel(
    n,
    chunk,
    subs,
    x_ref,
    fw_ref,
    gain_ref,
    wg_ref,
    win_ref,
    wout_ref,
    tin_ref,
    tout_ref,
    tbias_ref,
    labels_ref,
    ids_ref,
    table_ref,
    ring_ref,
    small_ref,
    ig_ref,
    pred_ref,
    wt_in,
    wt_out,
    w_in,
    w_out,
    a1,
    a2,
    a3,
    d_in,
    d_out,
    rb,
    rd,
    rv,
    part,
    pre0,
    pre1,
    pre2,
    pre,
    inbox,
    outbox,
    u_t,
    u_n,
    y_t,
    y_n,
    s_t,
    s_n,
    acc,
    gt,
    cs,
    dgt,
    dg,
    gb,
    sm,
    smo,
    ti,
    tp,
    tw,
    dp,
    send,
    recv,
    local,
    rs_send,
    rs_recv,
    ag_send,
    ag_recv,
):
    s = lax.axis_index("section")
    x = s // 2
    c = s % 2
    mate = s + 1 - 2 * c
    across = s + 2 - 4 * x
    diag = 3 - s
    R = part.shape[0] // 2
    mine = pl.ds(pl.multiple_of(c * R, R), R)
    theirs = pl.ds(pl.multiple_of((1 - c) * R, R), R)

    pos = lax.axis_index("dp")
    odd = pos % 2
    p = (1 - odd) * (pos // 2) + odd * (n - 1 - pos // 2)

    def ring_id(q):
        far = q // (n // 2)
        return (1 - far) * 2 * q + far * (2 * (n - 1 - q) + 1)

    nbr = [ring_id((p + 1) % n), ring_id((p + n - 1) % n)]

    barrier = pltpu.get_barrier_semaphore()
    for sec in (mate, across, diag):
        pl.semaphore_signal(barrier, inc=1, device_id={"section": sec}, device_id_type=MESH)
    for dev in nbr:
        pl.semaphore_signal(barrier, inc=1, device_id={"dp": dev}, device_id_type=MESH)
    pl.semaphore_wait(barrier, 5)

    def copy(src, dst, k, sec, ks=None):
        return pltpu.make_async_remote_copy(
            src_ref=src,
            dst_ref=dst,
            send_sem=send.at[k if ks is None else ks],
            recv_sem=recv.at[k],
            device_id={"section": sec},
            device_id_type=MESH,
        )

    part[...] = x_ref[:, :D] * fw_ref[0, 0] + x_ref[:, D:] * fw_ref[0, 1]
    to_mate = copy(part.at[theirs], pre0, K_P, mate)
    to_mate.start()
    swap_in = copy(win_ref, a2.at[pl.ds(0, HALF)], K_W, mate)
    swap_out = copy(wout_ref, a2.at[pl.ds(HALF, HALF)], K_W + 1, mate)
    own_in = pltpu.make_async_copy(win_ref, a1.at[pl.ds(0, HALF)], local.at[0])
    own_out = pltpu.make_async_copy(wout_ref, a1.at[pl.ds(HALF, HALF)], local.at[1])
    own_in.start()
    own_out.start()
    swap_in.start()
    swap_out.start()

    ids = jnp.broadcast_to(ids_ref[...], (SOURCES, 2 * R))
    hit = ids == lax.broadcasted_iota(jnp.int32, (SOURCES, 2 * R), 0)
    mask = jnp.sum(jnp.where(hit, table_ref[...].astype(F32), 0.0), axis=0, keepdims=True)
    smo[...] = jnp.zeros_like(smo)
    smo[0:1] = labels_ref[...]
    smo[1:2] = mask
    smo[2:3, :TOWER] = tout_ref[...]
    smo[3:4] = jnp.zeros((1, 2 * R), F32) + tbias_ref[0, 0]
    for k in range(2):

        @pl.when(s != 2 + k)
        def _():
            copy(smo, sm.at[s], K_SM + s, 2 + k, K_SM + k).start()
            copy(tin_ref, ti.at[s], K_TI + s, 2 + k, K_TI + k).start()

    to_mate.wait_recv()

    @pl.when(x == 1)
    def _():
        pre2[...] = part[mine] + pre0[...]
        copy(pre2, pre1, K_P + 1, across).start()
        sm[s] = smo[...]
        ti[s] = tin_ref[...]
        d_in[...] = jnp.zeros_like(d_in)
        d_out[...] = jnp.zeros_like(d_out)

    own_in.wait()
    own_out.wait()

    def prepare(e, at, src):
        for slot, (plain, flipped) in enumerate(((w_in, wt_in), (w_out, wt_out))):
            w = src[slot * HALF + e]
            hi, lo = split(w)
            plain[at + e] = jnp.concatenate([hi, lo], axis=1)
            hi, lo = split(w.T)
            flipped[at + e] = jnp.concatenate([hi, lo], axis=1)

    def prepare_own(e, carry):
        prepare(e, c * HALF, a1)
        return carry

    def prepare_other(e, carry):
        prepare(e, (1 - c) * HALF, a2)
        return carry

    lax.fori_loop(0, HALF, prepare_own, 0)
    swap_in.wait()
    swap_out.wait()
    lax.fori_loop(0, HALF, prepare_other, 0)

    TR = 64
    tiles = [slice(a, a + TR) for a in range(0, H, TR)]

    @pl.when(x == 0)
    def _():
        copy(pre2, pre1, K_P + 1, across).wait_recv()
        pre_rows = part[mine] + pre0[...] + pre1[...]
        pre[...] = pre_rows
        rho = lax.rsqrt(jnp.mean(pre_rows * pre_rows, axis=1, keepdims=True) + NORM_EPS)
        pooled = pre_rows * rho * gain_ref[...]
        u_n[...] = tall(pooled)
        pooled_t = pooled.T
        acc[...] = pooled_t
        u_t[...] = tall(pooled_t)

        def gates(t, carry):
            logits = mm(wide(wg_ref[0, t]), u_t[...])
            cs[t] = logits
            for j, g in enumerate(gate_forward(logits)):
                gt[t, j] = g
            return carry

        lax.fori_loop(0, TASKS, gates, 0)

        def expert(j, carry):
            b = mm(pair(wt_in[j]), u_t[...])
            his, los = [], []
            for tile in tiles:
                g, slope = gelu_pair(b[tile])
                a1[j, tile] = g
                a2[j, tile] = slope
                hi, lo = split(g)
                his.append(hi)
                los.append(lo)
            a3[j] = mm(pair(wt_out[j]), jnp.concatenate(his + his + los, axis=0))
            return carry

        lax.fori_loop(0, E, expert, 0)

        def stream(t, carry):
            for tile in [slice(a, a + 32) for a in range(0, D, 32)]:
                total = acc[tile]
                for j in range(E):
                    total = total + gt[t, j] * a3[j, tile]
                outbox[t, tile] = total
            copy(outbox.at[t], inbox.at[t], K_UP + t, across).start()
            return carry

        lax.fori_loop(0, TASKS, stream, 0)

    @pl.when(x == 1)
    def _():
        for q in range(TASKS):

            @pl.when(s != q)
            def _():
                copy(smo, sm.at[q], K_SM + q, q).wait_recv()
                copy(tin_ref, ti.at[q], K_TI + q, q).wait_recv()

        def task(t, carry):
            copy(outbox.at[t], inbox.at[t], K_UP + t, across).wait_recv()
            u = inbox[t]
            u_t[...] = tall(u)
            u_n[...] = tall(u.T)
            gate_w = wg_ref[1, t]
            logits = mm(wide(gate_w), u_t[...])
            for j, g in enumerate(gate_forward(logits)):
                gt[0, j] = g
            acc[...] = u

            def expert(j, carry):
                b = mm(pair(wt_in[j]), u_t[...])
                gate = gt[0, j]
                his, los = [], []
                for tile in tiles:
                    g, slope = gelu_pair(b[tile])
                    a1[j, tile] = g
                    a2[j, tile] = slope
                    hi, lo = split(g * gate)
                    his.append(hi)
                    los.append(lo)
                acc[...] += mm(pair(wt_out[j]), jnp.concatenate(his + his + los, axis=0))
                return carry

            lax.fori_loop(0, E, expert, 0)

            second = acc[...]
            s_t[...] = tall(second)
            s_n[...] = tall(second.T)
            tower = ti[t]
            g, slope = gelu_pair(mm(wide(tower.T), s_t[...]))
            info = sm[t]
            out_col = info[:, :TOWER].T[:, 2:3]
            here = sm[t, :, mine]
            logit = jnp.sum(g * out_col, axis=0, keepdims=True) + here[3:4]
            prob = jax.nn.sigmoid(logit)
            dlogit = here[1:2] * (prob - here[0:1])
            m = dlogit * out_col * slope
            out_grad = jnp.sum(g * dlogit, axis=1, keepdims=True)
            out_row = jnp.broadcast_to(out_grad, (TOWER, TOWER)).T[0:1]
            dy = mm(wide(tower), tall(m))
            tp[t, :TOWER] = mm(wide(m), s_n[...])
            tp[t, TOWER : TOWER + 1] = prob
            tp[t, TOWER + 1 : TOWER + 2] = jnp.concatenate([out_row, jnp.zeros_like(out_row)], axis=1)
            tp[t, TOWER + 2 : TOWER + 3] = dlogit
            tp[t, TOWER + 3 :] = jnp.zeros((5, R), F32)

            @pl.when(t != s)
            def _():
                copy(tp.at[t], tw.at[c], K_TW + c, t, K_TW + t).start()

            @pl.when(t == s)
            def _():
                tw[c] = tp[t]

            y_t[...] = tall(dy)
            y_n[...] = tall(dy.T)
            acc[...] = dy

            def back(j, carry):
                dh = mm(pair(w_out[j]), y_t[...])
                gate = gt[0, j]
                k_hi, k_lo, g_hi, g_lo = [], [], [], []
                total = jnp.zeros((8, R), F32)
                for tile in tiles:
                    g = a1[j, tile]
                    grad = dh[tile]
                    total = total + rows8(grad * g)
                    hi, lo = split(grad * a2[j, tile] * gate)
                    k_hi.append(hi)
                    k_lo.append(lo)
                    hi, lo = split(g * gate)
                    g_hi.append(hi)
                    g_lo.append(lo)
                dgt[0, j] = jnp.sum(total, axis=0, keepdims=True)
                k_hi, k_lo, g_hi, g_lo = (jnp.concatenate(v, axis=0) for v in (k_hi, k_lo, g_hi, g_lo))
                acc[...] += mm(pair(w_in[j]), jnp.concatenate([k_hi, k_hi, k_lo], axis=0))
                d_in[j] += mm(jnp.concatenate([k_hi, k_lo, k_hi], axis=1), u_n[...])
                d_out[j] += mm(jnp.concatenate([g_hi, g_lo, g_hi], axis=1), y_n[...])
                return carry

            lax.fori_loop(0, E, back, 0)
            dc = gate_backward(logits, [dgt[0, j] for j in range(E)])
            dg[t] = mm(wide(dc), u_n[...])
            outbox[t] = acc[...] + t_dot(gate_w, dc)
            copy(outbox.at[t], inbox.at[t], K_DOWN + t, across).start()
            return carry

        lax.fori_loop(0, TASKS, task, 0)

    @pl.when(x == 0)
    def _():
        total = jnp.zeros((D, R), F32)
        for t in range(TASKS):
            copy(outbox.at[t], inbox.at[t], K_DOWN + t, across).wait_recv()
            total = total + inbox[t]
        acc[...] = total

        def back(j, carry):
            gates = [gt[t, j] for t in range(TASKS)]
            sums = [jnp.zeros((8, R), F32) for _ in range(TASKS)]
            f_hi, f_lo = [], []
            for tile in [slice(a, a + 32) for a in range(0, D, 32)]:
                f = a3[j, tile]
                mixed = jnp.zeros((32, R), F32)
                for t in range(TASKS):
                    dy = inbox[t, tile]
                    mixed = mixed + gates[t] * dy
                    sums[t] = sums[t] + rows8(f * dy)
                hi, lo = split(mixed)
                f_hi.append(hi)
                f_lo.append(lo)
            for t in range(TASKS):
                dgt[t, j] = jnp.sum(sums[t], axis=0, keepdims=True)
            f_hi, f_lo = jnp.concatenate(f_hi, axis=0), jnp.concatenate(f_lo, axis=0)
            dh = mm(pair(w_out[j]), jnp.concatenate([f_hi, f_hi, f_lo], axis=0))
            k_hi, k_lo, g_hi, g_lo = [], [], [], []
            for tile in tiles:
                hi, lo = split(dh[tile] * a2[j, tile])
                k_hi.append(hi)
                k_lo.append(lo)
                hi, lo = split(a1[j, tile])
                g_hi.append(hi)
                g_lo.append(lo)
            k_hi, k_lo, g_hi, g_lo = (jnp.concatenate(v, axis=0) for v in (k_hi, k_lo, g_hi, g_lo))
            acc[...] += mm(pair(w_in[j]), jnp.concatenate([k_hi, k_hi, k_lo], axis=0))
            d_in[j] = mm(jnp.concatenate([k_hi, k_lo, k_hi], axis=1), u_n[...])
            d_out[j] = lax.dot_general(
                jnp.concatenate([g_hi, g_lo, g_hi], axis=1),
                jnp.concatenate([f_hi, f_hi, f_lo], axis=1),
                (((1,), (1,)), ((), ())),
                preferred_element_type=F32,
            )
            return carry

        lax.fori_loop(0, E, back, 0)

        def gates(t, carry):
            dc = gate_backward(cs[t], [dgt[t, j] for j in range(E)])
            dg[t] = mm(wide(dc), u_n[...])
            acc[...] += t_dot(wg_ref[0, t], dc)
            return carry

        lax.fori_loop(0, TASKS, gates, 0)
        dpool = acc[...].T
        pre_rows = pre[...]
        rho = lax.rsqrt(jnp.mean(pre_rows * pre_rows, axis=1, keepdims=True) + NORM_EPS)
        scaled = dpool * gain_ref[...]
        dots = jnp.mean(scaled * pre_rows, axis=1, keepdims=True)
        dp[mine] = rho * scaled - pre_rows * (rho * rho * rho * dots)
        tp[0, 0:1] = jnp.sum(dpool * pre_rows * rho, axis=0, keepdims=True)
        for k, sec in enumerate((mate, across, diag)):
            copy(dp.at[mine], dp.at[mine], K_DP + c, sec, K_DP + k).start()

    away = pl.ds(pl.multiple_of((1 - c) * HALF, HALF), HALF)
    copy(d_in.at[away], rb.at[0], K_DX, mate).start()
    copy(d_out.at[away], rb.at[1], K_DX + 1, mate).start()
    copy(dg.at[pl.ds(2 * (1 - c), 2)], gb, K_DG, mate).start()

    for half in range(2):

        @pl.when(s != half)
        def _():
            copy(dp.at[pl.ds(half * R, R)], dp.at[pl.ds(half * R, R)], K_DP + half, half).wait_recv()

    for k in range(2):

        @pl.when(s != 2 + k)
        def _():
            copy(tp.at[0], tw.at[k], K_TW + k, s).wait_recv()

    for k in range(2):
        grad = dp[pl.ds(k * R, R)]
        ig_ref[pl.ds(k * R, R), :D] = grad * fw_ref[0, 0]
        ig_ref[pl.ds(k * R, R), D:] = grad * fw_ref[0, 1]
        pred_ref[k : k + 1] = tw[k, TOWER : TOWER + 1]
    rd[1, MISC_AT : MISC_AT + 1] = jnp.where(x == 0, tp[0, 0:1], 0.0)
    rd[1, MISC_AT + 1 : MISC_AT + 3] = tw[0, TOWER + 1 : TOWER + 3] + tw[1, TOWER + 1 : TOWER + 3]
    rd[1, MISC_AT + 3 : MISC_AT + 4] = jnp.sum(x_ref[:, :D] * dp[...], axis=0, keepdims=True)
    rd[1, MISC_AT + 4 : MISC_AT + 5] = jnp.sum(x_ref[:, D:] * dp[...], axis=0, keepdims=True)
    rd[1, MISC_AT + 5 : MISC_AT + 6] = smo[1:2, :R] + smo[1:2, R:]
    rd[1, MISC_AT + 6 : MISC_AT + 8] = jnp.zeros((2, D), F32)
    rd[0, GATE_AT : GATE_AT + TOWER] = tw[0, :TOWER] + tw[1, :TOWER]
    end = n * chunk
    if end > GATE_AT + TOWER:
        rd[0, GATE_AT + TOWER :] = jnp.zeros((end - GATE_AT - TOWER, D), F32)
    rd[1, MISC_AT + 8 :] = jnp.zeros((end - MISC_AT - 8, D), F32)
    copy(dg.at[pl.ds(2 * (1 - c), 2)], gb, K_DG, mate).wait_recv()
    for k in range(2):
        rd[1, GATE_AT + k * GROWS : GATE_AT + (k + 1) * GROWS] = dg[2 * c + k] + gb[k]
    copy(d_in.at[away], rb.at[0], K_DX, mate).wait_recv()
    copy(d_out.at[away], rb.at[1], K_DX + 1, mate).wait_recv()

    def merge(e, carry):
        at = pl.ds(pl.multiple_of(e * H, H), H)
        rd[0, at] = d_in[c * HALF + e] + rb[0, e]
        rd[1, at] = d_out[c * HALF + e] + rb[1, e]
        return carry

    lax.fori_loop(0, HALF, merge, 0)

    sub = chunk // subs
    lanes = [(d, k) for d in range(2) for k in range(subs)]

    def at(d, k, q):
        return pl.ds(pl.multiple_of(q * chunk + k * sub, 8), sub)

    def holds(d, step):
        return (p + n - step) % n if d == 0 else (p + step) % n

    def rs(d, k, step, src):
        return pltpu.make_async_remote_copy(
            src_ref=src,
            dst_ref=rv.at[d, k, step],
            send_sem=rs_send.at[d, k, step],
            recv_sem=rs_recv.at[d, k, step],
            device_id={"dp": nbr[d]},
            device_id_type=MESH,
        )

    def ag(d, k, step, src, q):
        return pltpu.make_async_remote_copy(
            src_ref=src,
            dst_ref=ring_ref.at[d, at(d, k, q)],
            send_sem=ag_send.at[d, k, step],
            recv_sem=ag_recv.at[d, k, step],
            device_id={"dp": nbr[d]},
            device_id_type=MESH,
        )

    for d, k in lanes:
        rs(d, k, 0, rd.at[d, at(d, k, holds(d, 0))]).start()

    def reduce_step(step, carry):
        for d, k in lanes:
            rs(d, k, step - 1, rv.at[d, k, step - 1]).wait_recv()
            rv[d, k, step - 1] += rd[d, at(d, k, holds(d, step))]
            rs(d, k, step, rv.at[d, k, step - 1]).start()
        return carry

    lax.fori_loop(1, n - 1, reduce_step, 0)
    last = n - 2
    for d, k in lanes:
        q = holds(d, n - 1)
        rs(d, k, last, rv.at[d, k, last]).wait_recv()
        rv[d, k, last] += rd[d, at(d, k, q)]
        ag(d, k, 0, rv.at[d, k, last], q).start()
        pltpu.make_async_copy(rv.at[d, k, last], ring_ref.at[d, at(d, k, q)], local.at[2 + d * subs + k]).start()

    def gather_step(step, carry):
        for d, k in lanes:
            q = holds(d, step - 1)
            ag(d, k, step - 1, ring_ref.at[d, at(d, k, q)], q).wait_recv()
            ag(d, k, step, ring_ref.at[d, at(d, k, q)], q).start()
        return carry

    lax.fori_loop(1, n - 1, gather_step, 0)
    for d, k in lanes:
        q = holds(d, n - 2)
        ag(d, k, last, ring_ref.at[d, at(d, k, q)], q).wait_recv()
        q = holds(d, n - 1)
        pltpu.make_async_copy(rv.at[d, k, last], ring_ref.at[d, at(d, k, q)], local.at[2 + d * subs + k]).wait()

    block = ring_ref.at[1, pl.ds(GATE_AT, SMALL)]
    for k, sec in enumerate((mate, across, diag)):
        copy(block, small_ref.at[s], K_GO + s, sec, K_GO + k).start()
    keep = pltpu.make_async_copy(block, small_ref.at[s], local.at[0])
    keep.start()

    def sent(step, carry):
        for d, k in lanes:
            rs(d, k, step, rv.at[d, k, step]).wait_send()
            ag(d, k, step, rv.at[d, k, step], 0).wait_send()
        return carry

    lax.fori_loop(0, n - 1, sent, 0)
    to_mate.wait_send()
    for k in range(2):

        @pl.when(s != 2 + k)
        def _():
            copy(smo, sm.at[s], K_SM + s, 2 + k, K_SM + k).wait_send()
            copy(tin_ref, ti.at[s], K_TI + s, 2 + k, K_TI + k).wait_send()

    @pl.when(x == 0)
    def _():
        for t in range(TASKS):
            copy(outbox.at[t], inbox.at[t], K_UP + t, across).wait_send()
        for k, sec in enumerate((mate, across, diag)):
            copy(dp.at[mine], dp.at[mine], K_DP + c, sec, K_DP + k).wait_send()

    @pl.when(x == 1)
    def _():
        copy(pre2, pre1, K_P + 1, across).wait_send()
        for t in range(TASKS):
            copy(outbox.at[t], inbox.at[t], K_DOWN + t, across).wait_send()

            @pl.when(t != s)
            def _():
                copy(tp.at[t], tw.at[c], K_TW + c, t, K_TW + t).wait_send()

    copy(d_in.at[away], rb.at[0], K_DX, mate).wait_send()
    copy(d_out.at[away], rb.at[1], K_DX + 1, mate).wait_send()
    copy(dg.at[pl.ds(2 * (1 - c), 2)], gb, K_DG, mate).wait_send()
    for k, sec in enumerate((mate, across, diag)):
        copy(block, small_ref.at[s], K_GO + s, sec, K_GO + k).wait_send()
        copy(block, small_ref.at[sec], K_GO + sec, sec).wait_recv()
    keep.wait()


def body(
    field_inputs,
    field_weight,
    norm_gain,
    gate_weight,
    expert_in,
    expert_out,
    tower_in,
    tower_out,
    tower_bias,
    labels,
    source_ids,
    task_table,
):
    n = lax.axis_size("dp")
    rows = field_inputs.shape[0]
    half = rows // 2
    subs = 2 if n <= 16 else 1
    unit = n * subs * 8
    chunk = -(-(GATE_AT + TOWER) // unit) * subs * 8
    length = n * chunk

    gates = gate_weight.reshape(2, D, TASKS, SEL, BITS + 1).transpose(0, 2, 4, 3, 1)
    gates = gates.reshape(2, TASKS, SEL * (BITS + 1), D)
    gates = jnp.pad(gates, ((0, 0), (0, 0), (0, GROWS - SEL * (BITS + 1)), (0, 0)))

    vmem = pl.BlockSpec(memory_space=pltpu.VMEM)
    smem = pl.BlockSpec(memory_space=pltpu.SMEM)
    hbm = pl.BlockSpec(memory_space=pl.ANY)

    def bf(*shape):
        return pltpu.VMEM(shape, BF16)

    def f32(*shape):
        return pltpu.VMEM(shape, F32)

    ring, small, grads, probs = pl.pallas_call(
        partial(kernel, n, chunk, subs),
        out_shape=(
            jax.ShapeDtypeStruct((2, length, D), F32),
            jax.ShapeDtypeStruct((TASKS, SMALL, D), F32),
            jax.ShapeDtypeStruct((rows, 2 * D), F32),
            jax.ShapeDtypeStruct((2, half), F32),
        ),
        in_specs=[vmem, smem, vmem, vmem, hbm, hbm, vmem, vmem, smem, vmem, vmem, vmem],
        out_specs=(hbm, hbm, vmem, vmem),
        scratch_shapes=[
            bf(E, H, 2 * D),
            bf(E, D, 2 * H),
            bf(E, D, 2 * H),
            bf(E, H, 2 * D),
            f32(E, H, half),
            f32(E, H, half),
            f32(E, D, half),
            f32(E, H, D),
            f32(E, H, D),
            f32(2, HALF, H, D),
            f32(2, length, D),
            f32(2, subs, n - 1, chunk // subs, D),
            f32(rows, D),
            f32(half, D),
            f32(half, D),
            f32(half, D),
            f32(half, D),
            f32(TASKS, D, half),
            f32(TASKS, D, half),
            bf(3 * D, half),
            bf(3 * half, D),
            bf(3 * D, half),
            bf(3 * half, D),
            bf(3 * D, half),
            bf(3 * half, D),
            f32(D, half),
            f32(TASKS, E, 1, half),
            f32(TASKS, GROWS, half),
            f32(TASKS, E, 1, half),
            f32(TASKS, GROWS, D),
            f32(2, GROWS, D),
            f32(TASKS, 8, rows),
            f32(8, rows),
            f32(TASKS, D, TOWER),
            f32(TASKS, TOWER + 8, D),
            f32(2, TOWER + 8, D),
            f32(rows, D),
            pltpu.SemaphoreType.DMA((K_COUNT,)),
            pltpu.SemaphoreType.DMA((K_COUNT,)),
            pltpu.SemaphoreType.DMA((2 + 2 * subs,)),
            pltpu.SemaphoreType.DMA((2, subs, n - 1)),
            pltpu.SemaphoreType.DMA((2, subs, n - 1)),
            pltpu.SemaphoreType.DMA((2, subs, n - 1)),
            pltpu.SemaphoreType.DMA((2, subs, n - 1)),
        ],
        compiler_params=pltpu.CompilerParams(
            collective_id=0, has_side_effects=True, vmem_limit_bytes=64 * 1024 * 1024 - 65536
        ),
    )(
        field_inputs.reshape(rows, 2 * D),
        field_weight.reshape(1, 2),
        norm_gain.reshape(1, D),
        gates,
        expert_in,
        expert_out,
        tower_in.reshape(D, TOWER),
        tower_out,
        tower_bias.reshape(1, 1),
        labels.reshape(1, rows),
        source_ids.reshape(1, rows),
        task_table,
    )

    misc = small[:, 2 * GROWS :]
    scale = (rows * n) / jnp.sum(misc[:, 5])
    own = ring[1, MISC_AT : MISC_AT + 8]
    gate_grad = small[:, : 2 * GROWS].reshape(2, TASKS, GROWS, D)[:, :, : SEL * (BITS + 1)]
    gate_grad = gate_grad.reshape(2, TASKS, BITS + 1, SEL, D).transpose(0, 4, 1, 3, 2)
    return (
        probs.reshape(rows, 1),
        grads.reshape(rows, 2, D) * scale,
        jnp.sum(own[3:5], axis=1) * scale,
        jnp.sum(misc[:, 0], axis=0) * scale,
        gate_grad.reshape(2, D, TASKS * SEL * (BITS + 1)) * scale,
        ring[0, :GATE_AT].reshape(HALF, H, D).swapaxes(1, 2) * scale,
        ring[1, :GATE_AT].reshape(HALF, H, D) * scale,
        ring[0, GATE_AT : GATE_AT + TOWER].T.reshape(1, D, TOWER) * scale,
        own[1:2, :TOWER] * scale,
        jnp.sum(own[2:3], axis=1) * scale,
    )


def solution(mesh):
    in_specs = (
        P("dp", "section", None),
        P("section"),
        P(),
        P(),
        P("section", None, None),
        P("section", None, None),
        P("section", None, None),
        P("section", None),
        P("section"),
        P("dp", "section"),
        P("dp"),
        P(None, "section"),
    )
    out_specs = (
        P("dp", "section"),
        P("dp", "section", None),
        P("section"),
        P(),
        P(),
        P("section", None, None),
        P("section", None, None),
        P("section", None, None),
        P("section", None),
        P("section"),
    )
    return jax.shard_map(body, mesh=mesh, in_specs=in_specs, out_specs=out_specs, check_vma=False)
```

```python
from functools import partial

import jax
import jax.numpy as jnp
from jax import lax
from jax.experimental import pallas as pl
from jax.experimental.pallas import tpu as pltpu
from jax.sharding import PartitionSpec as P

D = 256
H = 256
E = 16
TASKS = 4
SEL = 4
BITS = 4
TOWER = 128
SOURCES = 32
HALF = E // 2
GROWS = 32
FROWS = 96

STEP_SLOPE = 0.6
ENTROPY_WEIGHT = 0.05
NORM_EPS = 1e-05
GELU_A = 0.7978845608028654
GELU_B = 0.044715

F32 = jnp.float32
BF16 = jnp.bfloat16
MESH = pl.DeviceIdType.MESH

K_W, K_P, K_SM, K_TI, K_UP, K_DOWN, K_TW, K_DX, K_DG, K_DP, K_GO = 0, 2, 4, 8, 12, 16, 20, 24, 26, 27, 30
K_COUNT = 34
GROUP = 2
TILE = 32

GATE_AT = HALF * H
MISC_AT = GATE_AT + 2 * GROWS
SMALL = 2 * GROWS + 8


def split(x):
    hi = x.astype(BF16)
    return hi, (x - hi.astype(F32)).astype(BF16)


def wide(x):
    hi, lo = split(x)
    return jnp.concatenate([hi, lo, hi], axis=1)


def tall(x):
    hi, lo = split(x)
    return jnp.concatenate([hi, hi, lo], axis=0)


def mm(a, b):
    return jnp.dot(a, b, preferred_element_type=F32)


def pair(x):
    k = x.shape[1] // 2
    return jnp.concatenate([x, x[:, :k]], axis=1)


def gelu_pair(x):
    x2 = x * x
    h = 0.5 + 0.5 * jnp.tanh(x * (GELU_A + (GELU_A * GELU_B) * x2))
    g = x * h
    slope = h + g * (1.0 - h) * (2.0 * GELU_A + (6.0 * GELU_A * GELU_B) * x2)
    return g, slope


def rows8(x):
    return jnp.sum(x.reshape(x.shape[0] // 8, 8, x.shape[1]), axis=0)


def over_selectors(v, groups, op):
    parts = [v[k * groups : (k + 1) * groups] for k in range(SEL)]
    return op(op(parts[0], parts[1]), op(parts[2], parts[3]))


def to_selectors(v):
    return jnp.concatenate([v] * SEL, axis=0)


def gate_state(c, groups):
    w = SEL * groups
    zs = [c[w * b : w * b + w] * STEP_SLOPE for b in range(BITS)]
    alpha = c[w * BITS : w * BITS + w]
    ups, downs, sig_p, sig_n = [], [], [], []
    for z in zs:
        e = jnp.exp(-jnp.abs(z))
        tail = jnp.log1p(e)
        ups.append(jnp.minimum(z, 0.0) - tail)
        downs.append(jnp.minimum(-z, 0.0) - tail)
        big = 1.0 / (1.0 + e)
        small = e * big
        sig_p.append(jnp.where(z >= 0.0, big, small))
        sig_n.append(jnp.where(z >= 0.0, small, big))
    low = [(ups[0] if k & 1 else downs[0]) + (ups[1] if k & 2 else downs[1]) for k in range(4)]
    high = [(ups[2] if k & 1 else downs[2]) + (ups[3] if k & 2 else downs[3]) for k in range(4)]
    log_r = [low[j & 3] + high[j >> 2] for j in range(E)]
    r = [jnp.exp(v) for v in log_r]
    top = jnp.exp(alpha - to_selectors(over_selectors(alpha, groups, jnp.maximum)))
    mix = top / to_selectors(over_selectors(top, groups, jnp.add))
    return log_r, r, mix, sig_p, sig_n


def gate_forward(c, groups):
    _, r, mix, _, _ = gate_state(c, groups)
    return [over_selectors(mix * v, groups, jnp.add) for v in r]


def gate_backward(c, dgate, groups):
    log_r, r, mix, sig_p, sig_n = gate_state(c, groups)
    total = jnp.zeros_like(mix)
    on = [jnp.zeros_like(mix) for _ in range(BITS)]
    off = [jnp.zeros_like(mix) for _ in range(BITS)]
    for j in range(E):
        dg = to_selectors(dgate[j])
        total = total + dg * r[j]
        dlog = r[j] * (mix * dg - ENTROPY_WEIGHT * (log_r[j] + 1.0))
        for b in range(BITS):
            if j >> b & 1:
                on[b] = on[b] + dlog
            else:
                off[b] = off[b] + dlog
    dalpha = mix * (total - to_selectors(over_selectors(mix * total, groups, jnp.add)))
    dz = [STEP_SLOPE * (on[b] * sig_n[b] - off[b] * sig_p[b]) for b in range(BITS)]
    used = SEL * (BITS + 1) * groups
    pad = jnp.zeros(((-used) % GROWS, c.shape[1]), F32)
    return jnp.concatenate(dz + [dalpha, pad], axis=0)


def pipeline(stages, count):
    depth = len(stages)

    def emit(step, parity):
        for k, stage in enumerate(stages):
            g = step - k
            if not isinstance(step, int) or 0 <= g < count:
                stage(g, (parity - k) % 2)

    first = depth - 1
    if (count - first) % 2:
        first += 1
    for step in range(first):
        emit(step, step % 2)

    def pair_of_steps(i, carry):
        step = first + 2 * i
        emit(step, first % 2)
        emit(step + 1, (first + 1) % 2)
        return carry

    lax.fori_loop(0, (count - first) // 2, pair_of_steps, 0)
    for step in range(count, count + depth - 1):
        emit(step, step % 2)


def t_dot(a, b):
    ah, al = split(a)
    left = jnp.concatenate([ah, al, ah], axis=0)
    return lax.dot_general(left, tall(b), (((0,), (0,)), ((), ())), preferred_element_type=F32)


def kernel(
    n,
    chunk,
    subs,
    x_ref,
    fw_ref,
    gain_ref,
    wg0_ref,
    wg1_ref,
    win_ref,
    wout_ref,
    tin_ref,
    tout_ref,
    tbias_ref,
    labels_ref,
    ids_ref,
    table_ref,
    ring_ref,
    small_ref,
    ig_ref,
    pred_ref,
    wt_in,
    wt_out,
    w_in,
    w_out,
    a1,
    a2,
    a3,
    d_in,
    d_out,
    rd,
    rv,
    part,
    pre0,
    pre1,
    pre2,
    pre,
    inbox,
    outbox,
    u_t,
    u_n,
    s_t,
    s_n,
    bb,
    k_h,
    k_l,
    g_h,
    g_l,
    f_h,
    f_l,
    acc,
    gt,
    gt0,
    cs,
    dgt,
    dg,
    gb,
    sm,
    smo,
    ti,
    tp,
    tw,
    dp,
    send,
    recv,
    local,
    rs_send,
    rs_recv,
    ag_send,
    ag_recv,
):
    s = lax.axis_index("section")
    x = s // 2
    c = s % 2
    mate = s + 1 - 2 * c
    across = s + 2 - 4 * x
    diag = 3 - s
    R = part.shape[0] // 2
    mine = pl.ds(pl.multiple_of(c * R, R), R)
    theirs = pl.ds(pl.multiple_of((1 - c) * R, R), R)

    pos = lax.axis_index("dp")
    odd = pos % 2
    p = (1 - odd) * (pos // 2) + odd * (n - 1 - pos // 2)

    def ring_id(q):
        far = q // (n // 2)
        return (1 - far) * 2 * q + far * (2 * (n - 1 - q) + 1)

    nbr = [ring_id((p + 1) % n), ring_id((p + n - 1) % n)]

    barrier = pltpu.get_barrier_semaphore()
    for sec in (mate, across, diag):
        pl.semaphore_signal(barrier, inc=1, device_id={"section": sec}, device_id_type=MESH)
    for dev in nbr:
        pl.semaphore_signal(barrier, inc=1, device_id={"dp": dev}, device_id_type=MESH)
    pl.semaphore_wait(barrier, 5)

    def copy(src, dst, k, sec, ks=None):
        return pltpu.make_async_remote_copy(
            src_ref=src,
            dst_ref=dst,
            send_sem=send.at[k if ks is None else ks],
            recv_sem=recv.at[k],
            device_id={"section": sec},
            device_id_type=MESH,
        )

    part[...] = x_ref[:, :D] * fw_ref[0, 0] + x_ref[:, D:] * fw_ref[0, 1]
    to_mate = copy(part.at[theirs], pre0, K_P, mate)
    to_mate.start()
    own = pl.ds(pl.multiple_of(c * HALF * H, HALF * H), HALF * H)
    away = pl.ds(pl.multiple_of((1 - c) * HALF * H, HALF * H), HALF * H)
    swap_in = copy(win_ref, d_in.at[own], K_W, mate)
    swap_out = copy(wout_ref, d_out.at[own], K_W + 1, mate)
    own_in = pltpu.make_async_copy(win_ref, d_in.at[own], local.at[0])
    own_out = pltpu.make_async_copy(wout_ref, d_out.at[own], local.at[1])
    own_in.start()
    own_out.start()
    swap_in.start()
    swap_out.start()

    ids = jnp.broadcast_to(ids_ref[...], (SOURCES, 2 * R))
    hit = ids == lax.broadcasted_iota(jnp.int32, (SOURCES, 2 * R), 0)
    mask = jnp.sum(jnp.where(hit, table_ref[...].astype(F32), 0.0), axis=0, keepdims=True)
    smo[...] = jnp.zeros_like(smo)
    smo[0:1] = labels_ref[...]
    smo[1:2] = mask
    smo[2:3, :TOWER] = tout_ref[...]
    smo[3:4] = jnp.zeros((1, 2 * R), F32) + tbias_ref[0, 0]
    for k in range(2):

        @pl.when(s != 2 + k)
        def _():
            copy(smo, sm.at[s], K_SM + s, 2 + k, K_SM + k).start()
            copy(tin_ref, ti.at[s], K_TI + s, 2 + k, K_TI + k).start()

    to_mate.wait_recv()

    @pl.when(x == 1)
    def _():
        pre2[...] = part[mine] + pre0[...]
        copy(pre2, pre1, K_P + 1, across).start()
        sm[s] = smo[...]
        ti[s] = tin_ref[...]

    own_in.wait()
    own_out.wait()

    def side(w):
        hi, lo = split(w)
        return jnp.concatenate([hi, lo], axis=1)

    def expert(j, count=1):
        return pl.ds(pl.multiple_of(j * H, H), count * H)

    def flip(base):
        def one(e, carry):
            wt_in[base + e] = side(d_in[expert(base + e)].T)
            wt_out[base + e] = side(d_out[expert(base + e)].T)
            return carry

        lax.fori_loop(0, HALF, one, 0)

    def keep_plain():
        def one(j, carry):
            w_in[j] = side(d_in[expert(j)])
            w_out[j] = side(d_out[expert(j)])
            return carry

        lax.fori_loop(0, E, one, 0)

    flip(c * HALF)
    swap_in.wait()
    swap_out.wait()
    flip((1 - c) * HALF)

    tiles = [(e, slice(a, a + TILE)) for e in range(GROUP) for a in range(0, H, TILE)]
    steps = E // GROUP

    def group(ref, g):
        v = ref[pl.ds(g * GROUP, GROUP)]
        return v.reshape(GROUP * v.shape[1], v.shape[2])

    def block(ref, par, e):
        return ref[par, e * H : (e + 1) * H]

    def first_product(weights, right):
        def stage(g, par):
            bb[par] = mm(pair(group(weights, g)), right[...])

        return stage

    @pl.when(x == 0)
    def _():
        copy(pre2, pre1, K_P + 1, across).wait_recv()
        pre_rows = part[mine] + pre0[...] + pre1[...]
        pre[...] = pre_rows
        rho = lax.rsqrt(jnp.mean(pre_rows * pre_rows, axis=1, keepdims=True) + NORM_EPS)
        pooled = pre_rows * rho * gain_ref[...]
        u_n[...] = tall(pooled)
        pooled_t = pooled.T
        acc[...] = pooled_t
        u_t[...] = tall(pooled_t)
        logits = mm(wide(wg0_ref[...]), u_t[...])
        cs[...] = logits
        for j, g in enumerate(gate_forward(logits, TASKS)):
            gt0[j] = g

        def activate(g, par):
            for e, tile in tiles:
                j = g * GROUP + e
                rows = slice(e * H + tile.start, e * H + tile.stop)
                value, slope = gelu_pair(bb[par, rows])
                a1[j, tile] = value
                a2[j, tile] = slope
                g_h[par, rows], g_l[par, rows] = split(value)

        def finish(g, par):
            for e in range(GROUP):
                hi, lo = block(g_h, par, e), block(g_l, par, e)
                j = g * GROUP + e
                a3[j] = mm(pair(wt_out[j]), jnp.concatenate([hi, hi, lo], axis=0))

        pipeline([first_product(wt_in, u_t), activate, finish], steps)

        def stream(t, carry):
            for tile in [slice(a, a + TILE) for a in range(0, D, TILE)]:
                total = acc[tile]
                for j in range(E):
                    total = total + gt0[j, pl.ds(t, 1)] * a3[j, tile]
                outbox[t, tile] = total
            copy(outbox.at[t], inbox.at[t], K_UP + t, across).start()
            return carry

        lax.fori_loop(0, TASKS, stream, 0)
        keep_plain()

    @pl.when(x == 1)
    def _():
        keep_plain()
        d_in[...] = jnp.zeros_like(d_in)
        d_out[...] = jnp.zeros_like(d_out)
        for q in range(TASKS):

            @pl.when(s != q)
            def _():
                copy(smo, sm.at[q], K_SM + q, q).wait_recv()
                copy(tin_ref, ti.at[q], K_TI + q, q).wait_recv()

        def task(t, carry):
            copy(outbox.at[t], inbox.at[t], K_UP + t, across).wait_recv()
            u = inbox[t]
            u_t[...] = tall(u)
            u_n[...] = tall(u.T)
            gate_w = wg1_ref[t]
            logits = mm(wide(gate_w), u_t[...])
            for j, g in enumerate(gate_forward(logits, 1)):
                gt[j] = g
            acc[...] = u

            def activate(g, par):
                for e, tile in tiles:
                    j = g * GROUP + e
                    rows = slice(e * H + tile.start, e * H + tile.stop)
                    value, slope = gelu_pair(bb[par, rows])
                    a1[j, tile] = value
                    a2[j, tile] = slope
                    g_h[par, rows], g_l[par, rows] = split(value * gt[j])

            def finish(g, par):
                right = []
                for e in range(GROUP):
                    hi, lo = block(g_h, par, e), block(g_l, par, e)
                    right += [hi, hi, lo]
                left = jnp.concatenate([pair(wt_out[g * GROUP + e]) for e in range(GROUP)], axis=1)
                acc[...] += mm(left, jnp.concatenate(right, axis=0))

            pipeline([first_product(wt_in, u_t), activate, finish], steps)

            second = acc[...]
            s_t[...] = tall(second)
            s_n[...] = tall(second.T)
            tower = ti[t]
            g, slope = gelu_pair(mm(wide(tower.T), s_t[...]))
            info = sm[t]
            out_col = info[:, :TOWER].T[:, 2:3]
            here = sm[t, :, mine]
            logit = jnp.sum(g * out_col, axis=0, keepdims=True) + here[3:4]
            prob = jax.nn.sigmoid(logit)
            dlogit = here[1:2] * (prob - here[0:1])
            m = dlogit * out_col * slope
            out_grad = jnp.sum(g * dlogit, axis=1, keepdims=True)
            out_row = jnp.broadcast_to(out_grad, (TOWER, TOWER)).T[0:1]
            dy = mm(wide(tower), tall(m))
            tp[t, :TOWER] = mm(wide(m), s_n[...])
            tp[t, TOWER : TOWER + 1] = prob
            tp[t, TOWER + 1 : TOWER + 2] = jnp.concatenate([out_row, jnp.zeros_like(out_row)], axis=1)
            tp[t, TOWER + 2 : TOWER + 3] = dlogit
            tp[t, TOWER + 3 :] = jnp.zeros((5, R), F32)

            @pl.when(t != s)
            def _():
                copy(tp.at[t], tw.at[c], K_TW + c, t, K_TW + t).start()

            @pl.when(t == s)
            def _():
                tw[c] = tp[t]

            s_t[...] = tall(dy)
            s_n[...] = tall(dy.T)
            acc[...] = dy

            def pull(g, par):
                for e in range(GROUP):
                    j = g * GROUP + e
                    gate = gt[j]
                    total = jnp.zeros((8, R), F32)
                    for tile in [slice(a, a + TILE) for a in range(0, H, TILE)]:
                        rows = slice(e * H + tile.start, e * H + tile.stop)
                        value = a1[j, tile]
                        grad = bb[par, rows]
                        total = total + rows8(grad * value)
                        k_h[par, rows], k_l[par, rows] = split(grad * a2[j, tile] * gate)
                        g_h[par, rows], g_l[par, rows] = split(value * gate)
                    dgt[j, 0:1] = jnp.sum(total, axis=0, keepdims=True)

            def spread(g, par):
                right = []
                for e in range(GROUP):
                    hi, lo = block(k_h, par, e), block(k_l, par, e)
                    right += [hi, hi, lo]
                left = jnp.concatenate([pair(w_in[g * GROUP + e]) for e in range(GROUP)], axis=1)
                acc[...] += mm(left, jnp.concatenate(right, axis=0))
                at = expert(g * GROUP, GROUP)
                hi, lo = k_h[par], k_l[par]
                d_in[at] += mm(jnp.concatenate([hi, lo, hi], axis=1), u_n[...])
                hi, lo = g_h[par], g_l[par]
                d_out[at] += mm(jnp.concatenate([hi, lo, hi], axis=1), s_n[...])

            pipeline([first_product(w_out, s_t), pull, spread], steps)
            dc = gate_backward(logits, [dgt[j, 0:1] for j in range(E)], 1)
            dg[pl.ds(pl.multiple_of(t * GROWS, GROWS), GROWS)] = mm(wide(dc), u_n[...])
            outbox[t] = acc[...] + t_dot(gate_w, dc)
            copy(outbox.at[t], inbox.at[t], K_DOWN + t, across).start()
            return carry

        lax.fori_loop(0, TASKS, task, 0)

    @pl.when(x == 0)
    def _():
        total = jnp.zeros((D, R), F32)
        for t in range(TASKS):
            copy(outbox.at[t], inbox.at[t], K_DOWN + t, across).wait_recv()
            total = total + inbox[t]
        acc[...] = total

        def mix(g, par):
            for e in range(GROUP):
                j = g * GROUP + e
                gates = gt0[j]
                sums = [jnp.zeros((8, R), F32) for _ in range(TASKS)]
                for tile in [slice(a, a + TILE) for a in range(0, D, TILE)]:
                    rows = slice(e * D + tile.start, e * D + tile.stop)
                    f = a3[j, tile]
                    mixed = jnp.zeros((TILE, R), F32)
                    for t in range(TASKS):
                        dy = inbox[t, tile]
                        mixed = mixed + gates[t : t + 1] * dy
                        sums[t] = sums[t] + rows8(f * dy)
                    f_h[par, rows], f_l[par, rows] = split(mixed)
                    g_h[par, rows], g_l[par, rows] = split(a1[j, tile])
                for t in range(TASKS):
                    dgt[j, t : t + 1] = jnp.sum(sums[t], axis=0, keepdims=True)

        def products(g, par):
            for e in range(GROUP):
                j = g * GROUP + e
                hi, lo = block(f_h, par, e), block(f_l, par, e)
                bb[par, e * H : (e + 1) * H] = mm(pair(w_out[j]), jnp.concatenate([hi, hi, lo], axis=0))
                g_hi, g_lo = block(g_h, par, e), block(g_l, par, e)
                d_out[expert(j)] = lax.dot_general(
                    jnp.concatenate([g_hi, g_lo, g_hi], axis=1),
                    jnp.concatenate([hi, hi, lo], axis=1),
                    (((1,), (1,)), ((), ())),
                    preferred_element_type=F32,
                )

        def pull(g, par):
            for e, tile in tiles:
                rows = slice(e * H + tile.start, e * H + tile.stop)
                k_h[par, rows], k_l[par, rows] = split(bb[par, rows] * a2[g * GROUP + e, tile])

        def spread(g, par):
            right = []
            for e in range(GROUP):
                hi, lo = block(k_h, par, e), block(k_l, par, e)
                right += [hi, hi, lo]
            left = jnp.concatenate([pair(w_in[g * GROUP + e]) for e in range(GROUP)], axis=1)
            acc[...] += mm(left, jnp.concatenate(right, axis=0))
            hi, lo = k_h[par], k_l[par]
            d_in[expert(g * GROUP, GROUP)] = mm(jnp.concatenate([hi, lo, hi], axis=1), u_n[...])

        pipeline([mix, products, pull, spread], steps)

        dc = gate_backward(cs[...], [dgt[j, :TASKS] for j in range(E)], TASKS)
        grad = mm(wide(dc), u_n[...])
        dg[: FROWS // 2] = grad[: FROWS // 2]
        dg[2 * GROWS : 2 * GROWS + FROWS // 2] = grad[FROWS // 2 :]
        dpool = (acc[...] + t_dot(wg0_ref[...], dc)).T
        pre_rows = pre[...]
        rho = lax.rsqrt(jnp.mean(pre_rows * pre_rows, axis=1, keepdims=True) + NORM_EPS)
        scaled = dpool * gain_ref[...]
        dots = jnp.mean(scaled * pre_rows, axis=1, keepdims=True)
        dp[mine] = rho * scaled - pre_rows * (rho * rho * rho * dots)
        tp[0, 0:1] = jnp.sum(dpool * pre_rows * rho, axis=0, keepdims=True)
        for k, sec in enumerate((mate, across, diag)):
            copy(dp.at[mine], dp.at[mine], K_DP + c, sec, K_DP + k).start()

    gates_own = pl.ds(pl.multiple_of(c * 2 * GROWS, 2 * GROWS), 2 * GROWS)
    gates_away = pl.ds(pl.multiple_of((1 - c) * 2 * GROWS, 2 * GROWS), 2 * GROWS)
    copy(d_in.at[away], rd.at[0, pl.ds(0, HALF * H)], K_DX, mate).start()
    copy(d_out.at[away], rd.at[1, pl.ds(0, HALF * H)], K_DX + 1, mate).start()
    copy(dg.at[gates_away], gb, K_DG, mate).start()

    for half in range(2):

        @pl.when(s != half)
        def _():
            copy(dp.at[pl.ds(half * R, R)], dp.at[pl.ds(half * R, R)], K_DP + half, half).wait_recv()

    for k in range(2):

        @pl.when(s != 2 + k)
        def _():
            copy(tp.at[0], tw.at[k], K_TW + k, s).wait_recv()

    for k in range(2):
        grad = dp[pl.ds(k * R, R)]
        ig_ref[pl.ds(k * R, R), :D] = grad * fw_ref[0, 0]
        ig_ref[pl.ds(k * R, R), D:] = grad * fw_ref[0, 1]
        pred_ref[k : k + 1] = tw[k, TOWER : TOWER + 1]
    rd[1, MISC_AT : MISC_AT + 1] = jnp.where(x == 0, tp[0, 0:1], 0.0)
    rd[1, MISC_AT + 1 : MISC_AT + 3] = tw[0, TOWER + 1 : TOWER + 3] + tw[1, TOWER + 1 : TOWER + 3]
    rd[1, MISC_AT + 3 : MISC_AT + 4] = jnp.sum(x_ref[:, :D] * dp[...], axis=0, keepdims=True)
    rd[1, MISC_AT + 4 : MISC_AT + 5] = jnp.sum(x_ref[:, D:] * dp[...], axis=0, keepdims=True)
    rd[1, MISC_AT + 5 : MISC_AT + 6] = smo[1:2, :R] + smo[1:2, R:]
    rd[1, MISC_AT + 6 : MISC_AT + 8] = jnp.zeros((2, D), F32)
    rd[0, GATE_AT : GATE_AT + TOWER] = tw[0, :TOWER] + tw[1, :TOWER]
    end = n * chunk
    if end > GATE_AT + TOWER:
        rd[0, GATE_AT + TOWER :] = jnp.zeros((end - GATE_AT - TOWER, D), F32)
    rd[1, MISC_AT + 8 :] = jnp.zeros((end - MISC_AT - 8, D), F32)
    copy(dg.at[gates_away], gb, K_DG, mate).wait_recv()
    rd[1, GATE_AT : GATE_AT + 2 * GROWS] = dg[gates_own] + gb[...]
    copy(d_in.at[away], rd.at[0, pl.ds(0, HALF * H)], K_DX, mate).wait_recv()
    copy(d_out.at[away], rd.at[1, pl.ds(0, HALF * H)], K_DX + 1, mate).wait_recv()

    def merge(e, carry):
        at = expert(e)
        rd[0, at] += d_in[expert(c * HALF + e)]
        rd[1, at] += d_out[expert(c * HALF + e)]
        return carry

    lax.fori_loop(0, HALF, merge, 0)

    sub = chunk // subs
    lanes = [(d, k) for d in range(2) for k in range(subs)]

    def at(d, k, q):
        return pl.ds(pl.multiple_of(q * chunk + k * sub, 8), sub)

    def holds(d, step):
        return (p + n - step) % n if d == 0 else (p + step) % n

    def rs(d, k, step, src):
        return pltpu.make_async_remote_copy(
            src_ref=src,
            dst_ref=rv.at[d, k, step],
            send_sem=rs_send.at[d, k, step],
            recv_sem=rs_recv.at[d, k, step],
            device_id={"dp": nbr[d]},
            device_id_type=MESH,
        )

    def ag(d, k, step, src, q):
        return pltpu.make_async_remote_copy(
            src_ref=src,
            dst_ref=ring_ref.at[d, at(d, k, q)],
            send_sem=ag_send.at[d, k, step],
            recv_sem=ag_recv.at[d, k, step],
            device_id={"dp": nbr[d]},
            device_id_type=MESH,
        )

    for d, k in lanes:
        rs(d, k, 0, rd.at[d, at(d, k, holds(d, 0))]).start()

    def reduce_step(step, carry):
        for d, k in lanes:
            rs(d, k, step - 1, rv.at[d, k, step - 1]).wait_recv()
            rv[d, k, step - 1] += rd[d, at(d, k, holds(d, step))]
            rs(d, k, step, rv.at[d, k, step - 1]).start()
        return carry

    lax.fori_loop(1, n - 1, reduce_step, 0)
    last = n - 2
    for d, k in lanes:
        q = holds(d, n - 1)
        rs(d, k, last, rv.at[d, k, last]).wait_recv()
        rv[d, k, last] += rd[d, at(d, k, q)]
        ag(d, k, 0, rv.at[d, k, last], q).start()
        pltpu.make_async_copy(rv.at[d, k, last], ring_ref.at[d, at(d, k, q)], local.at[2 + d * subs + k]).start()

    def gather_step(step, carry):
        for d, k in lanes:
            q = holds(d, step - 1)
            ag(d, k, step - 1, ring_ref.at[d, at(d, k, q)], q).wait_recv()
            ag(d, k, step, ring_ref.at[d, at(d, k, q)], q).start()
        return carry

    lax.fori_loop(1, n - 1, gather_step, 0)
    for d, k in lanes:
        q = holds(d, n - 2)
        ag(d, k, last, ring_ref.at[d, at(d, k, q)], q).wait_recv()
        q = holds(d, n - 1)
        pltpu.make_async_copy(rv.at[d, k, last], ring_ref.at[d, at(d, k, q)], local.at[2 + d * subs + k]).wait()

    piece = ring_ref.at[1, pl.ds(GATE_AT, SMALL)]
    for k, sec in enumerate((mate, across, diag)):
        copy(piece, small_ref.at[s], K_GO + s, sec, K_GO + k).start()
    keep = pltpu.make_async_copy(piece, small_ref.at[s], local.at[0])
    keep.start()

    def sent(step, carry):
        for d, k in lanes:
            rs(d, k, step, rv.at[d, k, step]).wait_send()
            ag(d, k, step, rv.at[d, k, step], 0).wait_send()
        return carry

    lax.fori_loop(0, n - 1, sent, 0)
    to_mate.wait_send()
    for k in range(2):

        @pl.when(s != 2 + k)
        def _():
            copy(smo, sm.at[s], K_SM + s, 2 + k, K_SM + k).wait_send()
            copy(tin_ref, ti.at[s], K_TI + s, 2 + k, K_TI + k).wait_send()

    @pl.when(x == 0)
    def _():
        for t in range(TASKS):
            copy(outbox.at[t], inbox.at[t], K_UP + t, across).wait_send()
        for k, sec in enumerate((mate, across, diag)):
            copy(dp.at[mine], dp.at[mine], K_DP + c, sec, K_DP + k).wait_send()

    @pl.when(x == 1)
    def _():
        copy(pre2, pre1, K_P + 1, across).wait_send()
        for t in range(TASKS):
            copy(outbox.at[t], inbox.at[t], K_DOWN + t, across).wait_send()

            @pl.when(t != s)
            def _():
                copy(tp.at[t], tw.at[c], K_TW + c, t, K_TW + t).wait_send()

    copy(d_in.at[away], rd.at[0, pl.ds(0, HALF * H)], K_DX, mate).wait_send()
    copy(d_out.at[away], rd.at[1, pl.ds(0, HALF * H)], K_DX + 1, mate).wait_send()
    copy(dg.at[gates_away], gb, K_DG, mate).wait_send()
    for k, sec in enumerate((mate, across, diag)):
        copy(piece, small_ref.at[s], K_GO + s, sec, K_GO + k).wait_send()
        copy(piece, small_ref.at[sec], K_GO + sec, sec).wait_recv()
    keep.wait()


def body(
    field_inputs,
    field_weight,
    norm_gain,
    gate_weight,
    expert_in,
    expert_out,
    tower_in,
    tower_out,
    tower_bias,
    labels,
    source_ids,
    task_table,
):
    n = lax.axis_size("dp")
    rows = field_inputs.shape[0]
    half = rows // 2
    subs = 2 if n <= 16 else 1
    unit = n * subs * 8
    chunk = -(-(GATE_AT + TOWER) // unit) * subs * 8
    length = n * chunk

    gates = gate_weight.reshape(2, D, TASKS, SEL, BITS + 1)
    gates0 = gates[0].transpose(3, 2, 1, 0).reshape(TASKS * SEL * (BITS + 1), D)
    gates0 = jnp.pad(gates0, ((0, FROWS - gates0.shape[0]), (0, 0)))
    gates1 = gates[1].transpose(1, 3, 2, 0).reshape(TASKS, SEL * (BITS + 1), D)
    gates1 = jnp.pad(gates1, ((0, 0), (0, GROWS - gates1.shape[1]), (0, 0)))

    vmem = pl.BlockSpec(memory_space=pltpu.VMEM)
    smem = pl.BlockSpec(memory_space=pltpu.SMEM)
    hbm = pl.BlockSpec(memory_space=pl.ANY)

    def bf(*shape):
        return pltpu.VMEM(shape, BF16)

    def f32(*shape):
        return pltpu.VMEM(shape, F32)

    ring, small, grads, probs = pl.pallas_call(
        partial(kernel, n, chunk, subs),
        out_shape=(
            jax.ShapeDtypeStruct((2, length, D), F32),
            jax.ShapeDtypeStruct((TASKS, SMALL, D), F32),
            jax.ShapeDtypeStruct((rows, 2 * D), F32),
            jax.ShapeDtypeStruct((2, half), F32),
        ),
        in_specs=[vmem, smem, vmem, vmem, vmem, hbm, hbm, vmem, vmem, smem, vmem, vmem, vmem],
        out_specs=(hbm, hbm, vmem, vmem),
        scratch_shapes=[
            bf(E, H, 2 * D),
            bf(E, D, 2 * H),
            bf(E, D, 2 * H),
            bf(E, H, 2 * D),
            f32(E, H, half),
            f32(E, H, half),
            f32(E, D, half),
            f32(E * H, D),
            f32(E * H, D),
            f32(2, length, D),
            f32(2, subs, n - 1, chunk // subs, D),
            f32(rows, D),
            f32(half, D),
            f32(half, D),
            f32(half, D),
            f32(half, D),
            f32(TASKS, D, half),
            f32(TASKS, D, half),
            bf(3 * D, half),
            bf(3 * half, D),
            bf(3 * D, half),
            bf(3 * half, D),
            f32(2, GROUP * H, half),
            bf(2, GROUP * H, half),
            bf(2, GROUP * H, half),
            bf(2, GROUP * H, half),
            bf(2, GROUP * H, half),
            bf(2, GROUP * D, half),
            bf(2, GROUP * D, half),
            f32(D, half),
            f32(E, 1, half),
            f32(E, TASKS, half),
            f32(FROWS, half),
            f32(E, TASKS, half),
            f32(TASKS * GROWS, D),
            f32(2 * GROWS, D),
            f32(TASKS, 8, rows),
            f32(8, rows),
            f32(TASKS, D, TOWER),
            f32(TASKS, TOWER + 8, D),
            f32(2, TOWER + 8, D),
            f32(rows, D),
            pltpu.SemaphoreType.DMA((K_COUNT,)),
            pltpu.SemaphoreType.DMA((K_COUNT,)),
            pltpu.SemaphoreType.DMA((2 + 2 * subs,)),
            pltpu.SemaphoreType.DMA((2, subs, n - 1)),
            pltpu.SemaphoreType.DMA((2, subs, n - 1)),
            pltpu.SemaphoreType.DMA((2, subs, n - 1)),
            pltpu.SemaphoreType.DMA((2, subs, n - 1)),
        ],
        compiler_params=pltpu.CompilerParams(
            collective_id=0, has_side_effects=True, vmem_limit_bytes=64 * 1024 * 1024 - 65536
        ),
    )(
        field_inputs.reshape(rows, 2 * D),
        field_weight.reshape(1, 2),
        norm_gain.reshape(1, D),
        gates0,
        gates1,
        expert_in.reshape(HALF * H, D),
        expert_out.reshape(HALF * H, D),
        tower_in.reshape(D, TOWER),
        tower_out,
        tower_bias.reshape(1, 1),
        labels.reshape(1, rows),
        source_ids.reshape(1, rows),
        task_table,
    )

    misc = small[:, 2 * GROWS :]
    scale = (rows * n) / jnp.sum(misc[:, 5])
    own = ring[1, MISC_AT : MISC_AT + 8]
    used = SEL * (BITS + 1)
    grad0 = small[:2, : FROWS // 2].reshape(FROWS, D)[: TASKS * used]
    grad0 = grad0.reshape(BITS + 1, SEL, TASKS, D).transpose(3, 2, 1, 0)
    grad1 = small[2:, : 2 * GROWS].reshape(TASKS, GROWS, D)[:, :used]
    grad1 = grad1.reshape(TASKS, BITS + 1, SEL, D).transpose(3, 0, 2, 1)
    gate_grad = jnp.stack([grad0, grad1])
    return (
        probs.reshape(rows, 1),
        grads.reshape(rows, 2, D) * scale,
        jnp.sum(own[3:5], axis=1) * scale,
        jnp.sum(misc[:, 0], axis=0) * scale,
        gate_grad.reshape(2, D, TASKS * SEL * (BITS + 1)) * scale,
        ring[0, :GATE_AT].reshape(HALF, H, D).swapaxes(1, 2) * scale,
        ring[1, :GATE_AT].reshape(HALF, H, D) * scale,
        ring[0, GATE_AT : GATE_AT + TOWER].T.reshape(1, D, TOWER) * scale,
        own[1:2, :TOWER] * scale,
        jnp.sum(own[2:3], axis=1) * scale,
    )


def solution(mesh):
    in_specs = (
        P("dp", "section", None),
        P("section"),
        P(),
        P(),
        P("section", None, None),
        P("section", None, None),
        P("section", None, None),
        P("section", None),
        P("section"),
        P("dp", "section"),
        P("dp"),
        P(None, "section"),
    )
    out_specs = (
        P("dp", "section"),
        P("dp", "section", None),
        P("section"),
        P(),
        P(),
        P("section", None, None),
        P("section", None, None),
        P("section", None, None),
        P("section", None),
        P("section"),
    )
    return jax.shard_map(body, mesh=mesh, in_specs=in_specs, out_specs=out_specs, check_vma=False)
```

```python
from functools import partial

import jax
import jax.numpy as jnp
from jax import lax
from jax.experimental import pallas as pl
from jax.experimental.pallas import tpu as pltpu
from jax.sharding import PartitionSpec as P

D = 256
H = 256
E = 16
TASKS = 4
SEL = 4
BITS = 4
TOWER = 128
SOURCES = 32
HALF = E // 2
GROWS = 32
FROWS = 96

STEP_SLOPE = 0.6
ENTROPY_WEIGHT = 0.05
NORM_EPS = 1e-05
GELU_A = 0.7978845608028654
GELU_B = 0.044715

F32 = jnp.float32
BF16 = jnp.bfloat16
MESH = pl.DeviceIdType.MESH

K_W, K_P, K_SM, K_TI, K_UP, K_DOWN, K_TW, K_DG, K_DP, K_GO, K_DX = 0, 2, 4, 8, 12, 16, 20, 24, 25, 28, 32
K_COUNT = 48
GROUP = 2
TILE = 32
STEPS = E // GROUP

GATE_AT = TOWER
MISC_AT = GATE_AT + 2 * GROWS
SMALL = MISC_AT + 8
KEPT = SMALL - GATE_AT


def split(x):
    hi = x.astype(BF16)
    return hi, (x - hi.astype(F32)).astype(BF16)


def wide(x):
    hi, lo = split(x)
    return jnp.concatenate([hi, lo, hi], axis=1)


def tall(x):
    hi, lo = split(x)
    return jnp.concatenate([hi, hi, lo], axis=0)


def put(ref, at, x):
    k = x.shape[1]
    hi, lo = split(x)
    ref[*at, :k] = hi
    ref[*at, k:] = lo


def stack(x):
    k = x.shape[1] // 2
    return jnp.concatenate([x[:, :k], x[:, :k], x[:, k:]], axis=0)


def mm(a, b):
    return jnp.dot(a, b, preferred_element_type=F32)


def pair(x):
    k = x.shape[1] // 2
    return jnp.concatenate([x, x[:, :k]], axis=1)


def gelu_pair(x):
    x2 = x * x
    h = 0.5 + 0.5 * jnp.tanh(x * (GELU_A + (GELU_A * GELU_B) * x2))
    g = x * h
    slope = h + g * (1.0 - h) * (2.0 * GELU_A + (6.0 * GELU_A * GELU_B) * x2)
    return g, slope


def rows8(x):
    return jnp.sum(x.reshape(x.shape[0] // 8, 8, x.shape[1]), axis=0)


def over_selectors(v, groups, op):
    parts = [v[k * groups : (k + 1) * groups] for k in range(SEL)]
    return op(op(parts[0], parts[1]), op(parts[2], parts[3]))


def to_selectors(v):
    return jnp.concatenate([v] * SEL, axis=0)


def gate_state(c, groups):
    w = SEL * groups
    zs = [c[w * b : w * b + w] * STEP_SLOPE for b in range(BITS)]
    alpha = c[w * BITS : w * BITS + w]
    ups, downs, sig_p, sig_n = [], [], [], []
    for z in zs:
        e = jnp.exp(-jnp.abs(z))
        tail = jnp.log1p(e)
        ups.append(jnp.minimum(z, 0.0) - tail)
        downs.append(jnp.minimum(-z, 0.0) - tail)
        big = 1.0 / (1.0 + e)
        small = e * big
        sig_p.append(jnp.where(z >= 0.0, big, small))
        sig_n.append(jnp.where(z >= 0.0, small, big))
    low = [(ups[0] if k & 1 else downs[0]) + (ups[1] if k & 2 else downs[1]) for k in range(4)]
    high = [(ups[2] if k & 1 else downs[2]) + (ups[3] if k & 2 else downs[3]) for k in range(4)]
    log_r = [low[j & 3] + high[j >> 2] for j in range(E)]
    r = [jnp.exp(v) for v in log_r]
    top = jnp.exp(alpha - to_selectors(over_selectors(alpha, groups, jnp.maximum)))
    mix = top / to_selectors(over_selectors(top, groups, jnp.add))
    return log_r, r, mix, sig_p, sig_n


def gate_forward(c, groups):
    _, r, mix, _, _ = gate_state(c, groups)
    return [over_selectors(mix * v, groups, jnp.add) for v in r]


def gate_backward(c, dgate, groups):
    log_r, r, mix, sig_p, sig_n = gate_state(c, groups)
    total = jnp.zeros_like(mix)
    on = [jnp.zeros_like(mix) for _ in range(BITS)]
    off = [jnp.zeros_like(mix) for _ in range(BITS)]
    for j in range(E):
        dg = to_selectors(dgate[j])
        total = total + dg * r[j]
        dlog = r[j] * (mix * dg - ENTROPY_WEIGHT * (log_r[j] + 1.0))
        for b in range(BITS):
            if j >> b & 1:
                on[b] = on[b] + dlog
            else:
                off[b] = off[b] + dlog
    dalpha = mix * (total - to_selectors(over_selectors(mix * total, groups, jnp.add)))
    dz = [STEP_SLOPE * (on[b] * sig_n[b] - off[b] * sig_p[b]) for b in range(BITS)]
    used = SEL * (BITS + 1) * groups
    pad = jnp.zeros(((-used) % GROWS, c.shape[1]), F32)
    return jnp.concatenate(dz + [dalpha, pad], axis=0)


def t_dot(a, b):
    ah, al = split(a)
    left = jnp.concatenate([ah, al, ah], axis=0)
    return lax.dot_general(left, tall(b), (((0,), (0,)), ((), ())), preferred_element_type=F32)


def pipeline(stages, count):
    for step in range(count + len(stages) - 1):
        for k, stage in enumerate(stages):
            if 0 <= step - k < count:
                stage(step - k, (step - k) % 2)


def kernel(
    n,
    subs,
    small_rows,
    x_ref,
    fw_ref,
    gain_ref,
    gate_ref,
    win_ref,
    wout_ref,
    tin_ref,
    tout_ref,
    tbias_ref,
    labels_ref,
    ids_ref,
    table_ref,
    o_pred,
    o_ig,
    o_fw,
    o_gain,
    o_gate,
    o_in,
    o_out,
    o_tin,
    o_tout,
    o_bias,
    kept,
    wt_in,
    wt_out,
    w_in,
    w_out,
    a1,
    a2,
    d_in,
    d_out,
    gbuf,
    kbuf,
    kp,
    rd,
    xf,
    part,
    pre0,
    pre1,
    pre2,
    pre,
    inbox,
    outbox,
    u_t,
    u_n,
    s_t,
    s_n,
    bb,
    acc,
    wg,
    gt,
    gt0,
    cs,
    dgt,
    dg,
    gb,
    sm,
    smo,
    ti,
    tp,
    tw,
    dp,
    gain_row,
    columns,
    sb,
    sr,
    so,
    sa,
    sg,
    send,
    recv,
    local,
    ready,
    rs_send,
    rs_recv,
    ag_send,
    ag_recv,
    sr_send,
    sr_recv,
    sa_send,
    sa_recv,
):
    s = lax.axis_index("section")
    x = s // 2
    c = s % 2
    mate = s + 1 - 2 * c
    across = s + 2 - 4 * x
    diag = 3 - s
    R = part.shape[0] // 2
    mine = pl.ds(pl.multiple_of(c * R, R), R)
    theirs = pl.ds(pl.multiple_of((1 - c) * R, R), R)

    me = lax.axis_index("dp")
    odd = me % 2
    p = (1 - odd) * (me // 2) + odd * (n - 1 - me // 2)

    def ring_id(q):
        far = q // (n // 2)
        return (1 - far) * 2 * q + far * (2 * (n - 1 - q) + 1)

    nbr = [ring_id((p + 1) % n), ring_id((p + n - 1) % n)]

    barrier = pltpu.get_barrier_semaphore()
    for sec in (mate, across, diag):
        pl.semaphore_signal(barrier, inc=1, device_id={"section": sec}, device_id_type=MESH)

    def greet(i, carry):
        pl.semaphore_signal(barrier, inc=1, device_id={"dp": (me + i) % n}, device_id_type=MESH)
        return carry

    lax.fori_loop(1, n, greet, 0)
    fields = [pltpu.make_async_copy(x_ref.at[:, f], xf.at[f], local.at[2 + f]) for f in range(2)]
    for f in fields:
        f.start()
    own = pl.ds(pl.multiple_of(c * HALF * H, HALF * H), HALF * H)
    own_in = pltpu.make_async_copy(win_ref, d_in.at[own], local.at[0])
    own_out = pltpu.make_async_copy(wout_ref, d_out.at[own], local.at[1])
    own_in.start()
    own_out.start()
    pl.semaphore_wait(barrier, 3 + n - 1)

    def copy(src, dst, k, sec, ks=None):
        return pltpu.make_async_remote_copy(
            src_ref=src,
            dst_ref=dst,
            send_sem=send.at[k if ks is None else ks],
            recv_sem=recv.at[k],
            device_id={"section": sec},
            device_id_type=MESH,
        )

    def expert(j, count=1):
        return pl.ds(pl.multiple_of(j * H, H), count * H)

    for f in fields:
        f.wait()
    part[...] = xf[0] * fw_ref[0, 0] + xf[1] * fw_ref[0, 1]
    to_mate = copy(part.at[theirs], pre0, K_P, mate)
    to_mate.start()
    swap_in = copy(win_ref, d_in.at[own], K_W, mate)
    swap_out = copy(wout_ref, d_out.at[own], K_W + 1, mate)
    swap_in.start()
    swap_out.start()

    ids = ids_ref[...]
    mask = jnp.zeros(ids.shape, F32)
    for q in range(SOURCES):
        mask = mask + jnp.where(ids == q, table_ref[0, q].astype(F32), 0.0)
    smo[...] = jnp.zeros_like(smo)
    smo[0:1] = labels_ref[...]
    smo[1:2] = mask
    smo[2:3, :TOWER] = tout_ref[...]
    smo[3:4] = jnp.zeros((1, 2 * R), F32) + tbias_ref[0, 0]
    for k in range(2):

        @pl.when(s != 2 + k)
        def _():
            copy(smo, sm.at[s], K_SM + s, 2 + k, K_SM + k).start()
            copy(tin_ref, ti.at[s], K_TI + s, 2 + k, K_TI + k).start()

    to_mate.wait_recv()

    @pl.when(x == 1)
    def _():
        pre2[...] = part[mine] + pre0[...]
        copy(pre2, pre1, K_P + 1, across).start()
        sm[s] = smo[...]
        ti[s] = tin_ref[...]

    wg[...] = jnp.zeros_like(wg)

    @pl.when(x == 0)
    def _():
        def order(t, carry):
            for sel in range(SEL):
                for e in range(BITS + 1):
                    row = t * (SEL * (BITS + 1)) + sel * (BITS + 1) + e
                    wg[pl.ds((e * SEL + sel) * TASKS + t, 1)] = gate_ref[0, pl.ds(row, 1)]
            return carry

        lax.fori_loop(0, TASKS, order, 0)

    @pl.when(x == 1)
    def _():
        def order(t, carry):
            for sel in range(SEL):
                for e in range(BITS + 1):
                    row = t * (SEL * (BITS + 1)) + sel * (BITS + 1) + e
                    wg[pl.ds(t * GROWS + e * SEL + sel, 1)] = gate_ref[1, pl.ds(row, 1)]
            return carry

        lax.fori_loop(0, TASKS, order, 0)

    own_in.wait()
    own_out.wait()

    def keep_plain(e, carry):
        put(w_in.at[e], (slice(None),), d_in[expert(e)])
        put(w_out.at[e], (slice(None),), d_out[expert(e)])
        return carry

    def keep_flipped(e, carry):
        put(wt_in.at[e], (slice(None),), d_in[expert(e)].T)
        put(wt_out.at[e], (slice(None),), d_out[expert(e)].T)
        return carry

    lax.fori_loop(c * HALF, c * HALF + HALF, keep_plain, 0)
    swap_in.wait()
    swap_out.wait()
    lax.fori_loop((1 - c) * HALF, (1 - c) * HALF + HALF, keep_plain, 0)

    def rows_of(size):
        return [slice(a, a + TILE) for a in range(0, size, TILE)]

    def shifted(tile, e):
        return slice(e * H + tile.start, e * H + tile.stop)

    @pl.when(x == 0)
    def _():
        copy(pre2, pre1, K_P + 1, across).wait_recv()
        pre_rows = part[mine] + pre0[...] + pre1[...]
        pre[...] = pre_rows
        rho = lax.rsqrt(jnp.mean(pre_rows * pre_rows, axis=1, keepdims=True) + NORM_EPS)
        pooled = pre_rows * rho * gain_ref[...]
        acc[...] = pooled
        u_n[0] = tall(pooled)
        u_t[...] = tall(pooled.T)
        logits = mm(wide(wg[:FROWS]), u_t[...])
        cs[...] = logits
        gates = gate_forward(logits, TASKS)
        for j, g in enumerate(gates):
            gt0[j] = g

        def first(g, par):
            left = jnp.concatenate([u_n[0, :R], u_n[0, 2 * R :], u_n[0, :R]], axis=1)
            for e in range(GROUP):
                bb[par, e * H : (e + 1) * H] = mm(left, stack(w_in[g * GROUP + e]))

        def activate(g, par):
            for e in range(GROUP):
                j = g * GROUP + e
                for tile in rows_of(R):
                    value, slope = gelu_pair(bb[par, shifted(tile, e)])
                    a1[shifted(tile, j)] = value
                    a2[j, tile] = slope
                    put(gbuf, (j, tile), value)

        def finish(g, par):
            for e in range(GROUP):
                j = g * GROUP + e
                d_in[expert(j)] = mm(pair(gbuf[j]), stack(w_out[j]))

        pipeline([first, activate, finish], STEPS)
        columns[...] = jnp.concatenate(gates, axis=0).T

        for t in range(TASKS):

            def mix(i, carry):
                tile = pl.ds(pl.multiple_of(i * TILE, TILE), TILE)
                cols = columns[tile]
                total = acc[tile]
                for j in range(E):
                    rows = pl.ds(pl.multiple_of(j * R + i * TILE, TILE), TILE)
                    total = total + cols[:, j * TASKS + t : j * TASKS + t + 1] * d_in[rows]
                outbox[t, tile] = total
                return carry

            lax.fori_loop(0, R // TILE, mix, 0)
            copy(outbox.at[t], inbox.at[t], K_UP + t, across).start()

        def flip(j, carry):
            value = a1[expert(j)].T
            a1[expert(j)] = value
            put(gbuf.at[j], (slice(None),), value)
            a2[j] = a2[j].T
            d_in[expert(j)] = d_in[expert(j)].T
            return carry

        lax.fori_loop(0, E, flip, 0)
        d_out[...] = jnp.zeros_like(d_out)
        acc[...] = jnp.zeros_like(acc)

    @pl.when(x == 1)
    def _():
        lax.fori_loop(0, E, keep_flipped, 0)
        for q in range(TASKS):

            @pl.when(s != q)
            def _():
                copy(smo, sm.at[q], K_SM + q, q).wait_recv()
                copy(tin_ref, ti.at[q], K_TI + q, q).wait_recv()

        def keep(k, t):
            return pltpu.make_async_copy((gbuf, kbuf)[k], kept.at[:, k * TASKS + t], local.at[4 + k])

        def task(t, carry):
            copy(outbox.at[t], inbox.at[t], K_UP + t, across).wait_recv()
            u = inbox[t]
            u_n[t] = tall(u)
            flipped = u.T
            u_t[...] = tall(flipped)
            acc[...] = flipped
            gate_rows = pl.ds(pl.multiple_of(t * GROWS, GROWS), GROWS)
            logits = mm(wide(wg[gate_rows]), u_t[...])
            for j, g in enumerate(gate_forward(logits, 1)):
                gt[j] = g

            @pl.when(t > 0)
            def _():
                keep(0, t).wait()

            def first(g, par):
                left = wt_in[g * GROUP : (g + 1) * GROUP].reshape(GROUP * H, 2 * D)
                bb[par] = mm(pair(left), u_t[...])

            def activate(g, par):
                for e in range(GROUP):
                    j = g * GROUP + e
                    for tile in rows_of(H):
                        value, slope = gelu_pair(bb[par, shifted(tile, e)])
                        a1[shifted(tile, j)] = value
                        a2[j, tile] = slope
                        put(gbuf, (j, tile), value * gt[j])

            def finish(g, par):
                js = range(g * GROUP, (g + 1) * GROUP)
                left = jnp.concatenate([pair(wt_out[j]) for j in js], axis=1)
                acc[...] += mm(left, jnp.concatenate([stack(gbuf[j]) for j in js], axis=0))

            pipeline([first, activate, finish], STEPS)
            keep(0, t).start()

            second = acc[...]
            s_t[...] = tall(second)
            natural = tall(second.T)
            tower = ti[t]
            g, slope = gelu_pair(mm(wide(tower.T), s_t[...]))
            info = sm[t]
            out_col = info[:, :TOWER].T[:, 2:3]
            here = sm[t, :, mine]
            logit = jnp.sum(g * out_col, axis=0, keepdims=True) + here[3:4]
            prob = jax.nn.sigmoid(logit)
            dlogit = here[1:2] * (prob - here[0:1])
            m = dlogit * out_col * slope
            out_grad = jnp.sum(g * dlogit, axis=1, keepdims=True)
            out_row = jnp.broadcast_to(out_grad, (TOWER, TOWER)).T[0:1]
            dy = mm(wide(tower), tall(m))
            tp[t, :TOWER] = mm(wide(m), natural)
            tp[t, TOWER : TOWER + 1] = prob
            tp[t, TOWER + 1 : TOWER + 2] = jnp.concatenate([out_row, jnp.zeros_like(out_row)], axis=1)
            tp[t, TOWER + 2 : TOWER + 3] = dlogit
            tp[t, TOWER + 3 :] = jnp.zeros((5, R), F32)

            @pl.when(t != s)
            def _():
                copy(tp.at[t], tw.at[c], K_TW + c, t, K_TW + t).start()

            @pl.when(t == s)
            def _():
                tw[c] = tp[t]

            s_t[...] = tall(dy)
            s_n[t] = tall(dy.T)
            acc[...] = dy

            @pl.when(t > 0)
            def _():
                keep(1, t).wait()

            def back(g, par):
                left = w_out[g * GROUP : (g + 1) * GROUP].reshape(GROUP * H, 2 * D)
                bb[par] = mm(pair(left), s_t[...])

            def pull(g, par):
                for e in range(GROUP):
                    j = g * GROUP + e
                    total = jnp.zeros((8, R), F32)
                    for tile in rows_of(H):
                        grad = bb[par, shifted(tile, e)]
                        total = total + rows8(grad * a1[shifted(tile, j)])
                        put(kbuf, (j, tile), grad * a2[j, tile] * gt[j])
                    dgt[j, 0:1] = jnp.sum(total, axis=0, keepdims=True)

            def spread(g, par):
                js = range(g * GROUP, (g + 1) * GROUP)
                left = jnp.concatenate([pair(w_in[j]) for j in js], axis=1)
                acc[...] += mm(left, jnp.concatenate([stack(kbuf[j]) for j in js], axis=0))

            pipeline([back, pull, spread], STEPS)
            keep(1, t).start()
            dc = gate_backward(logits, [dgt[j, 0:1] for j in range(E)], 1)
            outbox[t] = acc[...] + t_dot(wg[gate_rows], dc)
            copy(outbox.at[t], inbox.at[t], K_DOWN + t, across).start()
            dg[gate_rows] = mm(wide(dc), u_n[t])
            return carry

        lax.fori_loop(0, TASKS, task, 0)
        keep(0, 0).wait()
        keep(1, 0).wait()

    def give(e):
        j = (1 - c) * HALF + e
        return (
            copy(d_in.at[expert(j)], rd.at[0, expert(e)], K_DX + e, mate),
            copy(d_out.at[expert(j)], rd.at[1, expert(e)], K_DX + HALF + e, mate),
        )

    @pl.when(x == 1)
    def _():
        base = (1 - c) * HALF

        def fetch(i):
            j = (base + i) % E
            return pltpu.make_async_copy(
                kept.at[j], wt_in.at[pl.ds((i % 2) * 2 * TASKS, 2 * TASKS)], local.at[4 + i % 2]
            )

        fetch(0).start()

        def one(i, carry):
            fetch(i).wait()

            @pl.when(i < E - 1)
            def _():
                fetch(i + 1).start()

            at = expert((base + i) % E)
            for k, (grad, right) in enumerate(((d_out, s_n), (d_in, u_n))):
                left = [pair(wt_in[(i % 2) * 2 * TASKS + k * TASKS + t]) for t in range(TASKS)]
                grad[at] = mm(jnp.concatenate(left, axis=1), right[...].reshape(3 * TASKS * R, D))

            @pl.when(i < HALF)
            def _():
                for move in give(i):
                    move.start()

            return carry

        lax.fori_loop(0, E, one, 0)

    @pl.when(x == 0)
    def _():
        def arrive(t, carry):
            copy(outbox.at[t], inbox.at[t], K_DOWN + t, across).wait_recv()
            acc[...] += inbox[t]

            def one(j, inner):
                gate = gt0[j, pl.ds(t, 1)]
                total = jnp.zeros((8, R), F32)
                for tile in rows_of(D):
                    dy = inbox[t, tile]
                    rows = pl.ds(pl.multiple_of(j * D + tile.start, TILE), TILE)
                    total = total + rows8(d_in[rows] * dy)
                    d_out[rows] += gate * dy
                dgt[j, pl.ds(t, 1)] = jnp.sum(total, axis=0, keepdims=True)
                return inner

            lax.fori_loop(0, E, one, 0)
            return carry

        lax.fori_loop(0, TASKS - 1, arrive, 0)
        last = TASKS - 1
        copy(outbox.at[last], inbox.at[last], K_DOWN + last, across).wait_recv()
        acc[...] += inbox[last]

        def one(j, inner):
            gate = gt0[j, last : last + 1]
            total = jnp.zeros((8, R), F32)
            for tile in rows_of(D):
                dy = inbox[last, tile]
                rows = pl.ds(pl.multiple_of(j * D + tile.start, TILE), TILE)
                total = total + rows8(d_in[rows] * dy)
                put(kbuf.at[j], (tile,), d_out[rows] + gate * dy)
            dgt[j, last : last + 1] = jnp.sum(total, axis=0, keepdims=True)
            return inner

        lax.fori_loop(0, E, one, 0)

        def half(h, carry):
            base = ((1 - c) * (1 - h) + c * h) * HALF

            def products(g, par):
                for e in range(GROUP):
                    j = base + g * GROUP + e
                    mixed = kbuf[j]
                    bb[par, e * H : (e + 1) * H] = mm(pair(w_out[j]), stack(mixed))
                    right = jnp.concatenate([mixed[:, :R], mixed[:, :R], mixed[:, R:]], axis=1)
                    d_out[expert(j)] = lax.dot_general(
                        pair(gbuf[j]), right, (((1,), (1,)), ((), ())), preferred_element_type=F32
                    )

            def pull(g, par):
                for e in range(GROUP):
                    for tile in rows_of(H):
                        rows = shifted(tile, e)
                        put(kp, (par, rows), bb[par, rows] * a2[base + g * GROUP + e, tile])

            def spread(g, par):
                left = jnp.concatenate([pair(w_in[base + g * GROUP + e]) for e in range(GROUP)], axis=1)
                right = [stack(kp[par, e * H : (e + 1) * H]) for e in range(GROUP)]
                acc[...] += mm(left, jnp.concatenate(right, axis=0))
                d_in[expert(base + g * GROUP, GROUP)] = mm(pair(kp[par]), u_n[0])

            pipeline([products, pull, spread], HALF // GROUP)

            @pl.when(h == 0)
            def _():
                for e in range(HALF):
                    for move in give(e):
                        move.start()

            return carry

        lax.fori_loop(0, 2, half, 0)

    chunk = HALF * H // n
    sub = chunk // subs
    lanes = [(d, k) for d in range(2) for k in range(subs)]

    def at(k, q):
        return pl.ds(pl.multiple_of(q * chunk + k * sub, 8), sub)

    def holds(d, step):
        return (p + n - step) % n if d == 0 else (p + step) % n

    def slot(d, k, step):
        return pl.ds(pl.multiple_of(((d * subs + k) * (n - 1) + step) * sub, 8), sub)

    def rs(d, k, step, src):
        return pltpu.make_async_remote_copy(
            src_ref=src,
            dst_ref=a1.at[slot(d, k, step)],
            send_sem=rs_send.at[d, k, step],
            recv_sem=rs_recv.at[d, k, step],
            device_id={"dp": nbr[d]},
            device_id_type=MESH,
        )

    results = (o_in, o_out)

    def ag(d, k, step, src, q):
        return pltpu.make_async_remote_copy(
            src_ref=src,
            dst_ref=results[d].at[at(k, q)],
            send_sem=ag_send.at[d, k, step],
            recv_sem=ag_recv.at[d, k, step],
            device_id={"dp": nbr[d]},
            device_id_type=MESH,
        )

    def merge(i, carry):
        e = (p * chunk // H + i) % HALF
        mine_in, mine_out = give(e)
        mine_in.wait_recv()
        mine_out.wait_recv()
        rows = expert(e)
        rd[0, rows] = (rd[0, rows] + d_in[expert(c * HALF + e)]).T
        rd[1, rows] += d_out[expert(c * HALF + e)]
        return carry

    for dev in nbr:
        pl.semaphore_signal(ready, inc=1, device_id={"dp": dev}, device_id_type=MESH)
    merge(0, 0)
    pl.semaphore_wait(ready, 2)
    for d, k in lanes:
        rs(d, k, 0, rd.at[d, at(k, holds(d, 0))]).start()
    lax.fori_loop(1, HALF, merge, 0)

    def reduce_step(step, carry):
        for d, k in lanes:
            rs(d, k, step - 1, a1.at[slot(d, k, step - 1)]).wait_recv()
            a1[slot(d, k, step - 1)] += rd[d, at(k, holds(d, step))]
            rs(d, k, step, a1.at[slot(d, k, step - 1)]).start()
        return carry

    gates_own = pl.ds(pl.multiple_of(c * 2 * GROWS, 2 * GROWS), 2 * GROWS)
    gates_away = pl.ds(pl.multiple_of((1 - c) * 2 * GROWS, 2 * GROWS), 2 * GROWS)
    gain_row[...] = jnp.zeros_like(gain_row)

    @pl.when(x == 0)
    def _():
        dc = gate_backward(cs[...], [dgt[j, :TASKS] for j in range(E)], TASKS)
        dpool = (acc[...] + t_dot(wg[:FROWS], dc)).T
        pre_rows = pre[...]
        rho = lax.rsqrt(jnp.mean(pre_rows * pre_rows, axis=1, keepdims=True) + NORM_EPS)
        scaled = dpool * gain_ref[...]
        dots = jnp.mean(scaled * pre_rows, axis=1, keepdims=True)
        dp[mine] = rho * scaled - pre_rows * (rho * rho * rho * dots)
        for k, sec in enumerate((mate, across, diag)):
            copy(dp.at[mine], dp.at[mine], K_DP + c, sec, K_DP + k).start()
        gain_row[0:1] = jnp.sum(dpool * pre_rows * rho, axis=0, keepdims=True)
        grad = mm(wide(dc), u_n[0])
        dg[: FROWS // 2] = grad[: FROWS // 2]
        dg[2 * GROWS : 2 * GROWS + FROWS // 2] = grad[FROWS // 2 :]

    gates_move = copy(dg.at[gates_away], gb, K_DG, mate)
    gates_move.start()
    lax.fori_loop(1, 2, reduce_step, 0)

    for half_no in range(2):

        @pl.when(s != half_no)
        def _():
            rows = pl.ds(half_no * R, R)
            copy(dp.at[rows], dp.at[rows], K_DP + half_no, half_no).wait_recv()

    for k in range(2):

        @pl.when(s != 2 + k)
        def _():
            copy(tp.at[0], tw.at[k], K_TW + k, s).wait_recv()

    gates_move.wait_recv()
    sb[:TOWER] = tw[0, :TOWER] + tw[1, :TOWER]
    sb[GATE_AT:MISC_AT] = dg[gates_own] + gb[...]
    sb[MISC_AT : MISC_AT + 1] = gain_row[0:1]
    sb[MISC_AT + 1 : MISC_AT + 3] = tw[0, TOWER + 1 : TOWER + 3] + tw[1, TOWER + 1 : TOWER + 3]
    for f in range(2):
        sb[MISC_AT + 3 + f : MISC_AT + 4 + f] = jnp.sum(xf[f] * dp[...], axis=0, keepdims=True)
    sb[MISC_AT + 5 : MISC_AT + 6] = smo[1:2, :R] + smo[1:2, R:]
    sb[MISC_AT + 6 :] = jnp.zeros((sb.shape[0] - MISC_AT - 6, D), F32)

    def block(q):
        return pl.ds(pl.multiple_of(q * small_rows, 8), small_rows)

    def scatter(i):
        to = (me + i) % n
        return pltpu.make_async_remote_copy(
            src_ref=sb.at[block(to)],
            dst_ref=sr.at[me],
            send_sem=sr_send.at[i],
            recv_sem=sr_recv.at[me],
            device_id={"dp": to},
            device_id_type=MESH,
        )

    def scattered(i):
        by = (me + i) % n
        return pltpu.make_async_remote_copy(
            src_ref=sb.at[block(me)],
            dst_ref=sr.at[by],
            send_sem=sr_send.at[i],
            recv_sem=sr_recv.at[by],
            device_id={"dp": by},
            device_id_type=MESH,
        )

    def spread_sum(i):
        return pltpu.make_async_remote_copy(
            src_ref=so,
            dst_ref=sa.at[block(me)],
            send_sem=sa_send.at[i],
            recv_sem=sa_recv.at[me],
            device_id={"dp": (me + i) % n},
            device_id_type=MESH,
        )

    def gathered(i):
        by = (me + i) % n
        return pltpu.make_async_remote_copy(
            src_ref=so,
            dst_ref=sa.at[block(by)],
            send_sem=sa_send.at[i],
            recv_sem=sa_recv.at[by],
            device_id={"dp": by},
            device_id_type=MESH,
        )

    def each(act):
        def one(i, carry):
            act(i)
            return carry

        lax.fori_loop(1, n, one, 0)

    each(lambda i: scatter(i).start())
    lax.fori_loop(2, 4, reduce_step, 0)
    so[...] = sb[block(me)]

    def take(i):
        scattered(i).wait_recv()
        so[...] += sr[(me + i) % n]

    each(take)
    sa[block(me)] = so[...]
    each(lambda i: spread_sum(i).start())
    lax.fori_loop(4, 6, reduce_step, 0)
    each(lambda i: gathered(i).wait_recv())
    piece = sa.at[pl.ds(GATE_AT, KEPT)]
    for k, sec in enumerate((mate, across, diag)):
        copy(piece, sg.at[s], K_GO + s, sec, K_GO + k).start()
    sg[s] = sa[GATE_AT:SMALL]
    lax.fori_loop(6, n - 1, reduce_step, 0)
    for sec in (mate, across, diag):
        copy(piece, sg.at[sec], K_GO + sec, sec).wait_recv()
    misc = KEPT - 8
    count = sum(sg[q, misc + 5 : misc + 6] for q in range(TASKS))
    scale = float(2 * R * n) / jnp.sum(count, axis=1, keepdims=True)

    last = n - 2
    for d, k in lanes:
        q = holds(d, n - 1)
        rs(d, k, last, a1.at[slot(d, k, last)]).wait_recv()
        a1[slot(d, k, last)] = (a1[slot(d, k, last)] + rd[d, at(k, q)]) * scale
        ag(d, k, 0, a1.at[slot(d, k, last)], q).start()
        pltpu.make_async_copy(a1.at[slot(d, k, last)], results[d].at[at(k, q)], local.at[6 + d * subs + k]).start()

    for f in range(2):
        xf[f] = dp[...] * (scale * fw_ref[0, f])
        pltpu.make_async_copy(xf.at[f], o_ig.at[:, f], local.at[2 + f]).start()
    for k in range(2):
        o_pred[:, k * R : (k + 1) * R] = tw[k, TOWER : TOWER + 1]
    for f in range(2):
        o_fw[0, f] = jnp.sum(sa[MISC_AT + 3 + f : MISC_AT + 4 + f] * scale)
    o_bias[0, 0] = jnp.sum(sa[MISC_AT + 2 : MISC_AT + 3] * scale)
    o_gain[...] = (sg[0, misc : misc + 1] + sg[1, misc : misc + 1]) * scale
    o_tout[...] = sa[MISC_AT + 1 : MISC_AT + 2, :TOWER] * scale
    o_tin[...] = (sa[:TOWER] * scale).T

    def order(t, carry):
        for sel in range(SEL):
            for e in range(BITS + 1):
                row = t * (SEL * (BITS + 1)) + sel * (BITS + 1) + e
                at0 = (e * SEL + sel) * TASKS
                cut = FROWS // 2
                o_gate[0, pl.ds(row, 1)] = sg[at0 // cut, pl.ds(at0 % cut + t, 1)] * scale
                o_gate[1, pl.ds(row, 1)] = sg[2 + t // 2, pl.ds((t % 2) * GROWS + e * SEL + sel, 1)] * scale
        return carry

    lax.fori_loop(0, TASKS, order, 0)

    def gather_step(step, carry):
        for d, k in lanes:
            q = holds(d, step - 1)
            ag(d, k, step - 1, results[d].at[at(k, q)], q).wait_recv()
            ag(d, k, step, results[d].at[at(k, q)], q).start()
        return carry

    lax.fori_loop(1, n - 1, gather_step, 0)
    for d, k in lanes:
        q = holds(d, n - 2)
        ag(d, k, last, results[d].at[at(k, q)], q).wait_recv()
        q = holds(d, n - 1)
        pltpu.make_async_copy(a1.at[slot(d, k, last)], results[d].at[at(k, q)], local.at[6 + d * subs + k]).wait()

    def sent(step, carry):
        for d, k in lanes:
            rs(d, k, step, a1.at[slot(d, k, step)]).wait_send()
            ag(d, k, step, a1.at[slot(d, k, step)], 0).wait_send()
        return carry

    lax.fori_loop(0, n - 1, sent, 0)
    each(lambda i: scatter(i).wait_send())
    each(lambda i: spread_sum(i).wait_send())
    to_mate.wait_send()
    gates_move.wait_send()
    for e in range(HALF):
        for move in give(e):
            move.wait_send()
    for k in range(2):

        @pl.when(s != 2 + k)
        def _():
            copy(smo, sm.at[s], K_SM + s, 2 + k, K_SM + k).wait_send()
            copy(tin_ref, ti.at[s], K_TI + s, 2 + k, K_TI + k).wait_send()

    @pl.when(x == 0)
    def _():
        for t in range(TASKS):
            copy(outbox.at[t], inbox.at[t], K_UP + t, across).wait_send()
        for k, sec in enumerate((mate, across, diag)):
            copy(dp.at[mine], dp.at[mine], K_DP + c, sec, K_DP + k).wait_send()

    @pl.when(x == 1)
    def _():
        copy(pre2, pre1, K_P + 1, across).wait_send()
        for t in range(TASKS):
            copy(outbox.at[t], inbox.at[t], K_DOWN + t, across).wait_send()

            @pl.when(t != s)
            def _():
                copy(tp.at[t], tw.at[c], K_TW + c, t, K_TW + t).wait_send()

    for k, sec in enumerate((mate, across, diag)):
        copy(piece, sg.at[s], K_GO + s, sec, K_GO + k).wait_send()
    for f in range(2):
        pltpu.make_async_copy(xf.at[f], o_ig.at[:, f], local.at[2 + f]).wait()


def body(
    field_inputs,
    field_weight,
    norm_gain,
    gate_weight,
    expert_in,
    expert_out,
    tower_in,
    tower_out,
    tower_bias,
    labels,
    source_ids,
    task_table,
):
    n = lax.axis_size("dp")
    rows = field_inputs.shape[0]
    half = rows // 2
    subs = 2
    small_rows = -(-SMALL // (8 * n)) * 8
    used = TASKS * SEL * (BITS + 1)

    vmem = pl.BlockSpec(memory_space=pltpu.VMEM)
    smem = pl.BlockSpec(memory_space=pltpu.SMEM)
    hbm = pl.BlockSpec(memory_space=pl.ANY)

    def bf(*shape):
        return pltpu.VMEM(shape, BF16)

    def f32(*shape):
        return pltpu.VMEM(shape, F32)

    def out(*shape):
        return jax.ShapeDtypeStruct(shape, F32)

    dma = pltpu.SemaphoreType.DMA
    pred, ig, fw, gain, gate, d_in, d_out, tin, tout, bias, _ = pl.pallas_call(
        partial(kernel, n, subs, small_rows),
        out_shape=(
            out(1, rows),
            out(rows, 2, D),
            out(1, 2),
            out(1, D),
            out(2, used, D),
            out(HALF * H, D),
            out(HALF * H, D),
            out(D, TOWER),
            out(1, TOWER),
            out(1, 1),
            jax.ShapeDtypeStruct((E, 2 * TASKS, H, 2 * half), BF16),
        ),
        in_specs=[hbm, smem, vmem, vmem, hbm, hbm, vmem, vmem, smem, vmem, vmem, smem],
        out_specs=(vmem, hbm, smem, vmem, vmem, hbm, hbm, vmem, vmem, smem, hbm),
        scratch_shapes=[
            bf(E, H, 2 * D),
            bf(E, D, 2 * H),
            bf(E, D, 2 * H),
            bf(E, H, 2 * D),
            f32(E * H, half),
            f32(E, H, half),
            f32(E * H, D),
            f32(E * H, D),
            bf(E, H, 2 * half),
            bf(E, H, 2 * half),
            bf(2, GROUP * H, 2 * half),
            f32(2, HALF * H, D),
            f32(2, rows, D),
            f32(rows, D),
            f32(half, D),
            f32(half, D),
            f32(half, D),
            f32(half, D),
            f32(TASKS, D, half),
            f32(TASKS, D, half),
            bf(3 * D, half),
            bf(TASKS, 3 * half, D),
            bf(3 * D, half),
            bf(TASKS, 3 * half, D),
            f32(2, GROUP * H, half),
            f32(D, half),
            f32(TASKS * GROWS, D),
            f32(E, 1, half),
            f32(E, TASKS, half),
            f32(FROWS, half),
            f32(E, TASKS, half),
            f32(TASKS * GROWS, D),
            f32(2 * GROWS, D),
            f32(TASKS, 8, rows),
            f32(8, rows),
            f32(TASKS, D, TOWER),
            f32(TASKS, TOWER + 8, D),
            f32(2, TOWER + 8, D),
            f32(rows, D),
            f32(8, D),
            f32(half, E * TASKS),
            f32(n * small_rows, D),
            f32(n, small_rows, D),
            f32(small_rows, D),
            f32(n * small_rows, D),
            f32(TASKS, KEPT, D),
            dma((K_COUNT,)),
            dma((K_COUNT,)),
            dma((6 + 2 * subs,)),
            pltpu.SemaphoreType.REGULAR,
            dma((2, subs, n - 1)),
            dma((2, subs, n - 1)),
            dma((2, subs, n - 1)),
            dma((2, subs, n - 1)),
            dma((n,)),
            dma((n,)),
            dma((n,)),
            dma((n,)),
        ],
        compiler_params=pltpu.CompilerParams(
            collective_id=0, has_side_effects=True, vmem_limit_bytes=64 * 1024 * 1024 - 65536
        ),
    )(
        field_inputs,
        field_weight.reshape(1, 2),
        norm_gain.reshape(1, D),
        gate_weight.swapaxes(1, 2),
        expert_in.reshape(HALF * H, D),
        expert_out.reshape(HALF * H, D),
        tower_in.reshape(D, TOWER),
        tower_out,
        tower_bias.reshape(1, 1),
        labels.reshape(1, rows),
        source_ids.reshape(1, rows),
        task_table.reshape(1, SOURCES),
    )
    return (
        pred.reshape(rows, 1),
        ig,
        fw.reshape(2),
        gain.reshape(D),
        gate.swapaxes(1, 2),
        d_in.reshape(HALF, D, H),
        d_out.reshape(HALF, H, D),
        tin.reshape(1, D, TOWER),
        tout,
        bias.reshape(1),
    )


def solution(mesh):
    in_specs = (
        P("dp", "section", None),
        P("section"),
        P(),
        P(),
        P("section", None, None),
        P("section", None, None),
        P("section", None, None),
        P("section", None),
        P("section"),
        P("dp", "section"),
        P("dp"),
        P(None, "section"),
    )
    out_specs = (
        P("dp", "section"),
        P("dp", "section", None),
        P("section"),
        P(),
        P(),
        P("section", None, None),
        P("section", None, None),
        P("section", None, None),
        P("section", None),
        P("section"),
    )
    return jax.shard_map(body, mesh=mesh, in_specs=in_specs, out_specs=out_specs, check_vma=False)
```

```python
from functools import partial

import jax
import jax.numpy as jnp
from jax import lax
from jax.experimental import pallas as pl
from jax.experimental.pallas import tpu as pltpu
from jax.sharding import PartitionSpec as P

D = 256
H = 256
E = 16
TASKS = 4
SEL = 4
BITS = 4
TOWER = 128
SOURCES = 32
HALF = E // 2
GROWS = 32
FROWS = 96

STEP_SLOPE = 0.6
ENTROPY_WEIGHT = 0.05
NORM_EPS = 1e-05
GELU_A = 0.7978845608028654
GELU_B = 0.044715

F32 = jnp.float32
BF16 = jnp.bfloat16
MESH = pl.DeviceIdType.MESH

K_W, K_P, K_SM, K_TI, K_UP, K_DOWN, K_TW, K_DG, K_DP, K_GO, K_DX = 0, 2, 4, 8, 12, 16, 20, 24, 25, 28, 32
K_COUNT = 48
GROUP = 2
TILE = 32
STEPS = E // GROUP

GATE_AT = TOWER
MISC_AT = GATE_AT + 2 * GROWS
SMALL = MISC_AT + 8
KEPT = SMALL - GATE_AT


def split(x):
    hi = x.astype(BF16)
    return hi, (x - hi.astype(F32)).astype(BF16)


def wide(x):
    hi, lo = split(x)
    return jnp.concatenate([hi, lo, hi], axis=1)


def tall(x):
    hi, lo = split(x)
    return jnp.concatenate([hi, hi, lo], axis=0)


def put(ref, at, x):
    k = x.shape[1]
    hi, lo = split(x)
    ref[*at, :k] = hi
    ref[*at, k:] = lo


def stack(x):
    k = x.shape[1] // 2
    return jnp.concatenate([x[:, :k], x[:, :k], x[:, k:]], axis=0)


def mm(a, b):
    return jnp.dot(a, b, preferred_element_type=F32)


def pair(x):
    k = x.shape[1] // 2
    return jnp.concatenate([x, x[:, :k]], axis=1)


def gelu_pair(x):
    x2 = x * x
    h = 0.5 + 0.5 * jnp.tanh(x * (GELU_A + (GELU_A * GELU_B) * x2))
    g = x * h
    slope = h + g * (1.0 - h) * (2.0 * GELU_A + (6.0 * GELU_A * GELU_B) * x2)
    return g, slope


def rows8(x):
    return jnp.sum(x.reshape(x.shape[0] // 8, 8, x.shape[1]), axis=0)


def over_selectors(v, groups, op):
    parts = [v[k * groups : (k + 1) * groups] for k in range(SEL)]
    return op(op(parts[0], parts[1]), op(parts[2], parts[3]))


def to_selectors(v):
    return jnp.concatenate([v] * SEL, axis=0)


def gate_state(c, groups):
    w = SEL * groups
    zs = [c[w * b : w * b + w] * STEP_SLOPE for b in range(BITS)]
    alpha = c[w * BITS : w * BITS + w]
    ups, downs, sig_p, sig_n = [], [], [], []
    for z in zs:
        e = jnp.exp(-jnp.abs(z))
        tail = jnp.log1p(e)
        ups.append(jnp.minimum(z, 0.0) - tail)
        downs.append(jnp.minimum(-z, 0.0) - tail)
        big = 1.0 / (1.0 + e)
        small = e * big
        sig_p.append(jnp.where(z >= 0.0, big, small))
        sig_n.append(jnp.where(z >= 0.0, small, big))
    low = [(ups[0] if k & 1 else downs[0]) + (ups[1] if k & 2 else downs[1]) for k in range(4)]
    high = [(ups[2] if k & 1 else downs[2]) + (ups[3] if k & 2 else downs[3]) for k in range(4)]
    log_r = [low[j & 3] + high[j >> 2] for j in range(E)]
    r = [jnp.exp(v) for v in log_r]
    top = jnp.exp(alpha - to_selectors(over_selectors(alpha, groups, jnp.maximum)))
    mix = top / to_selectors(over_selectors(top, groups, jnp.add))
    return log_r, r, mix, sig_p, sig_n


def gate_forward(c, groups):
    _, r, mix, _, _ = gate_state(c, groups)
    return [over_selectors(mix * v, groups, jnp.add) for v in r]


def gate_backward(c, dgate, groups):
    log_r, r, mix, sig_p, sig_n = gate_state(c, groups)
    total = jnp.zeros_like(mix)
    on = [jnp.zeros_like(mix) for _ in range(BITS)]
    off = [jnp.zeros_like(mix) for _ in range(BITS)]
    for j in range(E):
        dg = to_selectors(dgate[j])
        total = total + dg * r[j]
        dlog = r[j] * (mix * dg - ENTROPY_WEIGHT * (log_r[j] + 1.0))
        for b in range(BITS):
            if j >> b & 1:
                on[b] = on[b] + dlog
            else:
                off[b] = off[b] + dlog
    dalpha = mix * (total - to_selectors(over_selectors(mix * total, groups, jnp.add)))
    dz = [STEP_SLOPE * (on[b] * sig_n[b] - off[b] * sig_p[b]) for b in range(BITS)]
    used = SEL * (BITS + 1) * groups
    pad = jnp.zeros(((-used) % GROWS, c.shape[1]), F32)
    return jnp.concatenate(dz + [dalpha, pad], axis=0)


def t_dot(a, b):
    ah, al = split(a)
    left = jnp.concatenate([ah, al, ah], axis=0)
    return lax.dot_general(left, tall(b), (((0,), (0,)), ((), ())), preferred_element_type=F32)


def pipeline(stages, count):
    for step in range(count + len(stages) - 1):
        for k, stage in enumerate(stages):
            if 0 <= step - k < count:
                stage(step - k, (step - k) % 2)


def kernel(
    n,
    subs,
    small_rows,
    x_ref,
    fw_ref,
    gain_ref,
    gate_ref,
    win_ref,
    wout_ref,
    tin_ref,
    tout_ref,
    tbias_ref,
    labels_ref,
    ids_ref,
    table_ref,
    o_pred,
    o_ig,
    o_fw,
    o_gain,
    o_gate,
    o_in,
    o_out,
    o_tin,
    o_tout,
    o_bias,
    kept,
    wt_in,
    wt_out,
    w_in,
    w_out,
    a1,
    a2,
    d_in,
    d_out,
    gbuf,
    kbuf,
    kp,
    rd,
    xf,
    part,
    pre0,
    pre1,
    pre2,
    pre,
    inbox,
    outbox,
    u_t,
    u_n,
    s_t,
    s_n,
    bb,
    acc,
    wg,
    gt,
    gt0,
    cs,
    dgt,
    dg,
    gb,
    sm,
    smo,
    ti,
    tp,
    tw,
    dp,
    gain_row,
    columns,
    u_next,
    gt_next,
    cs_next,
    acc_b,
    held,
    tm,
    sb,
    sr,
    so,
    sa,
    sg,
    send,
    recv,
    local,
    ready,
    rs_send,
    rs_recv,
    ag_send,
    ag_recv,
    sr_send,
    sr_recv,
    sa_send,
    sa_recv,
):
    s = lax.axis_index("section")
    x = s // 2
    c = s % 2
    mate = s + 1 - 2 * c
    across = s + 2 - 4 * x
    diag = 3 - s
    R = part.shape[0] // 2
    mine = pl.ds(pl.multiple_of(c * R, R), R)
    theirs = pl.ds(pl.multiple_of((1 - c) * R, R), R)

    me = lax.axis_index("dp")
    odd = me % 2
    p = (1 - odd) * (me // 2) + odd * (n - 1 - me // 2)

    def ring_id(q):
        far = q // (n // 2)
        return (1 - far) * 2 * q + far * (2 * (n - 1 - q) + 1)

    nbr = [ring_id((p + 1) % n), ring_id((p + n - 1) % n)]

    barrier = pltpu.get_barrier_semaphore()
    for sec in (mate, across, diag):
        pl.semaphore_signal(barrier, inc=1, device_id={"section": sec}, device_id_type=MESH)

    def greet(i, carry):
        pl.semaphore_signal(barrier, inc=1, device_id={"dp": (me + i) % n}, device_id_type=MESH)
        return carry

    lax.fori_loop(1, n, greet, 0)
    fields = [pltpu.make_async_copy(x_ref.at[:, f], xf.at[f], local.at[2 + f]) for f in range(2)]
    for f in fields:
        f.start()
    own = pl.ds(pl.multiple_of(c * HALF * H, HALF * H), HALF * H)
    own_in = pltpu.make_async_copy(win_ref, d_in.at[own], local.at[0])
    own_out = pltpu.make_async_copy(wout_ref, d_out.at[own], local.at[1])
    own_in.start()
    own_out.start()
    pl.semaphore_wait(barrier, 3 + n - 1)

    def copy(src, dst, k, sec, ks=None):
        return pltpu.make_async_remote_copy(
            src_ref=src,
            dst_ref=dst,
            send_sem=send.at[k if ks is None else ks],
            recv_sem=recv.at[k],
            device_id={"section": sec},
            device_id_type=MESH,
        )

    def expert(j, count=1):
        return pl.ds(pl.multiple_of(j * H, H), count * H)

    for f in fields:
        f.wait()
    part[...] = xf[0] * fw_ref[0, 0] + xf[1] * fw_ref[0, 1]
    to_mate = copy(part.at[theirs], pre0, K_P, mate)
    to_mate.start()
    swap_in = copy(win_ref, d_in.at[own], K_W, mate)
    swap_out = copy(wout_ref, d_out.at[own], K_W + 1, mate)
    swap_in.start()
    swap_out.start()

    ids = ids_ref[...]
    mask = jnp.zeros(ids.shape, F32)
    for q in range(SOURCES):
        mask = mask + jnp.where(ids == q, table_ref[0, q].astype(F32), 0.0)
    smo[...] = jnp.zeros_like(smo)
    smo[0:1] = labels_ref[...]
    smo[1:2] = mask
    smo[2:3, :TOWER] = tout_ref[...]
    smo[3:4] = jnp.zeros((1, 2 * R), F32) + tbias_ref[0, 0]
    for k in range(2):

        @pl.when(s != 2 + k)
        def _():
            copy(smo, sm.at[s], K_SM + s, 2 + k, K_SM + k).start()
            copy(tin_ref, ti.at[s], K_TI + s, 2 + k, K_TI + k).start()

    to_mate.wait_recv()

    @pl.when(x == 1)
    def _():
        pre2[...] = part[mine] + pre0[...]
        copy(pre2, pre1, K_P + 1, across).start()
        sm[s] = smo[...]
        ti[s] = tin_ref[...]

    wg[...] = jnp.zeros_like(wg)

    @pl.when(x == 0)
    def _():
        def order(t, carry):
            for sel in range(SEL):
                for e in range(BITS + 1):
                    row = t * (SEL * (BITS + 1)) + sel * (BITS + 1) + e
                    wg[pl.ds((e * SEL + sel) * TASKS + t, 1)] = gate_ref[0, pl.ds(row, 1)]
            return carry

        lax.fori_loop(0, TASKS, order, 0)

    @pl.when(x == 1)
    def _():
        def order(t, carry):
            for sel in range(SEL):
                for e in range(BITS + 1):
                    row = t * (SEL * (BITS + 1)) + sel * (BITS + 1) + e
                    wg[pl.ds(t * GROWS + e * SEL + sel, 1)] = gate_ref[1, pl.ds(row, 1)]
            return carry

        lax.fori_loop(0, TASKS, order, 0)

    own_in.wait()
    own_out.wait()

    def keep_plain(e, carry):
        put(w_in.at[e], (slice(None),), d_in[expert(e)])
        put(w_out.at[e], (slice(None),), d_out[expert(e)])
        return carry

    def keep_flipped(e, carry):
        put(wt_in.at[e], (slice(None),), d_in[expert(e)].T)
        put(wt_out.at[e], (slice(None),), d_out[expert(e)].T)
        return carry

    lax.fori_loop(c * HALF, c * HALF + HALF, keep_plain, 0)
    swap_in.wait()
    swap_out.wait()
    lax.fori_loop((1 - c) * HALF, (1 - c) * HALF + HALF, keep_plain, 0)

    def rows_of(size):
        return [slice(a, a + TILE) for a in range(0, size, TILE)]

    def shifted(tile, e):
        return slice(e * H + tile.start, e * H + tile.stop)

    @pl.when(x == 0)
    def _():
        copy(pre2, pre1, K_P + 1, across).wait_recv()
        pre_rows = part[mine] + pre0[...] + pre1[...]
        pre[...] = pre_rows
        rho = lax.rsqrt(jnp.mean(pre_rows * pre_rows, axis=1, keepdims=True) + NORM_EPS)
        pooled = pre_rows * rho * gain_ref[...]
        acc[...] = pooled
        u_n[0] = tall(pooled)
        u_t[...] = tall(pooled.T)
        logits = mm(wide(wg[:FROWS]), u_t[...])
        cs[...] = logits
        gates = gate_forward(logits, TASKS)
        for j, g in enumerate(gates):
            gt0[j] = g

        def first(g, par):
            left = jnp.concatenate([u_n[0, :R], u_n[0, 2 * R :], u_n[0, :R]], axis=1)
            for e in range(GROUP):
                bb[par, e * H : (e + 1) * H] = mm(left, stack(w_in[g * GROUP + e]))

        def activate(g, par):
            for e in range(GROUP):
                j = g * GROUP + e
                for tile in rows_of(R):
                    value, slope = gelu_pair(bb[par, shifted(tile, e)])
                    a1[shifted(tile, j)] = value
                    a2[j, tile] = slope
                    put(gbuf, (j, tile), value)

        def finish(g, par):
            for e in range(GROUP):
                j = g * GROUP + e
                d_in[expert(j)] = mm(pair(gbuf[j]), stack(w_out[j]))

        pipeline([first, activate, finish], STEPS)
        columns[...] = jnp.concatenate(gates, axis=0).T

        for t in range(TASKS):

            def mix(i, carry):
                tile = pl.ds(pl.multiple_of(i * TILE, TILE), TILE)
                cols = columns[tile]
                total = acc[tile]
                for j in range(E):
                    rows = pl.ds(pl.multiple_of(j * R + i * TILE, TILE), TILE)
                    total = total + cols[:, j * TASKS + t : j * TASKS + t + 1] * d_in[rows]
                outbox[t, tile] = total
                return carry

            lax.fori_loop(0, R // TILE, mix, 0)
            copy(outbox.at[t], inbox.at[t], K_UP + t, across).start()

        def flip(j, carry):
            value = a1[expert(j)].T
            a1[expert(j)] = value
            put(gbuf.at[j], (slice(None),), value)
            a2[j] = a2[j].T
            d_in[expert(j)] = d_in[expert(j)].T
            return carry

        lax.fori_loop(0, E, flip, 0)
        d_out[...] = jnp.zeros_like(d_out)
        acc[...] = jnp.zeros_like(acc)

    @pl.when(x == 1)
    def _():
        lax.fori_loop(0, E, keep_flipped, 0)
        for q in range(TASKS):

            @pl.when(s != q)
            def _():
                copy(smo, sm.at[q], K_SM + q, q).wait_recv()
                copy(tin_ref, ti.at[q], K_TI + q, q).wait_recv()

        def keep(k, t):
            return pltpu.make_async_copy((gbuf, kbuf)[k], kept.at[:, k * TASKS + t], local.at[4 + k])

        def gate_rows(t):
            return pl.ds(pl.multiple_of(t * GROWS, GROWS), GROWS)

        def enter(t):
            u = inbox[t]
            u_n[t] = tall(u)
            flipped = u.T
            stacked = tall(flipped)
            u_next[...] = stacked
            acc[...] = flipped
            logits = mm(wide(wg[gate_rows(t)]), stacked)
            cs_next[...] = logits
            for j, g in enumerate(gate_forward(logits, 1)):
                gt_next[j] = g

        def turn():
            u_t[...] = u_next[...]
            gt[...] = gt_next[...]
            cs[GROWS : 2 * GROWS] = cs[:GROWS]
            cs[:GROWS] = cs_next[...]

        def leave(t, at):
            dc = gate_backward(cs[at : at + GROWS], [dgt[j, 0:1] for j in range(E)], 1)
            outbox[t] = acc_b[...] + t_dot(wg[gate_rows(t)], dc)
            dg[gate_rows(t)] = mm(wide(dc), u_n[t])

        cs[...] = jnp.zeros_like(cs)
        dgt[...] = jnp.zeros_like(dgt)
        acc_b[...] = jnp.zeros_like(acc_b)
        copy(outbox.at[0], inbox.at[0], K_UP, across).wait_recv()
        enter(0)
        turn()

        def task(t, carry):
            @pl.when(t > 0)
            def _():
                keep(0, t).wait()

            def first(g, par):
                left = wt_in[g * GROUP : (g + 1) * GROUP].reshape(GROUP * H, 2 * D)
                bb[par] = mm(pair(left), u_t[...])

            def activate(g, par):
                for e in range(GROUP):
                    j = g * GROUP + e
                    for tile in rows_of(H):
                        value, slope = gelu_pair(bb[par, shifted(tile, e)])
                        a1[shifted(tile, j)] = value
                        a2[j, tile] = slope
                        put(gbuf, (j, tile), value * gt[j])

            def finish(g, par):
                js = range(g * GROUP, (g + 1) * GROUP)
                left = jnp.concatenate([pair(wt_out[j]) for j in js], axis=1)
                acc[...] += mm(left, jnp.concatenate([stack(gbuf[j]) for j in js], axis=0))

            before = (t + TASKS - 1) % TASKS
            leave(before, GROWS)
            pipeline([first, activate, finish], STEPS)
            keep(0, t).start()

            @pl.when(t > 0)
            def _():
                copy(outbox.at[before], inbox.at[before], K_DOWN + before, across).start()

            second = acc[...]
            held[...] = second
            tower = ti[t]
            g, slope = gelu_pair(mm(wide(tower.T), tall(second)))
            info = sm[t]
            out_col = info[:, :TOWER].T[:, 2:3]
            here = sm[t, :, mine]
            logit = jnp.sum(g * out_col, axis=0, keepdims=True) + here[3:4]
            prob = jax.nn.sigmoid(logit)
            dlogit = here[1:2] * (prob - here[0:1])
            m = dlogit * out_col * slope
            dy = mm(wide(tower), tall(m))
            s_t[...] = tall(dy)
            acc_b[...] = dy
            tm[:TOWER] = m
            tm[TOWER:] = g * dlogit
            tp[t, TOWER : TOWER + 1] = prob
            tp[t, TOWER + 2 : TOWER + 3] = dlogit
            tp[t, TOWER + 3 :] = jnp.zeros((5, R), F32)

            @pl.when(t > 0)
            def _():
                keep(1, t).wait()

            after = jnp.minimum(t + 1, TASKS - 1)

            @pl.when(t < TASKS - 1)
            def _():
                copy(outbox.at[after], inbox.at[after], K_UP + after, across).wait_recv()

            def back(g, par):
                left = w_out[g * GROUP : (g + 1) * GROUP].reshape(GROUP * H, 2 * D)
                bb[par] = mm(pair(left), s_t[...])

            def pull(g, par):
                for e in range(GROUP):
                    j = g * GROUP + e
                    total = jnp.zeros((8, R), F32)
                    for tile in rows_of(H):
                        grad = bb[par, shifted(tile, e)]
                        total = total + rows8(grad * a1[shifted(tile, j)])
                        put(kbuf, (j, tile), grad * a2[j, tile] * gt[j])
                    dgt[j, 0:1] = jnp.sum(total, axis=0, keepdims=True)

            def spread(g, par):
                js = range(g * GROUP, (g + 1) * GROUP)
                left = jnp.concatenate([pair(w_in[j]) for j in js], axis=1)
                acc_b[...] += mm(left, jnp.concatenate([stack(kbuf[j]) for j in js], axis=0))

            enter(after)
            s_n[t] = tall(acc_b[...].T)
            tp[t, :TOWER] = mm(wide(tm[:TOWER]), tall(held[...].T))
            out_grad = jnp.sum(tm[TOWER:], axis=1, keepdims=True)
            out_row = jnp.broadcast_to(out_grad, (TOWER, TOWER)).T[0:1]
            tp[t, TOWER + 1 : TOWER + 2] = jnp.concatenate([out_row, jnp.zeros_like(out_row)], axis=1)
            pipeline([back, pull, spread], STEPS)
            keep(1, t).start()
            turn()

            @pl.when(t != s)
            def _():
                copy(tp.at[t], tw.at[c], K_TW + c, t, K_TW + t).start()

            @pl.when(t == s)
            def _():
                tw[c] = tp[t]

            return carry

        lax.fori_loop(0, TASKS, task, 0)
        last_task = TASKS - 1
        leave(last_task, GROWS)
        copy(outbox.at[last_task], inbox.at[last_task], K_DOWN + last_task, across).start()
        keep(0, 0).wait()
        keep(1, 0).wait()

    def give(e):
        j = (1 - c) * HALF + e
        return (
            copy(d_in.at[expert(j)], rd.at[0, expert(e)], K_DX + e, mate),
            copy(d_out.at[expert(j)], rd.at[1, expert(e)], K_DX + HALF + e, mate),
        )

    @pl.when(x == 1)
    def _():
        base = (1 - c) * HALF

        def fetch(i):
            j = (base + i) % E
            return pltpu.make_async_copy(
                kept.at[j], wt_in.at[pl.ds((i % 2) * 2 * TASKS, 2 * TASKS)], local.at[4 + i % 2]
            )

        fetch(0).start()

        def one(i, carry):
            fetch(i).wait()

            @pl.when(i < E - 1)
            def _():
                fetch(i + 1).start()

            at = expert((base + i) % E)
            for k, (grad, right) in enumerate(((d_out, s_n), (d_in, u_n))):
                left = [pair(wt_in[(i % 2) * 2 * TASKS + k * TASKS + t]) for t in range(TASKS)]
                grad[at] = mm(jnp.concatenate(left, axis=1), right[...].reshape(3 * TASKS * R, D))

            @pl.when(i < HALF)
            def _():
                for move in give(i):
                    move.start()

            return carry

        lax.fori_loop(0, E, one, 0)

    @pl.when(x == 0)
    def _():
        def arrive(t, carry):
            copy(outbox.at[t], inbox.at[t], K_DOWN + t, across).wait_recv()
            acc[...] += inbox[t]

            def one(j, inner):
                gate = gt0[j, pl.ds(t, 1)]
                total = jnp.zeros((8, R), F32)
                for tile in rows_of(D):
                    dy = inbox[t, tile]
                    rows = pl.ds(pl.multiple_of(j * D + tile.start, TILE), TILE)
                    total = total + rows8(d_in[rows] * dy)
                    d_out[rows] += gate * dy
                dgt[j, pl.ds(t, 1)] = jnp.sum(total, axis=0, keepdims=True)
                return inner

            lax.fori_loop(0, E, one, 0)
            return carry

        lax.fori_loop(0, TASKS - 1, arrive, 0)
        last = TASKS - 1
        copy(outbox.at[last], inbox.at[last], K_DOWN + last, across).wait_recv()
        acc[...] += inbox[last]

        def one(j, inner):
            gate = gt0[j, last : last + 1]
            total = jnp.zeros((8, R), F32)
            for tile in rows_of(D):
                dy = inbox[last, tile]
                rows = pl.ds(pl.multiple_of(j * D + tile.start, TILE), TILE)
                total = total + rows8(d_in[rows] * dy)
                put(kbuf.at[j], (tile,), d_out[rows] + gate * dy)
            dgt[j, last : last + 1] = jnp.sum(total, axis=0, keepdims=True)
            return inner

        lax.fori_loop(0, E, one, 0)

        def half(h, carry):
            base = ((1 - c) * (1 - h) + c * h) * HALF

            def products(g, par):
                for e in range(GROUP):
                    j = base + g * GROUP + e
                    mixed = kbuf[j]
                    bb[par, e * H : (e + 1) * H] = mm(pair(w_out[j]), stack(mixed))
                    right = jnp.concatenate([mixed[:, :R], mixed[:, :R], mixed[:, R:]], axis=1)
                    d_out[expert(j)] = lax.dot_general(
                        pair(gbuf[j]), right, (((1,), (1,)), ((), ())), preferred_element_type=F32
                    )

            def pull(g, par):
                for e in range(GROUP):
                    for tile in rows_of(H):
                        rows = shifted(tile, e)
                        put(kp, (par, rows), bb[par, rows] * a2[base + g * GROUP + e, tile])

            def spread(g, par):
                left = jnp.concatenate([pair(w_in[base + g * GROUP + e]) for e in range(GROUP)], axis=1)
                right = [stack(kp[par, e * H : (e + 1) * H]) for e in range(GROUP)]
                acc[...] += mm(left, jnp.concatenate(right, axis=0))
                d_in[expert(base + g * GROUP, GROUP)] = mm(pair(kp[par]), u_n[0])

            pipeline([products, pull, spread], HALF // GROUP)

            @pl.when(h == 0)
            def _():
                for e in range(HALF):
                    for move in give(e):
                        move.start()

            return carry

        lax.fori_loop(0, 2, half, 0)

    chunk = HALF * H // n
    sub = chunk // subs
    lanes = [(d, k) for d in range(2) for k in range(subs)]

    def at(k, q):
        return pl.ds(pl.multiple_of(q * chunk + k * sub, 8), sub)

    def holds(d, step):
        return (p + n - step) % n if d == 0 else (p + step) % n

    def slot(d, k, step):
        return pl.ds(pl.multiple_of(((d * subs + k) * (n - 1) + step) * sub, 8), sub)

    def rs(d, k, step, src):
        return pltpu.make_async_remote_copy(
            src_ref=src,
            dst_ref=a1.at[slot(d, k, step)],
            send_sem=rs_send.at[d, k, step],
            recv_sem=rs_recv.at[d, k, step],
            device_id={"dp": nbr[d]},
            device_id_type=MESH,
        )

    results = (o_in, o_out)

    def ag(d, k, step, src, q):
        return pltpu.make_async_remote_copy(
            src_ref=src,
            dst_ref=results[d].at[at(k, q)],
            send_sem=ag_send.at[d, k, step],
            recv_sem=ag_recv.at[d, k, step],
            device_id={"dp": nbr[d]},
            device_id_type=MESH,
        )

    def merge(i, carry):
        e = (p * chunk // H + i) % HALF
        mine_in, mine_out = give(e)
        mine_in.wait_recv()
        mine_out.wait_recv()
        rows = expert(e)
        rd[0, rows] = (rd[0, rows] + d_in[expert(c * HALF + e)]).T
        rd[1, rows] += d_out[expert(c * HALF + e)]
        return carry

    for dev in nbr:
        pl.semaphore_signal(ready, inc=1, device_id={"dp": dev}, device_id_type=MESH)
    merge(0, 0)
    pl.semaphore_wait(ready, 2)
    for d, k in lanes:
        rs(d, k, 0, rd.at[d, at(k, holds(d, 0))]).start()
    lax.fori_loop(1, HALF, merge, 0)

    def reduce_step(step, carry):
        for d, k in lanes:
            rs(d, k, step - 1, a1.at[slot(d, k, step - 1)]).wait_recv()
            a1[slot(d, k, step - 1)] += rd[d, at(k, holds(d, step))]
            rs(d, k, step, a1.at[slot(d, k, step - 1)]).start()
        return carry

    gates_own = pl.ds(pl.multiple_of(c * 2 * GROWS, 2 * GROWS), 2 * GROWS)
    gates_away = pl.ds(pl.multiple_of((1 - c) * 2 * GROWS, 2 * GROWS), 2 * GROWS)
    gain_row[...] = jnp.zeros_like(gain_row)

    @pl.when(x == 0)
    def _():
        dc = gate_backward(cs[...], [dgt[j, :TASKS] for j in range(E)], TASKS)
        dpool = (acc[...] + t_dot(wg[:FROWS], dc)).T
        pre_rows = pre[...]
        rho = lax.rsqrt(jnp.mean(pre_rows * pre_rows, axis=1, keepdims=True) + NORM_EPS)
        scaled = dpool * gain_ref[...]
        dots = jnp.mean(scaled * pre_rows, axis=1, keepdims=True)
        dp[mine] = rho * scaled - pre_rows * (rho * rho * rho * dots)
        for k, sec in enumerate((mate, across, diag)):
            copy(dp.at[mine], dp.at[mine], K_DP + c, sec, K_DP + k).start()
        gain_row[0:1] = jnp.sum(dpool * pre_rows * rho, axis=0, keepdims=True)
        grad = mm(wide(dc), u_n[0])
        dg[: FROWS // 2] = grad[: FROWS // 2]
        dg[2 * GROWS : 2 * GROWS + FROWS // 2] = grad[FROWS // 2 :]

    gates_move = copy(dg.at[gates_away], gb, K_DG, mate)
    gates_move.start()
    lax.fori_loop(1, 2, reduce_step, 0)

    for half_no in range(2):

        @pl.when(s != half_no)
        def _():
            rows = pl.ds(half_no * R, R)
            copy(dp.at[rows], dp.at[rows], K_DP + half_no, half_no).wait_recv()

    for k in range(2):

        @pl.when(s != 2 + k)
        def _():
            copy(tp.at[0], tw.at[k], K_TW + k, s).wait_recv()

    gates_move.wait_recv()
    sb[:TOWER] = tw[0, :TOWER] + tw[1, :TOWER]
    sb[GATE_AT:MISC_AT] = dg[gates_own] + gb[...]
    sb[MISC_AT : MISC_AT + 1] = gain_row[0:1]
    sb[MISC_AT + 1 : MISC_AT + 3] = tw[0, TOWER + 1 : TOWER + 3] + tw[1, TOWER + 1 : TOWER + 3]
    for f in range(2):
        sb[MISC_AT + 3 + f : MISC_AT + 4 + f] = jnp.sum(xf[f] * dp[...], axis=0, keepdims=True)
    sb[MISC_AT + 5 : MISC_AT + 6] = smo[1:2, :R] + smo[1:2, R:]
    sb[MISC_AT + 6 :] = jnp.zeros((sb.shape[0] - MISC_AT - 6, D), F32)

    def block(q):
        return pl.ds(pl.multiple_of(q * small_rows, 8), small_rows)

    def scatter(i):
        to = (me + i) % n
        return pltpu.make_async_remote_copy(
            src_ref=sb.at[block(to)],
            dst_ref=sr.at[me],
            send_sem=sr_send.at[i],
            recv_sem=sr_recv.at[me],
            device_id={"dp": to},
            device_id_type=MESH,
        )

    def scattered(i):
        by = (me + i) % n
        return pltpu.make_async_remote_copy(
            src_ref=sb.at[block(me)],
            dst_ref=sr.at[by],
            send_sem=sr_send.at[i],
            recv_sem=sr_recv.at[by],
            device_id={"dp": by},
            device_id_type=MESH,
        )

    def spread_sum(i):
        return pltpu.make_async_remote_copy(
            src_ref=so,
            dst_ref=sa.at[block(me)],
            send_sem=sa_send.at[i],
            recv_sem=sa_recv.at[me],
            device_id={"dp": (me + i) % n},
            device_id_type=MESH,
        )

    def gathered(i):
        by = (me + i) % n
        return pltpu.make_async_remote_copy(
            src_ref=so,
            dst_ref=sa.at[block(by)],
            send_sem=sa_send.at[i],
            recv_sem=sa_recv.at[by],
            device_id={"dp": by},
            device_id_type=MESH,
        )

    def each(act):
        def one(i, carry):
            act(i)
            return carry

        lax.fori_loop(1, n, one, 0)

    each(lambda i: scatter(i).start())
    lax.fori_loop(2, 4, reduce_step, 0)
    so[...] = sb[block(me)]

    def take(i):
        scattered(i).wait_recv()
        so[...] += sr[(me + i) % n]

    each(take)
    sa[block(me)] = so[...]
    each(lambda i: spread_sum(i).start())
    lax.fori_loop(4, 6, reduce_step, 0)
    each(lambda i: gathered(i).wait_recv())
    piece = sa.at[pl.ds(GATE_AT, KEPT)]
    for k, sec in enumerate((mate, across, diag)):
        copy(piece, sg.at[s], K_GO + s, sec, K_GO + k).start()
    sg[s] = sa[GATE_AT:SMALL]
    lax.fori_loop(6, n - 1, reduce_step, 0)
    for sec in (mate, across, diag):
        copy(piece, sg.at[sec], K_GO + sec, sec).wait_recv()
    misc = KEPT - 8
    count = sum(sg[q, misc + 5 : misc + 6] for q in range(TASKS))
    scale = float(2 * R * n) / jnp.sum(count, axis=1, keepdims=True)

    last = n - 2
    for d, k in lanes:
        q = holds(d, n - 1)
        rs(d, k, last, a1.at[slot(d, k, last)]).wait_recv()
        a1[slot(d, k, last)] = (a1[slot(d, k, last)] + rd[d, at(k, q)]) * scale
        ag(d, k, 0, a1.at[slot(d, k, last)], q).start()
        pltpu.make_async_copy(a1.at[slot(d, k, last)], results[d].at[at(k, q)], local.at[6 + d * subs + k]).start()

    for f in range(2):
        xf[f] = dp[...] * (scale * fw_ref[0, f])
        pltpu.make_async_copy(xf.at[f], o_ig.at[:, f], local.at[2 + f]).start()
    for k in range(2):
        o_pred[:, k * R : (k + 1) * R] = tw[k, TOWER : TOWER + 1]
    for f in range(2):
        o_fw[0, f] = jnp.sum(sa[MISC_AT + 3 + f : MISC_AT + 4 + f] * scale)
    o_bias[0, 0] = jnp.sum(sa[MISC_AT + 2 : MISC_AT + 3] * scale)
    o_gain[...] = (sg[0, misc : misc + 1] + sg[1, misc : misc + 1]) * scale
    o_tout[...] = sa[MISC_AT + 1 : MISC_AT + 2, :TOWER] * scale
    o_tin[...] = (sa[:TOWER] * scale).T

    def order(t, carry):
        for sel in range(SEL):
            for e in range(BITS + 1):
                row = t * (SEL * (BITS + 1)) + sel * (BITS + 1) + e
                at0 = (e * SEL + sel) * TASKS
                cut = FROWS // 2
                o_gate[0, pl.ds(row, 1)] = sg[at0 // cut, pl.ds(at0 % cut + t, 1)] * scale
                o_gate[1, pl.ds(row, 1)] = sg[2 + t // 2, pl.ds((t % 2) * GROWS + e * SEL + sel, 1)] * scale
        return carry

    lax.fori_loop(0, TASKS, order, 0)

    def gather_step(step, carry):
        for d, k in lanes:
            q = holds(d, step - 1)
            ag(d, k, step - 1, results[d].at[at(k, q)], q).wait_recv()
            ag(d, k, step, results[d].at[at(k, q)], q).start()
        return carry

    lax.fori_loop(1, n - 1, gather_step, 0)
    for d, k in lanes:
        q = holds(d, n - 2)
        ag(d, k, last, results[d].at[at(k, q)], q).wait_recv()
        q = holds(d, n - 1)
        pltpu.make_async_copy(a1.at[slot(d, k, last)], results[d].at[at(k, q)], local.at[6 + d * subs + k]).wait()

    def sent(step, carry):
        for d, k in lanes:
            rs(d, k, step, a1.at[slot(d, k, step)]).wait_send()
            ag(d, k, step, a1.at[slot(d, k, step)], 0).wait_send()
        return carry

    lax.fori_loop(0, n - 1, sent, 0)
    each(lambda i: scatter(i).wait_send())
    each(lambda i: spread_sum(i).wait_send())
    to_mate.wait_send()
    gates_move.wait_send()
    for e in range(HALF):
        for move in give(e):
            move.wait_send()
    for k in range(2):

        @pl.when(s != 2 + k)
        def _():
            copy(smo, sm.at[s], K_SM + s, 2 + k, K_SM + k).wait_send()
            copy(tin_ref, ti.at[s], K_TI + s, 2 + k, K_TI + k).wait_send()

    @pl.when(x == 0)
    def _():
        for t in range(TASKS):
            copy(outbox.at[t], inbox.at[t], K_UP + t, across).wait_send()
        for k, sec in enumerate((mate, across, diag)):
            copy(dp.at[mine], dp.at[mine], K_DP + c, sec, K_DP + k).wait_send()

    @pl.when(x == 1)
    def _():
        copy(pre2, pre1, K_P + 1, across).wait_send()
        for t in range(TASKS):
            copy(outbox.at[t], inbox.at[t], K_DOWN + t, across).wait_send()

            @pl.when(t != s)
            def _():
                copy(tp.at[t], tw.at[c], K_TW + c, t, K_TW + t).wait_send()

    for k, sec in enumerate((mate, across, diag)):
        copy(piece, sg.at[s], K_GO + s, sec, K_GO + k).wait_send()
    for f in range(2):
        pltpu.make_async_copy(xf.at[f], o_ig.at[:, f], local.at[2 + f]).wait()


def hand_over(*refs):
    count = (len(refs) - 1) // 2
    sems = refs[-1]
    moves = [pltpu.make_async_copy(refs[k], refs[count + k], sems.at[k]) for k in range(count)]
    for move in moves:
        move.start()
    for move in moves:
        move.wait()


def body(
    field_inputs,
    field_weight,
    norm_gain,
    gate_weight,
    expert_in,
    expert_out,
    tower_in,
    tower_out,
    tower_bias,
    labels,
    source_ids,
    task_table,
):
    n = lax.axis_size("dp")
    rows = field_inputs.shape[0]
    half = rows // 2
    subs = 2
    small_rows = -(-SMALL // (8 * n)) * 8
    used = TASKS * SEL * (BITS + 1)

    vmem = pl.BlockSpec(memory_space=pltpu.VMEM)
    smem = pl.BlockSpec(memory_space=pltpu.SMEM)
    hbm = pl.BlockSpec(memory_space=pl.ANY)

    def bf(*shape):
        return pltpu.VMEM(shape, BF16)

    def f32(*shape):
        return pltpu.VMEM(shape, F32)

    def out(*shape):
        return jax.ShapeDtypeStruct(shape, F32)

    dma = pltpu.SemaphoreType.DMA
    *sums, _ = pl.pallas_call(
        partial(kernel, n, subs, small_rows),
        out_shape=(
            out(1, rows),
            out(rows, 2, D),
            out(1, 2),
            out(1, D),
            out(2, used, D),
            out(HALF * H, D),
            out(HALF * H, D),
            out(D, TOWER),
            out(1, TOWER),
            out(1, 1),
            jax.ShapeDtypeStruct((E, 2 * TASKS, H, 2 * half), BF16),
        ),
        in_specs=[hbm, smem, vmem, vmem, hbm, hbm, vmem, vmem, smem, vmem, vmem, smem],
        out_specs=(vmem, hbm, smem, vmem, vmem, hbm, hbm, vmem, vmem, smem, hbm),
        scratch_shapes=[
            bf(E, H, 2 * D),
            bf(E, D, 2 * H),
            bf(E, D, 2 * H),
            bf(E, H, 2 * D),
            f32(E * H, half),
            f32(E, H, half),
            f32(E * H, D),
            f32(E * H, D),
            bf(E, H, 2 * half),
            bf(E, H, 2 * half),
            bf(2, GROUP * H, 2 * half),
            f32(2, HALF * H, D),
            f32(2, rows, D),
            f32(rows, D),
            f32(half, D),
            f32(half, D),
            f32(half, D),
            f32(half, D),
            f32(TASKS, D, half),
            f32(TASKS, D, half),
            bf(3 * D, half),
            bf(TASKS, 3 * half, D),
            bf(3 * D, half),
            bf(TASKS, 3 * half, D),
            f32(2, GROUP * H, half),
            f32(D, half),
            f32(TASKS * GROWS, D),
            f32(E, 1, half),
            f32(E, TASKS, half),
            f32(FROWS, half),
            f32(E, TASKS, half),
            f32(TASKS * GROWS, D),
            f32(2 * GROWS, D),
            f32(TASKS, 8, rows),
            f32(8, rows),
            f32(TASKS, D, TOWER),
            f32(TASKS, TOWER + 8, D),
            f32(2, TOWER + 8, D),
            f32(rows, D),
            f32(8, D),
            f32(half, E * TASKS),
            bf(3 * D, half),
            f32(E, 1, half),
            f32(GROWS, half),
            f32(D, half),
            f32(D, half),
            f32(2 * TOWER, half),
            f32(n * small_rows, D),
            f32(n, small_rows, D),
            f32(small_rows, D),
            f32(n * small_rows, D),
            f32(TASKS, KEPT, D),
            dma((K_COUNT,)),
            dma((K_COUNT,)),
            dma((6 + 2 * subs,)),
            pltpu.SemaphoreType.REGULAR,
            dma((2, subs, n - 1)),
            dma((2, subs, n - 1)),
            dma((2, subs, n - 1)),
            dma((2, subs, n - 1)),
            dma((n,)),
            dma((n,)),
            dma((n,)),
            dma((n,)),
        ],
        compiler_params=pltpu.CompilerParams(
            collective_id=0, has_side_effects=True, vmem_limit_bytes=64 * 1024 * 1024 - 65536
        ),
    )(
        field_inputs,
        field_weight.reshape(1, 2),
        norm_gain.reshape(1, D),
        gate_weight.swapaxes(1, 2),
        expert_in.reshape(HALF * H, D),
        expert_out.reshape(HALF * H, D),
        tower_in.reshape(D, TOWER),
        tower_out,
        tower_bias.reshape(1, 1),
        labels.reshape(1, rows),
        source_ids.reshape(1, rows),
        task_table.reshape(1, SOURCES),
    )
    pred, ig, fw, gain, gate, d_in, d_out, tin, tout, bias = pl.pallas_call(
        hand_over,
        out_shape=tuple(jax.ShapeDtypeStruct(v.shape, v.dtype) for v in sums),
        in_specs=[hbm] * len(sums),
        out_specs=(hbm,) * len(sums),
        scratch_shapes=[dma((len(sums),))],
        compiler_params=pltpu.CompilerParams(vmem_limit_bytes=64 * 1024 * 1024 - 65536),
    )(*sums)
    return (
        pred.reshape(rows, 1),
        ig,
        fw.reshape(2),
        gain.reshape(D),
        gate.swapaxes(1, 2),
        d_in.reshape(HALF, D, H),
        d_out.reshape(HALF, H, D),
        tin.reshape(1, D, TOWER),
        tout,
        bias.reshape(1),
    )


def solution(mesh):
    in_specs = (
        P("dp", "section", None),
        P("section"),
        P(),
        P(),
        P("section", None, None),
        P("section", None, None),
        P("section", None, None),
        P("section", None),
        P("section"),
        P("dp", "section"),
        P("dp"),
        P(None, "section"),
    )
    out_specs = (
        P("dp", "section"),
        P("dp", "section", None),
        P("section"),
        P(),
        P(),
        P("section", None, None),
        P("section", None, None),
        P("section", None, None),
        P("section", None),
        P("section"),
    )
    return jax.shard_map(body, mesh=mesh, in_specs=in_specs, out_specs=out_specs, check_vma=False)
```

```python
from functools import partial

import jax
import jax.numpy as jnp
from jax import lax
from jax.experimental import pallas as pl
from jax.experimental.pallas import tpu as pltpu
from jax.sharding import PartitionSpec as P

D = 256
H = 256
E = 16
TASKS = 4
SEL = 4
BITS = 4
TOWER = 128
SOURCES = 32
HALF = E // 2
GROWS = 32
FROWS = 96

STEP_SLOPE = 0.6
ENTROPY_WEIGHT = 0.05
NORM_EPS = 1e-05
GELU_A = 0.7978845608028654
GELU_B = 0.044715

F32 = jnp.float32
BF16 = jnp.bfloat16
MESH = pl.DeviceIdType.MESH

K_W, K_P, K_SM, K_TI, K_UP, K_DOWN, K_TW, K_DG, K_DP, K_GO, K_DX = 0, 2, 4, 8, 12, 16, 20, 24, 25, 28, 32
K_COUNT = 48
GROUP = 2
TILE = 32
STEPS = E // GROUP

GATE_AT = TOWER
MISC_AT = GATE_AT + 2 * GROWS
SMALL = MISC_AT + 8
KEPT = SMALL - GATE_AT


def split(x):
    hi = x.astype(BF16)
    return hi, (x - hi.astype(F32)).astype(BF16)


def wide(x):
    hi, lo = split(x)
    return jnp.concatenate([hi, lo, hi], axis=1)


def tall(x):
    hi, lo = split(x)
    return jnp.concatenate([hi, hi, lo], axis=0)


def put(ref, at, x):
    k = x.shape[1]
    hi, lo = split(x)
    ref[*at, :k] = hi
    ref[*at, k:] = lo


def stack(x):
    k = x.shape[1] // 2
    return jnp.concatenate([x[:, :k], x[:, :k], x[:, k:]], axis=0)


def mm(a, b):
    return jnp.dot(a, b, preferred_element_type=F32)


def pair(x):
    k = x.shape[1] // 2
    return jnp.concatenate([x, x[:, :k]], axis=1)


def gelu_pair(x):
    x2 = x * x
    h = 0.5 + 0.5 * jnp.tanh(x * (GELU_A + (GELU_A * GELU_B) * x2))
    g = x * h
    slope = h + g * (1.0 - h) * (2.0 * GELU_A + (6.0 * GELU_A * GELU_B) * x2)
    return g, slope


def rows8(x):
    return jnp.sum(x.reshape(x.shape[0] // 8, 8, x.shape[1]), axis=0)


def over_selectors(v, groups, op):
    parts = [v[k * groups : (k + 1) * groups] for k in range(SEL)]
    return op(op(parts[0], parts[1]), op(parts[2], parts[3]))


def to_selectors(v):
    return jnp.concatenate([v] * SEL, axis=0)


def gate_state(c, groups):
    w = SEL * groups
    zs = [c[w * b : w * b + w] * STEP_SLOPE for b in range(BITS)]
    alpha = c[w * BITS : w * BITS + w]
    ups, downs, sig_p, sig_n = [], [], [], []
    for z in zs:
        e = jnp.exp(-jnp.abs(z))
        tail = jnp.log1p(e)
        ups.append(jnp.minimum(z, 0.0) - tail)
        downs.append(jnp.minimum(-z, 0.0) - tail)
        big = 1.0 / (1.0 + e)
        small = e * big
        sig_p.append(jnp.where(z >= 0.0, big, small))
        sig_n.append(jnp.where(z >= 0.0, small, big))
    low = [(ups[0] if k & 1 else downs[0]) + (ups[1] if k & 2 else downs[1]) for k in range(4)]
    high = [(ups[2] if k & 1 else downs[2]) + (ups[3] if k & 2 else downs[3]) for k in range(4)]
    log_r = [low[j & 3] + high[j >> 2] for j in range(E)]
    r = [jnp.exp(v) for v in log_r]
    top = jnp.exp(alpha - to_selectors(over_selectors(alpha, groups, jnp.maximum)))
    mix = top / to_selectors(over_selectors(top, groups, jnp.add))
    return log_r, r, mix, sig_p, sig_n


def gate_forward(c, groups):
    _, r, mix, _, _ = gate_state(c, groups)
    return [over_selectors(mix * v, groups, jnp.add) for v in r]


def gate_backward(c, dgate, groups):
    log_r, r, mix, sig_p, sig_n = gate_state(c, groups)
    total = jnp.zeros_like(mix)
    on = [jnp.zeros_like(mix) for _ in range(BITS)]
    off = [jnp.zeros_like(mix) for _ in range(BITS)]
    for j in range(E):
        dg = to_selectors(dgate[j])
        total = total + dg * r[j]
        dlog = r[j] * (mix * dg - ENTROPY_WEIGHT * (log_r[j] + 1.0))
        for b in range(BITS):
            if j >> b & 1:
                on[b] = on[b] + dlog
            else:
                off[b] = off[b] + dlog
    dalpha = mix * (total - to_selectors(over_selectors(mix * total, groups, jnp.add)))
    dz = [STEP_SLOPE * (on[b] * sig_n[b] - off[b] * sig_p[b]) for b in range(BITS)]
    used = SEL * (BITS + 1) * groups
    pad = jnp.zeros(((-used) % GROWS, c.shape[1]), F32)
    return jnp.concatenate(dz + [dalpha, pad], axis=0)


def t_dot(a, b):
    ah, al = split(a)
    left = jnp.concatenate([ah, al, ah], axis=0)
    return lax.dot_general(left, tall(b), (((0,), (0,)), ((), ())), preferred_element_type=F32)


def pipeline(stages, count):
    for step in range(count + len(stages) - 1):
        for k, stage in enumerate(stages):
            if 0 <= step - k < count:
                stage(step - k, (step - k) % 2)


def kernel(
    n,
    subs,
    small_rows,
    x_ref,
    fw_ref,
    gain_ref,
    gate_ref,
    win_ref,
    wout_ref,
    tin_ref,
    tout_ref,
    tbias_ref,
    labels_ref,
    ids_ref,
    table_ref,
    o_pred,
    o_ig,
    o_fw,
    o_gain,
    o_gate,
    o_in,
    o_out,
    o_tin,
    o_tout,
    o_bias,
    kept,
    wt_in,
    wt_out,
    w_in,
    w_out,
    a1,
    a2,
    d_in,
    d_out,
    gbuf,
    kbuf,
    kp,
    rd,
    xf,
    part,
    pre0,
    pre1,
    pre2,
    pre,
    inbox,
    outbox,
    u_t,
    u_n,
    s_t,
    s_n,
    bb,
    acc,
    wg,
    gt,
    gt0,
    cs,
    dgt,
    dg,
    gb,
    sm,
    smo,
    ti,
    tp,
    tw,
    dp,
    gain_row,
    columns,
    u_next,
    gt_next,
    cs_next,
    acc_b,
    held,
    tm,
    sb,
    sr,
    so,
    sa,
    sg,
    send,
    recv,
    local,
    ready,
    rs_send,
    rs_recv,
    ag_send,
    ag_recv,
    store_sem,
    sr_send,
    sr_recv,
    sa_send,
    sa_recv,
):
    s = lax.axis_index("section")
    x = s // 2
    c = s % 2
    mate = s + 1 - 2 * c
    across = s + 2 - 4 * x
    diag = 3 - s
    R = part.shape[0] // 2
    mine = pl.ds(pl.multiple_of(c * R, R), R)
    theirs = pl.ds(pl.multiple_of((1 - c) * R, R), R)

    me = lax.axis_index("dp")
    odd = me % 2
    p = (1 - odd) * (me // 2) + odd * (n - 1 - me // 2)

    def ring_id(q):
        far = q // (n // 2)
        return (1 - far) * 2 * q + far * (2 * (n - 1 - q) + 1)

    nbr = [ring_id((p + 1) % n), ring_id((p + n - 1) % n)]

    barrier = pltpu.get_barrier_semaphore()
    for sec in (mate, across, diag):
        pl.semaphore_signal(barrier, inc=1, device_id={"section": sec}, device_id_type=MESH)

    def greet(i, carry):
        pl.semaphore_signal(barrier, inc=1, device_id={"dp": (me + i) % n}, device_id_type=MESH)
        return carry

    lax.fori_loop(1, n, greet, 0)
    fields = [pltpu.make_async_copy(x_ref.at[:, f], xf.at[f], local.at[2 + f]) for f in range(2)]
    for f in fields:
        f.start()
    own = pl.ds(pl.multiple_of(c * HALF * H, HALF * H), HALF * H)
    own_in = pltpu.make_async_copy(win_ref, d_in.at[own], local.at[0])
    own_out = pltpu.make_async_copy(wout_ref, d_out.at[own], local.at[1])
    own_in.start()
    own_out.start()
    pl.semaphore_wait(barrier, 3 + n - 1)

    def copy(src, dst, k, sec, ks=None):
        return pltpu.make_async_remote_copy(
            src_ref=src,
            dst_ref=dst,
            send_sem=send.at[k if ks is None else ks],
            recv_sem=recv.at[k],
            device_id={"section": sec},
            device_id_type=MESH,
        )

    def expert(j, count=1):
        return pl.ds(pl.multiple_of(j * H, H), count * H)

    for f in fields:
        f.wait()
    part[...] = xf[0] * fw_ref[0, 0] + xf[1] * fw_ref[0, 1]
    to_mate = copy(part.at[theirs], pre0, K_P, mate)
    to_mate.start()
    swap_in = copy(d_in.at[own], d_in.at[own], K_W, mate)
    swap_out = copy(d_out.at[own], d_out.at[own], K_W + 1, mate)
    own_in.wait()
    swap_in.start()
    own_out.wait()
    swap_out.start()

    ids = ids_ref[...]
    mask = jnp.zeros(ids.shape, F32)
    for q in range(SOURCES):
        mask = mask + jnp.where(ids == q, table_ref[0, q].astype(F32), 0.0)
    smo[...] = jnp.zeros_like(smo)
    smo[0:1] = labels_ref[...]
    smo[1:2] = mask
    smo[2:3, :TOWER] = tout_ref[...]
    smo[3:4] = jnp.zeros((1, 2 * R), F32) + tbias_ref[0, 0]
    for k in range(2):

        @pl.when(s != 2 + k)
        def _():
            copy(smo, sm.at[s], K_SM + s, 2 + k, K_SM + k).start()
            copy(tin_ref, ti.at[s], K_TI + s, 2 + k, K_TI + k).start()

    to_mate.wait_recv()

    @pl.when(x == 1)
    def _():
        pre2[...] = part[mine] + pre0[...]
        copy(pre2, pre1, K_P + 1, across).start()
        sm[s] = smo[...]
        ti[s] = tin_ref[...]

    wg[...] = jnp.zeros_like(wg)

    @pl.when(x == 0)
    def _():
        def order(t, carry):
            for sel in range(SEL):
                for e in range(BITS + 1):
                    row = t * (SEL * (BITS + 1)) + sel * (BITS + 1) + e
                    wg[pl.ds((e * SEL + sel) * TASKS + t, 1)] = gate_ref[0, pl.ds(row, 1)]
            return carry

        lax.fori_loop(0, TASKS, order, 0)

    @pl.when(x == 1)
    def _():
        def order(t, carry):
            for sel in range(SEL):
                for e in range(BITS + 1):
                    row = t * (SEL * (BITS + 1)) + sel * (BITS + 1) + e
                    wg[pl.ds(t * GROWS + e * SEL + sel, 1)] = gate_ref[1, pl.ds(row, 1)]
            return carry

        lax.fori_loop(0, TASKS, order, 0)

    def keep_plain(e, carry):
        put(w_in.at[e], (slice(None),), d_in[expert(e)])
        put(w_out.at[e], (slice(None),), d_out[expert(e)])
        return carry

    def keep_flipped(e, carry):
        put(wt_in.at[e], (slice(None),), d_in[expert(e)].T)
        put(wt_out.at[e], (slice(None),), d_out[expert(e)].T)
        return carry

    lax.fori_loop(c * HALF, c * HALF + HALF, keep_plain, 0)
    swap_in.wait()
    swap_out.wait()
    lax.fori_loop((1 - c) * HALF, (1 - c) * HALF + HALF, keep_plain, 0)

    def rows_of(size):
        return [slice(a, a + TILE) for a in range(0, size, TILE)]

    def shifted(tile, e):
        return slice(e * H + tile.start, e * H + tile.stop)

    @pl.when(x == 0)
    def _():
        copy(pre2, pre1, K_P + 1, across).wait_recv()
        pre_rows = part[mine] + pre0[...] + pre1[...]
        pre[...] = pre_rows
        rho = lax.rsqrt(jnp.mean(pre_rows * pre_rows, axis=1, keepdims=True) + NORM_EPS)
        pooled = pre_rows * rho * gain_ref[...]
        acc[...] = pooled
        u_n[0] = tall(pooled)
        u_t[...] = tall(pooled.T)
        logits = mm(wide(wg[:FROWS]), u_t[...])
        cs[...] = logits
        gates = gate_forward(logits, TASKS)
        for j, g in enumerate(gates):
            gt0[j] = g

        def first(g, par):
            left = jnp.concatenate([u_n[0, :R], u_n[0, 2 * R :], u_n[0, :R]], axis=1)
            for e in range(GROUP):
                bb[par, e * H : (e + 1) * H] = mm(left, stack(w_in[g * GROUP + e]))

        def activate(g, par):
            for e in range(GROUP):
                j = g * GROUP + e
                for tile in rows_of(R):
                    value, slope = gelu_pair(bb[par, shifted(tile, e)])
                    a1[shifted(tile, j)] = value
                    a2[shifted(tile, j)] = slope
                    put(gbuf, (j, tile), value)

        def finish(g, par):
            for e in range(GROUP):
                j = g * GROUP + e
                d_in[expert(j)] = mm(pair(gbuf[j]), stack(w_out[j]))

        pipeline([first, activate, finish], STEPS)
        columns[...] = jnp.concatenate(gates, axis=0).T

        for t in range(TASKS):

            def mix(i, carry):
                tile = pl.ds(pl.multiple_of(i * TILE, TILE), TILE)
                cols = columns[tile]
                total = acc[tile]
                for j in range(E):
                    rows = pl.ds(pl.multiple_of(j * R + i * TILE, TILE), TILE)
                    total = total + cols[:, j * TASKS + t : j * TASKS + t + 1] * d_in[rows]
                outbox[t, tile] = total
                return carry

            lax.fori_loop(0, R // TILE, mix, 0)
            copy(outbox.at[t], inbox.at[t], K_UP + t, across).start()

        def flip(j, carry):
            value = a1[expert(j)].T
            a1[expert(j)] = value
            put(gbuf.at[j], (slice(None),), value)
            a2[expert(j)] = a2[expert(j)].T
            d_in[expert(j)] = d_in[expert(j)].T
            return carry

        lax.fori_loop(0, E, flip, 0)
        d_out[...] = jnp.zeros_like(d_out)
        acc[...] = jnp.zeros_like(acc)

    @pl.when(x == 1)
    def _():
        lax.fori_loop(0, E, keep_flipped, 0)
        for q in range(TASKS):

            @pl.when(s != q)
            def _():
                copy(smo, sm.at[q], K_SM + q, q).wait_recv()
                copy(tin_ref, ti.at[q], K_TI + q, q).wait_recv()

        def keep(k, t):
            return pltpu.make_async_copy((gbuf, kbuf)[k], kept.at[:, k * TASKS + t], local.at[4 + k])

        def gate_rows(t):
            return pl.ds(pl.multiple_of(t * GROWS, GROWS), GROWS)

        def enter(t):
            u = inbox[t]
            u_n[t] = tall(u)
            flipped = u.T
            stacked = tall(flipped)
            u_next[...] = stacked
            acc[...] = flipped
            logits = mm(wide(wg[gate_rows(t)]), stacked)
            cs_next[...] = logits
            for j, g in enumerate(gate_forward(logits, 1)):
                gt_next[j] = g

        def turn():
            u_t[...] = u_next[...]
            gt[...] = gt_next[...]
            cs[GROWS : 2 * GROWS] = cs[:GROWS]
            cs[:GROWS] = cs_next[...]

        def leave(t, at):
            dc = gate_backward(cs[at : at + GROWS], [dgt[j, 0:1] for j in range(E)], 1)
            outbox[t] = acc_b[...] + t_dot(wg[gate_rows(t)], dc)
            dg[gate_rows(t)] = mm(wide(dc), u_n[t])

        cs[...] = jnp.zeros_like(cs)
        dgt[...] = jnp.zeros_like(dgt)
        acc_b[...] = jnp.zeros_like(acc_b)
        copy(outbox.at[0], inbox.at[0], K_UP, across).wait_recv()
        enter(0)
        turn()

        def task(t, carry):
            @pl.when(t > 0)
            def _():
                keep(0, t).wait()

            def first(g, par):
                left = wt_in[g * GROUP : (g + 1) * GROUP].reshape(GROUP * H, 2 * D)
                bb[par] = mm(pair(left), u_t[...])

            def activate(g, par):
                for e in range(GROUP):
                    j = g * GROUP + e
                    for tile in rows_of(H):
                        value, slope = gelu_pair(bb[par, shifted(tile, e)])
                        a1[shifted(tile, j)] = value
                        a2[shifted(tile, j)] = slope
                        put(gbuf, (j, tile), value * gt[j])

            def finish(g, par):
                js = range(g * GROUP, (g + 1) * GROUP)
                left = jnp.concatenate([pair(wt_out[j]) for j in js], axis=1)
                acc[...] += mm(left, jnp.concatenate([stack(gbuf[j]) for j in js], axis=0))

            before = (t + TASKS - 1) % TASKS
            leave(before, GROWS)
            pipeline([first, activate, finish], STEPS)
            keep(0, t).start()

            @pl.when(t > 0)
            def _():
                copy(outbox.at[before], inbox.at[before], K_DOWN + before, across).start()

            second = acc[...]
            held[...] = second
            tower = ti[t]
            g, slope = gelu_pair(mm(wide(tower.T), tall(second)))
            info = sm[t]
            out_col = info[:, :TOWER].T[:, 2:3]
            here = sm[t, :, mine]
            logit = jnp.sum(g * out_col, axis=0, keepdims=True) + here[3:4]
            prob = jax.nn.sigmoid(logit)
            dlogit = here[1:2] * (prob - here[0:1])
            m = dlogit * out_col * slope
            dy = mm(wide(tower), tall(m))
            s_t[...] = tall(dy)
            acc_b[...] = dy
            tm[:TOWER] = m
            tm[TOWER:] = g * dlogit
            tp[t, TOWER : TOWER + 1] = prob
            tp[t, TOWER + 2 : TOWER + 3] = dlogit
            tp[t, TOWER + 3 :] = jnp.zeros((5, R), F32)

            @pl.when(t > 0)
            def _():
                keep(1, t).wait()

            after = jnp.minimum(t + 1, TASKS - 1)

            @pl.when(t < TASKS - 1)
            def _():
                copy(outbox.at[after], inbox.at[after], K_UP + after, across).wait_recv()

            def back(g, par):
                left = w_out[g * GROUP : (g + 1) * GROUP].reshape(GROUP * H, 2 * D)
                bb[par] = mm(pair(left), s_t[...])

            def pull(g, par):
                for e in range(GROUP):
                    j = g * GROUP + e
                    total = jnp.zeros((8, R), F32)
                    for tile in rows_of(H):
                        grad = bb[par, shifted(tile, e)]
                        total = total + rows8(grad * a1[shifted(tile, j)])
                        put(kbuf, (j, tile), grad * a2[shifted(tile, j)] * gt[j])
                    dgt[j, 0:1] = jnp.sum(total, axis=0, keepdims=True)

            def spread(g, par):
                js = range(g * GROUP, (g + 1) * GROUP)
                left = jnp.concatenate([pair(w_in[j]) for j in js], axis=1)
                acc_b[...] += mm(left, jnp.concatenate([stack(kbuf[j]) for j in js], axis=0))

            enter(after)
            s_n[t] = tall(acc_b[...].T)
            tp[t, :TOWER] = mm(wide(tm[:TOWER]), tall(held[...].T))
            out_grad = jnp.sum(tm[TOWER:], axis=1, keepdims=True)
            out_row = jnp.broadcast_to(out_grad, (TOWER, TOWER)).T[0:1]
            tp[t, TOWER + 1 : TOWER + 2] = jnp.concatenate([out_row, jnp.zeros_like(out_row)], axis=1)
            pipeline([back, pull, spread], STEPS)
            keep(1, t).start()
            turn()

            @pl.when(t != s)
            def _():
                copy(tp.at[t], tw.at[c], K_TW + c, t, K_TW + t).start()

            @pl.when(t == s)
            def _():
                tw[c] = tp[t]

            return carry

        lax.fori_loop(0, TASKS, task, 0)
        last_task = TASKS - 1
        leave(last_task, GROWS)
        copy(outbox.at[last_task], inbox.at[last_task], K_DOWN + last_task, across).start()
        keep(0, 0).wait()
        keep(1, 0).wait()

    def give(e):
        j = (1 - c) * HALF + e
        return (
            copy(d_in.at[expert(j)], rd.at[0, expert(e)], K_DX + e, mate),
            copy(d_out.at[expert(j)], rd.at[1, expert(e)], K_DX + HALF + e, mate),
        )

    @pl.when(x == 1)
    def _():
        base = (1 - c) * HALF

        def fetch(i):
            j = (base + i) % E
            return pltpu.make_async_copy(
                kept.at[j], wt_in.at[pl.ds((i % 2) * 2 * TASKS, 2 * TASKS)], local.at[4 + i % 2]
            )

        fetch(0).start()

        def one(i, carry):
            fetch(i).wait()

            @pl.when(i < E - 1)
            def _():
                fetch(i + 1).start()

            at = expert((base + i) % E)
            for k, (grad, right) in enumerate(((d_out, s_n), (d_in, u_n))):
                left = [pair(wt_in[(i % 2) * 2 * TASKS + k * TASKS + t]) for t in range(TASKS)]
                grad[at] = mm(jnp.concatenate(left, axis=1), right[...].reshape(3 * TASKS * R, D))

            @pl.when(i < HALF)
            def _():
                for move in give(i):
                    move.start()

            return carry

        lax.fori_loop(0, E, one, 0)

    @pl.when(x == 0)
    def _():
        def arrive(t, carry):
            copy(outbox.at[t], inbox.at[t], K_DOWN + t, across).wait_recv()
            acc[...] += inbox[t]

            def one(j, inner):
                gate = gt0[j, pl.ds(t, 1)]
                total = jnp.zeros((8, R), F32)
                for tile in rows_of(D):
                    dy = inbox[t, tile]
                    rows = pl.ds(pl.multiple_of(j * D + tile.start, TILE), TILE)
                    total = total + rows8(d_in[rows] * dy)
                    d_out[rows] += gate * dy
                dgt[j, pl.ds(t, 1)] = jnp.sum(total, axis=0, keepdims=True)
                return inner

            lax.fori_loop(0, E, one, 0)
            return carry

        lax.fori_loop(0, TASKS - 1, arrive, 0)
        last = TASKS - 1
        copy(outbox.at[last], inbox.at[last], K_DOWN + last, across).wait_recv()
        acc[...] += inbox[last]

        def one(j, inner):
            gate = gt0[j, last : last + 1]
            total = jnp.zeros((8, R), F32)
            for tile in rows_of(D):
                dy = inbox[last, tile]
                rows = pl.ds(pl.multiple_of(j * D + tile.start, TILE), TILE)
                total = total + rows8(d_in[rows] * dy)
                put(kbuf.at[j], (tile,), d_out[rows] + gate * dy)
            dgt[j, last : last + 1] = jnp.sum(total, axis=0, keepdims=True)
            return inner

        lax.fori_loop(0, E, one, 0)

        def half(h, carry):
            base = ((1 - c) * (1 - h) + c * h) * HALF

            def products(g, par):
                for e in range(GROUP):
                    j = base + g * GROUP + e
                    mixed = kbuf[j]
                    bb[par, e * H : (e + 1) * H] = mm(pair(w_out[j]), stack(mixed))
                    right = jnp.concatenate([mixed[:, :R], mixed[:, :R], mixed[:, R:]], axis=1)
                    d_out[expert(j)] = lax.dot_general(
                        pair(gbuf[j]), right, (((1,), (1,)), ((), ())), preferred_element_type=F32
                    )

            def pull(g, par):
                for e in range(GROUP):
                    for tile in rows_of(H):
                        rows = shifted(tile, e)
                        kept_rows = pl.ds(pl.multiple_of((base + g * GROUP + e) * H + tile.start, TILE), TILE)
                        put(kp, (par, rows), bb[par, rows] * a2[kept_rows])

            def spread(g, par):
                left = jnp.concatenate([pair(w_in[base + g * GROUP + e]) for e in range(GROUP)], axis=1)
                right = [stack(kp[par, e * H : (e + 1) * H]) for e in range(GROUP)]
                acc[...] += mm(left, jnp.concatenate(right, axis=0))
                d_in[expert(base + g * GROUP, GROUP)] = mm(pair(kp[par]), u_n[0])

            pipeline([products, pull, spread], HALF // GROUP)

            @pl.when(h == 0)
            def _():
                for e in range(HALF):
                    for move in give(e):
                        move.start()

            return carry

        lax.fori_loop(0, 2, half, 0)

    chunk = HALF * H // n
    sub = chunk // subs
    lanes = [(d, k) for d in range(2) for k in range(subs)]

    def at(k, q):
        return pl.ds(pl.multiple_of(q * chunk + k * sub, 8), sub)

    def holds(d, step):
        return (p + n - step) % n if d == 0 else (p + step) % n

    def slot(d, k, step):
        return pl.ds(pl.multiple_of(((d * subs + k) * (n - 1) + step) * sub, 8), sub)

    def rs(d, k, step, src):
        return pltpu.make_async_remote_copy(
            src_ref=src,
            dst_ref=a1.at[slot(d, k, step)],
            send_sem=rs_send.at[d, k, step],
            recv_sem=rs_recv.at[d, k, step],
            device_id={"dp": nbr[d]},
            device_id_type=MESH,
        )

    results = (o_in, o_out)

    def landed(d, k, q):
        return a2.at[pl.ds(pl.multiple_of(d * HALF * H + q * chunk + k * sub, 8), sub)]

    def store(d, k, q, src, step):
        return pltpu.make_async_copy(src, results[d].at[at(k, q)], store_sem.at[d, k, step])

    def ag(d, k, step, src, q):
        return pltpu.make_async_remote_copy(
            src_ref=src,
            dst_ref=landed(d, k, q),
            send_sem=ag_send.at[d, k, step],
            recv_sem=ag_recv.at[d, k, step],
            device_id={"dp": nbr[d]},
            device_id_type=MESH,
        )

    def merge(i, carry):
        e = (p * chunk // H + i) % HALF
        mine_in, mine_out = give(e)
        mine_in.wait_recv()
        mine_out.wait_recv()
        rows = expert(e)
        rd[0, rows] = (rd[0, rows] + d_in[expert(c * HALF + e)]).T
        rd[1, rows] += d_out[expert(c * HALF + e)]
        return carry

    for dev in nbr:
        pl.semaphore_signal(ready, inc=1, device_id={"dp": dev}, device_id_type=MESH)
    merge(0, 0)
    pl.semaphore_wait(ready, 2)
    for d, k in lanes:
        rs(d, k, 0, rd.at[d, at(k, holds(d, 0))]).start()
    lax.fori_loop(1, HALF, merge, 0)

    def reduce_step(step, carry):
        for d, k in lanes:
            rs(d, k, step - 1, a1.at[slot(d, k, step - 1)]).wait_recv()
            a1[slot(d, k, step - 1)] += rd[d, at(k, holds(d, step))]
            rs(d, k, step, a1.at[slot(d, k, step - 1)]).start()
        return carry

    gates_own = pl.ds(pl.multiple_of(c * 2 * GROWS, 2 * GROWS), 2 * GROWS)
    gates_away = pl.ds(pl.multiple_of((1 - c) * 2 * GROWS, 2 * GROWS), 2 * GROWS)
    gain_row[...] = jnp.zeros_like(gain_row)

    @pl.when(x == 0)
    def _():
        dc = gate_backward(cs[...], [dgt[j, :TASKS] for j in range(E)], TASKS)
        dpool = (acc[...] + t_dot(wg[:FROWS], dc)).T
        pre_rows = pre[...]
        rho = lax.rsqrt(jnp.mean(pre_rows * pre_rows, axis=1, keepdims=True) + NORM_EPS)
        scaled = dpool * gain_ref[...]
        dots = jnp.mean(scaled * pre_rows, axis=1, keepdims=True)
        dp[mine] = rho * scaled - pre_rows * (rho * rho * rho * dots)
        for k, sec in enumerate((mate, across, diag)):
            copy(dp.at[mine], dp.at[mine], K_DP + c, sec, K_DP + k).start()
        gain_row[0:1] = jnp.sum(dpool * pre_rows * rho, axis=0, keepdims=True)
        grad = mm(wide(dc), u_n[0])
        dg[: FROWS // 2] = grad[: FROWS // 2]
        dg[2 * GROWS : 2 * GROWS + FROWS // 2] = grad[FROWS // 2 :]

    gates_move = copy(dg.at[gates_away], gb, K_DG, mate)
    gates_move.start()
    lax.fori_loop(1, 2, reduce_step, 0)

    for half_no in range(2):

        @pl.when(s != half_no)
        def _():
            rows = pl.ds(half_no * R, R)
            copy(dp.at[rows], dp.at[rows], K_DP + half_no, half_no).wait_recv()

    for k in range(2):

        @pl.when(s != 2 + k)
        def _():
            copy(tp.at[0], tw.at[k], K_TW + k, s).wait_recv()

    gates_move.wait_recv()
    sb[:TOWER] = tw[0, :TOWER] + tw[1, :TOWER]
    sb[GATE_AT:MISC_AT] = dg[gates_own] + gb[...]
    sb[MISC_AT : MISC_AT + 1] = gain_row[0:1]
    sb[MISC_AT + 1 : MISC_AT + 3] = tw[0, TOWER + 1 : TOWER + 3] + tw[1, TOWER + 1 : TOWER + 3]
    for f in range(2):
        sb[MISC_AT + 3 + f : MISC_AT + 4 + f] = jnp.sum(xf[f] * dp[...], axis=0, keepdims=True)
    sb[MISC_AT + 5 : MISC_AT + 6] = smo[1:2, :R] + smo[1:2, R:]
    sb[MISC_AT + 6 :] = jnp.zeros((sb.shape[0] - MISC_AT - 6, D), F32)

    def block(q):
        return pl.ds(pl.multiple_of(q * small_rows, 8), small_rows)

    def scatter(i):
        to = (me + i) % n
        return pltpu.make_async_remote_copy(
            src_ref=sb.at[block(to)],
            dst_ref=sr.at[me],
            send_sem=sr_send.at[i],
            recv_sem=sr_recv.at[me],
            device_id={"dp": to},
            device_id_type=MESH,
        )

    def scattered(i):
        by = (me + i) % n
        return pltpu.make_async_remote_copy(
            src_ref=sb.at[block(me)],
            dst_ref=sr.at[by],
            send_sem=sr_send.at[i],
            recv_sem=sr_recv.at[by],
            device_id={"dp": by},
            device_id_type=MESH,
        )

    def spread_sum(i):
        return pltpu.make_async_remote_copy(
            src_ref=so,
            dst_ref=sa.at[block(me)],
            send_sem=sa_send.at[i],
            recv_sem=sa_recv.at[me],
            device_id={"dp": (me + i) % n},
            device_id_type=MESH,
        )

    def gathered(i):
        by = (me + i) % n
        return pltpu.make_async_remote_copy(
            src_ref=so,
            dst_ref=sa.at[block(by)],
            send_sem=sa_send.at[i],
            recv_sem=sa_recv.at[by],
            device_id={"dp": by},
            device_id_type=MESH,
        )

    def each(act):
        def one(i, carry):
            act(i)
            return carry

        lax.fori_loop(1, n, one, 0)

    each(lambda i: scatter(i).start())
    lax.fori_loop(2, 4, reduce_step, 0)
    so[...] = sb[block(me)]

    def take(i):
        scattered(i).wait_recv()
        so[...] += sr[(me + i) % n]

    each(take)
    sa[block(me)] = so[...]
    each(lambda i: spread_sum(i).start())
    lax.fori_loop(4, 6, reduce_step, 0)
    each(lambda i: gathered(i).wait_recv())
    piece = sa.at[pl.ds(GATE_AT, KEPT)]
    for k, sec in enumerate((mate, across, diag)):
        copy(piece, sg.at[s], K_GO + s, sec, K_GO + k).start()
    sg[s] = sa[GATE_AT:SMALL]
    lax.fori_loop(6, n - 1, reduce_step, 0)
    for sec in (mate, across, diag):
        copy(piece, sg.at[sec], K_GO + sec, sec).wait_recv()
    misc = KEPT - 8
    count = sum(sg[q, misc + 5 : misc + 6] for q in range(TASKS))
    scale = float(2 * R * n) / jnp.sum(count, axis=1, keepdims=True)

    last = n - 2
    for d, k in lanes:
        q = holds(d, n - 1)
        rs(d, k, last, a1.at[slot(d, k, last)]).wait_recv()
        a1[slot(d, k, last)] = (a1[slot(d, k, last)] + rd[d, at(k, q)]) * scale
        ag(d, k, 0, a1.at[slot(d, k, last)], q).start()
        store(d, k, q, a1.at[slot(d, k, last)], 0).start()

    for f in range(2):
        xf[f] = dp[...] * (scale * fw_ref[0, f])
        pltpu.make_async_copy(xf.at[f], o_ig.at[:, f], local.at[2 + f]).start()
    for k in range(2):
        o_pred[:, k * R : (k + 1) * R] = tw[k, TOWER : TOWER + 1]
    for f in range(2):
        o_fw[0, f] = jnp.sum(sa[MISC_AT + 3 + f : MISC_AT + 4 + f] * scale)
    o_bias[0, 0] = jnp.sum(sa[MISC_AT + 2 : MISC_AT + 3] * scale)
    o_gain[...] = (sg[0, misc : misc + 1] + sg[1, misc : misc + 1]) * scale
    o_tout[...] = sa[MISC_AT + 1 : MISC_AT + 2, :TOWER] * scale
    o_tin[...] = (sa[:TOWER] * scale).T

    def order(t, carry):
        for sel in range(SEL):
            for e in range(BITS + 1):
                row = t * (SEL * (BITS + 1)) + sel * (BITS + 1) + e
                at0 = (e * SEL + sel) * TASKS
                cut = FROWS // 2
                o_gate[0, pl.ds(row, 1)] = sg[at0 // cut, pl.ds(at0 % cut + t, 1)] * scale
                o_gate[1, pl.ds(row, 1)] = sg[2 + t // 2, pl.ds((t % 2) * GROWS + e * SEL + sel, 1)] * scale
        return carry

    lax.fori_loop(0, TASKS, order, 0)

    def gather_step(step, carry):
        for d, k in lanes:
            q = holds(d, step - 1)
            ag(d, k, step - 1, landed(d, k, q), q).wait_recv()
            ag(d, k, step, landed(d, k, q), q).start()
            store(d, k, q, landed(d, k, q), step).start()
        return carry

    lax.fori_loop(1, n - 1, gather_step, 0)
    for d, k in lanes:
        q = holds(d, n - 2)
        ag(d, k, last, landed(d, k, q), q).wait_recv()
        store(d, k, q, landed(d, k, q), n - 1).start()

    def stored(step, carry):
        for d, k in lanes:
            store(d, k, 0, landed(d, k, 0), step).wait()
        return carry

    lax.fori_loop(0, n, stored, 0)

    def sent(step, carry):
        for d, k in lanes:
            rs(d, k, step, a1.at[slot(d, k, step)]).wait_send()
            ag(d, k, step, a1.at[slot(d, k, step)], 0).wait_send()
        return carry

    lax.fori_loop(0, n - 1, sent, 0)
    each(lambda i: scatter(i).wait_send())
    each(lambda i: spread_sum(i).wait_send())
    to_mate.wait_send()
    gates_move.wait_send()
    for e in range(HALF):
        for move in give(e):
            move.wait_send()
    for k in range(2):

        @pl.when(s != 2 + k)
        def _():
            copy(smo, sm.at[s], K_SM + s, 2 + k, K_SM + k).wait_send()
            copy(tin_ref, ti.at[s], K_TI + s, 2 + k, K_TI + k).wait_send()

    @pl.when(x == 0)
    def _():
        for t in range(TASKS):
            copy(outbox.at[t], inbox.at[t], K_UP + t, across).wait_send()
        for k, sec in enumerate((mate, across, diag)):
            copy(dp.at[mine], dp.at[mine], K_DP + c, sec, K_DP + k).wait_send()

    @pl.when(x == 1)
    def _():
        copy(pre2, pre1, K_P + 1, across).wait_send()
        for t in range(TASKS):
            copy(outbox.at[t], inbox.at[t], K_DOWN + t, across).wait_send()

            @pl.when(t != s)
            def _():
                copy(tp.at[t], tw.at[c], K_TW + c, t, K_TW + t).wait_send()

    for k, sec in enumerate((mate, across, diag)):
        copy(piece, sg.at[s], K_GO + s, sec, K_GO + k).wait_send()
    for f in range(2):
        pltpu.make_async_copy(xf.at[f], o_ig.at[:, f], local.at[2 + f]).wait()


def hand_over(count, *refs):
    held = refs[2 * count : 3 * count]
    sems = refs[-1]
    reads = [pltpu.make_async_copy(refs[k], held[k], sems.at[0, k]) for k in range(count)]
    writes = [pltpu.make_async_copy(held[k], refs[count + k], sems.at[1, k]) for k in range(count)]
    for move in reads:
        move.start()
    for read, write in zip(reads, writes):
        read.wait()
        write.start()
    for move in writes:
        move.wait()


def body(
    field_inputs,
    field_weight,
    norm_gain,
    gate_weight,
    expert_in,
    expert_out,
    tower_in,
    tower_out,
    tower_bias,
    labels,
    source_ids,
    task_table,
):
    n = lax.axis_size("dp")
    rows = field_inputs.shape[0]
    half = rows // 2
    subs = 2
    small_rows = -(-SMALL // (8 * n)) * 8
    used = TASKS * SEL * (BITS + 1)

    vmem = pl.BlockSpec(memory_space=pltpu.VMEM)
    smem = pl.BlockSpec(memory_space=pltpu.SMEM)
    hbm = pl.BlockSpec(memory_space=pl.ANY)

    def bf(*shape):
        return pltpu.VMEM(shape, BF16)

    def f32(*shape):
        return pltpu.VMEM(shape, F32)

    def out(*shape):
        return jax.ShapeDtypeStruct(shape, F32)

    dma = pltpu.SemaphoreType.DMA
    *sums, _ = pl.pallas_call(
        partial(kernel, n, subs, small_rows),
        out_shape=(
            out(1, rows),
            out(rows, 2, D),
            out(1, 2),
            out(1, D),
            out(2, used, D),
            out(HALF * H, D),
            out(HALF * H, D),
            out(D, TOWER),
            out(1, TOWER),
            out(1, 1),
            jax.ShapeDtypeStruct((E, 2 * TASKS, H, 2 * half), BF16),
        ),
        in_specs=[hbm, smem, vmem, vmem, hbm, hbm, vmem, vmem, smem, vmem, vmem, smem],
        out_specs=(vmem, hbm, smem, vmem, vmem, hbm, hbm, vmem, vmem, smem, hbm),
        scratch_shapes=[
            bf(E, H, 2 * D),
            bf(E, D, 2 * H),
            bf(E, D, 2 * H),
            bf(E, H, 2 * D),
            f32(E * H, half),
            f32(E * H, half),
            f32(E * H, D),
            f32(E * H, D),
            bf(E, H, 2 * half),
            bf(E, H, 2 * half),
            bf(2, GROUP * H, 2 * half),
            f32(2, HALF * H, D),
            f32(2, rows, D),
            f32(rows, D),
            f32(half, D),
            f32(half, D),
            f32(half, D),
            f32(half, D),
            f32(TASKS, D, half),
            f32(TASKS, D, half),
            bf(3 * D, half),
            bf(TASKS, 3 * half, D),
            bf(3 * D, half),
            bf(TASKS, 3 * half, D),
            f32(2, GROUP * H, half),
            f32(D, half),
            f32(TASKS * GROWS, D),
            f32(E, 1, half),
            f32(E, TASKS, half),
            f32(FROWS, half),
            f32(E, TASKS, half),
            f32(TASKS * GROWS, D),
            f32(2 * GROWS, D),
            f32(TASKS, 8, rows),
            f32(8, rows),
            f32(TASKS, D, TOWER),
            f32(TASKS, TOWER + 8, D),
            f32(2, TOWER + 8, D),
            f32(rows, D),
            f32(8, D),
            f32(half, E * TASKS),
            bf(3 * D, half),
            f32(E, 1, half),
            f32(GROWS, half),
            f32(D, half),
            f32(D, half),
            f32(2 * TOWER, half),
            f32(n * small_rows, D),
            f32(n, small_rows, D),
            f32(small_rows, D),
            f32(n * small_rows, D),
            f32(TASKS, KEPT, D),
            dma((K_COUNT,)),
            dma((K_COUNT,)),
            dma((6,)),
            pltpu.SemaphoreType.REGULAR,
            dma((2, subs, n - 1)),
            dma((2, subs, n - 1)),
            dma((2, subs, n - 1)),
            dma((2, subs, n - 1)),
            dma((2, subs, n)),
            dma((n,)),
            dma((n,)),
            dma((n,)),
            dma((n,)),
        ],
        compiler_params=pltpu.CompilerParams(
            collective_id=0, has_side_effects=True, vmem_limit_bytes=64 * 1024 * 1024 - 65536
        ),
    )(
        field_inputs,
        field_weight.reshape(1, 2),
        norm_gain.reshape(1, D),
        gate_weight.swapaxes(1, 2),
        expert_in.reshape(HALF * H, D),
        expert_out.reshape(HALF * H, D),
        tower_in.reshape(D, TOWER),
        tower_out,
        tower_bias.reshape(1, 1),
        labels.reshape(1, rows),
        source_ids.reshape(1, rows),
        task_table.reshape(1, SOURCES),
    )
    pred, ig, fw, gain, gate, d_in, d_out, tin, tout, bias = pl.pallas_call(
        partial(hand_over, len(sums)),
        out_shape=tuple(jax.ShapeDtypeStruct(v.shape, v.dtype) for v in sums),
        in_specs=[hbm] * len(sums),
        out_specs=(hbm,) * len(sums),
        scratch_shapes=[pltpu.VMEM(v.shape, v.dtype) for v in sums] + [dma((2, len(sums)))],
        compiler_params=pltpu.CompilerParams(vmem_limit_bytes=64 * 1024 * 1024 - 65536),
    )(*sums)
    return (
        pred.reshape(rows, 1),
        ig,
        fw.reshape(2),
        gain.reshape(D),
        gate.swapaxes(1, 2),
        d_in.reshape(HALF, D, H),
        d_out.reshape(HALF, H, D),
        tin.reshape(1, D, TOWER),
        tout,
        bias.reshape(1),
    )


def solution(mesh):
    in_specs = (
        P("dp", "section", None),
        P("section"),
        P(),
        P(),
        P("section", None, None),
        P("section", None, None),
        P("section", None, None),
        P("section", None),
        P("section"),
        P("dp", "section"),
        P("dp"),
        P(None, "section"),
    )
    out_specs = (
        P("dp", "section"),
        P("dp", "section", None),
        P("section"),
        P(),
        P(),
        P("section", None, None),
        P("section", None, None),
        P("section", None, None),
        P("section", None),
        P("section"),
    )
    return jax.shard_map(body, mesh=mesh, in_specs=in_specs, out_specs=out_specs, check_vma=False)
```

```python
from functools import partial

import jax
import jax.numpy as jnp
from jax import lax
from jax.experimental import pallas as pl
from jax.experimental.pallas import tpu as pltpu
from jax.sharding import PartitionSpec as P

D = 256
H = 256
E = 16
TASKS = 4
SEL = 4
BITS = 4
TOWER = 128
SOURCES = 32
HALF = E // 2
GROWS = 32
FROWS = 96

STEP_SLOPE = 0.6
ENTROPY_WEIGHT = 0.05
NORM_EPS = 1e-05
GELU_A = 0.7978845608028654
GELU_B = 0.044715

F32 = jnp.float32
BF16 = jnp.bfloat16
MESH = pl.DeviceIdType.MESH

K_W, K_P, K_SM, K_TI, K_UP, K_DOWN, K_TW, K_DG, K_DP, K_GO, K_DX = 0, 2, 4, 8, 12, 16, 20, 24, 25, 28, 32
K_COUNT = 48
GROUP = 2
TILE = 32
STEPS = E // GROUP
SPILL = TASKS - 1
AHEAD = 3

GATE_AT = TOWER
MISC_AT = GATE_AT + 2 * GROWS
SMALL = MISC_AT + 8
KEPT = SMALL - GATE_AT


def split(x):
    hi = x.astype(BF16)
    return hi, (x - hi.astype(F32)).astype(BF16)


def wide(x):
    hi, lo = split(x)
    return jnp.concatenate([hi, lo, hi], axis=1)


def tall(x):
    hi, lo = split(x)
    return jnp.concatenate([hi, hi, lo], axis=0)


def put(ref, at, x):
    k = x.shape[1]
    hi, lo = split(x)
    ref[*at, :k] = hi
    ref[*at, k:] = lo


def stack(x):
    k = x.shape[1] // 2
    return jnp.concatenate([x[:, :k], x[:, :k], x[:, k:]], axis=0)


def mm(a, b):
    return jnp.dot(a, b, preferred_element_type=F32)


def pair(x):
    k = x.shape[1] // 2
    return jnp.concatenate([x, x[:, :k]], axis=1)


def gelu_pair(x):
    x2 = x * x
    h = 0.5 + 0.5 * jnp.tanh(x * (GELU_A + (GELU_A * GELU_B) * x2))
    g = x * h
    slope = h + g * (1.0 - h) * (2.0 * GELU_A + (6.0 * GELU_A * GELU_B) * x2)
    return g, slope


def rows8(x):
    return jnp.sum(x.reshape(x.shape[0] // 8, 8, x.shape[1]), axis=0)


def over_selectors(v, groups, op):
    parts = [v[k * groups : (k + 1) * groups] for k in range(SEL)]
    return op(op(parts[0], parts[1]), op(parts[2], parts[3]))


def to_selectors(v):
    return jnp.concatenate([v] * SEL, axis=0)


def gate_state(c, groups):
    w = SEL * groups
    zs = [c[w * b : w * b + w] * STEP_SLOPE for b in range(BITS)]
    alpha = c[w * BITS : w * BITS + w]
    ups, downs, sig_p, sig_n = [], [], [], []
    for z in zs:
        e = jnp.exp(-jnp.abs(z))
        tail = jnp.log1p(e)
        ups.append(jnp.minimum(z, 0.0) - tail)
        downs.append(jnp.minimum(-z, 0.0) - tail)
        big = 1.0 / (1.0 + e)
        small = e * big
        sig_p.append(jnp.where(z >= 0.0, big, small))
        sig_n.append(jnp.where(z >= 0.0, small, big))
    low = [(ups[0] if k & 1 else downs[0]) + (ups[1] if k & 2 else downs[1]) for k in range(4)]
    high = [(ups[2] if k & 1 else downs[2]) + (ups[3] if k & 2 else downs[3]) for k in range(4)]
    log_r = [low[j & 3] + high[j >> 2] for j in range(E)]
    r = [jnp.exp(v) for v in log_r]
    top = jnp.exp(alpha - to_selectors(over_selectors(alpha, groups, jnp.maximum)))
    mix = top / to_selectors(over_selectors(top, groups, jnp.add))
    return log_r, r, mix, sig_p, sig_n


def gate_forward(c, groups):
    _, r, mix, _, _ = gate_state(c, groups)
    return [over_selectors(mix * v, groups, jnp.add) for v in r]


def gate_backward(c, dgate, groups):
    log_r, r, mix, sig_p, sig_n = gate_state(c, groups)
    total = jnp.zeros_like(mix)
    on = [jnp.zeros_like(mix) for _ in range(BITS)]
    off = [jnp.zeros_like(mix) for _ in range(BITS)]
    for j in range(E):
        dg = to_selectors(dgate[j])
        total = total + dg * r[j]
        dlog = r[j] * (mix * dg - ENTROPY_WEIGHT * (log_r[j] + 1.0))
        for b in range(BITS):
            if j >> b & 1:
                on[b] = on[b] + dlog
            else:
                off[b] = off[b] + dlog
    dalpha = mix * (total - to_selectors(over_selectors(mix * total, groups, jnp.add)))
    dz = [STEP_SLOPE * (on[b] * sig_n[b] - off[b] * sig_p[b]) for b in range(BITS)]
    used = SEL * (BITS + 1) * groups
    pad = jnp.zeros(((-used) % GROWS, c.shape[1]), F32)
    return jnp.concatenate(dz + [dalpha, pad], axis=0)


def t_dot(a, b):
    ah, al = split(a)
    left = jnp.concatenate([ah, al, ah], axis=0)
    return lax.dot_general(left, tall(b), (((0,), (0,)), ((), ())), preferred_element_type=F32)


def pipeline(stages, count):
    for step in range(count + len(stages) - 1):
        for k, stage in enumerate(stages):
            if 0 <= step - k < count:
                stage(step - k, (step - k) % 2)


def kernel(
    n,
    subs,
    small_rows,
    x_ref,
    fw_ref,
    gain_ref,
    gate_ref,
    win_ref,
    wout_ref,
    tin_ref,
    tout_ref,
    tbias_ref,
    labels_ref,
    ids_ref,
    table_ref,
    o_pred,
    o_ig,
    o_fw,
    o_gain,
    o_gate,
    o_in,
    o_out,
    o_tin,
    o_tout,
    o_bias,
    kept,
    wt,
    w_in,
    w_out,
    a1,
    a2,
    d_in,
    d_out,
    gbuf,
    kbuf,
    kp,
    rd,
    xf,
    part,
    pre0,
    pre1,
    pre2,
    pre,
    inbox,
    outbox,
    u_t,
    u_n,
    s_t,
    s_n,
    bb,
    acc,
    wg,
    gt,
    gt0,
    cs,
    dgt,
    dg,
    gb,
    sm,
    smo,
    ti,
    tp,
    tw,
    dp,
    gain_row,
    columns,
    u_next,
    gt_next,
    cs_next,
    acc_b,
    held,
    tm,
    sb,
    sr,
    so,
    sa,
    sg,
    send,
    recv,
    local,
    fetch_sem,
    ready,
    rs_send,
    rs_recv,
    ag_send,
    ag_recv,
    store_sem,
    sr_send,
    sr_recv,
    sa_send,
    sa_recv,
):
    s = lax.axis_index("section")
    x = s // 2
    c = s % 2
    mate = s + 1 - 2 * c
    across = s + 2 - 4 * x
    diag = 3 - s
    R = part.shape[0] // 2
    mine = pl.ds(pl.multiple_of(c * R, R), R)
    theirs = pl.ds(pl.multiple_of((1 - c) * R, R), R)

    me = lax.axis_index("dp")
    odd = me % 2
    p = (1 - odd) * (me // 2) + odd * (n - 1 - me // 2)

    def ring_id(q):
        far = q // (n // 2)
        return (1 - far) * 2 * q + far * (2 * (n - 1 - q) + 1)

    nbr = [ring_id((p + 1) % n), ring_id((p + n - 1) % n)]

    barrier = pltpu.get_barrier_semaphore()
    for sec in (mate, across, diag):
        pl.semaphore_signal(barrier, inc=1, device_id={"section": sec}, device_id_type=MESH)

    def greet(i, carry):
        pl.semaphore_signal(barrier, inc=1, device_id={"dp": (me + i) % n}, device_id_type=MESH)
        return carry

    lax.fori_loop(1, n, greet, 0)
    fields = [pltpu.make_async_copy(x_ref.at[:, f], xf.at[f], local.at[2 + f]) for f in range(2)]
    for f in fields:
        f.start()
    own = pl.ds(pl.multiple_of(c * HALF * H, HALF * H), HALF * H)
    own_in = pltpu.make_async_copy(win_ref, d_in.at[own], local.at[0])
    own_out = pltpu.make_async_copy(wout_ref, d_out.at[own], local.at[1])
    own_in.start()
    own_out.start()
    pl.semaphore_wait(barrier, 3 + n - 1)

    def copy(src, dst, k, sec, ks=None):
        return pltpu.make_async_remote_copy(
            src_ref=src,
            dst_ref=dst,
            send_sem=send.at[k if ks is None else ks],
            recv_sem=recv.at[k],
            device_id={"section": sec},
            device_id_type=MESH,
        )

    def expert(j, count=1):
        return pl.ds(pl.multiple_of(j * H, H), count * H)

    for f in fields:
        f.wait()
    part[...] = xf[0] * fw_ref[0, 0] + xf[1] * fw_ref[0, 1]
    to_mate = copy(part.at[theirs], pre0, K_P, mate)
    to_mate.start()
    swap_in = copy(d_in.at[own], d_in.at[own], K_W, mate)
    swap_out = copy(d_out.at[own], d_out.at[own], K_W + 1, mate)
    own_in.wait()
    swap_in.start()
    own_out.wait()
    swap_out.start()

    ids = ids_ref[...]
    mask = jnp.zeros(ids.shape, F32)
    for q in range(SOURCES):
        mask = mask + jnp.where(ids == q, table_ref[0, q].astype(F32), 0.0)
    smo[...] = jnp.zeros_like(smo)
    smo[0:1] = labels_ref[...]
    smo[1:2] = mask
    smo[2:3, :TOWER] = tout_ref[...]
    smo[3:4] = jnp.zeros((1, 2 * R), F32) + tbias_ref[0, 0]
    for k in range(2):

        @pl.when(s != 2 + k)
        def _():
            copy(smo, sm.at[s], K_SM + s, 2 + k, K_SM + k).start()
            copy(tin_ref, ti.at[s], K_TI + s, 2 + k, K_TI + k).start()

    to_mate.wait_recv()

    @pl.when(x == 1)
    def _():
        pre2[...] = part[mine] + pre0[...]
        copy(pre2, pre1, K_P + 1, across).start()
        sm[s] = smo[...]
        ti[s] = tin_ref[...]

    wg[...] = jnp.zeros_like(wg)

    @pl.when(x == 0)
    def _():
        def order(t, carry):
            for sel in range(SEL):
                for e in range(BITS + 1):
                    row = t * (SEL * (BITS + 1)) + sel * (BITS + 1) + e
                    wg[pl.ds((e * SEL + sel) * TASKS + t, 1)] = gate_ref[0, pl.ds(row, 1)]
            return carry

        lax.fori_loop(0, TASKS, order, 0)

    @pl.when(x == 1)
    def _():
        def order(t, carry):
            for sel in range(SEL):
                for e in range(BITS + 1):
                    row = t * (SEL * (BITS + 1)) + sel * (BITS + 1) + e
                    wg[pl.ds(t * GROWS + e * SEL + sel, 1)] = gate_ref[1, pl.ds(row, 1)]
            return carry

        lax.fori_loop(0, TASKS, order, 0)

    def keep_plain(e, carry):
        put(w_in.at[e], (slice(None),), d_in[expert(e)])
        put(w_out.at[e], (slice(None),), d_out[expert(e)])
        return carry

    def keep_flipped(e, carry):
        put(wt.at[e], (slice(None),), d_in[expert(e)].T)
        put(wt.at[E + e], (slice(None),), d_out[expert(e)].T)
        return carry

    lax.fori_loop(c * HALF, c * HALF + HALF, keep_plain, 0)
    swap_in.wait()
    swap_out.wait()
    lax.fori_loop((1 - c) * HALF, (1 - c) * HALF + HALF, keep_plain, 0)

    def rows_of(size):
        return [slice(a, a + TILE) for a in range(0, size, TILE)]

    def shifted(tile, e):
        return slice(e * H + tile.start, e * H + tile.stop)

    chunk = HALF * H // n
    sub = chunk // subs
    lanes = [(d, k) for d in range(2) for k in range(subs)]

    def at(k, q):
        return pl.ds(pl.multiple_of(q * chunk + k * sub, 8), sub)

    def holds(d, step):
        return (p + n - step) % n if d == 0 else (p + step) % n

    def slot(d, k, step):
        return pl.ds(pl.multiple_of(((d * subs + k) * (n - 1) + step) * sub, 8), sub)

    def rs(d, k, step, src):
        return pltpu.make_async_remote_copy(
            src_ref=src,
            dst_ref=a1.at[slot(d, k, step)],
            send_sem=rs_send.at[d, k, step],
            recv_sem=rs_recv.at[d, k, step],
            device_id={"dp": nbr[d]},
            device_id_type=MESH,
        )

    results = (o_in, o_out)

    def landed(d, k, q):
        return a2.at[pl.ds(pl.multiple_of(d * HALF * H + q * chunk + k * sub, 8), sub)]

    def store(d, k, q, src, step):
        return pltpu.make_async_copy(src, results[d].at[at(k, q)], store_sem.at[d, k, step])

    def ag(d, k, step, src, q):
        return pltpu.make_async_remote_copy(
            src_ref=src,
            dst_ref=landed(d, k, q),
            send_sem=ag_send.at[d, k, step],
            recv_sem=ag_recv.at[d, k, step],
            device_id={"dp": nbr[d]},
            device_id_type=MESH,
        )

    def give(e):
        j = (1 - c) * HALF + e
        return (
            copy(d_in.at[expert(j)], rd.at[0, expert(e)], K_DX + e, mate),
            copy(d_out.at[expert(j)], rd.at[1, expert(e)], K_DX + HALF + e, mate),
        )

    start_at = p * chunk // H

    def near(k):
        return (start_at + HALF + ((k + 1) // 2) * (1 - 2 * (k % 2))) % HALF

    def turn_of(i):
        own_turn = i % 2
        return ((1 - own_turn) * (1 - c) + own_turn * c) * HALF + near(i // 2)

    def fetch(i):
        at = pl.ds((i % (AHEAD + 1)) * 8, 2 * SPILL)
        return pltpu.make_async_copy(kept.at[turn_of(i)], wt.at[at], fetch_sem.at[i % (AHEAD + 1)])

    def fetch_start(i):
        for k in range(2 * SPILL):
            slab = (i % (AHEAD + 1)) * 8 + k
            pltpu.make_async_copy(
                kept.at[turn_of(i), k], wt.at[slab], fetch_sem.at[i % (AHEAD + 1)]
            ).start()

    def greet_ring():
        for dev in nbr:
            pl.semaphore_signal(ready, inc=1, device_id={"dp": dev}, device_id_type=MESH)

    def merge(k, carry):
        e = near(k)
        for move in give(e):
            move.wait_recv()
        rows = expert(e)
        rd[0, rows] = (rd[0, rows] + d_in[expert(c * HALF + e)]).T
        rd[1, rows] += d_out[expert(c * HALF + e)]
        return carry

    def ring_start():
        pl.semaphore_wait(ready, 2)
        for d, k in lanes:
            rs(d, k, 0, rd.at[d, at(k, holds(d, 0))]).start()

    @pl.when(x == 0)
    def _():
        copy(pre2, pre1, K_P + 1, across).wait_recv()
        pre_rows = part[mine] + pre0[...] + pre1[...]
        pre[...] = pre_rows
        rho = lax.rsqrt(jnp.mean(pre_rows * pre_rows, axis=1, keepdims=True) + NORM_EPS)
        pooled = pre_rows * rho * gain_ref[...]
        acc[...] = pooled
        u_n[0] = tall(pooled)
        u_t[...] = tall(pooled.T)
        logits = mm(wide(wg[:FROWS]), u_t[...])
        cs[...] = logits
        gates = gate_forward(logits, TASKS)
        for j, g in enumerate(gates):
            gt0[j] = g

        def first(g, par):
            left = jnp.concatenate([u_n[0, :R], u_n[0, 2 * R :], u_n[0, :R]], axis=1)
            for e in range(GROUP):
                bb[par, e * H : (e + 1) * H] = mm(left, stack(w_in[g * GROUP + e]))

        def activate(g, par):
            for e in range(GROUP):
                j = g * GROUP + e
                for tile in rows_of(R):
                    value, slope = gelu_pair(bb[par, shifted(tile, e)])
                    a1[shifted(tile, j)] = value
                    a2[shifted(tile, j)] = slope
                    put(gbuf, (j, tile), value)

        def finish(g, par):
            for e in range(GROUP):
                j = g * GROUP + e
                d_in[expert(j)] = mm(pair(gbuf[j]), stack(w_out[j]))

        pipeline([first, activate, finish], STEPS)
        columns[...] = jnp.concatenate(gates, axis=0).T

        for t in range(TASKS):

            def mix(i, carry):
                tile = pl.ds(pl.multiple_of(i * TILE, TILE), TILE)
                cols = columns[tile]
                total = acc[tile]
                for j in range(E):
                    rows = pl.ds(pl.multiple_of(j * R + i * TILE, TILE), TILE)
                    total = total + cols[:, j * TASKS + t : j * TASKS + t + 1] * d_in[rows]
                outbox[t, tile] = total
                return carry

            lax.fori_loop(0, R // TILE, mix, 0)
            copy(outbox.at[t], inbox.at[t], K_UP + t, across).start()

        def flip(j, carry):
            value = a1[expert(j)].T
            a1[expert(j)] = value
            put(gbuf.at[j], (slice(None),), value)
            a2[expert(j)] = a2[expert(j)].T
            d_in[expert(j)] = d_in[expert(j)].T
            return carry

        lax.fori_loop(0, E, flip, 0)
        greet_ring()
        d_out[...] = jnp.zeros_like(d_out)
        acc[...] = jnp.zeros_like(acc)

    @pl.when(x == 1)
    def _():
        lax.fori_loop(0, E, keep_flipped, 0)
        for q in range(TASKS):

            @pl.when(s != q)
            def _():
                copy(smo, sm.at[q], K_SM + q, q).wait_recv()
                copy(tin_ref, ti.at[q], K_TI + q, q).wait_recv()

        def keep(k, t):
            return pltpu.make_async_copy((gbuf, kbuf)[k], kept.at[:, k * SPILL + t], local.at[4 + k])

        def keep_start(k, t):
            def one(j, carry):
                pltpu.make_async_copy((gbuf, kbuf)[k].at[j], kept.at[j, k * SPILL + t], local.at[4 + k]).start()
                return carry

            @pl.when(t < SPILL)
            def _():
                lax.fori_loop(0, E, one, 0)

        def gate_rows(t):
            return pl.ds(pl.multiple_of(t * GROWS, GROWS), GROWS)

        def enter(t):
            u = inbox[t]
            u_n[t] = tall(u)
            flipped = u.T
            stacked = tall(flipped)
            u_next[...] = stacked
            acc[...] = flipped
            logits = mm(wide(wg[gate_rows(t)]), stacked)
            cs_next[...] = logits
            for j, g in enumerate(gate_forward(logits, 1)):
                gt_next[j] = g

        def turn():
            u_t[...] = u_next[...]
            gt[...] = gt_next[...]
            cs[GROWS : 2 * GROWS] = cs[:GROWS]
            cs[:GROWS] = cs_next[...]

        def leave(t, at):
            dc = gate_backward(cs[at : at + GROWS], [dgt[j, 0:1] for j in range(E)], 1)
            outbox[t] = acc_b[...] + t_dot(wg[gate_rows(t)], dc)
            dg[gate_rows(t)] = mm(wide(dc), u_n[t])

        cs[...] = jnp.zeros_like(cs)
        dgt[...] = jnp.zeros_like(dgt)
        acc_b[...] = jnp.zeros_like(acc_b)
        copy(outbox.at[0], inbox.at[0], K_UP, across).wait_recv()
        enter(0)
        turn()

        def task(t, carry):
            @pl.when(t > 0)
            def _():
                keep(0, 0).wait()

            def first(g, par):
                left = wt[g * GROUP : (g + 1) * GROUP].reshape(GROUP * H, 2 * D)
                bb[par] = mm(pair(left), u_t[...])

            def activate(g, par):
                for e in range(GROUP):
                    j = g * GROUP + e
                    for tile in rows_of(H):
                        value, slope = gelu_pair(bb[par, shifted(tile, e)])
                        a1[shifted(tile, j)] = value
                        a2[shifted(tile, j)] = slope
                        put(gbuf, (j, tile), value * gt[j])

            def finish(g, par):
                js = range(g * GROUP, (g + 1) * GROUP)
                left = jnp.concatenate([pair(wt[E + j]) for j in js], axis=1)
                acc[...] += mm(left, jnp.concatenate([stack(gbuf[j]) for j in js], axis=0))

            before = (t + TASKS - 1) % TASKS
            leave(before, GROWS)
            pipeline([first, activate, finish], STEPS)
            keep_start(0, t)

            @pl.when(t > 0)
            def _():
                copy(outbox.at[before], inbox.at[before], K_DOWN + before, across).start()

            second = acc[...]
            held[...] = second
            tower = ti[t]
            g, slope = gelu_pair(mm(wide(tower.T), tall(second)))
            info = sm[t]
            out_col = info[:, :TOWER].T[:, 2:3]
            here = sm[t, :, mine]
            logit = jnp.sum(g * out_col, axis=0, keepdims=True) + here[3:4]
            prob = jax.nn.sigmoid(logit)
            dlogit = here[1:2] * (prob - here[0:1])
            m = dlogit * out_col * slope
            dy = mm(wide(tower), tall(m))
            s_t[...] = tall(dy)
            acc_b[...] = dy
            tm[:TOWER] = m
            tm[TOWER:] = g * dlogit
            tp[t, TOWER : TOWER + 1] = prob
            tp[t, TOWER + 2 : TOWER + 3] = dlogit
            tp[t, TOWER + 3 :] = jnp.zeros((5, R), F32)

            @pl.when(t > 0)
            def _():
                keep(1, 0).wait()

            @pl.when(t == TASKS - 1)
            def _():
                for i in range(AHEAD):
                    fetch_start(i)

            after = jnp.minimum(t + 1, TASKS - 1)

            @pl.when(t < TASKS - 1)
            def _():
                copy(outbox.at[after], inbox.at[after], K_UP + after, across).wait_recv()

            def back(g, par):
                left = w_out[g * GROUP : (g + 1) * GROUP].reshape(GROUP * H, 2 * D)
                bb[par] = mm(pair(left), s_t[...])

            def pull(g, par):
                for e in range(GROUP):
                    j = g * GROUP + e
                    total = jnp.zeros((8, R), F32)
                    for tile in rows_of(H):
                        grad = bb[par, shifted(tile, e)]
                        total = total + rows8(grad * a1[shifted(tile, j)])
                        put(kbuf, (j, tile), grad * a2[shifted(tile, j)] * gt[j])
                    dgt[j, 0:1] = jnp.sum(total, axis=0, keepdims=True)

            def spread(g, par):
                js = range(g * GROUP, (g + 1) * GROUP)
                left = jnp.concatenate([pair(w_in[j]) for j in js], axis=1)
                acc_b[...] += mm(left, jnp.concatenate([stack(kbuf[j]) for j in js], axis=0))

            enter(after)
            s_n[t] = tall(acc_b[...].T)
            tp[t, :TOWER] = mm(wide(tm[:TOWER]), tall(held[...].T))
            out_grad = jnp.sum(tm[TOWER:], axis=1, keepdims=True)
            out_row = jnp.broadcast_to(out_grad, (TOWER, TOWER)).T[0:1]
            tp[t, TOWER + 1 : TOWER + 2] = jnp.concatenate([out_row, jnp.zeros_like(out_row)], axis=1)
            pipeline([back, pull, spread], STEPS)
            keep_start(1, t)
            turn()

            @pl.when(t != s)
            def _():
                copy(tp.at[t], tw.at[c], K_TW + c, t, K_TW + t).start()

            @pl.when(t == s)
            def _():
                tw[c] = tp[t]

            return carry

        lax.fori_loop(0, TASKS, task, 0)
        last_task = TASKS - 1
        leave(last_task, GROWS)
        copy(outbox.at[last_task], inbox.at[last_task], K_DOWN + last_task, across).start()
        greet_ring()

    @pl.when(x == 1)
    def _():
        def one(i, carry):
            fetch(i).wait()

            @pl.when(i < E - AHEAD)
            def _():
                fetch_start(i + AHEAD)

            j = turn_of(i)
            slot_at = (i % (AHEAD + 1)) * 8
            for k, (grad, right, here) in enumerate(((d_out, s_n, gbuf), (d_in, u_n, kbuf))):
                left = [pair(wt[slot_at + k * SPILL + t]) for t in range(SPILL)] + [pair(here[j])]
                grad[expert(j)] = mm(jnp.concatenate(left, axis=1), right[...].reshape(3 * TASKS * R, D))

            @pl.when(i % 2 == 0)
            def _():
                for move in give(near(i // 2)):
                    move.start()

            @pl.when(i == 3)
            def _():
                merge(0, 0)
                ring_start()

            @pl.when((i % 2 == 1) & (i > 3))
            def _():
                merge((i - 3) // 2, 0)

            return carry

        lax.fori_loop(0, E, one, 0)
        merge(HALF - 1, 0)

    @pl.when(x == 0)
    def _():
        def arrive(t, carry):
            copy(outbox.at[t], inbox.at[t], K_DOWN + t, across).wait_recv()
            acc[...] += inbox[t]

            def one(j, inner):
                gate = gt0[j, pl.ds(t, 1)]
                total = jnp.zeros((8, R), F32)
                for tile in rows_of(D):
                    dy = inbox[t, tile]
                    rows = pl.ds(pl.multiple_of(j * D + tile.start, TILE), TILE)
                    total = total + rows8(d_in[rows] * dy)
                    d_out[rows] += gate * dy
                dgt[j, pl.ds(t, 1)] = jnp.sum(total, axis=0, keepdims=True)
                return inner

            lax.fori_loop(0, E, one, 0)
            return carry

        lax.fori_loop(0, TASKS - 1, arrive, 0)
        last = TASKS - 1
        copy(outbox.at[last], inbox.at[last], K_DOWN + last, across).wait_recv()
        acc[...] += inbox[last]

        def one(i, inner):
            j = turn_of(i)
            gate = gt0[j, last : last + 1]
            total = jnp.zeros((8, R), F32)
            for tile in rows_of(D):
                dy = inbox[last, tile]
                rows = pl.ds(pl.multiple_of(j * D + tile.start, TILE), TILE)
                total = total + rows8(d_in[rows] * dy)
                put(kbuf.at[j], (tile,), d_out[rows] + gate * dy)
            dgt[j, last : last + 1] = jnp.sum(total, axis=0, keepdims=True)
            return inner

        def part_of(first, stop):
            lax.fori_loop(2 * first, 2 * stop, one, 0)

            def js(g):
                return [turn_of(2 * (first + g) + r) for r in range(2)]

            def products(g, par):
                for e, j in enumerate(js(g)):
                    mixed = kbuf[j]
                    bb[par, e * H : (e + 1) * H] = mm(pair(w_out[j]), stack(mixed))
                    right = jnp.concatenate([mixed[:, :R], mixed[:, :R], mixed[:, R:]], axis=1)
                    d_out[expert(j)] = lax.dot_general(
                        pair(gbuf[j]), right, (((1,), (1,)), ((), ())), preferred_element_type=F32
                    )

            def pull(g, par):
                for e, j in enumerate(js(g)):
                    for tile in rows_of(H):
                        rows = shifted(tile, e)
                        kept_rows = pl.ds(pl.multiple_of(j * H + tile.start, TILE), TILE)
                        put(kp, (par, rows), bb[par, rows] * a2[kept_rows])

            def spread(g, par):
                left = jnp.concatenate([pair(w_in[j]) for j in js(g)], axis=1)
                right = [stack(kp[par, e * H : (e + 1) * H]) for e in range(GROUP)]
                acc[...] += mm(left, jnp.concatenate(right, axis=0))
                grad = mm(pair(kp[par]), u_n[0])
                for e, j in enumerate(js(g)):
                    d_in[expert(j)] = grad[e * H : (e + 1) * H]

            pipeline([products, pull, spread], stop - first)
            for k in range(first, stop):
                for move in give(near(k)):
                    move.start()

        part_of(0, 1)
        part_of(1, 4)
        merge(0, 0)
        ring_start()
        part_of(4, HALF)
        lax.fori_loop(1, HALF, merge, 0)

    def reduce_step(step, carry):
        for d, k in lanes:
            rs(d, k, step - 1, a1.at[slot(d, k, step - 1)]).wait_recv()
            a1[slot(d, k, step - 1)] += rd[d, at(k, holds(d, step))]
            rs(d, k, step, a1.at[slot(d, k, step - 1)]).start()
        return carry

    gates_own = pl.ds(pl.multiple_of(c * 2 * GROWS, 2 * GROWS), 2 * GROWS)
    gates_away = pl.ds(pl.multiple_of((1 - c) * 2 * GROWS, 2 * GROWS), 2 * GROWS)
    gain_row[...] = jnp.zeros_like(gain_row)

    @pl.when(x == 0)
    def _():
        dc = gate_backward(cs[...], [dgt[j, :TASKS] for j in range(E)], TASKS)
        dpool = (acc[...] + t_dot(wg[:FROWS], dc)).T
        pre_rows = pre[...]
        rho = lax.rsqrt(jnp.mean(pre_rows * pre_rows, axis=1, keepdims=True) + NORM_EPS)
        scaled = dpool * gain_ref[...]
        dots = jnp.mean(scaled * pre_rows, axis=1, keepdims=True)
        dp[mine] = rho * scaled - pre_rows * (rho * rho * rho * dots)
        for k, sec in enumerate((mate, across, diag)):
            copy(dp.at[mine], dp.at[mine], K_DP + c, sec, K_DP + k).start()
        gain_row[0:1] = jnp.sum(dpool * pre_rows * rho, axis=0, keepdims=True)
        grad = mm(wide(dc), u_n[0])
        dg[: FROWS // 2] = grad[: FROWS // 2]
        dg[2 * GROWS : 2 * GROWS + FROWS // 2] = grad[FROWS // 2 :]

    gates_move = copy(dg.at[gates_away], gb, K_DG, mate)
    gates_move.start()
    lax.fori_loop(1, 2, reduce_step, 0)

    for half_no in range(2):

        @pl.when(s != half_no)
        def _():
            rows = pl.ds(half_no * R, R)
            copy(dp.at[rows], dp.at[rows], K_DP + half_no, half_no).wait_recv()

    for k in range(2):

        @pl.when(s != 2 + k)
        def _():
            copy(tp.at[0], tw.at[k], K_TW + k, s).wait_recv()

    gates_move.wait_recv()
    sb[:TOWER] = tw[0, :TOWER] + tw[1, :TOWER]
    sb[GATE_AT:MISC_AT] = dg[gates_own] + gb[...]
    sb[MISC_AT : MISC_AT + 1] = gain_row[0:1]
    sb[MISC_AT + 1 : MISC_AT + 3] = tw[0, TOWER + 1 : TOWER + 3] + tw[1, TOWER + 1 : TOWER + 3]
    for f in range(2):
        sb[MISC_AT + 3 + f : MISC_AT + 4 + f] = jnp.sum(xf[f] * dp[...], axis=0, keepdims=True)
    sb[MISC_AT + 5 : MISC_AT + 6] = smo[1:2, :R] + smo[1:2, R:]
    sb[MISC_AT + 6 :] = jnp.zeros((sb.shape[0] - MISC_AT - 6, D), F32)

    def block(q):
        return pl.ds(pl.multiple_of(q * small_rows, 8), small_rows)

    def scatter(i):
        to = (me + i) % n
        return pltpu.make_async_remote_copy(
            src_ref=sb.at[block(to)],
            dst_ref=sr.at[me],
            send_sem=sr_send.at[i],
            recv_sem=sr_recv.at[me],
            device_id={"dp": to},
            device_id_type=MESH,
        )

    def scattered(i):
        by = (me + i) % n
        return pltpu.make_async_remote_copy(
            src_ref=sb.at[block(me)],
            dst_ref=sr.at[by],
            send_sem=sr_send.at[i],
            recv_sem=sr_recv.at[by],
            device_id={"dp": by},
            device_id_type=MESH,
        )

    def spread_sum(i):
        return pltpu.make_async_remote_copy(
            src_ref=so,
            dst_ref=sa.at[block(me)],
            send_sem=sa_send.at[i],
            recv_sem=sa_recv.at[me],
            device_id={"dp": (me + i) % n},
            device_id_type=MESH,
        )

    def gathered(i):
        by = (me + i) % n
        return pltpu.make_async_remote_copy(
            src_ref=so,
            dst_ref=sa.at[block(by)],
            send_sem=sa_send.at[i],
            recv_sem=sa_recv.at[by],
            device_id={"dp": by},
            device_id_type=MESH,
        )

    def each(act):
        def one(i, carry):
            act(i)
            return carry

        lax.fori_loop(1, n, one, 0)

    each(lambda i: scatter(i).start())
    lax.fori_loop(2, 4, reduce_step, 0)
    so[...] = sb[block(me)]

    def take(i):
        scattered(i).wait_recv()
        so[...] += sr[(me + i) % n]

    each(take)
    sa[block(me)] = so[...]
    each(lambda i: spread_sum(i).start())
    lax.fori_loop(4, 6, reduce_step, 0)
    each(lambda i: gathered(i).wait_recv())
    piece = sa.at[pl.ds(GATE_AT, KEPT)]
    for k, sec in enumerate((mate, across, diag)):
        copy(piece, sg.at[s], K_GO + s, sec, K_GO + k).start()
    sg[s] = sa[GATE_AT:SMALL]
    lax.fori_loop(6, n - 1, reduce_step, 0)
    for sec in (mate, across, diag):
        copy(piece, sg.at[sec], K_GO + sec, sec).wait_recv()
    misc = KEPT - 8
    count = sum(sg[q, misc + 5 : misc + 6] for q in range(TASKS))
    scale = float(2 * R * n) / jnp.sum(count, axis=1, keepdims=True)

    last = n - 2
    for d, k in lanes:
        q = holds(d, n - 1)
        rs(d, k, last, a1.at[slot(d, k, last)]).wait_recv()
        a1[slot(d, k, last)] = (a1[slot(d, k, last)] + rd[d, at(k, q)]) * scale
        ag(d, k, 0, a1.at[slot(d, k, last)], q).start()
        store(d, k, q, a1.at[slot(d, k, last)], 0).start()

    for f in range(2):
        xf[f] = dp[...] * (scale * fw_ref[0, f])
        pltpu.make_async_copy(xf.at[f], o_ig.at[:, f], local.at[2 + f]).start()
    for k in range(2):
        o_pred[:, k * R : (k + 1) * R] = tw[k, TOWER : TOWER + 1]
    for f in range(2):
        o_fw[0, f] = jnp.sum(sa[MISC_AT + 3 + f : MISC_AT + 4 + f] * scale)
    o_bias[0, 0] = jnp.sum(sa[MISC_AT + 2 : MISC_AT + 3] * scale)
    o_gain[...] = (sg[0, misc : misc + 1] + sg[1, misc : misc + 1]) * scale
    o_tout[...] = sa[MISC_AT + 1 : MISC_AT + 2, :TOWER] * scale
    o_tin[...] = (sa[:TOWER] * scale).T

    def order(t, carry):
        for sel in range(SEL):
            for e in range(BITS + 1):
                row = t * (SEL * (BITS + 1)) + sel * (BITS + 1) + e
                at0 = (e * SEL + sel) * TASKS
                cut = FROWS // 2
                o_gate[0, pl.ds(row, 1)] = sg[at0 // cut, pl.ds(at0 % cut + t, 1)] * scale
                o_gate[1, pl.ds(row, 1)] = sg[2 + t // 2, pl.ds((t % 2) * GROWS + e * SEL + sel, 1)] * scale
        return carry

    lax.fori_loop(0, TASKS, order, 0)

    def gather_step(step, carry):
        for d, k in lanes:
            q = holds(d, step - 1)
            ag(d, k, step - 1, landed(d, k, q), q).wait_recv()
            ag(d, k, step, landed(d, k, q), q).start()
            store(d, k, q, landed(d, k, q), step).start()
        return carry

    lax.fori_loop(1, n - 1, gather_step, 0)
    for d, k in lanes:
        q = holds(d, n - 2)
        ag(d, k, last, landed(d, k, q), q).wait_recv()
        store(d, k, q, landed(d, k, q), n - 1).start()

    def stored(step, carry):
        for d, k in lanes:
            store(d, k, 0, landed(d, k, 0), step).wait()
        return carry

    lax.fori_loop(0, n, stored, 0)

    def sent(step, carry):
        for d, k in lanes:
            rs(d, k, step, a1.at[slot(d, k, step)]).wait_send()
            ag(d, k, step, a1.at[slot(d, k, step)], 0).wait_send()
        return carry

    lax.fori_loop(0, n - 1, sent, 0)
    each(lambda i: scatter(i).wait_send())
    each(lambda i: spread_sum(i).wait_send())
    to_mate.wait_send()
    gates_move.wait_send()
    for e in range(HALF):
        for move in give(e):
            move.wait_send()
    for k in range(2):

        @pl.when(s != 2 + k)
        def _():
            copy(smo, sm.at[s], K_SM + s, 2 + k, K_SM + k).wait_send()
            copy(tin_ref, ti.at[s], K_TI + s, 2 + k, K_TI + k).wait_send()

    @pl.when(x == 0)
    def _():
        for t in range(TASKS):
            copy(outbox.at[t], inbox.at[t], K_UP + t, across).wait_send()
        for k, sec in enumerate((mate, across, diag)):
            copy(dp.at[mine], dp.at[mine], K_DP + c, sec, K_DP + k).wait_send()

    @pl.when(x == 1)
    def _():
        copy(pre2, pre1, K_P + 1, across).wait_send()
        for t in range(TASKS):
            copy(outbox.at[t], inbox.at[t], K_DOWN + t, across).wait_send()

            @pl.when(t != s)
            def _():
                copy(tp.at[t], tw.at[c], K_TW + c, t, K_TW + t).wait_send()

    for k, sec in enumerate((mate, across, diag)):
        copy(piece, sg.at[s], K_GO + s, sec, K_GO + k).wait_send()
    for f in range(2):
        pltpu.make_async_copy(xf.at[f], o_ig.at[:, f], local.at[2 + f]).wait()


def hand_over(count, *refs):
    held = refs[2 * count : 3 * count]
    sems = refs[-1]
    reads = [pltpu.make_async_copy(refs[k], held[k], sems.at[0, k]) for k in range(count)]
    writes = [pltpu.make_async_copy(held[k], refs[count + k], sems.at[1, k]) for k in range(count)]
    for move in reads:
        move.start()
    for read, write in zip(reads, writes):
        read.wait()
        write.start()
    for move in writes:
        move.wait()


def body(
    field_inputs,
    field_weight,
    norm_gain,
    gate_weight,
    expert_in,
    expert_out,
    tower_in,
    tower_out,
    tower_bias,
    labels,
    source_ids,
    task_table,
):
    n = lax.axis_size("dp")
    rows = field_inputs.shape[0]
    half = rows // 2
    subs = 2
    small_rows = -(-SMALL // (8 * n)) * 8
    used = TASKS * SEL * (BITS + 1)

    vmem = pl.BlockSpec(memory_space=pltpu.VMEM)
    smem = pl.BlockSpec(memory_space=pltpu.SMEM)
    hbm = pl.BlockSpec(memory_space=pl.ANY)

    def bf(*shape):
        return pltpu.VMEM(shape, BF16)

    def f32(*shape):
        return pltpu.VMEM(shape, F32)

    def out(*shape):
        return jax.ShapeDtypeStruct(shape, F32)

    dma = pltpu.SemaphoreType.DMA
    *sums, _ = pl.pallas_call(
        partial(kernel, n, subs, small_rows),
        out_shape=(
            out(1, rows),
            out(rows, 2, D),
            out(1, 2),
            out(1, D),
            out(2, used, D),
            out(HALF * H, D),
            out(HALF * H, D),
            out(D, TOWER),
            out(1, TOWER),
            out(1, 1),
            jax.ShapeDtypeStruct((E, 2 * SPILL, H, 2 * half), BF16),
        ),
        in_specs=[hbm, smem, vmem, vmem, hbm, hbm, vmem, vmem, smem, vmem, vmem, smem],
        out_specs=(vmem, hbm, smem, vmem, vmem, hbm, hbm, vmem, vmem, smem, hbm),
        scratch_shapes=[
            bf(2 * E, H, 2 * D),
            bf(E, D, 2 * H),
            bf(E, H, 2 * D),
            f32(E * H, half),
            f32(E * H, half),
            f32(E * H, D),
            f32(E * H, D),
            bf(E, H, 2 * half),
            bf(E, H, 2 * half),
            bf(2, GROUP * H, 2 * half),
            f32(2, HALF * H, D),
            f32(2, rows, D),
            f32(rows, D),
            f32(half, D),
            f32(half, D),
            f32(half, D),
            f32(half, D),
            f32(TASKS, D, half),
            f32(TASKS, D, half),
            bf(3 * D, half),
            bf(TASKS, 3 * half, D),
            bf(3 * D, half),
            bf(TASKS, 3 * half, D),
            f32(2, GROUP * H, half),
            f32(D, half),
            f32(TASKS * GROWS, D),
            f32(E, 1, half),
            f32(E, TASKS, half),
            f32(FROWS, half),
            f32(E, TASKS, half),
            f32(TASKS * GROWS, D),
            f32(2 * GROWS, D),
            f32(TASKS, 8, rows),
            f32(8, rows),
            f32(TASKS, D, TOWER),
            f32(TASKS, TOWER + 8, D),
            f32(2, TOWER + 8, D),
            f32(rows, D),
            f32(8, D),
            f32(half, E * TASKS),
            bf(3 * D, half),
            f32(E, 1, half),
            f32(GROWS, half),
            f32(D, half),
            f32(D, half),
            f32(2 * TOWER, half),
            f32(n * small_rows, D),
            f32(n, small_rows, D),
            f32(small_rows, D),
            f32(n * small_rows, D),
            f32(TASKS, KEPT, D),
            dma((K_COUNT,)),
            dma((K_COUNT,)),
            dma((6,)),
            dma((AHEAD + 1,)),
            pltpu.SemaphoreType.REGULAR,
            dma((2, subs, n - 1)),
            dma((2, subs, n - 1)),
            dma((2, subs, n - 1)),
            dma((2, subs, n - 1)),
            dma((2, subs, n)),
            dma((n,)),
            dma((n,)),
            dma((n,)),
            dma((n,)),
        ],
        compiler_params=pltpu.CompilerParams(
            collective_id=0, has_side_effects=True, vmem_limit_bytes=64 * 1024 * 1024 - 65536
        ),
    )(
        field_inputs,
        field_weight.reshape(1, 2),
        norm_gain.reshape(1, D),
        gate_weight.swapaxes(1, 2),
        expert_in.reshape(HALF * H, D),
        expert_out.reshape(HALF * H, D),
        tower_in.reshape(D, TOWER),
        tower_out,
        tower_bias.reshape(1, 1),
        labels.reshape(1, rows),
        source_ids.reshape(1, rows),
        task_table.reshape(1, SOURCES),
    )
    pred, ig, fw, gain, gate, d_in, d_out, tin, tout, bias = pl.pallas_call(
        partial(hand_over, len(sums)),
        out_shape=tuple(jax.ShapeDtypeStruct(v.shape, v.dtype) for v in sums),
        in_specs=[hbm] * len(sums),
        out_specs=(hbm,) * len(sums),
        scratch_shapes=[pltpu.VMEM(v.shape, v.dtype) for v in sums] + [dma((2, len(sums)))],
        compiler_params=pltpu.CompilerParams(vmem_limit_bytes=64 * 1024 * 1024 - 65536),
    )(*sums)
    return (
        pred.reshape(rows, 1),
        ig,
        fw.reshape(2),
        gain.reshape(D),
        gate.swapaxes(1, 2),
        d_in.reshape(HALF, D, H),
        d_out.reshape(HALF, H, D),
        tin.reshape(1, D, TOWER),
        tout,
        bias.reshape(1),
    )


def solution(mesh):
    in_specs = (
        P("dp", "section", None),
        P("section"),
        P(),
        P(),
        P("section", None, None),
        P("section", None, None),
        P("section", None, None),
        P("section", None),
        P("section"),
        P("dp", "section"),
        P("dp"),
        P(None, "section"),
    )
    out_specs = (
        P("dp", "section"),
        P("dp", "section", None),
        P("section"),
        P(),
        P(),
        P("section", None, None),
        P("section", None, None),
        P("section", None, None),
        P("section", None),
        P("section"),
    )
    return jax.shard_map(body, mesh=mesh, in_specs=in_specs, out_specs=out_specs, check_vma=False)
```

```python
from functools import partial

import jax
import jax.numpy as jnp
from jax import lax
from jax.experimental import pallas as pl
from jax.experimental.pallas import tpu as pltpu
from jax.sharding import PartitionSpec as P

D = 256
H = 256
E = 16
TASKS = 4
SEL = 4
BITS = 4
TOWER = 128
SOURCES = 32
HALF = E // 2
GROWS = 32
FROWS = 96

STEP_SLOPE = 0.6
ENTROPY_WEIGHT = 0.05
NORM_EPS = 1e-05
GELU_A = 0.7978845608028654
GELU_B = 0.044715

F32 = jnp.float32
BF16 = jnp.bfloat16
MESH = pl.DeviceIdType.MESH

K_W, K_P, K_SM, K_TI, K_UP, K_DOWN, K_TW, K_DG, K_DP, K_GO, K_DX = 0, 2, 4, 8, 12, 16, 20, 24, 25, 28, 32
K_COUNT = 48
GROUP = 2
TILE = 32
STEPS = E // GROUP
SPILL = TASKS - 1
AHEAD = 3

GATE_AT = TOWER
MISC_AT = GATE_AT + 2 * GROWS
SMALL = MISC_AT + 8
KEPT = SMALL - GATE_AT


def split(x):
    hi = x.astype(BF16)
    return hi, (x - hi.astype(F32)).astype(BF16)


def wide(x):
    hi, lo = split(x)
    return jnp.concatenate([hi, lo, hi], axis=1)


def tall(x):
    hi, lo = split(x)
    return jnp.concatenate([hi, hi, lo], axis=0)


def put(ref, at, x):
    k = x.shape[1]
    hi, lo = split(x)
    ref[*at, :k] = hi
    ref[*at, k:] = lo


def stack(x):
    k = x.shape[1] // 2
    return jnp.concatenate([x[:, :k], x[:, :k], x[:, k:]], axis=0)


def mm(a, b):
    return jnp.dot(a, b, preferred_element_type=F32)


def pair(x):
    k = x.shape[1] // 2
    return jnp.concatenate([x, x[:, :k]], axis=1)


def gelu_pair(x):
    x2 = x * x
    h = 0.5 + 0.5 * jnp.tanh(x * (GELU_A + (GELU_A * GELU_B) * x2))
    g = x * h
    slope = h + g * (1.0 - h) * (2.0 * GELU_A + (6.0 * GELU_A * GELU_B) * x2)
    return g, slope


def rows8(x):
    return jnp.sum(x.reshape(x.shape[0] // 8, 8, x.shape[1]), axis=0)


def over_selectors(v, groups, op):
    parts = [v[k * groups : (k + 1) * groups] for k in range(SEL)]
    return op(op(parts[0], parts[1]), op(parts[2], parts[3]))


def to_selectors(v):
    return jnp.concatenate([v] * SEL, axis=0)


def gate_state(c, groups):
    w = SEL * groups
    zs = [c[w * b : w * b + w] * STEP_SLOPE for b in range(BITS)]
    alpha = c[w * BITS : w * BITS + w]
    ups, downs, sig_p, sig_n = [], [], [], []
    for z in zs:
        e = jnp.exp(-jnp.abs(z))
        tail = jnp.log1p(e)
        ups.append(jnp.minimum(z, 0.0) - tail)
        downs.append(jnp.minimum(-z, 0.0) - tail)
        big = 1.0 / (1.0 + e)
        small = e * big
        sig_p.append(jnp.where(z >= 0.0, big, small))
        sig_n.append(jnp.where(z >= 0.0, small, big))
    low = [(ups[0] if k & 1 else downs[0]) + (ups[1] if k & 2 else downs[1]) for k in range(4)]
    high = [(ups[2] if k & 1 else downs[2]) + (ups[3] if k & 2 else downs[3]) for k in range(4)]
    log_r = [low[j & 3] + high[j >> 2] for j in range(E)]
    r = [jnp.exp(v) for v in log_r]
    top = jnp.exp(alpha - to_selectors(over_selectors(alpha, groups, jnp.maximum)))
    mix = top / to_selectors(over_selectors(top, groups, jnp.add))
    return log_r, r, mix, sig_p, sig_n


def gate_forward(c, groups):
    _, r, mix, _, _ = gate_state(c, groups)
    return [over_selectors(mix * v, groups, jnp.add) for v in r]


def gate_backward(c, dgate, groups):
    log_r, r, mix, sig_p, sig_n = gate_state(c, groups)
    total = jnp.zeros_like(mix)
    on = [jnp.zeros_like(mix) for _ in range(BITS)]
    off = [jnp.zeros_like(mix) for _ in range(BITS)]
    for j in range(E):
        dg = to_selectors(dgate[j])
        total = total + dg * r[j]
        dlog = r[j] * (mix * dg - ENTROPY_WEIGHT * (log_r[j] + 1.0))
        for b in range(BITS):
            if j >> b & 1:
                on[b] = on[b] + dlog
            else:
                off[b] = off[b] + dlog
    dalpha = mix * (total - to_selectors(over_selectors(mix * total, groups, jnp.add)))
    dz = [STEP_SLOPE * (on[b] * sig_n[b] - off[b] * sig_p[b]) for b in range(BITS)]
    used = SEL * (BITS + 1) * groups
    pad = jnp.zeros(((-used) % GROWS, c.shape[1]), F32)
    return jnp.concatenate(dz + [dalpha, pad], axis=0)


def t_dot(a, b):
    ah, al = split(a)
    left = jnp.concatenate([ah, al, ah], axis=0)
    return lax.dot_general(left, tall(b), (((0,), (0,)), ((), ())), preferred_element_type=F32)


def pipeline(stages, count):
    for step in range(count + len(stages) - 1):
        for k, stage in enumerate(stages):
            if 0 <= step - k < count:
                stage(step - k, (step - k) % 2)


def kernel(
    n,
    sizes,
    small_rows,
    x_ref,
    fw_ref,
    gain_ref,
    gate_ref,
    win_ref,
    wout_ref,
    tin_ref,
    tout_ref,
    tbias_ref,
    labels_ref,
    ids_ref,
    table_ref,
    o_pred,
    o_ig,
    o_fw,
    o_gain,
    o_gate,
    o_in,
    o_out,
    o_tin,
    o_tout,
    o_bias,
    kept,
    wt,
    w_in,
    w_out,
    a1,
    a2,
    d_in,
    d_out,
    gbuf,
    kbuf,
    kp,
    rd,
    xf,
    part,
    pre0,
    pre1,
    pre2,
    pre,
    inbox,
    outbox,
    u_t,
    u_n,
    s_t,
    s_n,
    bb,
    acc,
    wg,
    gt,
    gt0,
    cs,
    dgt,
    dg,
    gb,
    sm,
    smo,
    ti,
    tp,
    tw,
    dp,
    gain_row,
    columns,
    u_next,
    gt_next,
    cs_next,
    acc_b,
    held,
    tm,
    sb,
    sr,
    so,
    sa,
    sg,
    send,
    recv,
    local,
    fetch_sem,
    ready,
    rs_send,
    rs_recv,
    ag_send,
    ag_recv,
    store_sem,
    sr_send,
    sr_recv,
    sa_send,
    sa_recv,
):
    s = lax.axis_index("section")
    x = s // 2
    c = s % 2
    mate = s + 1 - 2 * c
    across = s + 2 - 4 * x
    diag = 3 - s
    R = part.shape[0] // 2
    mine = pl.ds(pl.multiple_of(c * R, R), R)
    theirs = pl.ds(pl.multiple_of((1 - c) * R, R), R)

    me = lax.axis_index("dp")
    odd = me % 2
    p = (1 - odd) * (me // 2) + odd * (n - 1 - me // 2)

    def ring_id(q):
        far = q // (n // 2)
        return (1 - far) * 2 * q + far * (2 * (n - 1 - q) + 1)

    nbr = [ring_id((p + 1) % n), ring_id((p + n - 1) % n)]

    barrier = pltpu.get_barrier_semaphore()
    for sec in (mate, across, diag):
        pl.semaphore_signal(barrier, inc=1, device_id={"section": sec}, device_id_type=MESH)

    def greet(i, carry):
        pl.semaphore_signal(barrier, inc=1, device_id={"dp": (me + i) % n}, device_id_type=MESH)
        return carry

    lax.fori_loop(1, n, greet, 0)
    fields = [pltpu.make_async_copy(x_ref.at[:, f], xf.at[f], local.at[2 + f]) for f in range(2)]
    for f in fields:
        f.start()
    own = pl.ds(pl.multiple_of(c * HALF * H, HALF * H), HALF * H)
    own_in = pltpu.make_async_copy(win_ref, d_in.at[own], local.at[0])
    own_out = pltpu.make_async_copy(wout_ref, d_out.at[own], local.at[1])
    own_in.start()
    own_out.start()
    pl.semaphore_wait(barrier, 3 + n - 1)

    def copy(src, dst, k, sec, ks=None):
        return pltpu.make_async_remote_copy(
            src_ref=src,
            dst_ref=dst,
            send_sem=send.at[k if ks is None else ks],
            recv_sem=recv.at[k],
            device_id={"section": sec},
            device_id_type=MESH,
        )

    def expert(j, count=1):
        return pl.ds(pl.multiple_of(j * H, H), count * H)

    for f in fields:
        f.wait()
    part[...] = xf[0] * fw_ref[0, 0] + xf[1] * fw_ref[0, 1]
    to_mate = copy(part.at[theirs], pre0, K_P, mate)
    to_mate.start()
    swap_in = copy(d_in.at[own], d_in.at[own], K_W, mate)
    swap_out = copy(d_out.at[own], d_out.at[own], K_W + 1, mate)
    own_in.wait()
    swap_in.start()
    own_out.wait()
    swap_out.start()

    ids = ids_ref[...]
    mask = jnp.zeros(ids.shape, F32)
    for q in range(SOURCES):
        mask = mask + jnp.where(ids == q, table_ref[0, q].astype(F32), 0.0)
    smo[...] = jnp.zeros_like(smo)
    smo[0:1] = labels_ref[...]
    smo[1:2] = mask
    smo[2:3, :TOWER] = tout_ref[...]
    smo[3:4] = jnp.zeros((1, 2 * R), F32) + tbias_ref[0, 0]
    for k in range(2):

        @pl.when(s != 2 + k)
        def _():
            copy(smo, sm.at[s], K_SM + s, 2 + k, K_SM + k).start()
            copy(tin_ref, ti.at[s], K_TI + s, 2 + k, K_TI + k).start()

    to_mate.wait_recv()

    @pl.when(x == 1)
    def _():
        pre2[...] = part[mine] + pre0[...]
        copy(pre2, pre1, K_P + 1, across).start()
        sm[s] = smo[...]
        ti[s] = tin_ref[...]

    wg[...] = jnp.zeros_like(wg)

    @pl.when(x == 0)
    def _():
        def order(t, carry):
            for sel in range(SEL):
                for e in range(BITS + 1):
                    row = t * (SEL * (BITS + 1)) + sel * (BITS + 1) + e
                    wg[pl.ds((e * SEL + sel) * TASKS + t, 1)] = gate_ref[0, pl.ds(row, 1)]
            return carry

        lax.fori_loop(0, TASKS, order, 0)

    @pl.when(x == 1)
    def _():
        def order(t, carry):
            for sel in range(SEL):
                for e in range(BITS + 1):
                    row = t * (SEL * (BITS + 1)) + sel * (BITS + 1) + e
                    wg[pl.ds(t * GROWS + e * SEL + sel, 1)] = gate_ref[1, pl.ds(row, 1)]
            return carry

        lax.fori_loop(0, TASKS, order, 0)

    def keep_plain(e, carry):
        put(w_in.at[e], (slice(None),), d_in[expert(e)])
        put(w_out.at[e], (slice(None),), d_out[expert(e)])
        return carry

    def keep_flipped(e, carry):
        put(wt.at[e], (slice(None),), d_in[expert(e)].T)
        put(wt.at[E + e], (slice(None),), d_out[expert(e)].T)
        return carry

    lax.fori_loop(c * HALF, c * HALF + HALF, keep_plain, 0)
    swap_in.wait()
    swap_out.wait()
    lax.fori_loop((1 - c) * HALF, (1 - c) * HALF + HALF, keep_plain, 0)

    def rows_of(size):
        return [slice(a, a + TILE) for a in range(0, size, TILE)]

    def shifted(tile, e):
        return slice(e * H + tile.start, e * H + tile.stop)

    chunk = HALF * H // n
    subs = len(sizes)
    starts = [sum(sizes[:k]) for k in range(subs)]
    lanes = [(d, k) for d in range(2) for k in range(subs)]

    def at(k, q):
        return pl.ds(pl.multiple_of(q * chunk + starts[k], 8), sizes[k])

    def holds(d, step):
        return (p + n - step) % n if d == 0 else (p + step) % n

    def slot(d, k, step):
        return pl.ds(pl.multiple_of((n - 1) * (d * chunk + starts[k]) + step * sizes[k], 8), sizes[k])

    def rs(d, k, step, src):
        return pltpu.make_async_remote_copy(
            src_ref=src,
            dst_ref=a1.at[slot(d, k, step)],
            send_sem=rs_send.at[d, k, step],
            recv_sem=rs_recv.at[d, k, step],
            device_id={"dp": nbr[d]},
            device_id_type=MESH,
        )

    results = (o_in, o_out)

    def landed(d, k, q):
        return a2.at[pl.ds(pl.multiple_of(d * HALF * H + q * chunk + starts[k], 8), sizes[k])]

    def store(d, k, q, src, step):
        return pltpu.make_async_copy(src, results[d].at[at(k, q)], store_sem.at[d, k, step])

    def ag(d, k, step, src, q):
        return pltpu.make_async_remote_copy(
            src_ref=src,
            dst_ref=landed(d, k, q),
            send_sem=ag_send.at[d, k, step],
            recv_sem=ag_recv.at[d, k, step],
            device_id={"dp": nbr[d]},
            device_id_type=MESH,
        )

    def give(e):
        j = (1 - c) * HALF + e
        return (
            copy(d_in.at[expert(j)], rd.at[0, expert(e)], K_DX + e, mate),
            copy(d_out.at[expert(j)], rd.at[1, expert(e)], K_DX + HALF + e, mate),
        )

    start_at = p * chunk // H

    def near(k):
        return (start_at + HALF + ((k + 1) // 2) * (1 - 2 * (k % 2))) % HALF

    def turn_of(i):
        own_turn = i % 2
        return ((1 - own_turn) * (1 - c) + own_turn * c) * HALF + near(i // 2)

    def fetch(i):
        at = pl.ds((i % (AHEAD + 1)) * 8, 2 * SPILL)
        return pltpu.make_async_copy(kept.at[turn_of(i)], wt.at[at], fetch_sem.at[i % (AHEAD + 1)])

    def fetch_start(i):
        for k in range(2 * SPILL):
            slab = (i % (AHEAD + 1)) * 8 + k
            pltpu.make_async_copy(
                kept.at[turn_of(i), k], wt.at[slab], fetch_sem.at[i % (AHEAD + 1)]
            ).start()

    def greet_ring():
        for dev in nbr:
            pl.semaphore_signal(ready, inc=1, device_id={"dp": dev}, device_id_type=MESH)

    def merge(k, carry):
        e = near(k)
        for move in give(e):
            move.wait_recv()
        rows = expert(e)
        rd[0, rows] = (rd[0, rows] + d_in[expert(c * HALF + e)]).T
        rd[1, rows] += d_out[expert(c * HALF + e)]
        return carry

    def ring_start():
        pl.semaphore_wait(ready, 2)
        for d, k in lanes:
            rs(d, k, 0, rd.at[d, at(k, holds(d, 0))]).start()

    @pl.when(x == 0)
    def _():
        copy(pre2, pre1, K_P + 1, across).wait_recv()
        pre_rows = part[mine] + pre0[...] + pre1[...]
        pre[...] = pre_rows
        rho = lax.rsqrt(jnp.mean(pre_rows * pre_rows, axis=1, keepdims=True) + NORM_EPS)
        pooled = pre_rows * rho * gain_ref[...]
        acc[...] = pooled
        u_n[0] = tall(pooled)
        u_t[...] = tall(pooled.T)
        logits = mm(wide(wg[:FROWS]), u_t[...])
        cs[...] = logits
        gates = gate_forward(logits, TASKS)
        for j, g in enumerate(gates):
            gt0[j] = g

        def first(g, par):
            left = jnp.concatenate([u_n[0, :R], u_n[0, 2 * R :], u_n[0, :R]], axis=1)
            for e in range(GROUP):
                bb[par, e * H : (e + 1) * H] = mm(left, stack(w_in[g * GROUP + e]))

        def activate(g, par):
            for e in range(GROUP):
                j = g * GROUP + e
                for tile in rows_of(R):
                    value, slope = gelu_pair(bb[par, shifted(tile, e)])
                    a1[shifted(tile, j)] = value
                    a2[shifted(tile, j)] = slope
                    put(gbuf, (j, tile), value)

        def finish(g, par):
            for e in range(GROUP):
                j = g * GROUP + e
                d_in[expert(j)] = mm(pair(gbuf[j]), stack(w_out[j]))

        pipeline([first, activate, finish], STEPS)
        columns[...] = jnp.concatenate(gates, axis=0).T

        for t in range(TASKS):

            def mix(i, carry):
                tile = pl.ds(pl.multiple_of(i * TILE, TILE), TILE)
                cols = columns[tile]
                total = acc[tile]
                for j in range(E):
                    rows = pl.ds(pl.multiple_of(j * R + i * TILE, TILE), TILE)
                    total = total + cols[:, j * TASKS + t : j * TASKS + t + 1] * d_in[rows]
                outbox[t, tile] = total
                return carry

            lax.fori_loop(0, R // TILE, mix, 0)
            copy(outbox.at[t], inbox.at[t], K_UP + t, across).start()

        def flip(j, carry):
            value = a1[expert(j)].T
            a1[expert(j)] = value
            put(gbuf.at[j], (slice(None),), value)
            a2[expert(j)] = a2[expert(j)].T
            d_in[expert(j)] = d_in[expert(j)].T
            return carry

        lax.fori_loop(0, E, flip, 0)
        greet_ring()
        d_out[...] = jnp.zeros_like(d_out)
        acc[...] = jnp.zeros_like(acc)

    @pl.when(x == 1)
    def _():
        lax.fori_loop(0, E, keep_flipped, 0)
        for q in range(TASKS):

            @pl.when(s != q)
            def _():
                copy(smo, sm.at[q], K_SM + q, q).wait_recv()
                copy(tin_ref, ti.at[q], K_TI + q, q).wait_recv()

        def keep(k, t):
            return pltpu.make_async_copy((gbuf, kbuf)[k], kept.at[:, k * SPILL + t], local.at[4 + k])

        def keep_start(k, t):
            def one(j, carry):
                pltpu.make_async_copy((gbuf, kbuf)[k].at[j], kept.at[j, k * SPILL + t], local.at[4 + k]).start()
                return carry

            @pl.when(t < SPILL)
            def _():
                lax.fori_loop(0, E, one, 0)

        def gate_rows(t):
            return pl.ds(pl.multiple_of(t * GROWS, GROWS), GROWS)

        def enter(t):
            u = inbox[t]
            u_n[t] = tall(u)
            flipped = u.T
            stacked = tall(flipped)
            u_next[...] = stacked
            acc[...] = flipped
            logits = mm(wide(wg[gate_rows(t)]), stacked)
            cs_next[...] = logits
            for j, g in enumerate(gate_forward(logits, 1)):
                gt_next[j] = g

        def turn():
            u_t[...] = u_next[...]
            gt[...] = gt_next[...]
            cs[GROWS : 2 * GROWS] = cs[:GROWS]
            cs[:GROWS] = cs_next[...]

        def leave(t, at):
            dc = gate_backward(cs[at : at + GROWS], [dgt[j, 0:1] for j in range(E)], 1)
            outbox[t] = acc_b[...] + t_dot(wg[gate_rows(t)], dc)
            dg[gate_rows(t)] = mm(wide(dc), u_n[t])

        cs[...] = jnp.zeros_like(cs)
        dgt[...] = jnp.zeros_like(dgt)
        acc_b[...] = jnp.zeros_like(acc_b)
        copy(outbox.at[0], inbox.at[0], K_UP, across).wait_recv()
        enter(0)
        turn()

        def task(t, carry):
            @pl.when(t > 0)
            def _():
                keep(0, 0).wait()

            def first(g, par):
                left = wt[g * GROUP : (g + 1) * GROUP].reshape(GROUP * H, 2 * D)
                bb[par] = mm(pair(left), u_t[...])

            def activate(g, par):
                for e in range(GROUP):
                    j = g * GROUP + e
                    for tile in rows_of(H):
                        value, slope = gelu_pair(bb[par, shifted(tile, e)])
                        a1[shifted(tile, j)] = value
                        a2[shifted(tile, j)] = slope
                        put(gbuf, (j, tile), value * gt[j])

            def finish(g, par):
                js = range(g * GROUP, (g + 1) * GROUP)
                left = jnp.concatenate([pair(wt[E + j]) for j in js], axis=1)
                acc[...] += mm(left, jnp.concatenate([stack(gbuf[j]) for j in js], axis=0))

            before = (t + TASKS - 1) % TASKS
            leave(before, GROWS)
            pipeline([first, activate, finish], STEPS)
            keep_start(0, t)

            @pl.when(t > 0)
            def _():
                copy(outbox.at[before], inbox.at[before], K_DOWN + before, across).start()

            second = acc[...]
            held[...] = second
            tower = ti[t]
            g, slope = gelu_pair(mm(wide(tower.T), tall(second)))
            info = sm[t]
            out_col = info[:, :TOWER].T[:, 2:3]
            here = sm[t, :, mine]
            logit = jnp.sum(g * out_col, axis=0, keepdims=True) + here[3:4]
            prob = jax.nn.sigmoid(logit)
            dlogit = here[1:2] * (prob - here[0:1])
            m = dlogit * out_col * slope
            dy = mm(wide(tower), tall(m))
            s_t[...] = tall(dy)
            acc_b[...] = dy
            tm[:TOWER] = m
            tm[TOWER:] = g * dlogit
            tp[t, TOWER : TOWER + 1] = prob
            tp[t, TOWER + 2 : TOWER + 3] = dlogit
            tp[t, TOWER + 3 :] = jnp.zeros((5, R), F32)

            @pl.when(t > 0)
            def _():
                keep(1, 0).wait()

            @pl.when(t == TASKS - 1)
            def _():
                for i in range(AHEAD):
                    fetch_start(i)

            after = jnp.minimum(t + 1, TASKS - 1)

            @pl.when(t < TASKS - 1)
            def _():
                copy(outbox.at[after], inbox.at[after], K_UP + after, across).wait_recv()

            def back(g, par):
                left = w_out[g * GROUP : (g + 1) * GROUP].reshape(GROUP * H, 2 * D)
                bb[par] = mm(pair(left), s_t[...])

            def pull(g, par):
                for e in range(GROUP):
                    j = g * GROUP + e
                    total = jnp.zeros((8, R), F32)
                    for tile in rows_of(H):
                        grad = bb[par, shifted(tile, e)]
                        total = total + rows8(grad * a1[shifted(tile, j)])
                        put(kbuf, (j, tile), grad * a2[shifted(tile, j)] * gt[j])
                    dgt[j, 0:1] = jnp.sum(total, axis=0, keepdims=True)

            def spread(g, par):
                js = range(g * GROUP, (g + 1) * GROUP)
                left = jnp.concatenate([pair(w_in[j]) for j in js], axis=1)
                acc_b[...] += mm(left, jnp.concatenate([stack(kbuf[j]) for j in js], axis=0))

            enter(after)
            s_n[t] = tall(acc_b[...].T)
            tp[t, :TOWER] = mm(wide(tm[:TOWER]), tall(held[...].T))
            out_grad = jnp.sum(tm[TOWER:], axis=1, keepdims=True)
            out_row = jnp.broadcast_to(out_grad, (TOWER, TOWER)).T[0:1]
            tp[t, TOWER + 1 : TOWER + 2] = jnp.concatenate([out_row, jnp.zeros_like(out_row)], axis=1)
            pipeline([back, pull, spread], STEPS)
            keep_start(1, t)
            turn()

            @pl.when(t != s)
            def _():
                copy(tp.at[t], tw.at[c], K_TW + c, t, K_TW + t).start()

            @pl.when(t == s)
            def _():
                tw[c] = tp[t]

            return carry

        lax.fori_loop(0, TASKS, task, 0)
        last_task = TASKS - 1
        leave(last_task, GROWS)
        copy(outbox.at[last_task], inbox.at[last_task], K_DOWN + last_task, across).start()
        greet_ring()

    @pl.when(x == 1)
    def _():
        def one(i, carry):
            fetch(i).wait()

            @pl.when(i < E - AHEAD)
            def _():
                fetch_start(i + AHEAD)

            j = turn_of(i)
            slot_at = (i % (AHEAD + 1)) * 8
            for k, (grad, right, here) in enumerate(((d_out, s_n, gbuf), (d_in, u_n, kbuf))):
                left = [pair(wt[slot_at + k * SPILL + t]) for t in range(SPILL)] + [pair(here[j])]
                grad[expert(j)] = mm(jnp.concatenate(left, axis=1), right[...].reshape(3 * TASKS * R, D))

            @pl.when(i % 2 == 0)
            def _():
                for move in give(near(i // 2)):
                    move.start()

            @pl.when(i == 3)
            def _():
                merge(0, 0)
                ring_start()

            @pl.when((i % 2 == 1) & (i > 3))
            def _():
                merge((i - 3) // 2, 0)

            return carry

        lax.fori_loop(0, E, one, 0)
        merge(HALF - 1, 0)

    @pl.when(x == 0)
    def _():
        def arrive(t, carry):
            copy(outbox.at[t], inbox.at[t], K_DOWN + t, across).wait_recv()
            acc[...] += inbox[t]

            def one(j, inner):
                gate = gt0[j, pl.ds(t, 1)]
                total = jnp.zeros((8, R), F32)
                for tile in rows_of(D):
                    dy = inbox[t, tile]
                    rows = pl.ds(pl.multiple_of(j * D + tile.start, TILE), TILE)
                    total = total + rows8(d_in[rows] * dy)
                    d_out[rows] += gate * dy
                dgt[j, pl.ds(t, 1)] = jnp.sum(total, axis=0, keepdims=True)
                return inner

            lax.fori_loop(0, E, one, 0)
            return carry

        lax.fori_loop(0, TASKS - 1, arrive, 0)
        last = TASKS - 1
        copy(outbox.at[last], inbox.at[last], K_DOWN + last, across).wait_recv()
        acc[...] += inbox[last]

        def one(i, inner):
            j = turn_of(i)
            gate = gt0[j, last : last + 1]
            total = jnp.zeros((8, R), F32)
            for tile in rows_of(D):
                dy = inbox[last, tile]
                rows = pl.ds(pl.multiple_of(j * D + tile.start, TILE), TILE)
                total = total + rows8(d_in[rows] * dy)
                put(kbuf.at[j], (tile,), d_out[rows] + gate * dy)
            dgt[j, last : last + 1] = jnp.sum(total, axis=0, keepdims=True)
            return inner

        def part_of(first, stop):
            lax.fori_loop(2 * first, 2 * stop, one, 0)

            def js(g):
                return [turn_of(2 * (first + g) + r) for r in range(2)]

            def products(g, par):
                for e, j in enumerate(js(g)):
                    mixed = kbuf[j]
                    bb[par, e * H : (e + 1) * H] = mm(pair(w_out[j]), stack(mixed))
                    right = jnp.concatenate([mixed[:, :R], mixed[:, :R], mixed[:, R:]], axis=1)
                    d_out[expert(j)] = lax.dot_general(
                        pair(gbuf[j]), right, (((1,), (1,)), ((), ())), preferred_element_type=F32
                    )

            def pull(g, par):
                for e, j in enumerate(js(g)):
                    for tile in rows_of(H):
                        rows = shifted(tile, e)
                        kept_rows = pl.ds(pl.multiple_of(j * H + tile.start, TILE), TILE)
                        put(kp, (par, rows), bb[par, rows] * a2[kept_rows])

            def spread(g, par):
                left = jnp.concatenate([pair(w_in[j]) for j in js(g)], axis=1)
                right = [stack(kp[par, e * H : (e + 1) * H]) for e in range(GROUP)]
                acc[...] += mm(left, jnp.concatenate(right, axis=0))
                grad = mm(pair(kp[par]), u_n[0])
                for e, j in enumerate(js(g)):
                    d_in[expert(j)] = grad[e * H : (e + 1) * H]

            pipeline([products, pull, spread], stop - first)
            for k in range(first, stop):
                for move in give(near(k)):
                    move.start()

        part_of(0, 1)
        part_of(1, 4)
        merge(0, 0)
        ring_start()
        part_of(4, HALF)
        lax.fori_loop(1, HALF, merge, 0)

    def reduce_step(step, carry):
        for d, k in lanes:
            rs(d, k, step - 1, a1.at[slot(d, k, step - 1)]).wait_recv()
            a1[slot(d, k, step - 1)] += rd[d, at(k, holds(d, step))]
            rs(d, k, step, a1.at[slot(d, k, step - 1)]).start()
        return carry

    gates_own = pl.ds(pl.multiple_of(c * 2 * GROWS, 2 * GROWS), 2 * GROWS)
    gates_away = pl.ds(pl.multiple_of((1 - c) * 2 * GROWS, 2 * GROWS), 2 * GROWS)
    gain_row[...] = jnp.zeros_like(gain_row)

    @pl.when(x == 0)
    def _():
        dc = gate_backward(cs[...], [dgt[j, :TASKS] for j in range(E)], TASKS)
        dpool = (acc[...] + t_dot(wg[:FROWS], dc)).T
        pre_rows = pre[...]
        rho = lax.rsqrt(jnp.mean(pre_rows * pre_rows, axis=1, keepdims=True) + NORM_EPS)
        scaled = dpool * gain_ref[...]
        dots = jnp.mean(scaled * pre_rows, axis=1, keepdims=True)
        dp[mine] = rho * scaled - pre_rows * (rho * rho * rho * dots)
        for k, sec in enumerate((mate, across, diag)):
            copy(dp.at[mine], dp.at[mine], K_DP + c, sec, K_DP + k).start()
        gain_row[0:1] = jnp.sum(dpool * pre_rows * rho, axis=0, keepdims=True)
        grad = mm(wide(dc), u_n[0])
        dg[: FROWS // 2] = grad[: FROWS // 2]
        dg[2 * GROWS : 2 * GROWS + FROWS // 2] = grad[FROWS // 2 :]

    gates_move = copy(dg.at[gates_away], gb, K_DG, mate)
    gates_move.start()
    lax.fori_loop(1, 2, reduce_step, 0)

    for half_no in range(2):

        @pl.when(s != half_no)
        def _():
            rows = pl.ds(half_no * R, R)
            copy(dp.at[rows], dp.at[rows], K_DP + half_no, half_no).wait_recv()

    for k in range(2):

        @pl.when(s != 2 + k)
        def _():
            copy(tp.at[0], tw.at[k], K_TW + k, s).wait_recv()

    gates_move.wait_recv()
    sb[:TOWER] = tw[0, :TOWER] + tw[1, :TOWER]
    sb[GATE_AT:MISC_AT] = dg[gates_own] + gb[...]
    sb[MISC_AT : MISC_AT + 1] = gain_row[0:1]
    sb[MISC_AT + 1 : MISC_AT + 3] = tw[0, TOWER + 1 : TOWER + 3] + tw[1, TOWER + 1 : TOWER + 3]
    for f in range(2):
        sb[MISC_AT + 3 + f : MISC_AT + 4 + f] = jnp.sum(xf[f] * dp[...], axis=0, keepdims=True)
    sb[MISC_AT + 5 : MISC_AT + 6] = smo[1:2, :R] + smo[1:2, R:]
    sb[MISC_AT + 6 :] = jnp.zeros((sb.shape[0] - MISC_AT - 6, D), F32)

    def block(q):
        return pl.ds(pl.multiple_of(q * small_rows, 8), small_rows)

    def scatter(i):
        to = (me + i) % n
        return pltpu.make_async_remote_copy(
            src_ref=sb.at[block(to)],
            dst_ref=sr.at[me],
            send_sem=sr_send.at[i],
            recv_sem=sr_recv.at[me],
            device_id={"dp": to},
            device_id_type=MESH,
        )

    def scattered(i):
        by = (me + i) % n
        return pltpu.make_async_remote_copy(
            src_ref=sb.at[block(me)],
            dst_ref=sr.at[by],
            send_sem=sr_send.at[i],
            recv_sem=sr_recv.at[by],
            device_id={"dp": by},
            device_id_type=MESH,
        )

    def spread_sum(i):
        return pltpu.make_async_remote_copy(
            src_ref=so,
            dst_ref=sa.at[block(me)],
            send_sem=sa_send.at[i],
            recv_sem=sa_recv.at[me],
            device_id={"dp": (me + i) % n},
            device_id_type=MESH,
        )

    def gathered(i):
        by = (me + i) % n
        return pltpu.make_async_remote_copy(
            src_ref=so,
            dst_ref=sa.at[block(by)],
            send_sem=sa_send.at[i],
            recv_sem=sa_recv.at[by],
            device_id={"dp": by},
            device_id_type=MESH,
        )

    def each(act):
        def one(i, carry):
            act(i)
            return carry

        lax.fori_loop(1, n, one, 0)

    each(lambda i: scatter(i).start())
    lax.fori_loop(2, 4, reduce_step, 0)
    so[...] = sb[block(me)]

    def take(i):
        scattered(i).wait_recv()
        so[...] += sr[(me + i) % n]

    each(take)
    sa[block(me)] = so[...]
    each(lambda i: spread_sum(i).start())
    lax.fori_loop(4, 6, reduce_step, 0)
    each(lambda i: gathered(i).wait_recv())
    piece = sa.at[pl.ds(GATE_AT, KEPT)]
    for k, sec in enumerate((mate, across, diag)):
        copy(piece, sg.at[s], K_GO + s, sec, K_GO + k).start()
    sg[s] = sa[GATE_AT:SMALL]
    lax.fori_loop(6, n - 1, reduce_step, 0)
    for sec in (mate, across, diag):
        copy(piece, sg.at[sec], K_GO + sec, sec).wait_recv()
    misc = KEPT - 8
    count = sum(sg[q, misc + 5 : misc + 6] for q in range(TASKS))
    scale = float(2 * R * n) / jnp.sum(count, axis=1, keepdims=True)

    last = n - 2
    for d, k in lanes:
        q = holds(d, n - 1)
        rs(d, k, last, a1.at[slot(d, k, last)]).wait_recv()
        a1[slot(d, k, last)] = (a1[slot(d, k, last)] + rd[d, at(k, q)]) * scale
        ag(d, k, 0, a1.at[slot(d, k, last)], q).start()
        store(d, k, q, a1.at[slot(d, k, last)], 0).start()

    for f in range(2):
        xf[f] = dp[...] * (scale * fw_ref[0, f])
        pltpu.make_async_copy(xf.at[f], o_ig.at[:, f], local.at[2 + f]).start()
    for k in range(2):
        o_pred[:, k * R : (k + 1) * R] = tw[k, TOWER : TOWER + 1]
    for f in range(2):
        o_fw[0, f] = jnp.sum(sa[MISC_AT + 3 + f : MISC_AT + 4 + f] * scale)
    o_bias[0, 0] = jnp.sum(sa[MISC_AT + 2 : MISC_AT + 3] * scale)
    o_gain[...] = (sg[0, misc : misc + 1] + sg[1, misc : misc + 1]) * scale
    o_tout[...] = sa[MISC_AT + 1 : MISC_AT + 2, :TOWER] * scale
    o_tin[...] = (sa[:TOWER] * scale).T

    def order(t, carry):
        for sel in range(SEL):
            for e in range(BITS + 1):
                row = t * (SEL * (BITS + 1)) + sel * (BITS + 1) + e
                at0 = (e * SEL + sel) * TASKS
                cut = FROWS // 2
                o_gate[0, pl.ds(row, 1)] = sg[at0 // cut, pl.ds(at0 % cut + t, 1)] * scale
                o_gate[1, pl.ds(row, 1)] = sg[2 + t // 2, pl.ds((t % 2) * GROWS + e * SEL + sel, 1)] * scale
        return carry

    lax.fori_loop(0, TASKS, order, 0)

    def gather_step(step, carry):
        for d, k in lanes:
            q = holds(d, step - 1)
            ag(d, k, step - 1, landed(d, k, q), q).wait_recv()
            ag(d, k, step, landed(d, k, q), q).start()
            store(d, k, q, landed(d, k, q), step).start()
        return carry

    lax.fori_loop(1, n - 1, gather_step, 0)
    for d, k in lanes:
        q = holds(d, n - 2)
        ag(d, k, last, landed(d, k, q), q).wait_recv()
        store(d, k, q, landed(d, k, q), n - 1).start()

    def stored(step, carry):
        for d, k in lanes:
            store(d, k, 0, landed(d, k, 0), step).wait()
        return carry

    lax.fori_loop(0, n, stored, 0)

    def sent(step, carry):
        for d, k in lanes:
            rs(d, k, step, a1.at[slot(d, k, step)]).wait_send()
            ag(d, k, step, a1.at[slot(d, k, step)], 0).wait_send()
        return carry

    lax.fori_loop(0, n - 1, sent, 0)
    each(lambda i: scatter(i).wait_send())
    each(lambda i: spread_sum(i).wait_send())
    to_mate.wait_send()
    gates_move.wait_send()
    for e in range(HALF):
        for move in give(e):
            move.wait_send()
    for k in range(2):

        @pl.when(s != 2 + k)
        def _():
            copy(smo, sm.at[s], K_SM + s, 2 + k, K_SM + k).wait_send()
            copy(tin_ref, ti.at[s], K_TI + s, 2 + k, K_TI + k).wait_send()

    @pl.when(x == 0)
    def _():
        for t in range(TASKS):
            copy(outbox.at[t], inbox.at[t], K_UP + t, across).wait_send()
        for k, sec in enumerate((mate, across, diag)):
            copy(dp.at[mine], dp.at[mine], K_DP + c, sec, K_DP + k).wait_send()

    @pl.when(x == 1)
    def _():
        copy(pre2, pre1, K_P + 1, across).wait_send()
        for t in range(TASKS):
            copy(outbox.at[t], inbox.at[t], K_DOWN + t, across).wait_send()

            @pl.when(t != s)
            def _():
                copy(tp.at[t], tw.at[c], K_TW + c, t, K_TW + t).wait_send()

    for k, sec in enumerate((mate, across, diag)):
        copy(piece, sg.at[s], K_GO + s, sec, K_GO + k).wait_send()
    for f in range(2):
        pltpu.make_async_copy(xf.at[f], o_ig.at[:, f], local.at[2 + f]).wait()


def hand_over(count, *refs):
    pieces = []
    for k in range(count):
        source, held, result = refs[k], refs[2 * count + k], refs[count + k]
        cuts = 8 if source.shape[0] >= 512 else 1
        size = source.shape[0] // cuts
        for i in range(cuts):
            part = pl.ds(i * size, size)
            pieces.append((source.at[part], held.at[part], result.at[part]))
    sems = refs[-1]
    reads = [pltpu.make_async_copy(a, b, sems.at[0, i]) for i, (a, b, _) in enumerate(pieces)]
    writes = [pltpu.make_async_copy(b, c, sems.at[1, i]) for i, (_, b, c) in enumerate(pieces)]
    for move in reads:
        move.start()
    for read, write in zip(reads, writes):
        read.wait()
        write.start()
    for move in writes:
        move.wait()


def body(
    field_inputs,
    field_weight,
    norm_gain,
    gate_weight,
    expert_in,
    expert_out,
    tower_in,
    tower_out,
    tower_bias,
    labels,
    source_ids,
    task_table,
):
    n = lax.axis_size("dp")
    rows = field_inputs.shape[0]
    half = rows // 2
    units = HALF * H // n // 8
    sizes = [max(1, units * 7 // 32) * 8, max(1, units * 10 // 32) * 8]
    sizes.append(units * 8 - sum(sizes))
    subs = len(sizes)
    small_rows = -(-SMALL // (8 * n)) * 8
    used = TASKS * SEL * (BITS + 1)

    vmem = pl.BlockSpec(memory_space=pltpu.VMEM)
    smem = pl.BlockSpec(memory_space=pltpu.SMEM)
    hbm = pl.BlockSpec(memory_space=pl.ANY)

    def bf(*shape):
        return pltpu.VMEM(shape, BF16)

    def f32(*shape):
        return pltpu.VMEM(shape, F32)

    def out(*shape):
        return jax.ShapeDtypeStruct(shape, F32)

    dma = pltpu.SemaphoreType.DMA
    *sums, _ = pl.pallas_call(
        partial(kernel, n, sizes, small_rows),
        out_shape=(
            out(1, rows),
            out(rows, 2, D),
            out(1, 2),
            out(1, D),
            out(2, used, D),
            out(HALF * H, D),
            out(HALF * H, D),
            out(D, TOWER),
            out(1, TOWER),
            out(1, 1),
            jax.ShapeDtypeStruct((E, 2 * SPILL, H, 2 * half), BF16),
        ),
        in_specs=[hbm, smem, vmem, vmem, hbm, hbm, vmem, vmem, smem, vmem, vmem, smem],
        out_specs=(vmem, hbm, smem, vmem, vmem, hbm, hbm, vmem, vmem, smem, hbm),
        scratch_shapes=[
            bf(2 * E, H, 2 * D),
            bf(E, D, 2 * H),
            bf(E, H, 2 * D),
            f32(E * H, half),
            f32(E * H, half),
            f32(E * H, D),
            f32(E * H, D),
            bf(E, H, 2 * half),
            bf(E, H, 2 * half),
            bf(2, GROUP * H, 2 * half),
            f32(2, HALF * H, D),
            f32(2, rows, D),
            f32(rows, D),
            f32(half, D),
            f32(half, D),
            f32(half, D),
            f32(half, D),
            f32(TASKS, D, half),
            f32(TASKS, D, half),
            bf(3 * D, half),
            bf(TASKS, 3 * half, D),
            bf(3 * D, half),
            bf(TASKS, 3 * half, D),
            f32(2, GROUP * H, half),
            f32(D, half),
            f32(TASKS * GROWS, D),
            f32(E, 1, half),
            f32(E, TASKS, half),
            f32(FROWS, half),
            f32(E, TASKS, half),
            f32(TASKS * GROWS, D),
            f32(2 * GROWS, D),
            f32(TASKS, 8, rows),
            f32(8, rows),
            f32(TASKS, D, TOWER),
            f32(TASKS, TOWER + 8, D),
            f32(2, TOWER + 8, D),
            f32(rows, D),
            f32(8, D),
            f32(half, E * TASKS),
            bf(3 * D, half),
            f32(E, 1, half),
            f32(GROWS, half),
            f32(D, half),
            f32(D, half),
            f32(2 * TOWER, half),
            f32(n * small_rows, D),
            f32(n, small_rows, D),
            f32(small_rows, D),
            f32(n * small_rows, D),
            f32(TASKS, KEPT, D),
            dma((K_COUNT,)),
            dma((K_COUNT,)),
            dma((6,)),
            dma((AHEAD + 1,)),
            pltpu.SemaphoreType.REGULAR,
            dma((2, subs, n - 1)),
            dma((2, subs, n - 1)),
            dma((2, subs, n - 1)),
            dma((2, subs, n - 1)),
            dma((2, subs, n)),
            dma((n,)),
            dma((n,)),
            dma((n,)),
            dma((n,)),
        ],
        compiler_params=pltpu.CompilerParams(
            collective_id=0, has_side_effects=True, vmem_limit_bytes=64 * 1024 * 1024 - 65536
        ),
    )(
        field_inputs,
        field_weight.reshape(1, 2),
        norm_gain.reshape(1, D),
        gate_weight.swapaxes(1, 2),
        expert_in.reshape(HALF * H, D),
        expert_out.reshape(HALF * H, D),
        tower_in.reshape(D, TOWER),
        tower_out,
        tower_bias.reshape(1, 1),
        labels.reshape(1, rows),
        source_ids.reshape(1, rows),
        task_table.reshape(1, SOURCES),
    )
    pred, ig, fw, gain, gate, d_in, d_out, tin, tout, bias = pl.pallas_call(
        partial(hand_over, len(sums)),
        out_shape=tuple(jax.ShapeDtypeStruct(v.shape, v.dtype) for v in sums),
        in_specs=[hbm] * len(sums),
        out_specs=(hbm,) * len(sums),
        scratch_shapes=[pltpu.VMEM(v.shape, v.dtype) for v in sums] + [dma((2, 32))],
        compiler_params=pltpu.CompilerParams(vmem_limit_bytes=64 * 1024 * 1024 - 65536),
    )(*sums)
    return (
        pred.reshape(rows, 1),
        ig,
        fw.reshape(2),
        gain.reshape(D),
        gate.swapaxes(1, 2),
        d_in.reshape(HALF, D, H),
        d_out.reshape(HALF, H, D),
        tin.reshape(1, D, TOWER),
        tout,
        bias.reshape(1),
    )


def solution(mesh):
    in_specs = (
        P("dp", "section", None),
        P("section"),
        P(),
        P(),
        P("section", None, None),
        P("section", None, None),
        P("section", None, None),
        P("section", None),
        P("section"),
        P("dp", "section"),
        P("dp"),
        P(None, "section"),
    )
    out_specs = (
        P("dp", "section"),
        P("dp", "section", None),
        P("section"),
        P(),
        P(),
        P("section", None, None),
        P("section", None, None),
        P("section", None, None),
        P("section", None),
        P("section"),
    )
    return jax.shard_map(body, mesh=mesh, in_specs=in_specs, out_specs=out_specs, check_vma=False)
```

```python
from functools import partial

import jax
import jax.numpy as jnp
from jax import lax
from jax.experimental import pallas as pl
from jax.experimental.pallas import tpu as pltpu
from jax.sharding import PartitionSpec as P

D = 256
H = 256
E = 16
TASKS = 4
SEL = 4
BITS = 4
TOWER = 128
SOURCES = 32
HALF = E // 2
GROWS = 32
FROWS = 96

STEP_SLOPE = 0.6
ENTROPY_WEIGHT = 0.05
NORM_EPS = 1e-05
GELU_A = 0.7978845608028654
GELU_B = 0.044715

F32 = jnp.float32
BF16 = jnp.bfloat16
MESH = pl.DeviceIdType.MESH

K_W, K_P, K_SM, K_TI, K_UP, K_DOWN, K_TW, K_DG, K_DP, K_GO, K_DX = 0, 2, 4, 8, 12, 16, 20, 24, 25, 28, 32
K_COUNT = 48
TILE = 32
SPILL = TASKS - 1
AHEAD = 3

GATE_AT = TOWER
MISC_AT = GATE_AT + 2 * GROWS
SMALL = MISC_AT + 8
KEPT = SMALL - GATE_AT


def split(x):
    hi = x.astype(BF16)
    return hi, (x - hi.astype(F32)).astype(BF16)


def wide(x):
    hi, lo = split(x)
    return jnp.concatenate([hi, lo, hi], axis=1)


def tall(x):
    hi, lo = split(x)
    return jnp.concatenate([hi, hi, lo], axis=0)


def put(ref, at, x):
    k = x.shape[1]
    hi, lo = split(x)
    ref[*at, :k] = hi
    ref[*at, k:] = lo


def stack(x):
    k = x.shape[1] // 2
    return jnp.concatenate([x[:, :k], x[:, :k], x[:, k:]], axis=0)


def mm(a, b):
    return jnp.dot(a, b, preferred_element_type=F32)


def pair(x):
    k = x.shape[1] // 2
    return jnp.concatenate([x, x[:, :k]], axis=1)


def gelu_pair(x):
    x2 = x * x
    h = 0.5 + 0.5 * jnp.tanh(x * (GELU_A + (GELU_A * GELU_B) * x2))
    g = x * h
    slope = h + g * (1.0 - h) * (2.0 * GELU_A + (6.0 * GELU_A * GELU_B) * x2)
    return g, slope


def rows8(x):
    return jnp.sum(x.reshape(x.shape[0] // 8, 8, x.shape[1]), axis=0)


def over_selectors(v, groups, op):
    parts = [v[k * groups : (k + 1) * groups] for k in range(SEL)]
    return op(op(parts[0], parts[1]), op(parts[2], parts[3]))


def to_selectors(v):
    return jnp.concatenate([v] * SEL, axis=0)


def gate_state(c, groups):
    w = SEL * groups
    zs = [c[w * b : w * b + w] * STEP_SLOPE for b in range(BITS)]
    alpha = c[w * BITS : w * BITS + w]
    ups, downs, sig_p, sig_n = [], [], [], []
    for z in zs:
        e = jnp.exp(-jnp.abs(z))
        tail = jnp.log1p(e)
        ups.append(jnp.minimum(z, 0.0) - tail)
        downs.append(jnp.minimum(-z, 0.0) - tail)
        big = 1.0 / (1.0 + e)
        small = e * big
        sig_p.append(jnp.where(z >= 0.0, big, small))
        sig_n.append(jnp.where(z >= 0.0, small, big))
    low = [(ups[0] if k & 1 else downs[0]) + (ups[1] if k & 2 else downs[1]) for k in range(4)]
    high = [(ups[2] if k & 1 else downs[2]) + (ups[3] if k & 2 else downs[3]) for k in range(4)]
    log_r = [low[j & 3] + high[j >> 2] for j in range(E)]
    r = [jnp.exp(v) for v in log_r]
    top = jnp.exp(alpha - to_selectors(over_selectors(alpha, groups, jnp.maximum)))
    mix = top / to_selectors(over_selectors(top, groups, jnp.add))
    return log_r, r, mix, sig_p, sig_n


def gate_forward(c, groups):
    _, r, mix, _, _ = gate_state(c, groups)
    return [over_selectors(mix * v, groups, jnp.add) for v in r]


def gate_backward(c, dgate, groups, out):
    log_r, r, mix, sig_p, sig_n = gate_state(c, groups)
    yield
    total = jnp.zeros_like(mix)
    on = [jnp.zeros_like(mix) for _ in range(BITS)]
    off = [jnp.zeros_like(mix) for _ in range(BITS)]
    for j in range(E):
        dg = to_selectors(dgate(j))
        total = total + dg * r[j]
        dlog = r[j] * (mix * dg - ENTROPY_WEIGHT * (log_r[j] + 1.0))
        for b in range(BITS):
            if j >> b & 1:
                on[b] = on[b] + dlog
            else:
                off[b] = off[b] + dlog
        yield
    dalpha = mix * (total - to_selectors(over_selectors(mix * total, groups, jnp.add)))
    dz = [STEP_SLOPE * (on[b] * sig_n[b] - off[b] * sig_p[b]) for b in range(BITS)]
    used = SEL * (BITS + 1) * groups
    pad = jnp.zeros(((-used) % GROWS, c.shape[1]), F32)
    out.append(jnp.concatenate(dz + [dalpha, pad], axis=0))
    yield


def t_dot(a, b):
    ah, al = split(a)
    left = jnp.concatenate([ah, al, ah], axis=0)
    return lax.dot_general(left, tall(b), (((0,), (0,)), ((), ())), preferred_element_type=F32)


def weave(count, first, middle, last, extra=()):
    extra = iter(extra)
    for step in range(count + 2):
        if step < count:
            first(step, step % 2)
        next(extra, None)
        if 0 <= step - 1 < count:
            middle(step - 1, (step - 1) % 2, 0)
        next(extra, None)
        if step >= 2:
            last(step - 2, step % 2)
        next(extra, None)
        if 0 <= step - 1 < count:
            middle(step - 1, (step - 1) % 2, 1)
        next(extra, None)
    for _ in extra:
        pass


def halves(size):
    tiles = [slice(a, a + TILE) for a in range(0, size, TILE)]
    return tiles[: len(tiles) // 2], tiles[len(tiles) // 2 :]


def kernel(
    n,
    subs,
    small_rows,
    x_ref,
    fw_ref,
    gain_ref,
    gate_ref,
    win_ref,
    wout_ref,
    tin_ref,
    tout_ref,
    tbias_ref,
    labels_ref,
    ids_ref,
    table_ref,
    o_pred,
    o_ig,
    o_fw,
    o_gain,
    o_gate,
    o_in,
    o_out,
    o_tin,
    o_tout,
    o_bias,
    kept,
    wt,
    w_in,
    w_out,
    a1,
    a2,
    d_in,
    d_out,
    gbuf,
    kbuf,
    kp,
    rd,
    xf,
    part,
    pre0,
    pre1,
    pre2,
    pre,
    inbox,
    outbox,
    u_t,
    u_n,
    s_t,
    s_n,
    bb,
    acc,
    wg,
    gt,
    gt0,
    cs,
    dgt,
    dg,
    gb,
    sm,
    smo,
    ti,
    tp,
    tw,
    dp,
    gain_row,
    columns,
    u_next,
    gt_next,
    cs_next,
    acc_b,
    dy_kept,
    held,
    tm,
    sb,
    sr,
    so,
    sa,
    sg,
    send,
    recv,
    local,
    fetch_sem,
    ready,
    rs_send,
    rs_recv,
    ag_send,
    ag_recv,
    store_sem,
    sr_send,
    sr_recv,
    sa_send,
    sa_recv,
):
    s = lax.axis_index("section")
    x = s // 2
    c = s % 2
    mate = s + 1 - 2 * c
    across = s + 2 - 4 * x
    diag = 3 - s
    R = part.shape[0] // 2
    mine = pl.ds(pl.multiple_of(c * R, R), R)
    theirs = pl.ds(pl.multiple_of((1 - c) * R, R), R)

    me = lax.axis_index("dp")
    odd = me % 2
    p = (1 - odd) * (me // 2) + odd * (n - 1 - me // 2)

    def ring_id(q):
        far = q // (n // 2)
        return (1 - far) * 2 * q + far * (2 * (n - 1 - q) + 1)

    nbr = [ring_id((p + 1) % n), ring_id((p + n - 1) % n)]

    barrier = pltpu.get_barrier_semaphore()
    for sec in (mate, across, diag):
        pl.semaphore_signal(barrier, inc=1, device_id={"section": sec}, device_id_type=MESH)

    def greet(i, carry):
        pl.semaphore_signal(barrier, inc=1, device_id={"dp": (me + i) % n}, device_id_type=MESH)
        return carry

    lax.fori_loop(1, n, greet, 0)
    fields = [pltpu.make_async_copy(x_ref.at[:, f], xf.at[f], local.at[2 + f]) for f in range(2)]
    for f in fields:
        f.start()
    own = pl.ds(pl.multiple_of(c * HALF * H, HALF * H), HALF * H)
    own_in = pltpu.make_async_copy(win_ref, d_in.at[own], local.at[0])
    own_out = pltpu.make_async_copy(wout_ref, d_out.at[own], local.at[1])
    own_in.start()
    own_out.start()
    pl.semaphore_wait(barrier, 3 + n - 1)

    def copy(src, dst, k, sec, ks=None):
        return pltpu.make_async_remote_copy(
            src_ref=src,
            dst_ref=dst,
            send_sem=send.at[k if ks is None else ks],
            recv_sem=recv.at[k],
            device_id={"section": sec},
            device_id_type=MESH,
        )

    def expert(j, count=1):
        return pl.ds(pl.multiple_of(j * H, H), count * H)

    for f in fields:
        f.wait()
    part[...] = xf[0] * fw_ref[0, 0] + xf[1] * fw_ref[0, 1]
    to_mate = copy(part.at[theirs], pre0, K_P, mate)
    to_mate.start()
    swap_in = copy(d_in.at[own], d_in.at[own], K_W, mate)
    swap_out = copy(d_out.at[own], d_out.at[own], K_W + 1, mate)
    own_in.wait()
    swap_in.start()
    own_out.wait()
    swap_out.start()

    ids = ids_ref[...]
    mask = jnp.zeros(ids.shape, F32)
    for q in range(SOURCES):
        mask = mask + jnp.where(ids == q, table_ref[0, q].astype(F32), 0.0)
    smo[...] = jnp.zeros_like(smo)
    smo[0:1] = labels_ref[...]
    smo[1:2] = mask
    smo[2:3, :TOWER] = tout_ref[...]
    smo[3:4] = jnp.zeros((1, 2 * R), F32) + tbias_ref[0, 0]
    for k in range(2):

        @pl.when(s != 2 + k)
        def _():
            copy(smo, sm.at[s], K_SM + s, 2 + k, K_SM + k).start()
            copy(tin_ref, ti.at[s], K_TI + s, 2 + k, K_TI + k).start()

    to_mate.wait_recv()

    @pl.when(x == 1)
    def _():
        pre2[...] = part[mine] + pre0[...]
        copy(pre2, pre1, K_P + 1, across).start()
        sm[s] = smo[...]
        ti[s] = tin_ref[...]

    wg[...] = jnp.zeros_like(wg)

    @pl.when(x == 0)
    def _():
        def order(t, carry):
            for sel in range(SEL):
                for e in range(BITS + 1):
                    row = t * (SEL * (BITS + 1)) + sel * (BITS + 1) + e
                    wg[pl.ds((e * SEL + sel) * TASKS + t, 1)] = gate_ref[0, pl.ds(row, 1)]
            return carry

        lax.fori_loop(0, TASKS, order, 0)

    @pl.when(x == 1)
    def _():
        def order(t, carry):
            for sel in range(SEL):
                for e in range(BITS + 1):
                    row = t * (SEL * (BITS + 1)) + sel * (BITS + 1) + e
                    wg[pl.ds(t * GROWS + e * SEL + sel, 1)] = gate_ref[1, pl.ds(row, 1)]
            return carry

        lax.fori_loop(0, TASKS, order, 0)

    def keep_plain(e, carry):
        put(w_in.at[e], (slice(None),), d_in[expert(e)])
        put(w_out.at[e], (slice(None),), d_out[expert(e)])
        return carry

    def keep_flipped(e, carry):
        put(wt.at[e], (slice(None),), d_in[expert(e)].T)
        put(wt.at[E + e], (slice(None),), d_out[expert(e)].T)
        return carry

    lax.fori_loop(c * HALF, c * HALF + HALF, keep_plain, 0)
    swap_in.wait()
    swap_out.wait()
    lax.fori_loop((1 - c) * HALF, (1 - c) * HALF + HALF, keep_plain, 0)

    def rows_of(size):
        return [slice(a, a + TILE) for a in range(0, size, TILE)]

    def shifted(tile, e):
        return slice(e * H + tile.start, e * H + tile.stop)

    chunk = HALF * H // n
    sub = chunk // subs
    lanes = [(d, k) for d in range(2) for k in range(subs)]

    def at(k, q):
        return pl.ds(pl.multiple_of(q * chunk + k * sub, 8), sub)

    def holds(d, step):
        return (p + n - step) % n if d == 0 else (p + step) % n

    def slot(d, k, step):
        return pl.ds(pl.multiple_of(((d * subs + k) * (n - 1) + step) * sub, 8), sub)

    def rs(d, k, step, src):
        return pltpu.make_async_remote_copy(
            src_ref=src,
            dst_ref=a1.at[slot(d, k, step)],
            send_sem=rs_send.at[d, k, step],
            recv_sem=rs_recv.at[d, k, step],
            device_id={"dp": nbr[d]},
            device_id_type=MESH,
        )

    results = (o_in, o_out)

    def landed(d, k, q):
        return a2.at[pl.ds(pl.multiple_of(d * HALF * H + q * chunk + k * sub, 8), sub)]

    def store(d, k, q, src, step):
        return pltpu.make_async_copy(src, results[d].at[at(k, q)], store_sem.at[d, k, step])

    def ag(d, k, step, src, q):
        return pltpu.make_async_remote_copy(
            src_ref=src,
            dst_ref=landed(d, k, q),
            send_sem=ag_send.at[d, k, step],
            recv_sem=ag_recv.at[d, k, step],
            device_id={"dp": nbr[d]},
            device_id_type=MESH,
        )

    def give(e):
        j = (1 - c) * HALF + e
        return (
            copy(d_in.at[expert(j)], rd.at[0, expert(e)], K_DX + e, mate),
            copy(d_out.at[expert(j)], rd.at[1, expert(e)], K_DX + HALF + e, mate),
        )

    start_at = p * chunk // H

    def near(k):
        return (start_at + HALF + ((k + 1) // 2) * (1 - 2 * (k % 2))) % HALF

    def turn_of(i):
        own_turn = i % 2
        return ((1 - own_turn) * (1 - c) + own_turn * c) * HALF + near(i // 2)

    def fetch(i):
        at = pl.ds((i % (AHEAD + 1)) * 8, 2 * SPILL)
        return pltpu.make_async_copy(kept.at[turn_of(i)], wt.at[at], fetch_sem.at[i % (AHEAD + 1)])

    def fetch_start(i):
        for k in range(2 * SPILL):
            slab = (i % (AHEAD + 1)) * 8 + k
            pltpu.make_async_copy(
                kept.at[turn_of(i), k], wt.at[slab], fetch_sem.at[i % (AHEAD + 1)]
            ).start()

    def greet_ring():
        for dev in nbr:
            pl.semaphore_signal(ready, inc=1, device_id={"dp": dev}, device_id_type=MESH)

    def merge(k, carry):
        e = near(k)
        for move in give(e):
            move.wait_recv()
        rows = expert(e)
        rd[0, rows] = (rd[0, rows] + d_in[expert(c * HALF + e)]).T
        rd[1, rows] += d_out[expert(c * HALF + e)]
        return carry

    def ring_start():
        pl.semaphore_wait(ready, 2)
        for d, k in lanes:
            rs(d, k, 0, rd.at[d, at(k, holds(d, 0))]).start()

    def reduce_step(step, carry):
        for d, k in lanes:
            rs(d, k, step - 1, a1.at[slot(d, k, step - 1)]).wait_recv()
            a1[slot(d, k, step - 1)] += rd[d, at(k, holds(d, step))]
            rs(d, k, step, a1.at[slot(d, k, step - 1)]).start()
        return carry

    @pl.when(x == 0)
    def _():
        copy(pre2, pre1, K_P + 1, across).wait_recv()
        pre_rows = part[mine] + pre0[...] + pre1[...]
        pre[...] = pre_rows
        rho = lax.rsqrt(jnp.mean(pre_rows * pre_rows, axis=1, keepdims=True) + NORM_EPS)
        pooled = pre_rows * rho * gain_ref[...]
        acc[...] = pooled
        u_n[0] = tall(pooled)
        u_t[...] = tall(pooled.T)
        logits = mm(wide(wg[:FROWS]), u_t[...])
        cs[...] = logits
        gates = gate_forward(logits, TASKS)
        for j, g in enumerate(gates):
            gt0[j] = g

        def first(j, par):
            left = jnp.concatenate([u_n[0, :R], u_n[0, 2 * R :], u_n[0, :R]], axis=1)
            bb[par] = mm(left, stack(w_in[j]))

        def activate(j, par, part_no):
            for tile in halves(R)[part_no]:
                value, slope = gelu_pair(bb[par, tile])
                a1[shifted(tile, j)] = value
                a2[shifted(tile, j)] = slope
                put(gbuf, (j, tile), value)

        def finish(j, par):
            d_in[expert(j)] = mm(pair(gbuf[j]), stack(w_out[j]))

        weave(E, first, activate, finish)
        columns[...] = jnp.concatenate(gates, axis=0).T

        for t in range(TASKS):

            def mix(i, carry):
                tile = pl.ds(pl.multiple_of(i * TILE, TILE), TILE)
                cols = columns[tile]
                total = acc[tile]
                for j in range(E):
                    rows = pl.ds(pl.multiple_of(j * R + i * TILE, TILE), TILE)
                    total = total + cols[:, j * TASKS + t : j * TASKS + t + 1] * d_in[rows]
                outbox[t, tile] = total
                return carry

            lax.fori_loop(0, R // TILE, mix, 0)
            copy(outbox.at[t], inbox.at[t], K_UP + t, across).start()

        def flip(j, carry):
            value = a1[expert(j)].T
            a1[expert(j)] = value
            put(gbuf.at[j], (slice(None),), value)
            a2[expert(j)] = a2[expert(j)].T
            d_in[expert(j)] = d_in[expert(j)].T
            return carry

        lax.fori_loop(0, E, flip, 0)
        greet_ring()
        d_out[...] = jnp.zeros_like(d_out)
        acc[...] = jnp.zeros_like(acc)

    @pl.when(x == 1)
    def _():
        lax.fori_loop(0, E, keep_flipped, 0)
        for q in range(TASKS):

            @pl.when(s != q)
            def _():
                copy(smo, sm.at[q], K_SM + q, q).wait_recv()
                copy(tin_ref, ti.at[q], K_TI + q, q).wait_recv()

        def keep(k, t):
            return pltpu.make_async_copy((gbuf, kbuf)[k], kept.at[:, k * SPILL + t], local.at[4 + k])

        def keep_start(k, t):
            def one(j, carry):
                pltpu.make_async_copy((gbuf, kbuf)[k].at[j], kept.at[j, k * SPILL + t], local.at[4 + k]).start()
                return carry

            @pl.when(t < SPILL)
            def _():
                lax.fori_loop(0, E, one, 0)

        def gate_rows(t):
            return pl.ds(pl.multiple_of(t * GROWS, GROWS), GROWS)

        def enter(t):
            for k in range(2):
                cols = slice(k * (R // 2), (k + 1) * (R // 2))
                flipped = inbox[t, cols].T
                hi, lo = split(flipped)
                u_next[:D, cols] = hi
                u_next[D : 2 * D, cols] = hi
                u_next[2 * D :, cols] = lo
                acc[:, cols] = flipped
                yield
            logits = mm(wide(wg[gate_rows(t)]), u_next[...])
            cs_next[...] = logits
            yield
            u_n[t] = tall(inbox[t])
            yield
            _, r, mix, _, _ = gate_state(logits, 1)
            yield
            for j in range(E):
                gt_next[j] = over_selectors(mix * r[j], 1, jnp.add)
                yield

        def turn():
            u_t[...] = u_next[...]
            gt[...] = gt_next[...]
            cs[GROWS : 2 * GROWS] = cs[:GROWS]
            cs[:GROWS] = cs_next[...]

        def leave(t, at):
            out = []
            yield from gate_backward(cs[at : at + GROWS], lambda j: dgt[j, 0:1], 1, out)
            outbox[t] = acc_b[...] + t_dot(wg[gate_rows(t)], out[0])
            yield
            dg[gate_rows(t)] = mm(wide(out[0]), u_n[t])
            yield

        def all_of(pieces):
            for _ in pieces:
                pass

        cs[...] = jnp.zeros_like(cs)
        dgt[...] = jnp.zeros_like(dgt)
        acc_b[...] = jnp.zeros_like(acc_b)
        copy(outbox.at[0], inbox.at[0], K_UP, across).wait_recv()
        all_of(enter(0))
        turn()

        def task(t, carry):
            @pl.when(t > 0)
            def _():
                keep(0, 0).wait()

            def first(j, par):
                bb[par] = mm(pair(wt[j]), u_t[...])

            def activate(j, par, part_no):
                for tile in halves(H)[part_no]:
                    value, slope = gelu_pair(bb[par, tile])
                    a1[shifted(tile, j)] = value
                    a2[shifted(tile, j)] = slope
                    put(gbuf, (j, tile), value * gt[j])

            def finish(j, par):
                acc[...] += mm(pair(wt[E + j]), stack(gbuf[j]))

            before = (t + TASKS - 1) % TASKS
            weave(E, first, activate, finish, leave(before, GROWS))
            keep_start(0, t)

            @pl.when(t > 0)
            def _():
                copy(outbox.at[before], inbox.at[before], K_DOWN + before, across).start()

            second = acc[...]
            held[...] = second
            tower = ti[t]
            g, slope = gelu_pair(mm(wide(tower.T), tall(second)))
            info = sm[t]
            out_col = info[:, :TOWER].T[:, 2:3]
            here = sm[t, :, mine]
            logit = jnp.sum(g * out_col, axis=0, keepdims=True) + here[3:4]
            prob = jax.nn.sigmoid(logit)
            dlogit = here[1:2] * (prob - here[0:1])
            m = dlogit * out_col * slope
            dy = mm(wide(tower), tall(m))
            s_t[...] = tall(dy)
            acc_b[...] = dy
            dy_kept[...] = dy
            tm[:TOWER] = m
            tm[TOWER:] = g * dlogit
            tp[t, TOWER : TOWER + 1] = prob
            tp[t, TOWER + 2 : TOWER + 3] = dlogit
            tp[t, TOWER + 3 :] = jnp.zeros((5, R), F32)

            @pl.when(t > 0)
            def _():
                keep(1, 0).wait()

            @pl.when(t == TASKS - 1)
            def _():
                for i in range(AHEAD):
                    fetch_start(i)

            after = jnp.minimum(t + 1, TASKS - 1)

            @pl.when(t < TASKS - 1)
            def _():
                copy(outbox.at[after], inbox.at[after], K_UP + after, across).wait_recv()

            def back(j, par):
                bb[par] = mm(pair(w_out[j]), s_t[...])

            def pull(j, par, part_no):
                total = jnp.zeros((8, R), F32)
                for tile in halves(H)[part_no]:
                    grad = bb[par, tile]
                    total = total + rows8(grad * a1[shifted(tile, j)])
                    put(kbuf, (j, tile), grad * a2[shifted(tile, j)] * gt[j])
                total = jnp.sum(total, axis=0, keepdims=True)
                if part_no == 0:
                    dgt[j, 0:1] = total
                else:
                    dgt[j, 0:1] += total

            def spread(j, par):
                acc_b[...] += mm(pair(w_in[j]), stack(kbuf[j]))

            def beside():
                s_n[t] = tall(dy_kept[...].T)
                yield
                yield from enter(after)
                flipped = tall(held[...].T)
                yield
                tp[t, :TOWER] = mm(wide(tm[:TOWER]), flipped)
                yield
                out_grad = jnp.sum(tm[TOWER:], axis=1, keepdims=True)
                out_row = jnp.broadcast_to(out_grad, (TOWER, TOWER)).T[0:1]
                tp[t, TOWER + 1 : TOWER + 2] = jnp.concatenate([out_row, jnp.zeros_like(out_row)], axis=1)
                yield

            weave(E, back, pull, spread, beside())
            keep_start(1, t)
            turn()

            @pl.when(t != s)
            def _():
                copy(tp.at[t], tw.at[c], K_TW + c, t, K_TW + t).start()

            @pl.when(t == s)
            def _():
                tw[c] = tp[t]

            return carry

        lax.fori_loop(0, TASKS, task, 0)
        last_task = TASKS - 1
        all_of(leave(last_task, GROWS))
        copy(outbox.at[last_task], inbox.at[last_task], K_DOWN + last_task, across).start()
        greet_ring()

    @pl.when(x == 1)
    def _():
        def one(i, carry):
            fetch(i).wait()

            @pl.when(i < E - AHEAD)
            def _():
                fetch_start(i + AHEAD)

            j = turn_of(i)
            slot_at = (i % (AHEAD + 1)) * 8
            for k, (grad, right, here) in enumerate(((d_out, s_n, gbuf), (d_in, u_n, kbuf))):
                left = [pair(wt[slot_at + k * SPILL + t]) for t in range(SPILL)] + [pair(here[j])]
                grad[expert(j)] = mm(jnp.concatenate(left, axis=1), right[...].reshape(3 * TASKS * R, D))

            @pl.when(i % 2 == 0)
            def _():
                for move in give(near(i // 2)):
                    move.start()

            @pl.when(i == 3)
            def _():
                merge(0, 0)
                ring_start()

            @pl.when((i % 2 == 1) & (i > 3))
            def _():
                merge((i - 3) // 2, 0)

            if n == HALF:

                @pl.when((i % 4 == 3) & (i > 3))
                def _():
                    reduce_step((i - 3) // 4, 0)

            return carry

        lax.fori_loop(0, E, one, 0)
        merge(HALF - 1, 0)
        if n != HALF:
            lax.fori_loop(1, 4, reduce_step, 0)

    @pl.when(x == 0)
    def _():
        def arrive(t, carry):
            copy(outbox.at[t], inbox.at[t], K_DOWN + t, across).wait_recv()
            acc[...] += inbox[t]

            def one(j, inner):
                gate = gt0[j, pl.ds(t, 1)]
                total = jnp.zeros((8, R), F32)
                for tile in rows_of(D):
                    dy = inbox[t, tile]
                    rows = pl.ds(pl.multiple_of(j * D + tile.start, TILE), TILE)
                    total = total + rows8(d_in[rows] * dy)
                    d_out[rows] += gate * dy
                dgt[j, pl.ds(t, 1)] = jnp.sum(total, axis=0, keepdims=True)
                return inner

            lax.fori_loop(0, E, one, 0)
            return carry

        lax.fori_loop(0, TASKS - 1, arrive, 0)
        last = TASKS - 1
        copy(outbox.at[last], inbox.at[last], K_DOWN + last, across).wait_recv()
        acc[...] += inbox[last]

        def one(i, inner):
            j = turn_of(i)
            gate = gt0[j, last : last + 1]
            total = jnp.zeros((8, R), F32)
            for tile in rows_of(D):
                dy = inbox[last, tile]
                rows = pl.ds(pl.multiple_of(j * D + tile.start, TILE), TILE)
                total = total + rows8(d_in[rows] * dy)
                put(kbuf.at[j], (tile,), d_out[rows] + gate * dy)
            dgt[j, last : last + 1] = jnp.sum(total, axis=0, keepdims=True)
            return inner

        def part_of(first, stop):
            lax.fori_loop(2 * first, 2 * stop, one, 0)

            def products(i, par):
                j = turn_of(2 * first + i)
                mixed = kbuf[j]
                bb[par] = mm(pair(w_out[j]), stack(mixed))
                right = jnp.concatenate([mixed[:, :R], mixed[:, :R], mixed[:, R:]], axis=1)
                d_out[expert(j)] = lax.dot_general(
                    pair(gbuf[j]), right, (((1,), (1,)), ((), ())), preferred_element_type=F32
                )

            def pull(i, par, part_no):
                j = turn_of(2 * first + i)
                for tile in halves(H)[part_no]:
                    kept_rows = pl.ds(pl.multiple_of(j * H + tile.start, TILE), TILE)
                    put(kp, (par, tile), bb[par, tile] * a2[kept_rows])

            def spread(i, par):
                j = turn_of(2 * first + i)
                acc[...] += mm(pair(w_in[j]), stack(kp[par]))
                d_in[expert(j)] = mm(pair(kp[par]), u_n[0])

            weave(2 * (stop - first), products, pull, spread)
            for k in range(first, stop):
                for move in give(near(k)):
                    move.start()

        part_of(0, 1)
        part_of(1, 4)
        merge(0, 0)
        ring_start()
        part_of(4, HALF)
        lax.fori_loop(1, HALF, merge, 0)
        lax.fori_loop(1, 2, reduce_step, 0)

    gates_own = pl.ds(pl.multiple_of(c * 2 * GROWS, 2 * GROWS), 2 * GROWS)
    gates_away = pl.ds(pl.multiple_of((1 - c) * 2 * GROWS, 2 * GROWS), 2 * GROWS)
    gain_row[...] = jnp.zeros_like(gain_row)

    @pl.when(x == 0)
    def _():
        out = []
        for _ in gate_backward(cs[...], lambda j: dgt[j, :TASKS], TASKS, out):
            pass
        dc = out[0]
        dpool = (acc[...] + t_dot(wg[:FROWS], dc)).T
        pre_rows = pre[...]
        rho = lax.rsqrt(jnp.mean(pre_rows * pre_rows, axis=1, keepdims=True) + NORM_EPS)
        scaled = dpool * gain_ref[...]
        dots = jnp.mean(scaled * pre_rows, axis=1, keepdims=True)
        dp[mine] = rho * scaled - pre_rows * (rho * rho * rho * dots)
        for k, sec in enumerate((mate, across, diag)):
            copy(dp.at[mine], dp.at[mine], K_DP + c, sec, K_DP + k).start()
        gain_row[0:1] = jnp.sum(dpool * pre_rows * rho, axis=0, keepdims=True)
        grad = mm(wide(dc), u_n[0])
        dg[: FROWS // 2] = grad[: FROWS // 2]
        dg[2 * GROWS : 2 * GROWS + FROWS // 2] = grad[FROWS // 2 :]

    gates_move = copy(dg.at[gates_away], gb, K_DG, mate)
    gates_move.start()

    @pl.when(x == 0)
    def _():
        lax.fori_loop(2, 4, reduce_step, 0)

    for half_no in range(2):

        @pl.when(s != half_no)
        def _():
            rows = pl.ds(half_no * R, R)
            copy(dp.at[rows], dp.at[rows], K_DP + half_no, half_no).wait_recv()

    for k in range(2):

        @pl.when(s != 2 + k)
        def _():
            copy(tp.at[0], tw.at[k], K_TW + k, s).wait_recv()

    gates_move.wait_recv()
    sb[:TOWER] = tw[0, :TOWER] + tw[1, :TOWER]
    sb[GATE_AT:MISC_AT] = dg[gates_own] + gb[...]
    sb[MISC_AT : MISC_AT + 1] = gain_row[0:1]
    sb[MISC_AT + 1 : MISC_AT + 3] = tw[0, TOWER + 1 : TOWER + 3] + tw[1, TOWER + 1 : TOWER + 3]
    for f in range(2):
        sb[MISC_AT + 3 + f : MISC_AT + 4 + f] = jnp.sum(xf[f] * dp[...], axis=0, keepdims=True)
    sb[MISC_AT + 5 : MISC_AT + 6] = smo[1:2, :R] + smo[1:2, R:]
    sb[MISC_AT + 6 :] = jnp.zeros((sb.shape[0] - MISC_AT - 6, D), F32)

    def block(q):
        return pl.ds(pl.multiple_of(q * small_rows, 8), small_rows)

    def scatter(i):
        to = (me + i) % n
        return pltpu.make_async_remote_copy(
            src_ref=sb.at[block(to)],
            dst_ref=sr.at[me],
            send_sem=sr_send.at[i],
            recv_sem=sr_recv.at[me],
            device_id={"dp": to},
            device_id_type=MESH,
        )

    def scattered(i):
        by = (me + i) % n
        return pltpu.make_async_remote_copy(
            src_ref=sb.at[block(me)],
            dst_ref=sr.at[by],
            send_sem=sr_send.at[i],
            recv_sem=sr_recv.at[by],
            device_id={"dp": by},
            device_id_type=MESH,
        )

    def spread_sum(i):
        return pltpu.make_async_remote_copy(
            src_ref=so,
            dst_ref=sa.at[block(me)],
            send_sem=sa_send.at[i],
            recv_sem=sa_recv.at[me],
            device_id={"dp": (me + i) % n},
            device_id_type=MESH,
        )

    def gathered(i):
        by = (me + i) % n
        return pltpu.make_async_remote_copy(
            src_ref=so,
            dst_ref=sa.at[block(by)],
            send_sem=sa_send.at[i],
            recv_sem=sa_recv.at[by],
            device_id={"dp": by},
            device_id_type=MESH,
        )

    def each(act):
        def one(i, carry):
            act(i)
            return carry

        lax.fori_loop(1, n, one, 0)

    each(lambda i: scatter(i).start())
    lax.fori_loop(4, 5, reduce_step, 0)
    so[...] = sb[block(me)]

    def take(i):
        scattered(i).wait_recv()
        so[...] += sr[(me + i) % n]

    each(take)
    sa[block(me)] = so[...]
    each(lambda i: spread_sum(i).start())
    lax.fori_loop(5, 6, reduce_step, 0)
    each(lambda i: gathered(i).wait_recv())
    piece = sa.at[pl.ds(GATE_AT, KEPT)]
    for k, sec in enumerate((mate, across, diag)):
        copy(piece, sg.at[s], K_GO + s, sec, K_GO + k).start()
    sg[s] = sa[GATE_AT:SMALL]
    lax.fori_loop(6, n - 1, reduce_step, 0)
    for sec in (mate, across, diag):
        copy(piece, sg.at[sec], K_GO + sec, sec).wait_recv()
    misc = KEPT - 8
    count = sum(sg[q, misc + 5 : misc + 6] for q in range(TASKS))
    scale = float(2 * R * n) / jnp.sum(count, axis=1, keepdims=True)

    last = n - 2
    for d, k in lanes:
        q = holds(d, n - 1)
        rs(d, k, last, a1.at[slot(d, k, last)]).wait_recv()
        a1[slot(d, k, last)] = (a1[slot(d, k, last)] + rd[d, at(k, q)]) * scale
        ag(d, k, 0, a1.at[slot(d, k, last)], q).start()
        store(d, k, q, a1.at[slot(d, k, last)], 0).start()

    for f in range(2):
        xf[f] = dp[...] * (scale * fw_ref[0, f])
        pltpu.make_async_copy(xf.at[f], o_ig.at[:, f], local.at[2 + f]).start()
    for k in range(2):
        o_pred[:, k * R : (k + 1) * R] = tw[k, TOWER : TOWER + 1]
    for f in range(2):
        o_fw[0, f] = jnp.sum(sa[MISC_AT + 3 + f : MISC_AT + 4 + f] * scale)
    o_bias[0, 0] = jnp.sum(sa[MISC_AT + 2 : MISC_AT + 3] * scale)
    o_gain[...] = (sg[0, misc : misc + 1] + sg[1, misc : misc + 1]) * scale
    o_tout[...] = sa[MISC_AT + 1 : MISC_AT + 2, :TOWER] * scale
    o_tin[...] = (sa[:TOWER] * scale).T

    def order(t, carry):
        for sel in range(SEL):
            for e in range(BITS + 1):
                row = t * (SEL * (BITS + 1)) + sel * (BITS + 1) + e
                at0 = (e * SEL + sel) * TASKS
                cut = FROWS // 2
                o_gate[0, pl.ds(row, 1)] = sg[at0 // cut, pl.ds(at0 % cut + t, 1)] * scale
                o_gate[1, pl.ds(row, 1)] = sg[2 + t // 2, pl.ds((t % 2) * GROWS + e * SEL + sel, 1)] * scale
        return carry

    lax.fori_loop(0, TASKS, order, 0)

    def gather_step(step, carry):
        for d, k in lanes:
            q = holds(d, step - 1)
            ag(d, k, step - 1, landed(d, k, q), q).wait_recv()
            ag(d, k, step, landed(d, k, q), q).start()
            store(d, k, q, landed(d, k, q), step).start()
        return carry

    lax.fori_loop(1, n - 1, gather_step, 0)
    for d, k in lanes:
        q = holds(d, n - 2)
        ag(d, k, last, landed(d, k, q), q).wait_recv()
        store(d, k, q, landed(d, k, q), n - 1).start()

    def stored(step, carry):
        for d, k in lanes:
            store(d, k, 0, landed(d, k, 0), step).wait()
        return carry

    lax.fori_loop(0, n, stored, 0)

    def sent(step, carry):
        for d, k in lanes:
            rs(d, k, step, a1.at[slot(d, k, step)]).wait_send()
            ag(d, k, step, a1.at[slot(d, k, step)], 0).wait_send()
        return carry

    lax.fori_loop(0, n - 1, sent, 0)
    each(lambda i: scatter(i).wait_send())
    each(lambda i: spread_sum(i).wait_send())
    to_mate.wait_send()
    gates_move.wait_send()
    for e in range(HALF):
        for move in give(e):
            move.wait_send()
    for k in range(2):

        @pl.when(s != 2 + k)
        def _():
            copy(smo, sm.at[s], K_SM + s, 2 + k, K_SM + k).wait_send()
            copy(tin_ref, ti.at[s], K_TI + s, 2 + k, K_TI + k).wait_send()

    @pl.when(x == 0)
    def _():
        for t in range(TASKS):
            copy(outbox.at[t], inbox.at[t], K_UP + t, across).wait_send()
        for k, sec in enumerate((mate, across, diag)):
            copy(dp.at[mine], dp.at[mine], K_DP + c, sec, K_DP + k).wait_send()

    @pl.when(x == 1)
    def _():
        copy(pre2, pre1, K_P + 1, across).wait_send()
        for t in range(TASKS):
            copy(outbox.at[t], inbox.at[t], K_DOWN + t, across).wait_send()

            @pl.when(t != s)
            def _():
                copy(tp.at[t], tw.at[c], K_TW + c, t, K_TW + t).wait_send()

    for k, sec in enumerate((mate, across, diag)):
        copy(piece, sg.at[s], K_GO + s, sec, K_GO + k).wait_send()
    for f in range(2):
        pltpu.make_async_copy(xf.at[f], o_ig.at[:, f], local.at[2 + f]).wait()


def hand_over(count, *refs):
    held = refs[2 * count : 3 * count]
    sems = refs[-1]
    reads = [pltpu.make_async_copy(refs[k], held[k], sems.at[0, k]) for k in range(count)]
    writes = [pltpu.make_async_copy(held[k], refs[count + k], sems.at[1, k]) for k in range(count)]
    for move in reads:
        move.start()
    for read, write in zip(reads, writes):
        read.wait()
        write.start()
    for move in writes:
        move.wait()


def body(
    field_inputs,
    field_weight,
    norm_gain,
    gate_weight,
    expert_in,
    expert_out,
    tower_in,
    tower_out,
    tower_bias,
    labels,
    source_ids,
    task_table,
):
    n = lax.axis_size("dp")
    rows = field_inputs.shape[0]
    half = rows // 2
    subs = 2
    small_rows = -(-SMALL // (8 * n)) * 8
    used = TASKS * SEL * (BITS + 1)

    vmem = pl.BlockSpec(memory_space=pltpu.VMEM)
    smem = pl.BlockSpec(memory_space=pltpu.SMEM)
    hbm = pl.BlockSpec(memory_space=pl.ANY)

    def bf(*shape):
        return pltpu.VMEM(shape, BF16)

    def f32(*shape):
        return pltpu.VMEM(shape, F32)

    def out(*shape):
        return jax.ShapeDtypeStruct(shape, F32)

    dma = pltpu.SemaphoreType.DMA
    *sums, _ = pl.pallas_call(
        partial(kernel, n, subs, small_rows),
        out_shape=(
            out(1, rows),
            out(rows, 2, D),
            out(1, 2),
            out(1, D),
            out(2, used, D),
            out(HALF * H, D),
            out(HALF * H, D),
            out(D, TOWER),
            out(1, TOWER),
            out(1, 1),
            jax.ShapeDtypeStruct((E, 2 * SPILL, H, 2 * half), BF16),
        ),
        in_specs=[hbm, smem, vmem, vmem, hbm, hbm, vmem, vmem, smem, vmem, vmem, smem],
        out_specs=(vmem, hbm, smem, vmem, vmem, hbm, hbm, vmem, vmem, smem, hbm),
        scratch_shapes=[
            bf(2 * E, H, 2 * D),
            bf(E, D, 2 * H),
            bf(E, H, 2 * D),
            f32(E * H, half),
            f32(E * H, half),
            f32(E * H, D),
            f32(E * H, D),
            bf(E, H, 2 * half),
            bf(E, H, 2 * half),
            bf(2, H, 2 * half),
            f32(2, HALF * H, D),
            f32(2, rows, D),
            f32(rows, D),
            f32(half, D),
            f32(half, D),
            f32(half, D),
            f32(half, D),
            f32(TASKS, D, half),
            f32(TASKS, D, half),
            bf(3 * D, half),
            bf(TASKS, 3 * half, D),
            bf(3 * D, half),
            bf(TASKS, 3 * half, D),
            f32(2, H, half),
            f32(D, half),
            f32(TASKS * GROWS, D),
            f32(E, 1, half),
            f32(E, TASKS, half),
            f32(FROWS, half),
            f32(E, TASKS, half),
            f32(TASKS * GROWS, D),
            f32(2 * GROWS, D),
            f32(TASKS, 8, rows),
            f32(8, rows),
            f32(TASKS, D, TOWER),
            f32(TASKS, TOWER + 8, D),
            f32(2, TOWER + 8, D),
            f32(rows, D),
            f32(8, D),
            f32(half, E * TASKS),
            bf(3 * D, half),
            f32(E, 1, half),
            f32(GROWS, half),
            f32(D, half),
            f32(D, half),
            f32(D, half),
            f32(2 * TOWER, half),
            f32(n * small_rows, D),
            f32(n, small_rows, D),
            f32(small_rows, D),
            f32(n * small_rows, D),
            f32(TASKS, KEPT, D),
            dma((K_COUNT,)),
            dma((K_COUNT,)),
            dma((6,)),
            dma((AHEAD + 1,)),
            pltpu.SemaphoreType.REGULAR,
            dma((2, subs, n - 1)),
            dma((2, subs, n - 1)),
            dma((2, subs, n - 1)),
            dma((2, subs, n - 1)),
            dma((2, subs, n)),
            dma((n,)),
            dma((n,)),
            dma((n,)),
            dma((n,)),
        ],
        compiler_params=pltpu.CompilerParams(
            collective_id=0, has_side_effects=True, vmem_limit_bytes=64 * 1024 * 1024 - 65536
        ),
    )(
        field_inputs,
        field_weight.reshape(1, 2),
        norm_gain.reshape(1, D),
        gate_weight.swapaxes(1, 2),
        expert_in.reshape(HALF * H, D),
        expert_out.reshape(HALF * H, D),
        tower_in.reshape(D, TOWER),
        tower_out,
        tower_bias.reshape(1, 1),
        labels.reshape(1, rows),
        source_ids.reshape(1, rows),
        task_table.reshape(1, SOURCES),
    )
    pred, ig, fw, gain, gate, d_in, d_out, tin, tout, bias = pl.pallas_call(
        partial(hand_over, len(sums)),
        out_shape=tuple(jax.ShapeDtypeStruct(v.shape, v.dtype) for v in sums),
        in_specs=[hbm] * len(sums),
        out_specs=(hbm,) * len(sums),
        scratch_shapes=[pltpu.VMEM(v.shape, v.dtype) for v in sums] + [dma((2, len(sums)))],
        compiler_params=pltpu.CompilerParams(vmem_limit_bytes=64 * 1024 * 1024 - 65536),
    )(*sums)
    return (
        pred.reshape(rows, 1),
        ig,
        fw.reshape(2),
        gain.reshape(D),
        gate.swapaxes(1, 2),
        d_in.reshape(HALF, D, H),
        d_out.reshape(HALF, H, D),
        tin.reshape(1, D, TOWER),
        tout,
        bias.reshape(1),
    )


def solution(mesh):
    in_specs = (
        P("dp", "section", None),
        P("section"),
        P(),
        P(),
        P("section", None, None),
        P("section", None, None),
        P("section", None, None),
        P("section", None),
        P("section"),
        P("dp", "section"),
        P("dp"),
        P(None, "section"),
    )
    out_specs = (
        P("dp", "section"),
        P("dp", "section", None),
        P("section"),
        P(),
        P(),
        P("section", None, None),
        P("section", None, None),
        P("section", None, None),
        P("section", None),
        P("section"),
    )
    return jax.shard_map(body, mesh=mesh, in_specs=in_specs, out_specs=out_specs, check_vma=False)
```

```python
from functools import partial

import jax
import jax.numpy as jnp
from jax import lax
from jax.experimental import pallas as pl
from jax.experimental.pallas import tpu as pltpu
from jax.sharding import PartitionSpec as P

D = 256
H = 256
E = 16
TASKS = 4
SEL = 4
BITS = 4
TOWER = 128
SOURCES = 32
HALF = E // 2
GROWS = 32
FROWS = 96

STEP_SLOPE = 0.6
ENTROPY_WEIGHT = 0.05
NORM_EPS = 1e-05
GELU_A = 0.7978845608028654
GELU_B = 0.044715

F32 = jnp.float32
BF16 = jnp.bfloat16
MESH = pl.DeviceIdType.MESH

K_W, K_P, K_SM, K_TI, K_UP, K_DOWN, K_TW, K_DG, K_DP, K_GO, K_DX = 0, 2, 4, 8, 12, 16, 20, 24, 25, 28, 32
K_COUNT = 48
TILE = 32
SPILL = TASKS - 1
AHEAD = 3

GATE_AT = TOWER
MISC_AT = GATE_AT + 2 * GROWS
SMALL = MISC_AT + 8
KEPT = SMALL - GATE_AT


def split(x):
    hi = x.astype(BF16)
    return hi, (x - hi.astype(F32)).astype(BF16)


def wide(x):
    hi, lo = split(x)
    return jnp.concatenate([hi, lo, hi], axis=1)


def tall(x):
    hi, lo = split(x)
    return jnp.concatenate([hi, hi, lo], axis=0)


def put(ref, at, x):
    k = x.shape[1]
    hi, lo = split(x)
    ref[*at, :k] = hi
    ref[*at, k:] = lo


def stack(x):
    k = x.shape[1] // 2
    return jnp.concatenate([x[:, :k], x[:, :k], x[:, k:]], axis=0)


def mm(a, b):
    return jnp.dot(a, b, preferred_element_type=F32)


def pair(x):
    k = x.shape[1] // 2
    return jnp.concatenate([x, x[:, :k]], axis=1)


def gelu_pair(x):
    x2 = x * x
    h = 0.5 + 0.5 * jnp.tanh(x * (GELU_A + (GELU_A * GELU_B) * x2))
    g = x * h
    slope = h + g * (1.0 - h) * (2.0 * GELU_A + (6.0 * GELU_A * GELU_B) * x2)
    return g, slope


def rows8(x):
    return jnp.sum(x.reshape(x.shape[0] // 8, 8, x.shape[1]), axis=0)


def over_selectors(v, groups, op):
    parts = [v[k * groups : (k + 1) * groups] for k in range(SEL)]
    return op(op(parts[0], parts[1]), op(parts[2], parts[3]))


def to_selectors(v):
    return jnp.concatenate([v] * SEL, axis=0)


def gate_state(c, groups):
    w = SEL * groups
    zs = [c[w * b : w * b + w] * STEP_SLOPE for b in range(BITS)]
    alpha = c[w * BITS : w * BITS + w]
    ups, downs, sig_p, sig_n = [], [], [], []
    for z in zs:
        e = jnp.exp(-jnp.abs(z))
        tail = jnp.log1p(e)
        ups.append(jnp.minimum(z, 0.0) - tail)
        downs.append(jnp.minimum(-z, 0.0) - tail)
        big = 1.0 / (1.0 + e)
        small = e * big
        sig_p.append(jnp.where(z >= 0.0, big, small))
        sig_n.append(jnp.where(z >= 0.0, small, big))
    low = [(ups[0] if k & 1 else downs[0]) + (ups[1] if k & 2 else downs[1]) for k in range(4)]
    high = [(ups[2] if k & 1 else downs[2]) + (ups[3] if k & 2 else downs[3]) for k in range(4)]
    log_r = [low[j & 3] + high[j >> 2] for j in range(E)]
    r = [jnp.exp(v) for v in log_r]
    top = jnp.exp(alpha - to_selectors(over_selectors(alpha, groups, jnp.maximum)))
    mix = top / to_selectors(over_selectors(top, groups, jnp.add))
    return log_r, r, mix, sig_p, sig_n


def gate_forward(c, groups):
    _, r, mix, _, _ = gate_state(c, groups)
    return [over_selectors(mix * v, groups, jnp.add) for v in r]


def gate_backward(c, dgate, groups, out):
    log_r, r, mix, sig_p, sig_n = gate_state(c, groups)
    yield
    total = jnp.zeros_like(mix)
    on = [jnp.zeros_like(mix) for _ in range(BITS)]
    off = [jnp.zeros_like(mix) for _ in range(BITS)]
    for j in range(E):
        dg = to_selectors(dgate(j))
        total = total + dg * r[j]
        dlog = r[j] * (mix * dg - ENTROPY_WEIGHT * (log_r[j] + 1.0))
        for b in range(BITS):
            if j >> b & 1:
                on[b] = on[b] + dlog
            else:
                off[b] = off[b] + dlog
        yield
    dalpha = mix * (total - to_selectors(over_selectors(mix * total, groups, jnp.add)))
    dz = [STEP_SLOPE * (on[b] * sig_n[b] - off[b] * sig_p[b]) for b in range(BITS)]
    used = SEL * (BITS + 1) * groups
    pad = jnp.zeros(((-used) % GROWS, c.shape[1]), F32)
    out.append(jnp.concatenate(dz + [dalpha, pad], axis=0))
    yield


def t_dot(a, b):
    ah, al = split(a)
    left = jnp.concatenate([ah, al, ah], axis=0)
    return lax.dot_general(left, tall(b), (((0,), (0,)), ((), ())), preferred_element_type=F32)


def weave(count, first, middle, last, extra=()):
    extra = iter(extra)
    for step in range(count + 2):
        if step < count:
            first(step, step % 2)
        next(extra, None)
        if 0 <= step - 1 < count:
            middle(step - 1, (step - 1) % 2, 0)
        next(extra, None)
        if step >= 2:
            last(step - 2, step % 2)
        next(extra, None)
        if 0 <= step - 1 < count:
            middle(step - 1, (step - 1) % 2, 1)
        next(extra, None)
    for _ in extra:
        pass


def halves(size):
    tiles = [slice(a, a + TILE) for a in range(0, size, TILE)]
    return tiles[: len(tiles) // 2], tiles[len(tiles) // 2 :]


def kernel(
    n,
    subs,
    small_rows,
    x_ref,
    fw_ref,
    gain_ref,
    gate_ref,
    win_ref,
    wout_ref,
    tin_ref,
    tout_ref,
    tbias_ref,
    labels_ref,
    ids_ref,
    table_ref,
    o_pred,
    o_ig,
    o_fw,
    o_gain,
    o_gate,
    o_in,
    o_out,
    o_tin,
    o_tout,
    o_bias,
    o_scale,
    kept,
    wt,
    w_in,
    w_out,
    a1,
    a2,
    d_in,
    d_out,
    gbuf,
    kbuf,
    kp,
    rd,
    xf,
    part,
    pre0,
    pre1,
    pre2,
    pre,
    inbox,
    outbox,
    u_t,
    u_n,
    s_t,
    s_n,
    bb,
    acc,
    wg,
    gt,
    gt0,
    cs,
    dgt,
    dg,
    gb,
    sm,
    smo,
    ti,
    tp,
    tw,
    dp,
    gain_row,
    columns,
    u_next,
    gt_next,
    cs_next,
    acc_b,
    dy_kept,
    held,
    tm,
    sb,
    sr,
    so,
    sa,
    sg,
    send,
    recv,
    local,
    fetch_sem,
    ready,
    rs_send,
    rs_recv,
    ag_send,
    ag_recv,
    store_sem,
    sr_send,
    sr_recv,
    sa_send,
    sa_recv,
):
    s = lax.axis_index("section")
    x = s // 2
    c = s % 2
    mate = s + 1 - 2 * c
    across = s + 2 - 4 * x
    diag = 3 - s
    R = part.shape[0] // 2
    mine = pl.ds(pl.multiple_of(c * R, R), R)
    theirs = pl.ds(pl.multiple_of((1 - c) * R, R), R)

    me = lax.axis_index("dp")
    odd = me % 2
    p = (1 - odd) * (me // 2) + odd * (n - 1 - me // 2)

    def ring_id(q):
        far = q // (n // 2)
        return (1 - far) * 2 * q + far * (2 * (n - 1 - q) + 1)

    nbr = [ring_id((p + 1) % n), ring_id((p + n - 1) % n)]

    barrier = pltpu.get_barrier_semaphore()
    for sec in (mate, across, diag):
        pl.semaphore_signal(barrier, inc=1, device_id={"section": sec}, device_id_type=MESH)

    def greet(i, carry):
        pl.semaphore_signal(barrier, inc=1, device_id={"dp": (me + i) % n}, device_id_type=MESH)
        return carry

    lax.fori_loop(1, n, greet, 0)
    fields = [pltpu.make_async_copy(x_ref.at[:, f], xf.at[f], local.at[2 + f]) for f in range(2)]
    for f in fields:
        f.start()
    own = pl.ds(pl.multiple_of(c * HALF * H, HALF * H), HALF * H)
    own_in = pltpu.make_async_copy(win_ref, d_in.at[own], local.at[0])
    own_out = pltpu.make_async_copy(wout_ref, d_out.at[own], local.at[1])
    own_in.start()
    own_out.start()
    pl.semaphore_wait(barrier, 3 + n - 1)

    def copy(src, dst, k, sec, ks=None):
        return pltpu.make_async_remote_copy(
            src_ref=src,
            dst_ref=dst,
            send_sem=send.at[k if ks is None else ks],
            recv_sem=recv.at[k],
            device_id={"section": sec},
            device_id_type=MESH,
        )

    def expert(j, count=1):
        return pl.ds(pl.multiple_of(j * H, H), count * H)

    for f in fields:
        f.wait()
    part[...] = xf[0] * fw_ref[0, 0] + xf[1] * fw_ref[0, 1]
    to_mate = copy(part.at[theirs], pre0, K_P, mate)
    to_mate.start()
    swap_in = copy(win_ref, d_in.at[own], K_W, mate)
    swap_out = copy(wout_ref, d_out.at[own], K_W + 1, mate)
    swap_in.start()
    swap_out.start()
    own_in.wait()
    own_out.wait()

    ids = ids_ref[...]
    mask = jnp.zeros(ids.shape, F32)
    for q in range(SOURCES):
        mask = mask + jnp.where(ids == q, table_ref[0, q].astype(F32), 0.0)
    smo[...] = jnp.zeros_like(smo)
    smo[0:1] = labels_ref[...]
    smo[1:2] = mask
    smo[2:3, :TOWER] = tout_ref[...]
    smo[3:4] = jnp.zeros((1, 2 * R), F32) + tbias_ref[0, 0]
    for k in range(2):

        @pl.when(s != 2 + k)
        def _():
            copy(smo, sm.at[s], K_SM + s, 2 + k, K_SM + k).start()
            copy(tin_ref, ti.at[s], K_TI + s, 2 + k, K_TI + k).start()

    to_mate.wait_recv()

    @pl.when(x == 1)
    def _():
        pre2[...] = part[mine] + pre0[...]
        copy(pre2, pre1, K_P + 1, across).start()
        sm[s] = smo[...]
        ti[s] = tin_ref[...]

    wg[...] = jnp.zeros_like(wg)

    @pl.when(x == 0)
    def _():
        def order(t, carry):
            for sel in range(SEL):
                for e in range(BITS + 1):
                    row = t * (SEL * (BITS + 1)) + sel * (BITS + 1) + e
                    wg[pl.ds((e * SEL + sel) * TASKS + t, 1)] = gate_ref[0, pl.ds(row, 1)]
            return carry

        lax.fori_loop(0, TASKS, order, 0)

    @pl.when(x == 1)
    def _():
        def order(t, carry):
            for sel in range(SEL):
                for e in range(BITS + 1):
                    row = t * (SEL * (BITS + 1)) + sel * (BITS + 1) + e
                    wg[pl.ds(t * GROWS + e * SEL + sel, 1)] = gate_ref[1, pl.ds(row, 1)]
            return carry

        lax.fori_loop(0, TASKS, order, 0)

    def keep_plain(e, carry):
        put(w_in.at[e], (slice(None),), d_in[expert(e)])
        put(w_out.at[e], (slice(None),), d_out[expert(e)])
        return carry

    def keep_flipped(e, carry):
        put(wt.at[e], (slice(None),), d_in[expert(e)].T)
        put(wt.at[E + e], (slice(None),), d_out[expert(e)].T)
        return carry

    lax.fori_loop(c * HALF, c * HALF + HALF, keep_plain, 0)

    def keep_mates():
        swap_in.wait()
        swap_out.wait()
        lax.fori_loop((1 - c) * HALF, (1 - c) * HALF + HALF, keep_plain, 0)

    def rows_of(size):
        return [slice(a, a + TILE) for a in range(0, size, TILE)]

    def shifted(tile, e):
        return slice(e * H + tile.start, e * H + tile.stop)

    chunk = HALF * H // n
    sub = chunk // subs
    lanes = [(d, k) for d in range(2) for k in range(subs)]

    def at(k, q):
        return pl.ds(pl.multiple_of(q * chunk + k * sub, 8), sub)

    def holds(d, step):
        return (p + n - step) % n if d == 0 else (p + step) % n

    def slot(d, k, step):
        return pl.ds(pl.multiple_of(((d * subs + k) * (n - 1) + step) * sub, 8), sub)

    def rs(d, k, step, src):
        return pltpu.make_async_remote_copy(
            src_ref=src,
            dst_ref=a1.at[slot(d, k, step)],
            send_sem=rs_send.at[d, k, step],
            recv_sem=rs_recv.at[d, k, step],
            device_id={"dp": nbr[d]},
            device_id_type=MESH,
        )

    results = (o_in, o_out)

    def landed(d, k, q):
        return a2.at[pl.ds(pl.multiple_of(d * HALF * H + q * chunk + k * sub, 8), sub)]

    def store(d, k, q, src, step):
        return pltpu.make_async_copy(src, results[d].at[at(k, q)], store_sem.at[d, k, step])

    def ag(d, k, step, src, q):
        return pltpu.make_async_remote_copy(
            src_ref=src,
            dst_ref=landed(d, k, q),
            send_sem=ag_send.at[d, k, step],
            recv_sem=ag_recv.at[d, k, step],
            device_id={"dp": nbr[d]},
            device_id_type=MESH,
        )

    def give(e):
        j = (1 - c) * HALF + e
        return (
            copy(d_in.at[expert(j)], rd.at[0, expert(e)], K_DX + e, mate),
            copy(d_out.at[expert(j)], rd.at[1, expert(e)], K_DX + HALF + e, mate),
        )

    start_at = p * chunk // H

    def near(k):
        return (start_at + HALF + ((k + 1) // 2) * (1 - 2 * (k % 2))) % HALF

    def turn_of(i):
        own_turn = i % 2
        return ((1 - own_turn) * (1 - c) + own_turn * c) * HALF + near(i // 2)

    def fetch(i):
        at = pl.ds((i % (AHEAD + 1)) * 8, 2 * SPILL)
        return pltpu.make_async_copy(kept.at[turn_of(i)], wt.at[at], fetch_sem.at[i % (AHEAD + 1)])

    def fetch_start(i):
        for k in range(2 * SPILL):
            slab = (i % (AHEAD + 1)) * 8 + k
            pltpu.make_async_copy(
                kept.at[turn_of(i), k], wt.at[slab], fetch_sem.at[i % (AHEAD + 1)]
            ).start()

    def greet_ring():
        for dev in nbr:
            pl.semaphore_signal(ready, inc=1, device_id={"dp": dev}, device_id_type=MESH)

    def merge(k, carry):
        e = near(k)
        for move in give(e):
            move.wait_recv()
        rows = expert(e)
        rd[0, rows] = (rd[0, rows] + d_in[expert(c * HALF + e)]).T
        rd[1, rows] += d_out[expert(c * HALF + e)]
        return carry

    def ring_start():
        pl.semaphore_wait(ready, 2)
        for d, k in lanes:
            rs(d, k, 0, rd.at[d, at(k, holds(d, 0))]).start()

    def reduce_step(step, carry):
        for d, k in lanes:
            rs(d, k, step - 1, a1.at[slot(d, k, step - 1)]).wait_recv()
            a1[slot(d, k, step - 1)] += rd[d, at(k, holds(d, step))]
            rs(d, k, step, a1.at[slot(d, k, step - 1)]).start()
        return carry

    @pl.when(x == 0)
    def _():
        copy(pre2, pre1, K_P + 1, across).wait_recv()
        pre_rows = part[mine] + pre0[...] + pre1[...]
        pre[...] = pre_rows
        rho = lax.rsqrt(jnp.mean(pre_rows * pre_rows, axis=1, keepdims=True) + NORM_EPS)
        pooled = pre_rows * rho * gain_ref[...]
        acc[...] = pooled
        u_n[0] = tall(pooled)
        u_t[...] = tall(pooled.T)
        logits = mm(wide(wg[:FROWS]), u_t[...])
        cs[...] = logits
        gates = gate_forward(logits, TASKS)
        for j, g in enumerate(gates):
            gt0[j] = g

        def rows_at(j, tile):
            return pl.ds(pl.multiple_of(j * H + tile.start, TILE), TILE)

        def forward(base):
            def first(i, par):
                left = jnp.concatenate([u_n[0, :R], u_n[0, 2 * R :], u_n[0, :R]], axis=1)
                bb[par] = mm(left, stack(w_in[base + i]))

            def activate(i, par, part_no):
                for tile in halves(R)[part_no]:
                    value, slope = gelu_pair(bb[par, tile])
                    a1[rows_at(base + i, tile)] = value
                    a2[rows_at(base + i, tile)] = slope
                    put(gbuf, (base + i, tile), value)

            def finish(i, par):
                d_in[expert(base + i)] = mm(pair(gbuf[base + i]), stack(w_out[base + i]))

            weave(HALF, first, activate, finish)

        forward(c * HALF)
        keep_mates()
        forward((1 - c) * HALF)
        columns[...] = jnp.concatenate(gates, axis=0).T

        for t in range(TASKS):

            def mix(i, carry):
                tile = pl.ds(pl.multiple_of(i * TILE, TILE), TILE)
                cols = columns[tile]
                total = acc[tile]
                for j in range(E):
                    rows = pl.ds(pl.multiple_of(j * R + i * TILE, TILE), TILE)
                    total = total + cols[:, j * TASKS + t : j * TASKS + t + 1] * d_in[rows]
                outbox[t, tile] = total
                return carry

            lax.fori_loop(0, R // TILE, mix, 0)
            copy(outbox.at[t], inbox.at[t], K_UP + t, across).start()

        def flip(j, carry):
            value = a1[expert(j)].T
            a1[expert(j)] = value
            put(gbuf.at[j], (slice(None),), value)
            a2[expert(j)] = a2[expert(j)].T
            d_in[expert(j)] = d_in[expert(j)].T
            return carry

        lax.fori_loop(0, E, flip, 0)
        greet_ring()
        d_out[...] = jnp.zeros_like(d_out)
        acc[...] = jnp.zeros_like(acc)

    @pl.when(x == 1)
    def _():
        keep_mates()
        lax.fori_loop(0, E, keep_flipped, 0)
        for q in range(TASKS):

            @pl.when(s != q)
            def _():
                copy(smo, sm.at[q], K_SM + q, q).wait_recv()
                copy(tin_ref, ti.at[q], K_TI + q, q).wait_recv()

        def keep(k, t):
            return pltpu.make_async_copy((gbuf, kbuf)[k], kept.at[:, k * SPILL + t], local.at[4 + k])

        def keep_start(k, t):
            def one(j, carry):
                pltpu.make_async_copy((gbuf, kbuf)[k].at[j], kept.at[j, k * SPILL + t], local.at[4 + k]).start()
                return carry

            @pl.when(t < SPILL)
            def _():
                lax.fori_loop(0, E, one, 0)

        def gate_rows(t):
            return pl.ds(pl.multiple_of(t * GROWS, GROWS), GROWS)

        def enter(t):
            for k in range(2):
                cols = slice(k * (R // 2), (k + 1) * (R // 2))
                flipped = inbox[t, cols].T
                hi, lo = split(flipped)
                u_next[:D, cols] = hi
                u_next[D : 2 * D, cols] = hi
                u_next[2 * D :, cols] = lo
                acc[:, cols] = flipped
                yield
            logits = mm(wide(wg[gate_rows(t)]), u_next[...])
            cs_next[...] = logits
            yield
            u_n[t] = tall(inbox[t])
            yield
            _, r, mix, _, _ = gate_state(logits, 1)
            yield
            for j in range(E):
                gt_next[j] = over_selectors(mix * r[j], 1, jnp.add)
                yield

        def turn():
            u_t[...] = u_next[...]
            gt[...] = gt_next[...]
            cs[GROWS : 2 * GROWS] = cs[:GROWS]
            cs[:GROWS] = cs_next[...]

        def leave(t, at):
            out = []
            yield from gate_backward(cs[at : at + GROWS], lambda j: dgt[j, 0:1], 1, out)
            outbox[t] = acc_b[...] + t_dot(wg[gate_rows(t)], out[0])
            yield
            dg[gate_rows(t)] = mm(wide(out[0]), u_n[t])
            yield

        def all_of(pieces):
            for _ in pieces:
                pass

        cs[...] = jnp.zeros_like(cs)
        dgt[...] = jnp.zeros_like(dgt)
        acc_b[...] = jnp.zeros_like(acc_b)
        copy(outbox.at[0], inbox.at[0], K_UP, across).wait_recv()
        all_of(enter(0))
        turn()

        def task(t, carry):
            @pl.when(t > 0)
            def _():
                keep(0, 0).wait()

            def first(j, par):
                bb[par] = mm(pair(wt[j]), u_t[...])

            def activate(j, par, part_no):
                for tile in halves(H)[part_no]:
                    value, slope = gelu_pair(bb[par, tile])
                    a1[shifted(tile, j)] = value
                    a2[shifted(tile, j)] = slope
                    put(gbuf, (j, tile), value * gt[j])

            def finish(j, par):
                acc[...] += mm(pair(wt[E + j]), stack(gbuf[j]))

            before = (t + TASKS - 1) % TASKS
            weave(E, first, activate, finish, leave(before, GROWS))
            keep_start(0, t)

            @pl.when(t > 0)
            def _():
                copy(outbox.at[before], inbox.at[before], K_DOWN + before, across).start()

            second = acc[...]
            held[...] = second
            tower = ti[t]
            g, slope = gelu_pair(mm(wide(tower.T), tall(second)))
            info = sm[t]
            out_col = info[:, :TOWER].T[:, 2:3]
            here = sm[t, :, mine]
            logit = jnp.sum(g * out_col, axis=0, keepdims=True) + here[3:4]
            prob = jax.nn.sigmoid(logit)
            dlogit = here[1:2] * (prob - here[0:1])
            m = dlogit * out_col * slope
            dy = mm(wide(tower), tall(m))
            s_t[...] = tall(dy)
            acc_b[...] = dy
            dy_kept[...] = dy
            tm[:TOWER] = m
            tm[TOWER:] = g * dlogit
            tp[t, TOWER : TOWER + 1] = prob
            tp[t, TOWER + 2 : TOWER + 3] = dlogit
            tp[t, TOWER + 3 :] = jnp.zeros((5, R), F32)

            @pl.when(t > 0)
            def _():
                keep(1, 0).wait()

            @pl.when(t == TASKS - 1)
            def _():
                for i in range(AHEAD):
                    fetch_start(i)

            after = jnp.minimum(t + 1, TASKS - 1)

            @pl.when(t < TASKS - 1)
            def _():
                copy(outbox.at[after], inbox.at[after], K_UP + after, across).wait_recv()

            def back(j, par):
                bb[par] = mm(pair(w_out[j]), s_t[...])

            def pull(j, par, part_no):
                total = jnp.zeros((8, R), F32)
                for tile in halves(H)[part_no]:
                    grad = bb[par, tile]
                    total = total + rows8(grad * a1[shifted(tile, j)])
                    put(kbuf, (j, tile), grad * a2[shifted(tile, j)] * gt[j])
                total = jnp.sum(total, axis=0, keepdims=True)
                if part_no == 0:
                    dgt[j, 0:1] = total
                else:
                    dgt[j, 0:1] += total

            def spread(j, par):
                acc_b[...] += mm(pair(w_in[j]), stack(kbuf[j]))

            def beside():
                s_n[t] = tall(dy_kept[...].T)
                yield
                yield from enter(after)
                flipped = tall(held[...].T)
                yield
                tp[t, :TOWER] = mm(wide(tm[:TOWER]), flipped)
                yield
                out_grad = jnp.sum(tm[TOWER:], axis=1, keepdims=True)
                out_row = jnp.broadcast_to(out_grad, (TOWER, TOWER)).T[0:1]
                tp[t, TOWER + 1 : TOWER + 2] = jnp.concatenate([out_row, jnp.zeros_like(out_row)], axis=1)
                yield

            weave(E, back, pull, spread, beside())
            keep_start(1, t)
            turn()

            @pl.when(t != s)
            def _():
                copy(tp.at[t], tw.at[c], K_TW + c, t, K_TW + t).start()

            @pl.when(t == s)
            def _():
                tw[c] = tp[t]

            return carry

        lax.fori_loop(0, TASKS, task, 0)
        last_task = TASKS - 1
        all_of(leave(last_task, GROWS))
        copy(outbox.at[last_task], inbox.at[last_task], K_DOWN + last_task, across).start()
        greet_ring()

    @pl.when(x == 1)
    def _():
        def one(i, carry):
            fetch(i).wait()

            @pl.when(i < E - AHEAD)
            def _():
                fetch_start(i + AHEAD)

            j = turn_of(i)
            slot_at = (i % (AHEAD + 1)) * 8
            for k, (grad, right, here) in enumerate(((d_out, s_n, gbuf), (d_in, u_n, kbuf))):
                left = [pair(wt[slot_at + k * SPILL + t]) for t in range(SPILL)] + [pair(here[j])]
                grad[expert(j)] = mm(jnp.concatenate(left, axis=1), right[...].reshape(3 * TASKS * R, D))

            @pl.when(i % 2 == 0)
            def _():
                for move in give(near(i // 2)):
                    move.start()

            @pl.when(i == 3)
            def _():
                merge(0, 0)
                ring_start()

            @pl.when((i % 2 == 1) & (i > 3))
            def _():
                merge((i - 3) // 2, 0)

            if n == HALF:

                @pl.when((i % 4 == 3) & (i > 3))
                def _():
                    reduce_step((i - 3) // 4, 0)

            return carry

        lax.fori_loop(0, E, one, 0)
        merge(HALF - 1, 0)
        if n != HALF:
            lax.fori_loop(1, 4, reduce_step, 0)

    @pl.when(x == 0)
    def _():
        def arrive(t, carry):
            copy(outbox.at[t], inbox.at[t], K_DOWN + t, across).wait_recv()
            acc[...] += inbox[t]

            def one(j, inner):
                gate = gt0[j, pl.ds(t, 1)]
                total = jnp.zeros((8, R), F32)
                for tile in rows_of(D):
                    dy = inbox[t, tile]
                    rows = pl.ds(pl.multiple_of(j * D + tile.start, TILE), TILE)
                    total = total + rows8(d_in[rows] * dy)
                    d_out[rows] += gate * dy
                dgt[j, pl.ds(t, 1)] = jnp.sum(total, axis=0, keepdims=True)
                return inner

            lax.fori_loop(0, E, one, 0)
            return carry

        lax.fori_loop(0, TASKS - 1, arrive, 0)
        last = TASKS - 1
        copy(outbox.at[last], inbox.at[last], K_DOWN + last, across).wait_recv()
        acc[...] += inbox[last]

        def one(i, inner):
            j = turn_of(i)
            gate = gt0[j, last : last + 1]
            total = jnp.zeros((8, R), F32)
            for tile in rows_of(D):
                dy = inbox[last, tile]
                rows = pl.ds(pl.multiple_of(j * D + tile.start, TILE), TILE)
                total = total + rows8(d_in[rows] * dy)
                put(kbuf.at[j], (tile,), d_out[rows] + gate * dy)
            dgt[j, last : last + 1] = jnp.sum(total, axis=0, keepdims=True)
            return inner

        def part_of(first, stop):
            lax.fori_loop(2 * first, 2 * stop, one, 0)

            def products(i, par):
                j = turn_of(2 * first + i)
                mixed = kbuf[j]
                bb[par] = mm(pair(w_out[j]), stack(mixed))
                right = jnp.concatenate([mixed[:, :R], mixed[:, :R], mixed[:, R:]], axis=1)
                d_out[expert(j)] = lax.dot_general(
                    pair(gbuf[j]), right, (((1,), (1,)), ((), ())), preferred_element_type=F32
                )

            def pull(i, par, part_no):
                j = turn_of(2 * first + i)
                for tile in halves(H)[part_no]:
                    kept_rows = pl.ds(pl.multiple_of(j * H + tile.start, TILE), TILE)
                    put(kp, (par, tile), bb[par, tile] * a2[kept_rows])

            def spread(i, par):
                j = turn_of(2 * first + i)
                acc[...] += mm(pair(w_in[j]), stack(kp[par]))
                d_in[expert(j)] = mm(pair(kp[par]), u_n[0])

            weave(2 * (stop - first), products, pull, spread)
            for k in range(first, stop):
                for move in give(near(k)):
                    move.start()

        part_of(0, 1)
        part_of(1, 2)
        merge(0, 0)
        ring_start()
        for k in range(2, HALF, 2):
            part_of(k, k + 2)
            lax.fori_loop(k - 1, k + 1, merge, 0)
            if n == HALF:
                reduce_step(k // 2, 0)
        merge(HALF - 1, 0)
        if n != HALF:
            lax.fori_loop(1, HALF // 2, reduce_step, 0)

    gates_own = pl.ds(pl.multiple_of(c * 2 * GROWS, 2 * GROWS), 2 * GROWS)
    gates_away = pl.ds(pl.multiple_of((1 - c) * 2 * GROWS, 2 * GROWS), 2 * GROWS)
    gain_row[...] = jnp.zeros_like(gain_row)

    @pl.when(x == 0)
    def _():
        out = []
        for _ in gate_backward(cs[...], lambda j: dgt[j, :TASKS], TASKS, out):
            pass
        dc = out[0]
        dpool = (acc[...] + t_dot(wg[:FROWS], dc)).T
        pre_rows = pre[...]
        rho = lax.rsqrt(jnp.mean(pre_rows * pre_rows, axis=1, keepdims=True) + NORM_EPS)
        scaled = dpool * gain_ref[...]
        dots = jnp.mean(scaled * pre_rows, axis=1, keepdims=True)
        dp[mine] = rho * scaled - pre_rows * (rho * rho * rho * dots)
        for k, sec in enumerate((mate, across, diag)):
            copy(dp.at[mine], dp.at[mine], K_DP + c, sec, K_DP + k).start()
        gain_row[0:1] = jnp.sum(dpool * pre_rows * rho, axis=0, keepdims=True)
        grad = mm(wide(dc), u_n[0])
        dg[: FROWS // 2] = grad[: FROWS // 2]
        dg[2 * GROWS : 2 * GROWS + FROWS // 2] = grad[FROWS // 2 :]

    gates_move = copy(dg.at[gates_away], gb, K_DG, mate)
    gates_move.start()

    lax.fori_loop(4, 6, reduce_step, 0)

    for half_no in range(2):

        @pl.when(s != half_no)
        def _():
            rows = pl.ds(half_no * R, R)
            copy(dp.at[rows], dp.at[rows], K_DP + half_no, half_no).wait_recv()

    for k in range(2):

        @pl.when(s != 2 + k)
        def _():
            copy(tp.at[0], tw.at[k], K_TW + k, s).wait_recv()

    gates_move.wait_recv()
    sb[:TOWER] = tw[0, :TOWER] + tw[1, :TOWER]
    sb[GATE_AT:MISC_AT] = dg[gates_own] + gb[...]
    sb[MISC_AT : MISC_AT + 1] = gain_row[0:1]
    sb[MISC_AT + 1 : MISC_AT + 3] = tw[0, TOWER + 1 : TOWER + 3] + tw[1, TOWER + 1 : TOWER + 3]
    for f in range(2):
        sb[MISC_AT + 3 + f : MISC_AT + 4 + f] = jnp.sum(xf[f] * dp[...], axis=0, keepdims=True)
    sb[MISC_AT + 5 : MISC_AT + 6] = smo[1:2, :R] + smo[1:2, R:]
    sb[MISC_AT + 6 :] = jnp.zeros((sb.shape[0] - MISC_AT - 6, D), F32)

    def block(q):
        return pl.ds(pl.multiple_of(q * small_rows, 8), small_rows)

    def scatter(i):
        to = (me + i) % n
        return pltpu.make_async_remote_copy(
            src_ref=sb.at[block(to)],
            dst_ref=sr.at[me],
            send_sem=sr_send.at[i],
            recv_sem=sr_recv.at[me],
            device_id={"dp": to},
            device_id_type=MESH,
        )

    def scattered(i):
        by = (me + i) % n
        return pltpu.make_async_remote_copy(
            src_ref=sb.at[block(me)],
            dst_ref=sr.at[by],
            send_sem=sr_send.at[i],
            recv_sem=sr_recv.at[by],
            device_id={"dp": by},
            device_id_type=MESH,
        )

    def spread_sum(i):
        return pltpu.make_async_remote_copy(
            src_ref=so,
            dst_ref=sa.at[block(me)],
            send_sem=sa_send.at[i],
            recv_sem=sa_recv.at[me],
            device_id={"dp": (me + i) % n},
            device_id_type=MESH,
        )

    def gathered(i):
        by = (me + i) % n
        return pltpu.make_async_remote_copy(
            src_ref=so,
            dst_ref=sa.at[block(by)],
            send_sem=sa_send.at[i],
            recv_sem=sa_recv.at[by],
            device_id={"dp": by},
            device_id_type=MESH,
        )

    def each(act):
        def one(i, carry):
            act(i)
            return carry

        lax.fori_loop(1, n, one, 0)

    each(lambda i: scatter(i).start())
    lax.fori_loop(6, n - 1, reduce_step, 0)
    last = n - 2
    for d, k in lanes:
        q = holds(d, n - 1)
        rs(d, k, last, a1.at[slot(d, k, last)]).wait_recv()
        a1[slot(d, k, last)] += rd[d, at(k, q)]
        ag(d, k, 0, a1.at[slot(d, k, last)], q).start()
        store(d, k, q, a1.at[slot(d, k, last)], 0).start()

    def gather_step(step, carry):
        for d, k in lanes:
            q = holds(d, step - 1)
            ag(d, k, step - 1, landed(d, k, q), q).wait_recv()
            ag(d, k, step, landed(d, k, q), q).start()
            store(d, k, q, landed(d, k, q), step).start()
        return carry

    so[...] = sb[block(me)]

    def take(i):
        scattered(i).wait_recv()
        so[...] += sr[(me + i) % n]

    each(take)
    sa[block(me)] = so[...]
    each(lambda i: spread_sum(i).start())
    lax.fori_loop(1, 3, gather_step, 0)
    each(lambda i: gathered(i).wait_recv())
    piece = sa.at[pl.ds(GATE_AT, KEPT)]
    for k, sec in enumerate((mate, across, diag)):
        copy(piece, sg.at[s], K_GO + s, sec, K_GO + k).start()
    sg[s] = sa[GATE_AT:SMALL]
    lax.fori_loop(3, 4, gather_step, 0)
    for sec in (mate, across, diag):
        copy(piece, sg.at[sec], K_GO + sec, sec).wait_recv()
    misc = KEPT - 8
    count = sum(sg[q, misc + 5 : misc + 6] for q in range(TASKS))
    scale = float(2 * R * n) / jnp.sum(count, axis=1, keepdims=True)

    o_scale[...] = jnp.broadcast_to(scale, o_scale.shape)

    for f in range(2):
        xf[f] = dp[...] * (scale * fw_ref[0, f])
        pltpu.make_async_copy(xf.at[f], o_ig.at[:, f], local.at[2 + f]).start()
    for k in range(2):
        o_pred[:, k * R : (k + 1) * R] = tw[k, TOWER : TOWER + 1]
    for f in range(2):
        o_fw[0, f] = jnp.sum(sa[MISC_AT + 3 + f : MISC_AT + 4 + f] * scale)
    o_bias[0, 0] = jnp.sum(sa[MISC_AT + 2 : MISC_AT + 3] * scale)
    o_gain[...] = (sg[0, misc : misc + 1] + sg[1, misc : misc + 1]) * scale
    o_tout[...] = sa[MISC_AT + 1 : MISC_AT + 2, :TOWER] * scale
    o_tin[...] = (sa[:TOWER] * scale).T

    def order(t, carry):
        for sel in range(SEL):
            for e in range(BITS + 1):
                row = t * (SEL * (BITS + 1)) + sel * (BITS + 1) + e
                at0 = (e * SEL + sel) * TASKS
                cut = FROWS // 2
                o_gate[0, pl.ds(row, 1)] = sg[at0 // cut, pl.ds(at0 % cut + t, 1)] * scale
                o_gate[1, pl.ds(row, 1)] = sg[2 + t // 2, pl.ds((t % 2) * GROWS + e * SEL + sel, 1)] * scale
        return carry

    lax.fori_loop(0, TASKS, order, 0)

    lax.fori_loop(4, n - 1, gather_step, 0)
    for d, k in lanes:
        q = holds(d, n - 2)
        ag(d, k, last, landed(d, k, q), q).wait_recv()
        store(d, k, q, landed(d, k, q), n - 1).start()

    def stored(step, carry):
        for d, k in lanes:
            store(d, k, 0, landed(d, k, 0), step).wait()
        return carry

    lax.fori_loop(0, n, stored, 0)

    def sent(step, carry):
        for d, k in lanes:
            rs(d, k, step, a1.at[slot(d, k, step)]).wait_send()
            ag(d, k, step, a1.at[slot(d, k, step)], 0).wait_send()
        return carry

    lax.fori_loop(0, n - 1, sent, 0)
    each(lambda i: scatter(i).wait_send())
    each(lambda i: spread_sum(i).wait_send())
    to_mate.wait_send()
    gates_move.wait_send()
    for e in range(HALF):
        for move in give(e):
            move.wait_send()
    for k in range(2):

        @pl.when(s != 2 + k)
        def _():
            copy(smo, sm.at[s], K_SM + s, 2 + k, K_SM + k).wait_send()
            copy(tin_ref, ti.at[s], K_TI + s, 2 + k, K_TI + k).wait_send()

    @pl.when(x == 0)
    def _():
        for t in range(TASKS):
            copy(outbox.at[t], inbox.at[t], K_UP + t, across).wait_send()
        for k, sec in enumerate((mate, across, diag)):
            copy(dp.at[mine], dp.at[mine], K_DP + c, sec, K_DP + k).wait_send()

    @pl.when(x == 1)
    def _():
        copy(pre2, pre1, K_P + 1, across).wait_send()
        for t in range(TASKS):
            copy(outbox.at[t], inbox.at[t], K_DOWN + t, across).wait_send()

            @pl.when(t != s)
            def _():
                copy(tp.at[t], tw.at[c], K_TW + c, t, K_TW + t).wait_send()

    for k, sec in enumerate((mate, across, diag)):
        copy(piece, sg.at[s], K_GO + s, sec, K_GO + k).wait_send()
    for f in range(2):
        pltpu.make_async_copy(xf.at[f], o_ig.at[:, f], local.at[2 + f]).wait()


def hand_over(count, scaled, scale_ref, *refs):
    held = refs[2 * count : 3 * count]
    sems = refs[-1]
    reads = [pltpu.make_async_copy(refs[k], held[k], sems.at[0, k]) for k in range(count)]
    writes = [pltpu.make_async_copy(held[k], refs[count + k], sems.at[1, k]) for k in range(count)]
    order = list(scaled) + [k for k in range(count) if k not in scaled]
    for k in order:
        reads[k].start()
    scale = scale_ref[0:1, 0:1]
    for k in order:
        reads[k].wait()
        if k in scaled:

            def one(i, carry):
                rows = pl.ds(pl.multiple_of(i * H, H), H)
                held[k][rows] = held[k][rows] * scale
                return carry

            lax.fori_loop(0, held[k].shape[0] // H, one, 0)
        writes[k].start()
    for move in writes:
        move.wait()


def body(
    field_inputs,
    field_weight,
    norm_gain,
    gate_weight,
    expert_in,
    expert_out,
    tower_in,
    tower_out,
    tower_bias,
    labels,
    source_ids,
    task_table,
):
    n = lax.axis_size("dp")
    rows = field_inputs.shape[0]
    half = rows // 2
    subs = 2
    small_rows = -(-SMALL // (8 * n)) * 8
    used = TASKS * SEL * (BITS + 1)

    vmem = pl.BlockSpec(memory_space=pltpu.VMEM)
    smem = pl.BlockSpec(memory_space=pltpu.SMEM)
    hbm = pl.BlockSpec(memory_space=pl.ANY)

    def bf(*shape):
        return pltpu.VMEM(shape, BF16)

    def f32(*shape):
        return pltpu.VMEM(shape, F32)

    def out(*shape):
        return jax.ShapeDtypeStruct(shape, F32)

    dma = pltpu.SemaphoreType.DMA
    *sums, scale, _ = pl.pallas_call(
        partial(kernel, n, subs, small_rows),
        out_shape=(
            out(1, rows),
            out(rows, 2, D),
            out(1, 2),
            out(1, D),
            out(2, used, D),
            out(HALF * H, D),
            out(HALF * H, D),
            out(D, TOWER),
            out(1, TOWER),
            out(1, 1),
            out(1, TOWER),
            jax.ShapeDtypeStruct((E, 2 * SPILL, H, 2 * half), BF16),
        ),
        in_specs=[hbm, smem, vmem, vmem, hbm, hbm, vmem, vmem, smem, vmem, vmem, smem],
        out_specs=(vmem, hbm, smem, vmem, vmem, hbm, hbm, vmem, vmem, smem, vmem, hbm),
        scratch_shapes=[
            bf(2 * E, H, 2 * D),
            bf(E, D, 2 * H),
            bf(E, H, 2 * D),
            f32(E * H, half),
            f32(E * H, half),
            f32(E * H, D),
            f32(E * H, D),
            bf(E, H, 2 * half),
            bf(E, H, 2 * half),
            bf(2, H, 2 * half),
            f32(2, HALF * H, D),
            f32(2, rows, D),
            f32(rows, D),
            f32(half, D),
            f32(half, D),
            f32(half, D),
            f32(half, D),
            f32(TASKS, D, half),
            f32(TASKS, D, half),
            bf(3 * D, half),
            bf(TASKS, 3 * half, D),
            bf(3 * D, half),
            bf(TASKS, 3 * half, D),
            f32(2, H, half),
            f32(D, half),
            f32(TASKS * GROWS, D),
            f32(E, 1, half),
            f32(E, TASKS, half),
            f32(FROWS, half),
            f32(E, TASKS, half),
            f32(TASKS * GROWS, D),
            f32(2 * GROWS, D),
            f32(TASKS, 8, rows),
            f32(8, rows),
            f32(TASKS, D, TOWER),
            f32(TASKS, TOWER + 8, D),
            f32(2, TOWER + 8, D),
            f32(rows, D),
            f32(8, D),
            f32(half, E * TASKS),
            bf(3 * D, half),
            f32(E, 1, half),
            f32(GROWS, half),
            f32(D, half),
            f32(D, half),
            f32(D, half),
            f32(2 * TOWER, half),
            f32(n * small_rows, D),
            f32(n, small_rows, D),
            f32(small_rows, D),
            f32(n * small_rows, D),
            f32(TASKS, KEPT, D),
            dma((K_COUNT,)),
            dma((K_COUNT,)),
            dma((6,)),
            dma((AHEAD + 1,)),
            pltpu.SemaphoreType.REGULAR,
            dma((2, subs, n - 1)),
            dma((2, subs, n - 1)),
            dma((2, subs, n - 1)),
            dma((2, subs, n - 1)),
            dma((2, subs, n)),
            dma((n,)),
            dma((n,)),
            dma((n,)),
            dma((n,)),
        ],
        compiler_params=pltpu.CompilerParams(
            collective_id=0, has_side_effects=True, vmem_limit_bytes=64 * 1024 * 1024 - 65536
        ),
    )(
        field_inputs,
        field_weight.reshape(1, 2),
        norm_gain.reshape(1, D),
        gate_weight.swapaxes(1, 2),
        expert_in.reshape(HALF * H, D),
        expert_out.reshape(HALF * H, D),
        tower_in.reshape(D, TOWER),
        tower_out,
        tower_bias.reshape(1, 1),
        labels.reshape(1, rows),
        source_ids.reshape(1, rows),
        task_table.reshape(1, SOURCES),
    )
    pred, ig, fw, gain, gate, d_in, d_out, tin, tout, bias = pl.pallas_call(
        partial(hand_over, len(sums), (5, 6)),
        out_shape=tuple(jax.ShapeDtypeStruct(v.shape, v.dtype) for v in sums),
        in_specs=[vmem] + [hbm] * len(sums),
        out_specs=(hbm,) * len(sums),
        scratch_shapes=[pltpu.VMEM(v.shape, v.dtype) for v in sums] + [dma((2, len(sums)))],
        compiler_params=pltpu.CompilerParams(vmem_limit_bytes=64 * 1024 * 1024 - 65536),
    )(scale, *sums)
    return (
        pred.reshape(rows, 1),
        ig,
        fw.reshape(2),
        gain.reshape(D),
        gate.swapaxes(1, 2),
        d_in.reshape(HALF, D, H),
        d_out.reshape(HALF, H, D),
        tin.reshape(1, D, TOWER),
        tout,
        bias.reshape(1),
    )


def solution(mesh):
    in_specs = (
        P("dp", "section", None),
        P("section"),
        P(),
        P(),
        P("section", None, None),
        P("section", None, None),
        P("section", None, None),
        P("section", None),
        P("section"),
        P("dp", "section"),
        P("dp"),
        P(None, "section"),
    )
    out_specs = (
        P("dp", "section"),
        P("dp", "section", None),
        P("section"),
        P(),
        P(),
        P("section", None, None),
        P("section", None, None),
        P("section", None, None),
        P("section", None),
        P("section"),
    )
    return jax.shard_map(body, mesh=mesh, in_specs=in_specs, out_specs=out_specs, check_vma=False)
```

```python
from functools import partial

import jax
import jax.numpy as jnp
from jax import lax
from jax.experimental import pallas as pl
from jax.experimental.pallas import tpu as pltpu
from jax.sharding import PartitionSpec as P

D = 256
H = 256
E = 16
TASKS = 4
SEL = 4
BITS = 4
TOWER = 128
SOURCES = 32
HALF = E // 2
GROWS = 32
FROWS = 96

STEP_SLOPE = 0.6
ENTROPY_WEIGHT = 0.05
NORM_EPS = 1e-05
GELU_A = 0.7978845608028654
GELU_B = 0.044715

F32 = jnp.float32
BF16 = jnp.bfloat16
MESH = pl.DeviceIdType.MESH

K_W, K_P, K_SM, K_TI, K_UP, K_DOWN, K_TW, K_DG, K_DP, K_GO, K_DX = 0, 2, 4, 8, 12, 16, 20, 24, 25, 28, 32
K_COUNT = 48
TILE = 32
SPILL = TASKS - 1
AHEAD = 3

GATE_AT = TOWER
MISC_AT = GATE_AT + 2 * GROWS
SMALL = MISC_AT + 8
KEPT = SMALL - GATE_AT


def split(x):
    hi = x.astype(BF16)
    return hi, (x - hi.astype(F32)).astype(BF16)


def wide(x):
    hi, lo = split(x)
    return jnp.concatenate([hi, lo, hi], axis=1)


def tall(x):
    hi, lo = split(x)
    return jnp.concatenate([hi, hi, lo], axis=0)


def put(ref, at, x):
    k = x.shape[1]
    hi, lo = split(x)
    ref[*at, :k] = hi
    ref[*at, k:] = lo


def stack(x):
    k = x.shape[1] // 2
    return jnp.concatenate([x[:, :k], x[:, :k], x[:, k:]], axis=0)


def mm(a, b):
    return jnp.dot(a, b, preferred_element_type=F32)


def pair(x):
    k = x.shape[1] // 2
    return jnp.concatenate([x, x[:, :k]], axis=1)


def gelu_pair(x):
    x2 = x * x
    h = 0.5 + 0.5 * jnp.tanh(x * (GELU_A + (GELU_A * GELU_B) * x2))
    g = x * h
    slope = h + g * (1.0 - h) * (2.0 * GELU_A + (6.0 * GELU_A * GELU_B) * x2)
    return g, slope


def rows8(x):
    return jnp.sum(x.reshape(x.shape[0] // 8, 8, x.shape[1]), axis=0)


def over_selectors(v, groups, op):
    parts = [v[k * groups : (k + 1) * groups] for k in range(SEL)]
    return op(op(parts[0], parts[1]), op(parts[2], parts[3]))


def to_selectors(v):
    return jnp.concatenate([v] * SEL, axis=0)


def gate_state(c, groups, swapped):
    w = SEL * groups
    zs = [c[w * b : w * b + w] * STEP_SLOPE for b in range(BITS)]
    alpha = c[w * BITS : w * BITS + w]
    ups, downs, sig_p, sig_n = [], [], [], []
    for z in zs:
        e = jnp.exp(-jnp.abs(z))
        tail = jnp.log1p(e)
        ups.append(jnp.minimum(z, 0.0) - tail)
        downs.append(jnp.minimum(-z, 0.0) - tail)
        big = 1.0 / (1.0 + e)
        small = e * big
        sig_p.append(jnp.where(z >= 0.0, big, small))
        sig_n.append(jnp.where(z >= 0.0, small, big))
    last_on, last_off = ups[3], downs[3]
    ups[3], downs[3] = jnp.where(swapped, last_off, last_on), jnp.where(swapped, last_on, last_off)
    low = [(ups[0] if k & 1 else downs[0]) + (ups[1] if k & 2 else downs[1]) for k in range(4)]
    high = [(ups[2] if k & 1 else downs[2]) + (ups[3] if k & 2 else downs[3]) for k in range(4)]
    log_r = [low[j & 3] + high[j >> 2] for j in range(E)]
    r = [jnp.exp(v) for v in log_r]
    top = jnp.exp(alpha - to_selectors(over_selectors(alpha, groups, jnp.maximum)))
    mix = top / to_selectors(over_selectors(top, groups, jnp.add))
    return log_r, r, mix, sig_p, sig_n


def gate_forward(c, groups, swapped):
    _, r, mix, _, _ = gate_state(c, groups, swapped)
    return [over_selectors(mix * v, groups, jnp.add) for v in r]


class GateBackward:
    def __init__(self, c, groups, swapped):
        self.log_r, self.r, self.mix, self.sig_p, self.sig_n = gate_state(c, groups, swapped)
        self.swapped = swapped
        self.groups = groups
        self.total = jnp.zeros_like(self.mix)
        self.on = [jnp.zeros_like(self.mix) for _ in range(BITS)]
        self.off = [jnp.zeros_like(self.mix) for _ in range(BITS)]

    def add(self, j, dg):
        dg = to_selectors(dg)
        self.total = self.total + dg * self.r[j]
        dlog = self.r[j] * (self.mix * dg - ENTROPY_WEIGHT * (self.log_r[j] + 1.0))
        for b in range(BITS):
            if j >> b & 1:
                self.on[b] = self.on[b] + dlog
            else:
                self.off[b] = self.off[b] + dlog

    def result(self):
        mix, groups = self.mix, self.groups
        dalpha = mix * (self.total - to_selectors(over_selectors(mix * self.total, groups, jnp.add)))
        on, off = self.on[3], self.off[3]
        self.on[3], self.off[3] = jnp.where(self.swapped, off, on), jnp.where(self.swapped, on, off)
        dz = [STEP_SLOPE * (self.on[b] * self.sig_n[b] - self.off[b] * self.sig_p[b]) for b in range(BITS)]
        used = SEL * (BITS + 1) * groups
        pad = jnp.zeros(((-used) % GROWS, mix.shape[1]), F32)
        return jnp.concatenate(dz + [dalpha, pad], axis=0)


def t_dot(a, b):
    ah, al = split(a)
    left = jnp.concatenate([ah, al, ah], axis=0)
    return lax.dot_general(left, tall(b), (((0,), (0,)), ((), ())), preferred_element_type=F32)


def weave(count, first, middle, last, extra=(), after=None):
    extra = iter(extra)
    for step in range(count + 2):
        if step < count:
            first(step, step % 2)
        next(extra, None)
        if 0 <= step - 1 < count:
            middle(step - 1, (step - 1) % 2, 0)
        next(extra, None)
        if step >= 2:
            last(step - 2, step % 2)
        next(extra, None)
        if 0 <= step - 1 < count:
            middle(step - 1, (step - 1) % 2, 1)
            if after is not None:
                after(step - 1)
        next(extra, None)
    for _ in extra:
        pass


def halves(size):
    tiles = [slice(a, a + TILE) for a in range(0, size, TILE)]
    return tiles[: len(tiles) // 2], tiles[len(tiles) // 2 :]


def kernel(
    n,
    subs,
    small_rows,
    x_ref,
    fw_ref,
    gain_ref,
    gate_ref,
    win_ref,
    wout_ref,
    tin_ref,
    tout_ref,
    tbias_ref,
    labels_ref,
    ids_ref,
    table_ref,
    o_pred,
    o_ig,
    o_fw,
    o_gain,
    o_gate,
    o_in,
    o_out,
    o_tin,
    o_tout,
    o_bias,
    o_scale,
    kept,
    wt,
    w_in,
    w_out,
    a1,
    a2,
    d_in,
    d_out,
    gbuf,
    kbuf,
    kp,
    rd,
    xf,
    part,
    pre0,
    pre1,
    pre2,
    pre,
    inbox,
    outbox,
    u_t,
    u_n,
    s_t,
    s_n,
    bb,
    acc,
    wg,
    gt,
    gt0,
    cs,
    dgt,
    dg,
    gb,
    sm,
    smo,
    ti,
    tp,
    tw,
    dp,
    gain_row,
    columns,
    u_next,
    gt_next,
    cs_next,
    acc_b,
    dy_kept,
    tower_t,
    tower_n,
    out_cols,
    dcs,
    held,
    tm,
    sb,
    sr,
    so,
    sa,
    sg,
    send,
    recv,
    local,
    fetch_sem,
    ready,
    turns,
    rs_send,
    rs_recv,
    ag_send,
    ag_recv,
    store_sem,
    sr_send,
    sr_recv,
    sa_send,
    sa_recv,
):
    s = lax.axis_index("section")
    x = s // 2
    c = s % 2
    mate = s + 1 - 2 * c
    across = s + 2 - 4 * x
    diag = 3 - s
    R = part.shape[0] // 2
    mine = pl.ds(pl.multiple_of(c * R, R), R)
    theirs = pl.ds(pl.multiple_of((1 - c) * R, R), R)

    me = lax.axis_index("dp")
    odd = me % 2
    p = (1 - odd) * (me // 2) + odd * (n - 1 - me // 2)

    def ring_id(q):
        far = q // (n // 2)
        return (1 - far) * 2 * q + far * (2 * (n - 1 - q) + 1)

    nbr = [ring_id((p + 1) % n), ring_id((p + n - 1) % n)]

    barrier = pltpu.get_barrier_semaphore()
    for sec in (mate, across, diag):
        pl.semaphore_signal(barrier, inc=1, device_id={"section": sec}, device_id_type=MESH)

    def greet(i, carry):
        pl.semaphore_signal(barrier, inc=1, device_id={"dp": (me + i) % n}, device_id_type=MESH)
        return carry

    lax.fori_loop(1, n, greet, 0)
    fields = [pltpu.make_async_copy(x_ref.at[:, f], xf.at[f], local.at[2 + f]) for f in range(2)]
    for f in fields:
        f.start()
    own = pl.ds(0, HALF * H)
    mates = pl.ds(HALF * H, HALF * H)
    swapped = c == 1
    own_in = pltpu.make_async_copy(win_ref, d_in.at[own], local.at[0])
    own_out = pltpu.make_async_copy(wout_ref, d_out.at[own], local.at[1])
    own_in.start()
    own_out.start()
    pl.semaphore_wait(barrier, 3 + n - 1)

    def copy(src, dst, k, sec, ks=None):
        return pltpu.make_async_remote_copy(
            src_ref=src,
            dst_ref=dst,
            send_sem=send.at[k if ks is None else ks],
            recv_sem=recv.at[k],
            device_id={"section": sec},
            device_id_type=MESH,
        )

    def expert(j, count=1):
        return pl.ds(pl.multiple_of(j * H, H), count * H)

    for f in fields:
        f.wait()
    part[...] = xf[0] * fw_ref[0, 0] + xf[1] * fw_ref[0, 1]
    to_mate = copy(part.at[theirs], pre0, K_P, mate)
    to_mate.start()
    swap_in = copy(win_ref, d_in.at[mates], K_W, mate)
    swap_out = copy(wout_ref, d_out.at[mates], K_W + 1, mate)
    swap_in.start()
    swap_out.start()
    own_in.wait()
    own_out.wait()

    ids = ids_ref[...]
    mask = jnp.zeros(ids.shape, F32)
    for q in range(SOURCES):
        mask = mask + jnp.where(ids == q, table_ref[0, q].astype(F32), 0.0)
    smo[...] = jnp.zeros_like(smo)
    smo[0:1] = labels_ref[...]
    smo[1:2] = mask
    smo[2:3, :TOWER] = tout_ref[...]
    smo[3:4] = jnp.zeros((1, 2 * R), F32) + tbias_ref[0, 0]
    for k in range(2):

        @pl.when(s != 2 + k)
        def _():
            copy(smo, sm.at[s], K_SM + s, 2 + k, K_SM + k).start()
            copy(tin_ref, ti.at[s], K_TI + s, 2 + k, K_TI + k).start()

    to_mate.wait_recv()

    @pl.when(x == 1)
    def _():
        pre2[...] = part[mine] + pre0[...]
        copy(pre2, pre1, K_P + 1, across).start()
        sm[s] = smo[...]
        ti[s] = tin_ref[...]

    wg[...] = jnp.zeros_like(wg)

    @pl.when(x == 0)
    def _():
        def order(t, carry):
            for sel in range(SEL):
                for e in range(BITS + 1):
                    row = t * (SEL * (BITS + 1)) + sel * (BITS + 1) + e
                    wg[pl.ds((e * SEL + sel) * TASKS + t, 1)] = gate_ref[0, pl.ds(row, 1)]
            return carry

        lax.fori_loop(0, TASKS, order, 0)

    @pl.when(x == 1)
    def _():
        def order(t, carry):
            for sel in range(SEL):
                for e in range(BITS + 1):
                    row = t * (SEL * (BITS + 1)) + sel * (BITS + 1) + e
                    wg[pl.ds(t * GROWS + e * SEL + sel, 1)] = gate_ref[1, pl.ds(row, 1)]
            return carry

        lax.fori_loop(0, TASKS, order, 0)

    def keep_plain(e, carry):
        put(w_in.at[e], (slice(None),), d_in[expert(e)])
        put(w_out.at[e], (slice(None),), d_out[expert(e)])
        return carry

    def keep_flipped(e, carry):
        put(wt.at[e], (slice(None),), d_in[expert(e)].T)
        put(wt.at[E + e], (slice(None),), d_out[expert(e)].T)
        return carry

    lax.fori_loop(0, HALF, keep_plain, 0)

    def keep_mates():
        swap_in.wait()
        swap_out.wait()
        lax.fori_loop(HALF, E, keep_plain, 0)

    def rows_of(size):
        return [slice(a, a + TILE) for a in range(0, size, TILE)]

    def shifted(tile, e):
        return slice(e * H + tile.start, e * H + tile.stop)

    chunk = HALF * H // n
    sub = chunk // subs
    lanes = [(d, k) for d in range(2) for k in range(subs)]

    def at(k, q):
        return pl.ds(pl.multiple_of(q * chunk + k * sub, 8), sub)

    def holds(d, step):
        return (p + n - step) % n if d == 0 else (p + step) % n

    def slot(d, k, step):
        return pl.ds(pl.multiple_of(((d * subs + k) * (n - 1) + step) * sub, 8), sub)

    def rs(d, k, step, src):
        return pltpu.make_async_remote_copy(
            src_ref=src,
            dst_ref=a1.at[slot(d, k, step)],
            send_sem=rs_send.at[d, k, step],
            recv_sem=rs_recv.at[d, k, step],
            device_id={"dp": nbr[d]},
            device_id_type=MESH,
        )

    results = (o_in, o_out)

    def landed(d, k, q):
        return a2.at[pl.ds(pl.multiple_of(d * HALF * H + q * chunk + k * sub, 8), sub)]

    def store(d, k, q, src, step):
        return pltpu.make_async_copy(src, results[d].at[at(k, q)], store_sem.at[d, k, step])

    def ag(d, k, step, src, q):
        return pltpu.make_async_remote_copy(
            src_ref=src,
            dst_ref=landed(d, k, q),
            send_sem=ag_send.at[d, k, step],
            recv_sem=ag_recv.at[d, k, step],
            device_id={"dp": nbr[d]},
            device_id_type=MESH,
        )

    def give(e):
        j = HALF + e
        return (
            copy(d_in.at[expert(j)], rd.at[0, expert(e)], K_DX + e, mate),
            copy(d_out.at[expert(j)], rd.at[1, expert(e)], K_DX + HALF + e, mate),
        )

    start_at = p * chunk // H

    def near(k):
        return (start_at + HALF + ((k + 1) // 2) * (1 - 2 * (k % 2))) % HALF

    def turn_of(i):
        own_turn = i % 2
        return (1 - own_turn) * HALF + near(i // 2)

    def fetch(i):
        at = pl.ds((i % (AHEAD + 1)) * 8, 2 * SPILL)
        return pltpu.make_async_copy(kept.at[turn_of(i)], wt.at[at], fetch_sem.at[i % (AHEAD + 1)])

    def fetch_start(i):
        for k in range(2 * SPILL):
            slab = (i % (AHEAD + 1)) * 8 + k
            pltpu.make_async_copy(
                kept.at[turn_of(i), k], wt.at[slab], fetch_sem.at[i % (AHEAD + 1)]
            ).start()

    def greet_ring():
        for dev in nbr:
            pl.semaphore_signal(ready, inc=1, device_id={"dp": dev}, device_id_type=MESH)

    def merge(k, carry):
        e = near(k)
        for move in give(e):
            move.wait_recv()
        rows = expert(e)
        rd[0, rows] = (rd[0, rows] + d_in[rows]).T
        rd[1, rows] += d_out[rows]
        return carry

    def ring_start():
        pl.semaphore_wait(ready, 2)
        for d, k in lanes:
            rs(d, k, 0, rd.at[d, at(k, holds(d, 0))]).start()

    def reduce_step(step, carry):
        for d, k in lanes:
            rs(d, k, step - 1, a1.at[slot(d, k, step - 1)]).wait_recv()
            a1[slot(d, k, step - 1)] += rd[d, at(k, holds(d, step))]
            rs(d, k, step, a1.at[slot(d, k, step - 1)]).start()
        return carry

    @pl.when(x == 0)
    def _():
        copy(pre2, pre1, K_P + 1, across).wait_recv()
        pre_rows = part[mine] + pre0[...] + pre1[...]
        pre[...] = pre_rows
        rho = lax.rsqrt(jnp.mean(pre_rows * pre_rows, axis=1, keepdims=True) + NORM_EPS)
        pooled = pre_rows * rho * gain_ref[...]
        acc[...] = pooled
        u_n[0] = tall(pooled)
        u_t[...] = tall(pooled.T)
        logits = mm(wide(wg[:FROWS]), u_t[...])
        cs[...] = logits
        gates = gate_forward(logits, TASKS, swapped)
        for j, g in enumerate(gates):
            gt0[j] = g

        def forward(base):
            def first(i, par):
                left = jnp.concatenate([u_n[0, :R], u_n[0, 2 * R :], u_n[0, :R]], axis=1)
                bb[par] = mm(left, stack(w_in[base + i]))

            def activate(i, par, part_no):
                for tile in halves(R)[part_no]:
                    value, slope = gelu_pair(bb[par, tile])
                    a1[shifted(tile, base + i)] = value
                    a2[shifted(tile, base + i)] = slope
                    put(gbuf, (base + i, tile), value)

            def finish(i, par):
                d_in[expert(base + i)] = mm(pair(gbuf[base + i]), stack(w_out[base + i]))

            weave(HALF, first, activate, finish)

        forward(0)
        keep_mates()
        forward(HALF)
        columns[...] = jnp.concatenate(gates, axis=0).T

        for t in range(TASKS):

            def mix(i, carry):
                tile = pl.ds(pl.multiple_of(i * TILE, TILE), TILE)
                cols = columns[tile]
                total = acc[tile]
                for j in range(E):
                    rows = pl.ds(pl.multiple_of(j * R + i * TILE, TILE), TILE)
                    total = total + cols[:, j * TASKS + t : j * TASKS + t + 1] * d_in[rows]
                outbox[t, tile] = total
                return carry

            lax.fori_loop(0, R // TILE, mix, 0)

            @pl.when(c == 0)
            def _():
                if t == 0:
                    copy(outbox.at[t], inbox.at[t], K_UP + t, across).start()

        first_up = copy(outbox.at[0], inbox.at[0], K_UP, across)

        @pl.when(c == 0)
        def _():
            first_up.wait_send()
            pl.semaphore_signal(turns, inc=1, device_id={"section": mate}, device_id_type=MESH)
            pl.semaphore_wait(turns, 1)

        @pl.when(c == 1)
        def _():
            pl.semaphore_wait(turns, 1)
            first_up.start()
            first_up.wait_send()
            pl.semaphore_signal(turns, inc=1, device_id={"section": mate}, device_id_type=MESH)

        for t in range(1, TASKS):
            copy(outbox.at[t], inbox.at[t], K_UP + t, across).start()

        def flip(j, carry):
            value = a1[expert(j)].T
            a1[expert(j)] = value
            put(gbuf.at[j], (slice(None),), value)
            a2[expert(j)] = a2[expert(j)].T
            d_in[expert(j)] = d_in[expert(j)].T
            return carry

        lax.fori_loop(0, E, flip, 0)
        greet_ring()
        d_out[...] = jnp.zeros_like(d_out)
        acc[...] = jnp.zeros_like(acc)

    @pl.when(x == 1)
    def _():
        keep_mates()
        lax.fori_loop(0, E, keep_flipped, 0)
        for q in range(TASKS):

            @pl.when(s != q)
            def _():
                copy(smo, sm.at[q], K_SM + q, q).wait_recv()
                copy(tin_ref, ti.at[q], K_TI + q, q).wait_recv()

        def keep(k, t):
            return pltpu.make_async_copy((gbuf, kbuf)[k], kept.at[:, k * SPILL + t], local.at[4 + k])

        def keep_start(k, t):
            def one(j, carry):
                pltpu.make_async_copy((gbuf, kbuf)[k].at[j], kept.at[j, k * SPILL + t], local.at[4 + k]).start()
                return carry

            @pl.when(t < SPILL)
            def _():
                lax.fori_loop(0, E, one, 0)

        def gate_rows(t):
            return pl.ds(pl.multiple_of(t * GROWS, GROWS), GROWS)

        def enter(t):
            for k in range(2):
                cols = slice(k * (R // 2), (k + 1) * (R // 2))
                flipped = inbox[t, cols].T
                hi, lo = split(flipped)
                u_next[:D, cols] = hi
                u_next[D : 2 * D, cols] = hi
                u_next[2 * D :, cols] = lo
                acc[:, cols] = flipped
                yield
            logits = mm(wide(wg[gate_rows(t)]), u_next[...])
            cs_next[...] = logits
            yield
            u_n[t] = tall(inbox[t])
            yield
            _, r, mix, _, _ = gate_state(logits, 1, swapped)
            yield
            for j in range(E):
                gt_next[j] = over_selectors(mix * r[j], 1, jnp.add)
                yield

        def turn():
            u_t[...] = u_next[...]
            gt[...] = gt_next[...]
            cs[:GROWS] = cs_next[...]

        def all_of(pieces):
            for _ in pieces:
                pass

        for q in range(TASKS):
            tower_t[q] = wide(ti[q].T)
            tower_n[q] = wide(ti[q])
            out_cols[q] = jnp.broadcast_to(sm[q][:, :TOWER].T[:, 2:3], (TOWER, R))
        copy(outbox.at[0], inbox.at[0], K_UP, across).wait_recv()
        all_of(enter(0))
        turn()

        def task(t, carry):
            @pl.when(t > 0)
            def _():
                keep(0, 0).wait()

            def first(j, par):
                bb[par] = mm(pair(wt[j]), u_t[...])

            def activate(j, par, part_no):
                for tile in halves(H)[part_no]:
                    value, slope = gelu_pair(bb[par, tile])
                    a1[shifted(tile, j)] = value
                    a2[shifted(tile, j)] = slope
                    put(gbuf, (j, tile), value * gt[j])

            def finish(j, par):
                acc[...] += mm(pair(wt[E + j]), stack(gbuf[j]))

            weave(E, first, activate, finish)
            keep_start(0, t)

            second = acc[...]
            held[...] = second
            g, slope = gelu_pair(mm(tower_t[t], tall(second)))
            out_col = out_cols[t]
            here = sm[t, :, mine]
            logit = jnp.sum(g * out_col, axis=0, keepdims=True) + here[3:4]
            prob = jax.nn.sigmoid(logit)
            dlogit = here[1:2] * (prob - here[0:1])
            m = dlogit * out_col * slope
            dy = mm(tower_n[t], tall(m))
            s_t[...] = tall(dy)
            acc_b[...] = dy
            dy_kept[...] = dy
            tm[:TOWER] = m
            tm[TOWER:] = g * dlogit
            tp[t, TOWER : TOWER + 1] = prob
            tp[t, TOWER + 2 : TOWER + 3] = dlogit
            tp[t, TOWER + 3 :] = jnp.zeros((5, R), F32)

            @pl.when(t > 0)
            def _():
                keep(1, 0).wait()

            @pl.when(t == TASKS - 1)
            def _():
                for i in range(AHEAD):
                    fetch_start(i)

            after = jnp.minimum(t + 1, TASKS - 1)

            @pl.when(t < TASKS - 1)
            def _():
                copy(outbox.at[after], inbox.at[after], K_UP + after, across).wait_recv()

            def back(j, par):
                bb[par] = mm(pair(w_out[j]), s_t[...])

            def pull(j, par, part_no):
                total = jnp.zeros((8, R), F32)
                for tile in halves(H)[part_no]:
                    grad = bb[par, tile]
                    total = total + rows8(grad * a1[shifted(tile, j)])
                    put(kbuf, (j, tile), grad * a2[shifted(tile, j)] * gt[j])
                total = jnp.sum(total, axis=0, keepdims=True)
                if part_no == 0:
                    dgt[j, 0:1] = total
                else:
                    dgt[j, 0:1] += total

            def spread(j, par):
                acc_b[...] += mm(pair(w_in[j]), stack(kbuf[j]))

            def beside():
                s_n[t] = tall(dy_kept[...].T)
                yield
                yield from enter(after)
                flipped = tall(held[...].T)
                yield
                tp[t, :TOWER] = mm(wide(tm[:TOWER]), flipped)
                yield
                out_grad = jnp.sum(tm[TOWER:], axis=1, keepdims=True)
                out_row = jnp.broadcast_to(out_grad, (TOWER, TOWER)).T[0:1]
                tp[t, TOWER + 1 : TOWER + 2] = jnp.concatenate([out_row, jnp.zeros_like(out_row)], axis=1)
                yield

            gates_back = GateBackward(cs[:GROWS], 1, swapped)
            weave(E, back, pull, spread, beside(), lambda j: gates_back.add(j, dgt[j, 0:1]))
            dc = gates_back.result()
            outbox[t] = acc_b[...] + t_dot(wg[gate_rows(t)], dc)
            copy(outbox.at[t], inbox.at[t], K_DOWN + t, across).start()
            dcs[gate_rows(t)] = dc
            keep_start(1, t)
            turn()

            @pl.when(t != s)
            def _():
                copy(tp.at[t], tw.at[c], K_TW + c, t, K_TW + t).start()

            @pl.when(t == s)
            def _():
                tw[c] = tp[t]

            return carry

        lax.fori_loop(0, TASKS, task, 0)
        for q in range(TASKS):
            rows = slice(q * GROWS, (q + 1) * GROWS)
            dg[rows] = mm(wide(dcs[rows]), u_n[q])
        greet_ring()

    @pl.when(x == 1)
    def _():
        def one(i, carry):
            fetch(i).wait()

            @pl.when(i < E - AHEAD)
            def _():
                fetch_start(i + AHEAD)

            j = turn_of(i)
            slot_at = (i % (AHEAD + 1)) * 8
            for k, (grad, right, here) in enumerate(((d_out, s_n, gbuf), (d_in, u_n, kbuf))):
                left = [pair(wt[slot_at + k * SPILL + t]) for t in range(SPILL)] + [pair(here[j])]
                grad[expert(j)] = mm(jnp.concatenate(left, axis=1), right[...].reshape(3 * TASKS * R, D))

            @pl.when(i % 2 == 0)
            def _():
                for move in give(near(i // 2)):
                    move.start()

            @pl.when(i == 3)
            def _():
                merge(0, 0)
                ring_start()

            @pl.when((i % 2 == 1) & (i > 3))
            def _():
                merge((i - 3) // 2, 0)

            if n == HALF:

                @pl.when((i % 4 == 3) & (i > 3))
                def _():
                    reduce_step((i - 3) // 4, 0)

            return carry

        lax.fori_loop(0, E, one, 0)
        merge(HALF - 1, 0)
        if n != HALF:
            lax.fori_loop(1, 4, reduce_step, 0)

    @pl.when(x == 0)
    def _():
        def arrive(t, carry):
            copy(outbox.at[t], inbox.at[t], K_DOWN + t, across).wait_recv()
            acc[...] += inbox[t]

            def one(j, inner):
                gate = gt0[j, pl.ds(t, 1)]
                total = jnp.zeros((8, R), F32)
                for tile in rows_of(D):
                    dy = inbox[t, tile]
                    rows = pl.ds(pl.multiple_of(j * D + tile.start, TILE), TILE)
                    total = total + rows8(d_in[rows] * dy)
                    d_out[rows] += gate * dy
                dgt[j, pl.ds(t, 1)] = jnp.sum(total, axis=0, keepdims=True)
                return inner

            lax.fori_loop(0, E, one, 0)
            return carry

        lax.fori_loop(0, TASKS - 1, arrive, 0)
        last = TASKS - 1
        copy(outbox.at[last], inbox.at[last], K_DOWN + last, across).wait_recv()
        acc[...] += inbox[last]

        def one(i, inner):
            j = turn_of(i)
            gate = gt0[j, last : last + 1]
            total = jnp.zeros((8, R), F32)
            for tile in rows_of(D):
                dy = inbox[last, tile]
                rows = pl.ds(pl.multiple_of(j * D + tile.start, TILE), TILE)
                total = total + rows8(d_in[rows] * dy)
                put(kbuf.at[j], (tile,), d_out[rows] + gate * dy)
            dgt[j, last : last + 1] = jnp.sum(total, axis=0, keepdims=True)
            return inner

        def part_of(first, stop):
            lax.fori_loop(2 * first, 2 * stop, one, 0)

            def products(i, par):
                j = turn_of(2 * first + i)
                mixed = kbuf[j]
                bb[par] = mm(pair(w_out[j]), stack(mixed))
                right = jnp.concatenate([mixed[:, :R], mixed[:, :R], mixed[:, R:]], axis=1)
                d_out[expert(j)] = lax.dot_general(
                    pair(gbuf[j]), right, (((1,), (1,)), ((), ())), preferred_element_type=F32
                )

            def pull(i, par, part_no):
                j = turn_of(2 * first + i)
                for tile in halves(H)[part_no]:
                    kept_rows = pl.ds(pl.multiple_of(j * H + tile.start, TILE), TILE)
                    put(kp, (par, tile), bb[par, tile] * a2[kept_rows])

            def spread(i, par):
                j = turn_of(2 * first + i)
                acc[...] += mm(pair(w_in[j]), stack(kp[par]))
                d_in[expert(j)] = mm(pair(kp[par]), u_n[0])

            weave(2 * (stop - first), products, pull, spread)
            for k in range(first, stop):
                for move in give(near(k)):
                    move.start()

        part_of(0, 1)
        part_of(1, 2)
        merge(0, 0)
        ring_start()
        for k in range(2, HALF, 2):
            part_of(k, k + 2)
            lax.fori_loop(k - 1, k + 1, merge, 0)
            if n == HALF:
                reduce_step(k // 2, 0)
        merge(HALF - 1, 0)
        if n != HALF:
            lax.fori_loop(1, HALF // 2, reduce_step, 0)

    gates_own = pl.ds(pl.multiple_of(c * 2 * GROWS, 2 * GROWS), 2 * GROWS)
    gates_away = pl.ds(pl.multiple_of((1 - c) * 2 * GROWS, 2 * GROWS), 2 * GROWS)
    gain_row[...] = jnp.zeros_like(gain_row)

    @pl.when(x == 0)
    def _():
        gates_back = GateBackward(cs[...], TASKS, swapped)
        for j in range(E):
            gates_back.add(j, dgt[j, :TASKS])
        dc = gates_back.result()
        dpool = (acc[...] + t_dot(wg[:FROWS], dc)).T
        pre_rows = pre[...]
        rho = lax.rsqrt(jnp.mean(pre_rows * pre_rows, axis=1, keepdims=True) + NORM_EPS)
        scaled = dpool * gain_ref[...]
        dots = jnp.mean(scaled * pre_rows, axis=1, keepdims=True)
        dp[mine] = rho * scaled - pre_rows * (rho * rho * rho * dots)
        for k, sec in enumerate((mate, across, diag)):
            copy(dp.at[mine], dp.at[mine], K_DP + c, sec, K_DP + k).start()
        gain_row[0:1] = jnp.sum(dpool * pre_rows * rho, axis=0, keepdims=True)
        grad = mm(wide(dc), u_n[0])
        dg[: FROWS // 2] = grad[: FROWS // 2]
        dg[2 * GROWS : 2 * GROWS + FROWS // 2] = grad[FROWS // 2 :]

    gates_move = copy(dg.at[gates_away], gb, K_DG, mate)
    gates_move.start()

    lax.fori_loop(4, 6, reduce_step, 0)

    for half_no in range(2):

        @pl.when(s != half_no)
        def _():
            rows = pl.ds(half_no * R, R)
            copy(dp.at[rows], dp.at[rows], K_DP + half_no, half_no).wait_recv()

    for k in range(2):

        @pl.when(s != 2 + k)
        def _():
            copy(tp.at[0], tw.at[k], K_TW + k, s).wait_recv()

    gates_move.wait_recv()
    sb[:TOWER] = tw[0, :TOWER] + tw[1, :TOWER]
    sb[GATE_AT:MISC_AT] = dg[gates_own] + gb[...]
    sb[MISC_AT : MISC_AT + 1] = gain_row[0:1]
    sb[MISC_AT + 1 : MISC_AT + 3] = tw[0, TOWER + 1 : TOWER + 3] + tw[1, TOWER + 1 : TOWER + 3]
    for f in range(2):
        sb[MISC_AT + 3 + f : MISC_AT + 4 + f] = jnp.sum(xf[f] * dp[...], axis=0, keepdims=True)
    sb[MISC_AT + 5 : MISC_AT + 6] = smo[1:2, :R] + smo[1:2, R:]
    sb[MISC_AT + 6 :] = jnp.zeros((sb.shape[0] - MISC_AT - 6, D), F32)

    def block(q):
        return pl.ds(pl.multiple_of(q * small_rows, 8), small_rows)

    def scatter(i):
        to = (me + i) % n
        return pltpu.make_async_remote_copy(
            src_ref=sb.at[block(to)],
            dst_ref=sr.at[me],
            send_sem=sr_send.at[i],
            recv_sem=sr_recv.at[me],
            device_id={"dp": to},
            device_id_type=MESH,
        )

    def scattered(i):
        by = (me + i) % n
        return pltpu.make_async_remote_copy(
            src_ref=sb.at[block(me)],
            dst_ref=sr.at[by],
            send_sem=sr_send.at[i],
            recv_sem=sr_recv.at[by],
            device_id={"dp": by},
            device_id_type=MESH,
        )

    def spread_sum(i):
        return pltpu.make_async_remote_copy(
            src_ref=so,
            dst_ref=sa.at[block(me)],
            send_sem=sa_send.at[i],
            recv_sem=sa_recv.at[me],
            device_id={"dp": (me + i) % n},
            device_id_type=MESH,
        )

    def gathered(i):
        by = (me + i) % n
        return pltpu.make_async_remote_copy(
            src_ref=so,
            dst_ref=sa.at[block(by)],
            send_sem=sa_send.at[i],
            recv_sem=sa_recv.at[by],
            device_id={"dp": by},
            device_id_type=MESH,
        )

    def each(act):
        def one(i, carry):
            act(i)
            return carry

        lax.fori_loop(1, n, one, 0)

    each(lambda i: scatter(i).start())
    lax.fori_loop(6, n - 1, reduce_step, 0)
    last = n - 2
    for d, k in lanes:
        q = holds(d, n - 1)
        rs(d, k, last, a1.at[slot(d, k, last)]).wait_recv()
        a1[slot(d, k, last)] += rd[d, at(k, q)]
        ag(d, k, 0, a1.at[slot(d, k, last)], q).start()
        store(d, k, q, a1.at[slot(d, k, last)], 0).start()

    def gather_step(step, carry):
        for d, k in lanes:
            q = holds(d, step - 1)
            ag(d, k, step - 1, landed(d, k, q), q).wait_recv()
            ag(d, k, step, landed(d, k, q), q).start()
            store(d, k, q, landed(d, k, q), step).start()
        return carry

    so[...] = sb[block(me)]

    def take(i):
        scattered(i).wait_recv()
        so[...] += sr[(me + i) % n]

    each(take)
    sa[block(me)] = so[...]
    each(lambda i: spread_sum(i).start())
    lax.fori_loop(1, 3, gather_step, 0)
    each(lambda i: gathered(i).wait_recv())
    piece = sa.at[pl.ds(GATE_AT, KEPT)]
    for k, sec in enumerate((mate, across, diag)):
        copy(piece, sg.at[s], K_GO + s, sec, K_GO + k).start()
    sg[s] = sa[GATE_AT:SMALL]
    lax.fori_loop(3, 4, gather_step, 0)
    for sec in (mate, across, diag):
        copy(piece, sg.at[sec], K_GO + sec, sec).wait_recv()
    misc = KEPT - 8
    count = sum(sg[q, misc + 5 : misc + 6] for q in range(TASKS))
    scale = float(2 * R * n) / jnp.sum(count, axis=1, keepdims=True)

    o_scale[...] = jnp.broadcast_to(scale, o_scale.shape)

    for f in range(2):
        xf[f] = dp[...] * (scale * fw_ref[0, f])
        pltpu.make_async_copy(xf.at[f], o_ig.at[:, f], local.at[2 + f]).start()
    for k in range(2):
        o_pred[:, k * R : (k + 1) * R] = tw[k, TOWER : TOWER + 1]
    for f in range(2):
        o_fw[0, f] = jnp.sum(sa[MISC_AT + 3 + f : MISC_AT + 4 + f] * scale)
    o_bias[0, 0] = jnp.sum(sa[MISC_AT + 2 : MISC_AT + 3] * scale)
    o_gain[...] = (sg[0, misc : misc + 1] + sg[1, misc : misc + 1]) * scale
    o_tout[...] = sa[MISC_AT + 1 : MISC_AT + 2, :TOWER] * scale
    o_tin[...] = (sa[:TOWER] * scale).T

    def order(t, carry):
        for sel in range(SEL):
            for e in range(BITS + 1):
                row = t * (SEL * (BITS + 1)) + sel * (BITS + 1) + e
                at0 = (e * SEL + sel) * TASKS
                cut = FROWS // 2
                o_gate[0, pl.ds(row, 1)] = sg[at0 // cut, pl.ds(at0 % cut + t, 1)] * scale
                o_gate[1, pl.ds(row, 1)] = sg[2 + t // 2, pl.ds((t % 2) * GROWS + e * SEL + sel, 1)] * scale
        return carry

    lax.fori_loop(0, TASKS, order, 0)

    lax.fori_loop(4, n - 1, gather_step, 0)
    for d, k in lanes:
        q = holds(d, n - 2)
        ag(d, k, last, landed(d, k, q), q).wait_recv()
        store(d, k, q, landed(d, k, q), n - 1).start()

    def stored(step, carry):
        for d, k in lanes:
            store(d, k, 0, landed(d, k, 0), step).wait()
        return carry

    lax.fori_loop(0, n, stored, 0)

    def sent(step, carry):
        for d, k in lanes:
            rs(d, k, step, a1.at[slot(d, k, step)]).wait_send()
            ag(d, k, step, a1.at[slot(d, k, step)], 0).wait_send()
        return carry

    lax.fori_loop(0, n - 1, sent, 0)
    each(lambda i: scatter(i).wait_send())
    each(lambda i: spread_sum(i).wait_send())
    to_mate.wait_send()
    gates_move.wait_send()
    for e in range(HALF):
        for move in give(e):
            move.wait_send()
    for k in range(2):

        @pl.when(s != 2 + k)
        def _():
            copy(smo, sm.at[s], K_SM + s, 2 + k, K_SM + k).wait_send()
            copy(tin_ref, ti.at[s], K_TI + s, 2 + k, K_TI + k).wait_send()

    @pl.when(x == 0)
    def _():
        for t in range(1, TASKS):
            copy(outbox.at[t], inbox.at[t], K_UP + t, across).wait_send()
        for k, sec in enumerate((mate, across, diag)):
            copy(dp.at[mine], dp.at[mine], K_DP + c, sec, K_DP + k).wait_send()

    @pl.when(x == 1)
    def _():
        copy(pre2, pre1, K_P + 1, across).wait_send()
        for t in range(TASKS):
            copy(outbox.at[t], inbox.at[t], K_DOWN + t, across).wait_send()

            @pl.when(t != s)
            def _():
                copy(tp.at[t], tw.at[c], K_TW + c, t, K_TW + t).wait_send()

    for k, sec in enumerate((mate, across, diag)):
        copy(piece, sg.at[s], K_GO + s, sec, K_GO + k).wait_send()
    for f in range(2):
        pltpu.make_async_copy(xf.at[f], o_ig.at[:, f], local.at[2 + f]).wait()


def hand_over(count, scaled, scale_ref, *refs):
    held = refs[2 * count : 3 * count]
    sems = refs[-1]
    reads = [pltpu.make_async_copy(refs[k], held[k], sems.at[0, k]) for k in range(count)]
    writes = [pltpu.make_async_copy(held[k], refs[count + k], sems.at[1, k]) for k in range(count)]
    order = list(scaled) + [k for k in range(count) if k not in scaled]
    for k in order:
        reads[k].start()
    scale = scale_ref[0:1, 0:1]
    for k in order:
        reads[k].wait()
        if k in scaled:

            def one(i, carry):
                rows = pl.ds(pl.multiple_of(i * H, H), H)
                held[k][rows] = held[k][rows] * scale
                return carry

            lax.fori_loop(0, held[k].shape[0] // H, one, 0)
        writes[k].start()
    for move in writes:
        move.wait()


def body(
    field_inputs,
    field_weight,
    norm_gain,
    gate_weight,
    expert_in,
    expert_out,
    tower_in,
    tower_out,
    tower_bias,
    labels,
    source_ids,
    task_table,
):
    n = lax.axis_size("dp")
    rows = field_inputs.shape[0]
    half = rows // 2
    subs = 2
    small_rows = -(-SMALL // (8 * n)) * 8
    used = TASKS * SEL * (BITS + 1)

    vmem = pl.BlockSpec(memory_space=pltpu.VMEM)
    smem = pl.BlockSpec(memory_space=pltpu.SMEM)
    hbm = pl.BlockSpec(memory_space=pl.ANY)

    def bf(*shape):
        return pltpu.VMEM(shape, BF16)

    def f32(*shape):
        return pltpu.VMEM(shape, F32)

    def out(*shape):
        return jax.ShapeDtypeStruct(shape, F32)

    dma = pltpu.SemaphoreType.DMA
    *sums, scale, _ = pl.pallas_call(
        partial(kernel, n, subs, small_rows),
        out_shape=(
            out(1, rows),
            out(rows, 2, D),
            out(1, 2),
            out(1, D),
            out(2, used, D),
            out(HALF * H, D),
            out(HALF * H, D),
            out(D, TOWER),
            out(1, TOWER),
            out(1, 1),
            out(1, TOWER),
            jax.ShapeDtypeStruct((E, 2 * SPILL, H, 2 * half), BF16),
        ),
        in_specs=[hbm, smem, vmem, vmem, hbm, hbm, vmem, vmem, smem, vmem, vmem, smem],
        out_specs=(vmem, hbm, smem, vmem, vmem, hbm, hbm, vmem, vmem, smem, vmem, hbm),
        scratch_shapes=[
            bf(2 * E, H, 2 * D),
            bf(E, D, 2 * H),
            bf(E, H, 2 * D),
            f32(E * H, half),
            f32(E * H, half),
            f32(E * H, D),
            f32(E * H, D),
            bf(E, H, 2 * half),
            bf(E, H, 2 * half),
            bf(2, H, 2 * half),
            f32(2, HALF * H, D),
            f32(2, rows, D),
            f32(rows, D),
            f32(half, D),
            f32(half, D),
            f32(half, D),
            f32(half, D),
            f32(TASKS, D, half),
            f32(TASKS, D, half),
            bf(3 * D, half),
            bf(TASKS, 3 * half, D),
            bf(3 * D, half),
            bf(TASKS, 3 * half, D),
            f32(2, H, half),
            f32(D, half),
            f32(TASKS * GROWS, D),
            f32(E, 1, half),
            f32(E, TASKS, half),
            f32(FROWS, half),
            f32(E, TASKS, half),
            f32(TASKS * GROWS, D),
            f32(2 * GROWS, D),
            f32(TASKS, 8, rows),
            f32(8, rows),
            f32(TASKS, D, TOWER),
            f32(TASKS, TOWER + 8, D),
            f32(2, TOWER + 8, D),
            f32(rows, D),
            f32(8, D),
            f32(half, E * TASKS),
            bf(3 * D, half),
            f32(E, 1, half),
            f32(GROWS, half),
            f32(D, half),
            f32(D, half),
            bf(TASKS, TOWER, 3 * D),
            bf(TASKS, D, 3 * TOWER),
            f32(TASKS, TOWER, half),
            f32(TASKS * GROWS, half),
            f32(D, half),
            f32(2 * TOWER, half),
            f32(n * small_rows, D),
            f32(n, small_rows, D),
            f32(small_rows, D),
            f32(n * small_rows, D),
            f32(TASKS, KEPT, D),
            dma((K_COUNT,)),
            dma((K_COUNT,)),
            dma((6,)),
            dma((AHEAD + 1,)),
            pltpu.SemaphoreType.REGULAR,
            pltpu.SemaphoreType.REGULAR,
            dma((2, subs, n - 1)),
            dma((2, subs, n - 1)),
            dma((2, subs, n - 1)),
            dma((2, subs, n - 1)),
            dma((2, subs, n)),
            dma((n,)),
            dma((n,)),
            dma((n,)),
            dma((n,)),
        ],
        compiler_params=pltpu.CompilerParams(
            collective_id=0, has_side_effects=True, vmem_limit_bytes=64 * 1024 * 1024 - 65536
        ),
    )(
        field_inputs,
        field_weight.reshape(1, 2),
        norm_gain.reshape(1, D),
        gate_weight.swapaxes(1, 2),
        expert_in.reshape(HALF * H, D),
        expert_out.reshape(HALF * H, D),
        tower_in.reshape(D, TOWER),
        tower_out,
        tower_bias.reshape(1, 1),
        labels.reshape(1, rows),
        source_ids.reshape(1, rows),
        task_table.reshape(1, SOURCES),
    )
    pred, ig, fw, gain, gate, d_in, d_out, tin, tout, bias = pl.pallas_call(
        partial(hand_over, len(sums), (5, 6)),
        out_shape=tuple(jax.ShapeDtypeStruct(v.shape, v.dtype) for v in sums),
        in_specs=[vmem] + [hbm] * len(sums),
        out_specs=(hbm,) * len(sums),
        scratch_shapes=[pltpu.VMEM(v.shape, v.dtype) for v in sums] + [dma((2, len(sums)))],
        compiler_params=pltpu.CompilerParams(vmem_limit_bytes=64 * 1024 * 1024 - 65536),
    )(scale, *sums)
    return (
        pred.reshape(rows, 1),
        ig,
        fw.reshape(2),
        gain.reshape(D),
        gate.swapaxes(1, 2),
        d_in.reshape(HALF, D, H),
        d_out.reshape(HALF, H, D),
        tin.reshape(1, D, TOWER),
        tout,
        bias.reshape(1),
    )


def solution(mesh):
    in_specs = (
        P("dp", "section", None),
        P("section"),
        P(),
        P(),
        P("section", None, None),
        P("section", None, None),
        P("section", None, None),
        P("section", None),
        P("section"),
        P("dp", "section"),
        P("dp"),
        P(None, "section"),
    )
    out_specs = (
        P("dp", "section"),
        P("dp", "section", None),
        P("section"),
        P(),
        P(),
        P("section", None, None),
        P("section", None, None),
        P("section", None, None),
        P("section", None),
        P("section"),
    )
    return jax.shard_map(body, mesh=mesh, in_specs=in_specs, out_specs=out_specs, check_vma=False)
```

```python
from functools import partial

import jax
import jax.numpy as jnp
from jax import lax
from jax.experimental import pallas as pl
from jax.experimental.pallas import tpu as pltpu
from jax.sharding import PartitionSpec as P

D = 256
H = 256
E = 16
TASKS = 4
SEL = 4
BITS = 4
TOWER = 128
SOURCES = 32
HALF = E // 2
GROWS = 32
FROWS = 96

STEP_SLOPE = 0.6
ENTROPY_WEIGHT = 0.05
NORM_EPS = 1e-05
GELU_A = 0.7978845608028654
GELU_B = 0.044715

F32 = jnp.float32
BF16 = jnp.bfloat16
MESH = pl.DeviceIdType.MESH

K_W, K_P, K_SM, K_TI, K_UP, K_DOWN, K_TW, K_DG, K_DP, K_GO, K_DX = 0, 2, 4, 8, 12, 16, 20, 24, 25, 28, 32
K_COUNT = 48
TILE = 32
SPILL = TASKS - 1
AHEAD = 3

GATE_AT = TOWER
MISC_AT = GATE_AT + 2 * GROWS
SMALL = MISC_AT + 8
KEPT = SMALL - GATE_AT


def split(x):
    hi = x.astype(BF16)
    return hi, (x - hi.astype(F32)).astype(BF16)


def wide(x):
    hi, lo = split(x)
    return jnp.concatenate([hi, lo, hi], axis=1)


def tall(x):
    hi, lo = split(x)
    return jnp.concatenate([hi, hi, lo], axis=0)


def put(ref, at, x):
    k = x.shape[1]
    hi, lo = split(x)
    ref[*at, :k] = hi
    ref[*at, k:] = lo


def stack(x):
    k = x.shape[1] // 2
    return jnp.concatenate([x[:, :k], x[:, :k], x[:, k:]], axis=0)


def mm(a, b):
    return jnp.dot(a, b, preferred_element_type=F32)


def pair(x):
    k = x.shape[1] // 2
    return jnp.concatenate([x, x[:, :k]], axis=1)


def gelu_pair(x):
    x2 = x * x
    h = 0.5 + 0.5 * jnp.tanh(x * (GELU_A + (GELU_A * GELU_B) * x2))
    g = x * h
    slope = h + g * (1.0 - h) * (2.0 * GELU_A + (6.0 * GELU_A * GELU_B) * x2)
    return g, slope


def rows8(x):
    return jnp.sum(x.reshape(x.shape[0] // 8, 8, x.shape[1]), axis=0)


def over_selectors(v, groups, op):
    parts = [v[k * groups : (k + 1) * groups] for k in range(SEL)]
    return op(op(parts[0], parts[1]), op(parts[2], parts[3]))


def to_selectors(v):
    return jnp.concatenate([v] * SEL, axis=0)


def gate_state(c, groups, swapped):
    w = SEL * groups
    zs = [c[w * b : w * b + w] * STEP_SLOPE for b in range(BITS)]
    alpha = c[w * BITS : w * BITS + w]
    ups, downs, sig_p, sig_n = [], [], [], []
    for z in zs:
        e = jnp.exp(-jnp.abs(z))
        tail = jnp.log1p(e)
        ups.append(jnp.minimum(z, 0.0) - tail)
        downs.append(jnp.minimum(-z, 0.0) - tail)
        big = 1.0 / (1.0 + e)
        small = e * big
        sig_p.append(jnp.where(z >= 0.0, big, small))
        sig_n.append(jnp.where(z >= 0.0, small, big))
    last_on, last_off = ups[3], downs[3]
    ups[3], downs[3] = jnp.where(swapped, last_off, last_on), jnp.where(swapped, last_on, last_off)
    low = [(ups[0] if k & 1 else downs[0]) + (ups[1] if k & 2 else downs[1]) for k in range(4)]
    high = [(ups[2] if k & 1 else downs[2]) + (ups[3] if k & 2 else downs[3]) for k in range(4)]
    log_r = [low[j & 3] + high[j >> 2] for j in range(E)]
    r = [jnp.exp(v) for v in log_r]
    top = jnp.exp(alpha - to_selectors(over_selectors(alpha, groups, jnp.maximum)))
    mix = top / to_selectors(over_selectors(top, groups, jnp.add))
    return log_r, r, mix, sig_p, sig_n


def gate_forward(c, groups, swapped):
    _, r, mix, _, _ = gate_state(c, groups, swapped)
    return [over_selectors(mix * v, groups, jnp.add) for v in r]


class GateBackward:
    def __init__(self, c, groups, swapped):
        self.log_r, self.r, self.mix, self.sig_p, self.sig_n = gate_state(c, groups, swapped)
        self.swapped = swapped
        self.groups = groups
        self.total = jnp.zeros_like(self.mix)
        self.on = [jnp.zeros_like(self.mix) for _ in range(BITS)]
        self.off = [jnp.zeros_like(self.mix) for _ in range(BITS)]

    def add(self, j, dg):
        dg = to_selectors(dg)
        self.total = self.total + dg * self.r[j]
        dlog = self.r[j] * (self.mix * dg - ENTROPY_WEIGHT * (self.log_r[j] + 1.0))
        for b in range(BITS):
            if j >> b & 1:
                self.on[b] = self.on[b] + dlog
            else:
                self.off[b] = self.off[b] + dlog

    def result(self):
        mix, groups = self.mix, self.groups
        dalpha = mix * (self.total - to_selectors(over_selectors(mix * self.total, groups, jnp.add)))
        on, off = self.on[3], self.off[3]
        self.on[3], self.off[3] = jnp.where(self.swapped, off, on), jnp.where(self.swapped, on, off)
        dz = [STEP_SLOPE * (self.on[b] * self.sig_n[b] - self.off[b] * self.sig_p[b]) for b in range(BITS)]
        used = SEL * (BITS + 1) * groups
        pad = jnp.zeros(((-used) % GROWS, mix.shape[1]), F32)
        return jnp.concatenate(dz + [dalpha, pad], axis=0)


def t_dot(a, b):
    ah, al = split(a)
    left = jnp.concatenate([ah, al, ah], axis=0)
    return lax.dot_general(left, tall(b), (((0,), (0,)), ((), ())), preferred_element_type=F32)


def weave(count, first, middle, last, extra=(), after=None):
    extra = iter(extra)
    for step in range(count + 2):
        if step < count:
            first(step, step % 2)
        next(extra, None)
        if 0 <= step - 1 < count:
            middle(step - 1, (step - 1) % 2, 0)
        next(extra, None)
        if step >= 2:
            last(step - 2, step % 2)
        next(extra, None)
        if 0 <= step - 1 < count:
            middle(step - 1, (step - 1) % 2, 1)
            if after is not None:
                after(step - 1)
        next(extra, None)
    for _ in extra:
        pass


def halves(size):
    tiles = [slice(a, a + TILE) for a in range(0, size, TILE)]
    return tiles[: len(tiles) // 2], tiles[len(tiles) // 2 :]


def kernel(
    n,
    subs,
    small_rows,
    x_ref,
    fw_ref,
    gain_ref,
    gate_ref,
    win_ref,
    wout_ref,
    tin_ref,
    tout_ref,
    tbias_ref,
    labels_ref,
    ids_ref,
    table_ref,
    o_pred,
    o_ig,
    o_fw,
    o_gain,
    o_gate,
    o_in,
    o_out,
    o_tin,
    o_tout,
    o_bias,
    o_scale,
    kept,
    wt,
    w_in,
    w_out,
    a1,
    a2,
    d_in,
    d_out,
    gbuf,
    kbuf,
    kp,
    rd,
    xf,
    part,
    pre0,
    pre1,
    pre2,
    pre,
    inbox,
    outbox,
    u_t,
    u_n,
    s_t,
    s_n,
    bb,
    acc,
    wg,
    gt,
    gt0,
    cs,
    dgt,
    dg,
    gb,
    sm,
    smo,
    ti,
    tp,
    tw,
    dp,
    gain_row,
    columns,
    u_next,
    gt_next,
    cs_next,
    acc_b,
    dy_kept,
    tower_t,
    tower_n,
    out_cols,
    dcs,
    held,
    tm,
    sb,
    sr,
    so,
    sa,
    sg,
    send,
    recv,
    local,
    fetch_sem,
    ready,
    turns,
    rs_send,
    rs_recv,
    ag_send,
    ag_recv,
    store_sem,
    sr_send,
    sr_recv,
    sa_send,
    sa_recv,
):
    s = lax.axis_index("section")
    x = s // 2
    c = s % 2
    mate = s + 1 - 2 * c
    across = s + 2 - 4 * x
    diag = 3 - s
    R = part.shape[0] // 2
    mine = pl.ds(pl.multiple_of(c * R, R), R)
    theirs = pl.ds(pl.multiple_of((1 - c) * R, R), R)

    me = lax.axis_index("dp")
    odd = me % 2
    p = (1 - odd) * (me // 2) + odd * (n - 1 - me // 2)

    def ring_id(q):
        far = q // (n // 2)
        return (1 - far) * 2 * q + far * (2 * (n - 1 - q) + 1)

    nbr = [ring_id((p + 1) % n), ring_id((p + n - 1) % n)]

    barrier = pltpu.get_barrier_semaphore()
    for sec in (mate, across, diag):
        pl.semaphore_signal(barrier, inc=1, device_id={"section": sec}, device_id_type=MESH)

    def greet(i, carry):
        pl.semaphore_signal(barrier, inc=1, device_id={"dp": (me + i) % n}, device_id_type=MESH)
        return carry

    lax.fori_loop(1, n, greet, 0)
    fields = [pltpu.make_async_copy(x_ref.at[:, f], xf.at[f], local.at[2 + f]) for f in range(2)]
    for f in fields:
        f.start()
    own = pl.ds(0, HALF * H)
    mates = pl.ds(HALF * H, HALF * H)
    swapped = c == 1
    own_in = pltpu.make_async_copy(win_ref, d_in.at[own], local.at[0])
    own_out = pltpu.make_async_copy(wout_ref, d_out.at[own], local.at[1])
    own_in.start()
    own_out.start()
    pl.semaphore_wait(barrier, 3 + n - 1)

    def copy(src, dst, k, sec, ks=None):
        return pltpu.make_async_remote_copy(
            src_ref=src,
            dst_ref=dst,
            send_sem=send.at[k if ks is None else ks],
            recv_sem=recv.at[k],
            device_id={"section": sec},
            device_id_type=MESH,
        )

    def expert(j, count=1):
        return pl.ds(pl.multiple_of(j * H, H), count * H)

    for f in fields:
        f.wait()
    part[...] = xf[0] * fw_ref[0, 0] + xf[1] * fw_ref[0, 1]
    to_mate = copy(part.at[theirs], pre0, K_P, mate)
    to_mate.start()
    swap_in = copy(win_ref, d_in.at[mates], K_W, mate)
    swap_out = copy(wout_ref, d_out.at[mates], K_W + 1, mate)
    swap_in.start()
    swap_out.start()
    own_in.wait()
    own_out.wait()

    ids = ids_ref[...]
    mask = jnp.zeros(ids.shape, F32)
    for q in range(SOURCES):
        mask = mask + jnp.where(ids == q, table_ref[0, q].astype(F32), 0.0)
    smo[...] = jnp.zeros_like(smo)
    smo[0:1] = labels_ref[...]
    smo[1:2] = mask
    smo[2:3, :TOWER] = tout_ref[...]
    smo[3:4] = jnp.zeros((1, 2 * R), F32) + tbias_ref[0, 0]
    for k in range(2):

        @pl.when(s != 2 + k)
        def _():
            copy(smo, sm.at[s], K_SM + s, 2 + k, K_SM + k).start()
            copy(tin_ref, ti.at[s], K_TI + s, 2 + k, K_TI + k).start()

    to_mate.wait_recv()

    @pl.when(x == 1)
    def _():
        pre2[...] = part[mine] + pre0[...]
        copy(pre2, pre1, K_P + 1, across).start()
        sm[s] = smo[...]
        ti[s] = tin_ref[...]

    wg[...] = jnp.zeros_like(wg)

    @pl.when(x == 0)
    def _():
        def order(t, carry):
            for sel in range(SEL):
                for e in range(BITS + 1):
                    row = t * (SEL * (BITS + 1)) + sel * (BITS + 1) + e
                    wg[pl.ds((e * SEL + sel) * TASKS + t, 1)] = gate_ref[0, pl.ds(row, 1)]
            return carry

        lax.fori_loop(0, TASKS, order, 0)

    @pl.when(x == 1)
    def _():
        def order(t, carry):
            for sel in range(SEL):
                for e in range(BITS + 1):
                    row = t * (SEL * (BITS + 1)) + sel * (BITS + 1) + e
                    wg[pl.ds(t * GROWS + e * SEL + sel, 1)] = gate_ref[1, pl.ds(row, 1)]
            return carry

        lax.fori_loop(0, TASKS, order, 0)

    def keep_plain(e, carry):
        put(w_in.at[e], (slice(None),), d_in[expert(e)])
        put(w_out.at[e], (slice(None),), d_out[expert(e)])
        return carry

    def keep_flipped(e, carry):
        put(wt.at[e], (slice(None),), d_in[expert(e)].T)
        put(wt.at[E + e], (slice(None),), d_out[expert(e)].T)
        return carry

    def keep_both(e, carry):
        keep_plain(e, carry)
        return keep_flipped(e, carry)

    def mates_arrive():
        swap_in.wait()
        swap_out.wait()

    def rows_of(size):
        return [slice(a, a + TILE) for a in range(0, size, TILE)]

    def shifted(tile, e):
        return slice(e * H + tile.start, e * H + tile.stop)

    chunk = HALF * H // n
    sub = chunk // subs
    lanes = [(d, k) for d in range(2) for k in range(subs)]

    def at(k, q):
        return pl.ds(pl.multiple_of(q * chunk + k * sub, 8), sub)

    def holds(d, step):
        return (p + n - step) % n if d == 0 else (p + step) % n

    def slot(d, k, step):
        return pl.ds(pl.multiple_of(((d * subs + k) * (n - 1) + step) * sub, 8), sub)

    def rs(d, k, step, src):
        return pltpu.make_async_remote_copy(
            src_ref=src,
            dst_ref=a1.at[slot(d, k, step)],
            send_sem=rs_send.at[d, k, step],
            recv_sem=rs_recv.at[d, k, step],
            device_id={"dp": nbr[d]},
            device_id_type=MESH,
        )

    results = (o_in, o_out)

    def landed(d, k, q):
        return a2.at[pl.ds(pl.multiple_of(d * HALF * H + q * chunk + k * sub, 8), sub)]

    def store(d, k, q, src, step):
        return pltpu.make_async_copy(src, results[d].at[at(k, q)], store_sem.at[d, k, step])

    def ag(d, k, step, src, q):
        return pltpu.make_async_remote_copy(
            src_ref=src,
            dst_ref=landed(d, k, q),
            send_sem=ag_send.at[d, k, step],
            recv_sem=ag_recv.at[d, k, step],
            device_id={"dp": nbr[d]},
            device_id_type=MESH,
        )

    def give(e):
        j = HALF + e
        return (
            copy(d_in.at[expert(j)], rd.at[0, expert(e)], K_DX + e, mate),
            copy(d_out.at[expert(j)], rd.at[1, expert(e)], K_DX + HALF + e, mate),
        )

    start_at = p * chunk // H

    def near(k):
        return (start_at + HALF + ((k + 1) // 2) * (1 - 2 * (k % 2))) % HALF

    def turn_of(i):
        own_turn = i % 2
        return (1 - own_turn) * HALF + near(i // 2)

    def fetch(i):
        at = pl.ds((i % (AHEAD + 1)) * 8, 2 * SPILL)
        return pltpu.make_async_copy(kept.at[turn_of(i)], wt.at[at], fetch_sem.at[i % (AHEAD + 1)])

    def fetch_start(i):
        for k in range(2 * SPILL):
            slab = (i % (AHEAD + 1)) * 8 + k
            pltpu.make_async_copy(
                kept.at[turn_of(i), k], wt.at[slab], fetch_sem.at[i % (AHEAD + 1)]
            ).start()

    def greet_ring():
        for dev in nbr:
            pl.semaphore_signal(ready, inc=1, device_id={"dp": dev}, device_id_type=MESH)

    def merge(k, carry):
        e = near(k)
        for move in give(e):
            move.wait_recv()
        rows = expert(e)
        rd[0, rows] = (rd[0, rows] + d_in[rows]).T
        rd[1, rows] += d_out[rows]
        return carry

    def ring_start():
        pl.semaphore_wait(ready, 2)
        for d, k in lanes:
            rs(d, k, 0, rd.at[d, at(k, holds(d, 0))]).start()

    def reduce_step(step, carry):
        for d, k in lanes:
            rs(d, k, step - 1, a1.at[slot(d, k, step - 1)]).wait_recv()
            a1[slot(d, k, step - 1)] += rd[d, at(k, holds(d, step))]
            rs(d, k, step, a1.at[slot(d, k, step - 1)]).start()
        return carry

    @pl.when(x == 0)
    def _():
        lax.fori_loop(0, HALF, keep_plain, 0)
        copy(pre2, pre1, K_P + 1, across).wait_recv()
        pre_rows = part[mine] + pre0[...] + pre1[...]
        pre[...] = pre_rows
        rho = lax.rsqrt(jnp.mean(pre_rows * pre_rows, axis=1, keepdims=True) + NORM_EPS)
        pooled = pre_rows * rho * gain_ref[...]
        acc[...] = pooled
        u_n[0] = tall(pooled)
        u_t[...] = tall(pooled.T)
        logits = mm(wide(wg[:FROWS]), u_t[...])
        cs[...] = logits
        gates = gate_forward(logits, TASKS, swapped)
        for j, g in enumerate(gates):
            gt0[j] = g

        def forward(base):
            def first(i, par):
                left = jnp.concatenate([u_n[0, :R], u_n[0, 2 * R :], u_n[0, :R]], axis=1)
                bb[par] = mm(left, stack(w_in[base + i]))

            def activate(i, par, part_no):
                for tile in halves(R)[part_no]:
                    value, slope = gelu_pair(bb[par, tile])
                    a1[shifted(tile, base + i)] = value
                    a2[shifted(tile, base + i)] = slope
                    put(gbuf, (base + i, tile), value)

            def finish(i, par):
                d_in[expert(base + i)] = mm(pair(gbuf[base + i]), stack(w_out[base + i]))

            weave(HALF, first, activate, finish)

        forward(0)
        mates_arrive()
        lax.fori_loop(HALF, E, keep_plain, 0)
        forward(HALF)
        columns[...] = jnp.concatenate(gates, axis=0).T

        for t in range(TASKS):

            def mix(i, carry):
                tile = pl.ds(pl.multiple_of(i * TILE, TILE), TILE)
                cols = columns[tile]
                total = acc[tile]
                for j in range(E):
                    rows = pl.ds(pl.multiple_of(j * R + i * TILE, TILE), TILE)
                    total = total + cols[:, j * TASKS + t : j * TASKS + t + 1] * d_in[rows]
                outbox[t, tile] = total
                return carry

            lax.fori_loop(0, R // TILE, mix, 0)

            @pl.when(c == 0)
            def _():
                if t == 0:
                    copy(outbox.at[t], inbox.at[t], K_UP + t, across).start()

        first_up = copy(outbox.at[0], inbox.at[0], K_UP, across)

        @pl.when(c == 0)
        def _():
            first_up.wait_send()
            pl.semaphore_signal(turns, inc=1, device_id={"section": mate}, device_id_type=MESH)
            pl.semaphore_wait(turns, 1)

        @pl.when(c == 1)
        def _():
            pl.semaphore_wait(turns, 1)
            first_up.start()
            first_up.wait_send()
            pl.semaphore_signal(turns, inc=1, device_id={"section": mate}, device_id_type=MESH)

        for t in range(1, TASKS):
            copy(outbox.at[t], inbox.at[t], K_UP + t, across).start()

        def flip(j, carry):
            value = a1[expert(j)].T
            a1[expert(j)] = value
            put(gbuf.at[j], (slice(None),), value)
            a2[expert(j)] = a2[expert(j)].T
            d_in[expert(j)] = d_in[expert(j)].T
            return carry

        lax.fori_loop(0, E, flip, 0)
        greet_ring()
        d_out[...] = jnp.zeros_like(d_out)
        acc[...] = jnp.zeros_like(acc)

    @pl.when(x == 1)
    def _():
        for q in range(TASKS):

            @pl.when(s != q)
            def _():
                copy(smo, sm.at[q], K_SM + q, q).wait_recv()
                copy(tin_ref, ti.at[q], K_TI + q, q).wait_recv()

        for q in range(TASKS):
            tower_t[q] = wide(ti[q].T)
            tower_n[q] = wide(ti[q])
            out_cols[q] = jnp.broadcast_to(sm[q][:, :TOWER].T[:, 2:3], (TOWER, R))
        lax.fori_loop(0, HALF, keep_both, 0)
        mates_arrive()
        lax.fori_loop(HALF, E, keep_both, 0)

        def keep(k, t):
            return pltpu.make_async_copy((gbuf, kbuf)[k], kept.at[:, k * SPILL + t], local.at[4 + k])

        def keep_start(k, t):
            def one(j, carry):
                pltpu.make_async_copy((gbuf, kbuf)[k].at[j], kept.at[j, k * SPILL + t], local.at[4 + k]).start()
                return carry

            @pl.when(t < SPILL)
            def _():
                lax.fori_loop(0, E, one, 0)

        def gate_rows(t):
            return pl.ds(pl.multiple_of(t * GROWS, GROWS), GROWS)

        def enter(t):
            for k in range(2):
                cols = slice(k * (R // 2), (k + 1) * (R // 2))
                flipped = inbox[t, cols].T
                hi, lo = split(flipped)
                u_next[:D, cols] = hi
                u_next[D : 2 * D, cols] = hi
                u_next[2 * D :, cols] = lo
                acc[:, cols] = flipped
                yield
            logits = mm(wide(wg[gate_rows(t)]), u_next[...])
            cs_next[...] = logits
            yield
            u_n[t] = tall(inbox[t])
            yield
            _, r, mix, _, _ = gate_state(logits, 1, swapped)
            yield
            for j in range(E):
                gt_next[j] = over_selectors(mix * r[j], 1, jnp.add)
                yield

        def turn():
            u_t[...] = u_next[...]
            gt[...] = gt_next[...]
            cs[:GROWS] = cs_next[...]

        def all_of(pieces):
            for _ in pieces:
                pass

        copy(outbox.at[0], inbox.at[0], K_UP, across).wait_recv()
        all_of(enter(0))
        turn()

        def task(t, carry):
            @pl.when(t > 0)
            def _():
                keep(0, 0).wait()

            def first(j, par):
                bb[par] = mm(pair(wt[j]), u_t[...])

            def activate(j, par, part_no):
                for tile in halves(H)[part_no]:
                    value, slope = gelu_pair(bb[par, tile])
                    a1[shifted(tile, j)] = value
                    a2[shifted(tile, j)] = slope
                    put(gbuf, (j, tile), value * gt[j])

            def finish(j, par):
                acc[...] += mm(pair(wt[E + j]), stack(gbuf[j]))

            weave(E, first, activate, finish)
            keep_start(0, t)

            second = acc[...]
            held[...] = second
            g, slope = gelu_pair(mm(tower_t[t], tall(second)))
            out_col = out_cols[t]
            here = sm[t, :, mine]
            logit = jnp.sum(g * out_col, axis=0, keepdims=True) + here[3:4]
            prob = jax.nn.sigmoid(logit)
            dlogit = here[1:2] * (prob - here[0:1])
            m = dlogit * out_col * slope
            dy = mm(tower_n[t], tall(m))
            s_t[...] = tall(dy)
            acc_b[...] = dy
            dy_kept[...] = dy
            tm[:TOWER] = m
            tm[TOWER:] = g * dlogit
            tp[t, TOWER : TOWER + 1] = prob
            tp[t, TOWER + 2 : TOWER + 3] = dlogit
            tp[t, TOWER + 3 :] = jnp.zeros((5, R), F32)

            @pl.when(t > 0)
            def _():
                keep(1, 0).wait()

            @pl.when(t == TASKS - 1)
            def _():
                for i in range(AHEAD):
                    fetch_start(i)

            after = jnp.minimum(t + 1, TASKS - 1)

            @pl.when(t < TASKS - 1)
            def _():
                copy(outbox.at[after], inbox.at[after], K_UP + after, across).wait_recv()

            def back(j, par):
                bb[par] = mm(pair(w_out[j]), s_t[...])

            def pull(j, par, part_no):
                total = jnp.zeros((8, R), F32)
                for tile in halves(H)[part_no]:
                    grad = bb[par, tile]
                    total = total + rows8(grad * a1[shifted(tile, j)])
                    put(kbuf, (j, tile), grad * a2[shifted(tile, j)] * gt[j])
                total = jnp.sum(total, axis=0, keepdims=True)
                if part_no == 0:
                    dgt[j, 0:1] = total
                else:
                    dgt[j, 0:1] += total

            def spread(j, par):
                acc_b[...] += mm(pair(w_in[j]), stack(kbuf[j]))

            def beside():
                s_n[t] = tall(dy_kept[...].T)
                yield
                yield from enter(after)
                flipped = tall(held[...].T)
                yield
                tp[t, :TOWER] = mm(wide(tm[:TOWER]), flipped)
                yield
                out_grad = jnp.sum(tm[TOWER:], axis=1, keepdims=True)
                out_row = jnp.broadcast_to(out_grad, (TOWER, TOWER)).T[0:1]
                tp[t, TOWER + 1 : TOWER + 2] = jnp.concatenate([out_row, jnp.zeros_like(out_row)], axis=1)
                yield

            gates_back = GateBackward(cs[:GROWS], 1, swapped)
            weave(E, back, pull, spread, beside(), lambda j: gates_back.add(j, dgt[j, 0:1]))
            dc = gates_back.result()
            outbox[t] = acc_b[...] + t_dot(wg[gate_rows(t)], dc)
            copy(outbox.at[t], inbox.at[t], K_DOWN + t, across).start()
            dcs[gate_rows(t)] = dc
            keep_start(1, t)
            turn()

            @pl.when(t != s)
            def _():
                copy(tp.at[t], tw.at[c], K_TW + c, t, K_TW + t).start()

            @pl.when(t == s)
            def _():
                tw[c] = tp[t]

            return carry

        lax.fori_loop(0, TASKS, task, 0)
        for q in range(TASKS):
            rows = slice(q * GROWS, (q + 1) * GROWS)
            dg[rows] = mm(wide(dcs[rows]), u_n[q])
        greet_ring()

    @pl.when(x == 1)
    def _():
        def one(i, carry):
            fetch(i).wait()

            @pl.when(i < E - AHEAD)
            def _():
                fetch_start(i + AHEAD)

            j = turn_of(i)
            slot_at = (i % (AHEAD + 1)) * 8
            for k, (grad, right, here) in enumerate(((d_out, s_n, gbuf), (d_in, u_n, kbuf))):
                left = [pair(wt[slot_at + k * SPILL + t]) for t in range(SPILL)] + [pair(here[j])]
                grad[expert(j)] = mm(jnp.concatenate(left, axis=1), right[...].reshape(3 * TASKS * R, D))

            @pl.when(i % 2 == 0)
            def _():
                for move in give(near(i // 2)):
                    move.start()

            @pl.when(i == 3)
            def _():
                merge(0, 0)
                ring_start()

            @pl.when((i % 2 == 1) & (i > 3))
            def _():
                merge((i - 3) // 2, 0)

            if n == HALF:

                @pl.when((i % 4 == 3) & (i > 3))
                def _():
                    reduce_step((i - 3) // 4, 0)

            return carry

        lax.fori_loop(0, E, one, 0)
        merge(HALF - 1, 0)
        if n != HALF:
            lax.fori_loop(1, 4, reduce_step, 0)

    @pl.when(x == 0)
    def _():
        def arrive(t, carry):
            copy(outbox.at[t], inbox.at[t], K_DOWN + t, across).wait_recv()
            acc[...] += inbox[t]

            def one(j, inner):
                gate = gt0[j, pl.ds(t, 1)]
                total = jnp.zeros((8, R), F32)
                for tile in rows_of(D):
                    dy = inbox[t, tile]
                    rows = pl.ds(pl.multiple_of(j * D + tile.start, TILE), TILE)
                    total = total + rows8(d_in[rows] * dy)
                    d_out[rows] += gate * dy
                dgt[j, pl.ds(t, 1)] = jnp.sum(total, axis=0, keepdims=True)
                return inner

            lax.fori_loop(0, E, one, 0)
            return carry

        lax.fori_loop(0, TASKS - 1, arrive, 0)
        last = TASKS - 1
        copy(outbox.at[last], inbox.at[last], K_DOWN + last, across).wait_recv()
        acc[...] += inbox[last]

        def one(i, inner):
            j = turn_of(i)
            gate = gt0[j, last : last + 1]
            total = jnp.zeros((8, R), F32)
            for tile in rows_of(D):
                dy = inbox[last, tile]
                rows = pl.ds(pl.multiple_of(j * D + tile.start, TILE), TILE)
                total = total + rows8(d_in[rows] * dy)
                put(kbuf.at[j], (tile,), d_out[rows] + gate * dy)
            dgt[j, last : last + 1] = jnp.sum(total, axis=0, keepdims=True)
            return inner

        def part_of(first, stop):
            lax.fori_loop(2 * first, 2 * stop, one, 0)

            def products(i, par):
                j = turn_of(2 * first + i)
                mixed = kbuf[j]
                bb[par] = mm(pair(w_out[j]), stack(mixed))
                right = jnp.concatenate([mixed[:, :R], mixed[:, :R], mixed[:, R:]], axis=1)
                d_out[expert(j)] = lax.dot_general(
                    pair(gbuf[j]), right, (((1,), (1,)), ((), ())), preferred_element_type=F32
                )

            def pull(i, par, part_no):
                j = turn_of(2 * first + i)
                for tile in halves(H)[part_no]:
                    kept_rows = pl.ds(pl.multiple_of(j * H + tile.start, TILE), TILE)
                    put(kp, (par, tile), bb[par, tile] * a2[kept_rows])

            def spread(i, par):
                j = turn_of(2 * first + i)
                acc[...] += mm(pair(w_in[j]), stack(kp[par]))
                d_in[expert(j)] = mm(pair(kp[par]), u_n[0])

            weave(2 * (stop - first), products, pull, spread)
            for k in range(first, stop):
                for move in give(near(k)):
                    move.start()

        part_of(0, 1)
        part_of(1, 2)
        merge(0, 0)
        ring_start()
        for k in range(2, HALF, 2):
            part_of(k, k + 2)
            lax.fori_loop(k - 1, k + 1, merge, 0)
            if n == HALF:
                reduce_step(k // 2, 0)
        merge(HALF - 1, 0)
        if n != HALF:
            lax.fori_loop(1, HALF // 2, reduce_step, 0)

    gates_own = pl.ds(pl.multiple_of(c * 2 * GROWS, 2 * GROWS), 2 * GROWS)
    gates_away = pl.ds(pl.multiple_of((1 - c) * 2 * GROWS, 2 * GROWS), 2 * GROWS)
    gain_row[...] = jnp.zeros_like(gain_row)

    @pl.when(x == 0)
    def _():
        gates_back = GateBackward(cs[...], TASKS, swapped)
        for j in range(E):
            gates_back.add(j, dgt[j, :TASKS])
        dc = gates_back.result()
        dpool = (acc[...] + t_dot(wg[:FROWS], dc)).T
        pre_rows = pre[...]
        rho = lax.rsqrt(jnp.mean(pre_rows * pre_rows, axis=1, keepdims=True) + NORM_EPS)
        scaled = dpool * gain_ref[...]
        dots = jnp.mean(scaled * pre_rows, axis=1, keepdims=True)
        dp[mine] = rho * scaled - pre_rows * (rho * rho * rho * dots)
        for k, sec in enumerate((mate, across, diag)):
            copy(dp.at[mine], dp.at[mine], K_DP + c, sec, K_DP + k).start()
        gain_row[0:1] = jnp.sum(dpool * pre_rows * rho, axis=0, keepdims=True)
        grad = mm(wide(dc), u_n[0])
        dg[: FROWS // 2] = grad[: FROWS // 2]
        dg[2 * GROWS : 2 * GROWS + FROWS // 2] = grad[FROWS // 2 :]

    gates_move = copy(dg.at[gates_away], gb, K_DG, mate)
    gates_move.start()

    lax.fori_loop(4, 6, reduce_step, 0)

    for half_no in range(2):

        @pl.when(s != half_no)
        def _():
            rows = pl.ds(half_no * R, R)
            copy(dp.at[rows], dp.at[rows], K_DP + half_no, half_no).wait_recv()

    for k in range(2):

        @pl.when(s != 2 + k)
        def _():
            copy(tp.at[0], tw.at[k], K_TW + k, s).wait_recv()

    gates_move.wait_recv()
    sb[:TOWER] = tw[0, :TOWER] + tw[1, :TOWER]
    sb[GATE_AT:MISC_AT] = dg[gates_own] + gb[...]
    sb[MISC_AT : MISC_AT + 1] = gain_row[0:1]
    sb[MISC_AT + 1 : MISC_AT + 3] = tw[0, TOWER + 1 : TOWER + 3] + tw[1, TOWER + 1 : TOWER + 3]
    for f in range(2):
        sb[MISC_AT + 3 + f : MISC_AT + 4 + f] = jnp.sum(xf[f] * dp[...], axis=0, keepdims=True)
    sb[MISC_AT + 5 : MISC_AT + 6] = smo[1:2, :R] + smo[1:2, R:]
    sb[MISC_AT + 6 :] = jnp.zeros((sb.shape[0] - MISC_AT - 6, D), F32)

    def block(q):
        return pl.ds(pl.multiple_of(q * small_rows, 8), small_rows)

    def scatter(i):
        to = (me + i) % n
        return pltpu.make_async_remote_copy(
            src_ref=sb.at[block(to)],
            dst_ref=sr.at[me],
            send_sem=sr_send.at[i],
            recv_sem=sr_recv.at[me],
            device_id={"dp": to},
            device_id_type=MESH,
        )

    def scattered(i):
        by = (me + i) % n
        return pltpu.make_async_remote_copy(
            src_ref=sb.at[block(me)],
            dst_ref=sr.at[by],
            send_sem=sr_send.at[i],
            recv_sem=sr_recv.at[by],
            device_id={"dp": by},
            device_id_type=MESH,
        )

    def spread_sum(i):
        return pltpu.make_async_remote_copy(
            src_ref=so,
            dst_ref=sa.at[block(me)],
            send_sem=sa_send.at[i],
            recv_sem=sa_recv.at[me],
            device_id={"dp": (me + i) % n},
            device_id_type=MESH,
        )

    def gathered(i):
        by = (me + i) % n
        return pltpu.make_async_remote_copy(
            src_ref=so,
            dst_ref=sa.at[block(by)],
            send_sem=sa_send.at[i],
            recv_sem=sa_recv.at[by],
            device_id={"dp": by},
            device_id_type=MESH,
        )

    def each(act):
        def one(i, carry):
            act(i)
            return carry

        lax.fori_loop(1, n, one, 0)

    each(lambda i: scatter(i).start())
    lax.fori_loop(6, n - 1, reduce_step, 0)
    last = n - 2
    for d, k in lanes:
        q = holds(d, n - 1)
        rs(d, k, last, a1.at[slot(d, k, last)]).wait_recv()
        a1[slot(d, k, last)] += rd[d, at(k, q)]
        ag(d, k, 0, a1.at[slot(d, k, last)], q).start()
        store(d, k, q, a1.at[slot(d, k, last)], 0).start()

    def gather_step(step, carry):
        for d, k in lanes:
            q = holds(d, step - 1)
            ag(d, k, step - 1, landed(d, k, q), q).wait_recv()
            ag(d, k, step, landed(d, k, q), q).start()
            store(d, k, q, landed(d, k, q), step).start()
        return carry

    so[...] = sb[block(me)]

    def take(i):
        scattered(i).wait_recv()
        so[...] += sr[(me + i) % n]

    each(take)
    sa[block(me)] = so[...]
    each(lambda i: spread_sum(i).start())
    lax.fori_loop(1, 3, gather_step, 0)
    each(lambda i: gathered(i).wait_recv())
    piece = sa.at[pl.ds(GATE_AT, KEPT)]
    for k, sec in enumerate((mate, across, diag)):
        copy(piece, sg.at[s], K_GO + s, sec, K_GO + k).start()
    sg[s] = sa[GATE_AT:SMALL]
    lax.fori_loop(3, 4, gather_step, 0)
    for sec in (mate, across, diag):
        copy(piece, sg.at[sec], K_GO + sec, sec).wait_recv()
    misc = KEPT - 8
    count = sum(sg[q, misc + 5 : misc + 6] for q in range(TASKS))
    scale = float(2 * R * n) / jnp.sum(count, axis=1, keepdims=True)

    o_scale[...] = jnp.broadcast_to(scale, o_scale.shape)

    for f in range(2):
        xf[f] = dp[...] * (scale * fw_ref[0, f])
        pltpu.make_async_copy(xf.at[f], o_ig.at[:, f], local.at[2 + f]).start()
    for k in range(2):
        o_pred[:, k * R : (k + 1) * R] = tw[k, TOWER : TOWER + 1]
    for f in range(2):
        o_fw[0, f] = jnp.sum(sa[MISC_AT + 3 + f : MISC_AT + 4 + f] * scale)
    o_bias[0, 0] = jnp.sum(sa[MISC_AT + 2 : MISC_AT + 3] * scale)
    o_gain[...] = (sg[0, misc : misc + 1] + sg[1, misc : misc + 1]) * scale
    o_tout[...] = sa[MISC_AT + 1 : MISC_AT + 2, :TOWER] * scale
    o_tin[...] = (sa[:TOWER] * scale).T

    def order(t, carry):
        for sel in range(SEL):
            for e in range(BITS + 1):
                row = t * (SEL * (BITS + 1)) + sel * (BITS + 1) + e
                at0 = (e * SEL + sel) * TASKS
                cut = FROWS // 2
                o_gate[0, pl.ds(row, 1)] = sg[at0 // cut, pl.ds(at0 % cut + t, 1)] * scale
                o_gate[1, pl.ds(row, 1)] = sg[2 + t // 2, pl.ds((t % 2) * GROWS + e * SEL + sel, 1)] * scale
        return carry

    lax.fori_loop(0, TASKS, order, 0)

    lax.fori_loop(4, n - 1, gather_step, 0)
    for d, k in lanes:
        q = holds(d, n - 2)
        ag(d, k, last, landed(d, k, q), q).wait_recv()
        store(d, k, q, landed(d, k, q), n - 1).start()

    def stored(step, carry):
        for d, k in lanes:
            store(d, k, 0, landed(d, k, 0), step).wait()
        return carry

    lax.fori_loop(0, n, stored, 0)

    def sent(step, carry):
        for d, k in lanes:
            rs(d, k, step, a1.at[slot(d, k, step)]).wait_send()
            ag(d, k, step, a1.at[slot(d, k, step)], 0).wait_send()
        return carry

    lax.fori_loop(0, n - 1, sent, 0)
    each(lambda i: scatter(i).wait_send())
    each(lambda i: spread_sum(i).wait_send())
    to_mate.wait_send()
    gates_move.wait_send()
    for e in range(HALF):
        for move in give(e):
            move.wait_send()
    for k in range(2):

        @pl.when(s != 2 + k)
        def _():
            copy(smo, sm.at[s], K_SM + s, 2 + k, K_SM + k).wait_send()
            copy(tin_ref, ti.at[s], K_TI + s, 2 + k, K_TI + k).wait_send()

    @pl.when(x == 0)
    def _():
        for t in range(1, TASKS):
            copy(outbox.at[t], inbox.at[t], K_UP + t, across).wait_send()
        for k, sec in enumerate((mate, across, diag)):
            copy(dp.at[mine], dp.at[mine], K_DP + c, sec, K_DP + k).wait_send()

    @pl.when(x == 1)
    def _():
        copy(pre2, pre1, K_P + 1, across).wait_send()
        for t in range(TASKS):
            copy(outbox.at[t], inbox.at[t], K_DOWN + t, across).wait_send()

            @pl.when(t != s)
            def _():
                copy(tp.at[t], tw.at[c], K_TW + c, t, K_TW + t).wait_send()

    for k, sec in enumerate((mate, across, diag)):
        copy(piece, sg.at[s], K_GO + s, sec, K_GO + k).wait_send()
    for f in range(2):
        pltpu.make_async_copy(xf.at[f], o_ig.at[:, f], local.at[2 + f]).wait()


def hand_over(count, scaled, scale_ref, *refs):
    held = refs[2 * count : 3 * count]
    sems = refs[-1]
    reads = [pltpu.make_async_copy(refs[k], held[k], sems.at[0, k]) for k in range(count)]
    writes = [pltpu.make_async_copy(held[k], refs[count + k], sems.at[1, k]) for k in range(count)]
    order = list(scaled) + [k for k in range(count) if k not in scaled]
    for k in order:
        reads[k].start()
    scale = scale_ref[0:1, 0:1]
    for k in order:
        reads[k].wait()
        if k in scaled:

            def one(i, carry):
                rows = pl.ds(pl.multiple_of(i * H, H), H)
                held[k][rows] = held[k][rows] * scale
                return carry

            lax.fori_loop(0, held[k].shape[0] // H, one, 0)
        writes[k].start()
    for move in writes:
        move.wait()


def body(
    field_inputs,
    field_weight,
    norm_gain,
    gate_weight,
    expert_in,
    expert_out,
    tower_in,
    tower_out,
    tower_bias,
    labels,
    source_ids,
    task_table,
):
    n = lax.axis_size("dp")
    rows = field_inputs.shape[0]
    half = rows // 2
    subs = 2
    small_rows = -(-SMALL // (8 * n)) * 8
    used = TASKS * SEL * (BITS + 1)

    vmem = pl.BlockSpec(memory_space=pltpu.VMEM)
    smem = pl.BlockSpec(memory_space=pltpu.SMEM)
    hbm = pl.BlockSpec(memory_space=pl.ANY)

    def bf(*shape):
        return pltpu.VMEM(shape, BF16)

    def f32(*shape):
        return pltpu.VMEM(shape, F32)

    def out(*shape):
        return jax.ShapeDtypeStruct(shape, F32)

    dma = pltpu.SemaphoreType.DMA
    *sums, scale, _ = pl.pallas_call(
        partial(kernel, n, subs, small_rows),
        out_shape=(
            out(1, rows),
            out(rows, 2, D),
            out(1, 2),
            out(1, D),
            out(2, used, D),
            out(HALF * H, D),
            out(HALF * H, D),
            out(D, TOWER),
            out(1, TOWER),
            out(1, 1),
            out(1, TOWER),
            jax.ShapeDtypeStruct((E, 2 * SPILL, H, 2 * half), BF16),
        ),
        in_specs=[hbm, smem, vmem, vmem, hbm, hbm, vmem, vmem, smem, vmem, vmem, smem],
        out_specs=(vmem, hbm, smem, vmem, vmem, hbm, hbm, vmem, vmem, smem, vmem, hbm),
        scratch_shapes=[
            bf(2 * E, H, 2 * D),
            bf(E, D, 2 * H),
            bf(E, H, 2 * D),
            f32(E * H, half),
            f32(E * H, half),
            f32(E * H, D),
            f32(E * H, D),
            bf(E, H, 2 * half),
            bf(E, H, 2 * half),
            bf(2, H, 2 * half),
            f32(2, HALF * H, D),
            f32(2, rows, D),
            f32(rows, D),
            f32(half, D),
            f32(half, D),
            f32(half, D),
            f32(half, D),
            f32(TASKS, D, half),
            f32(TASKS, D, half),
            bf(3 * D, half),
            bf(TASKS, 3 * half, D),
            bf(3 * D, half),
            bf(TASKS, 3 * half, D),
            f32(2, H, half),
            f32(D, half),
            f32(TASKS * GROWS, D),
            f32(E, 1, half),
            f32(E, TASKS, half),
            f32(FROWS, half),
            f32(E, TASKS, half),
            f32(TASKS * GROWS, D),
            f32(2 * GROWS, D),
            f32(TASKS, 8, rows),
            f32(8, rows),
            f32(TASKS, D, TOWER),
            f32(TASKS, TOWER + 8, D),
            f32(2, TOWER + 8, D),
            f32(rows, D),
            f32(8, D),
            f32(half, E * TASKS),
            bf(3 * D, half),
            f32(E, 1, half),
            f32(GROWS, half),
            f32(D, half),
            f32(D, half),
            bf(TASKS, TOWER, 3 * D),
            bf(TASKS, D, 3 * TOWER),
            f32(TASKS, TOWER, half),
            f32(TASKS * GROWS, half),
            f32(D, half),
            f32(2 * TOWER, half),
            f32(n * small_rows, D),
            f32(n, small_rows, D),
            f32(small_rows, D),
            f32(n * small_rows, D),
            f32(TASKS, KEPT, D),
            dma((K_COUNT,)),
            dma((K_COUNT,)),
            dma((6,)),
            dma((AHEAD + 1,)),
            pltpu.SemaphoreType.REGULAR,
            pltpu.SemaphoreType.REGULAR,
            dma((2, subs, n - 1)),
            dma((2, subs, n - 1)),
            dma((2, subs, n - 1)),
            dma((2, subs, n - 1)),
            dma((2, subs, n)),
            dma((n,)),
            dma((n,)),
            dma((n,)),
            dma((n,)),
        ],
        compiler_params=pltpu.CompilerParams(
            collective_id=0, has_side_effects=True, vmem_limit_bytes=64 * 1024 * 1024 - 65536
        ),
    )(
        field_inputs,
        field_weight.reshape(1, 2),
        norm_gain.reshape(1, D),
        gate_weight.swapaxes(1, 2),
        expert_in.reshape(HALF * H, D),
        expert_out.reshape(HALF * H, D),
        tower_in.reshape(D, TOWER),
        tower_out,
        tower_bias.reshape(1, 1),
        labels.reshape(1, rows),
        source_ids.reshape(1, rows),
        task_table.reshape(1, SOURCES),
    )
    pred, ig, fw, gain, gate, d_in, d_out, tin, tout, bias = pl.pallas_call(
        partial(hand_over, len(sums), (5, 6)),
        out_shape=tuple(jax.ShapeDtypeStruct(v.shape, v.dtype) for v in sums),
        in_specs=[vmem] + [hbm] * len(sums),
        out_specs=(hbm,) * len(sums),
        scratch_shapes=[pltpu.VMEM(v.shape, v.dtype) for v in sums] + [dma((2, len(sums)))],
        compiler_params=pltpu.CompilerParams(vmem_limit_bytes=64 * 1024 * 1024 - 65536),
    )(scale, *sums)
    return (
        pred.reshape(rows, 1),
        ig,
        fw.reshape(2),
        gain.reshape(D),
        gate.swapaxes(1, 2),
        d_in.reshape(HALF, D, H),
        d_out.reshape(HALF, H, D),
        tin.reshape(1, D, TOWER),
        tout,
        bias.reshape(1),
    )


def solution(mesh):
    in_specs = (
        P("dp", "section", None),
        P("section"),
        P(),
        P(),
        P("section", None, None),
        P("section", None, None),
        P("section", None, None),
        P("section", None),
        P("section"),
        P("dp", "section"),
        P("dp"),
        P(None, "section"),
    )
    out_specs = (
        P("dp", "section"),
        P("dp", "section", None),
        P("section"),
        P(),
        P(),
        P("section", None, None),
        P("section", None, None),
        P("section", None, None),
        P("section", None),
        P("section"),
    )
    return jax.shard_map(body, mesh=mesh, in_specs=in_specs, out_specs=out_specs, check_vma=False)
```

```python
from functools import partial

import jax
import jax.numpy as jnp
from jax import lax
from jax.experimental import pallas as pl
from jax.experimental.pallas import tpu as pltpu
from jax.sharding import PartitionSpec as P

D = 256
H = 256
E = 16
TASKS = 4
SEL = 4
BITS = 4
TOWER = 128
SOURCES = 32
HALF = E // 2
GROWS = 32
FROWS = 96

STEP_SLOPE = 0.6
ENTROPY_WEIGHT = 0.05
NORM_EPS = 1e-05
GELU_A = 0.7978845608028654
GELU_B = 0.044715

F32 = jnp.float32
BF16 = jnp.bfloat16
MESH = pl.DeviceIdType.MESH

K_W, K_P, K_SM, K_TI, K_UP, K_DOWN, K_TW, K_DG, K_DP, K_GO, K_DX = 48, 2, 4, 8, 12, 16, 20, 24, 25, 28, 32
K_COUNT = 64
TILE = 32
SPILL = TASKS - 1
AHEAD = 3

GATE_AT = TOWER
MISC_AT = GATE_AT + 2 * GROWS
SMALL = MISC_AT + 8
KEPT = SMALL - GATE_AT


def split(x):
    hi = x.astype(BF16)
    return hi, (x - hi.astype(F32)).astype(BF16)


def wide(x):
    hi, lo = split(x)
    return jnp.concatenate([hi, lo, hi], axis=1)


def tall(x):
    hi, lo = split(x)
    return jnp.concatenate([hi, hi, lo], axis=0)


def put(ref, at, x):
    k = x.shape[1]
    hi, lo = split(x)
    ref[*at, :k] = hi
    ref[*at, k:] = lo


def stack(x):
    k = x.shape[1] // 2
    return jnp.concatenate([x[:, :k], x[:, :k], x[:, k:]], axis=0)


def mm(a, b):
    return jnp.dot(a, b, preferred_element_type=F32)


def pair(x):
    k = x.shape[1] // 2
    return jnp.concatenate([x, x[:, :k]], axis=1)


def gelu_pair(x):
    x2 = x * x
    h = 0.5 + 0.5 * jnp.tanh(x * (GELU_A + (GELU_A * GELU_B) * x2))
    g = x * h
    slope = h + g * (1.0 - h) * (2.0 * GELU_A + (6.0 * GELU_A * GELU_B) * x2)
    return g, slope


def rows8(x):
    return jnp.sum(x.reshape(x.shape[0] // 8, 8, x.shape[1]), axis=0)


def over_selectors(v, groups, op):
    parts = [v[k * groups : (k + 1) * groups] for k in range(SEL)]
    return op(op(parts[0], parts[1]), op(parts[2], parts[3]))


def to_selectors(v):
    return jnp.concatenate([v] * SEL, axis=0)


def gate_state(c, groups, swapped):
    w = SEL * groups
    zs = [c[w * b : w * b + w] * STEP_SLOPE for b in range(BITS)]
    alpha = c[w * BITS : w * BITS + w]
    ups, downs, sig_p, sig_n = [], [], [], []
    for z in zs:
        e = jnp.exp(-jnp.abs(z))
        tail = jnp.log1p(e)
        ups.append(jnp.minimum(z, 0.0) - tail)
        downs.append(jnp.minimum(-z, 0.0) - tail)
        big = 1.0 / (1.0 + e)
        small = e * big
        sig_p.append(jnp.where(z >= 0.0, big, small))
        sig_n.append(jnp.where(z >= 0.0, small, big))
    last_on, last_off = ups[3], downs[3]
    ups[3], downs[3] = jnp.where(swapped, last_off, last_on), jnp.where(swapped, last_on, last_off)
    low = [(ups[0] if k & 1 else downs[0]) + (ups[1] if k & 2 else downs[1]) for k in range(4)]
    high = [(ups[2] if k & 1 else downs[2]) + (ups[3] if k & 2 else downs[3]) for k in range(4)]
    log_r = [low[j & 3] + high[j >> 2] for j in range(E)]
    r = [jnp.exp(v) for v in log_r]
    top = jnp.exp(alpha - to_selectors(over_selectors(alpha, groups, jnp.maximum)))
    mix = top / to_selectors(over_selectors(top, groups, jnp.add))
    return log_r, r, mix, sig_p, sig_n


def gate_forward(c, groups, swapped):
    _, r, mix, _, _ = gate_state(c, groups, swapped)
    return [over_selectors(mix * v, groups, jnp.add) for v in r]


class GateBackward:
    def __init__(self, c, groups, swapped):
        self.log_r, self.r, self.mix, self.sig_p, self.sig_n = gate_state(c, groups, swapped)
        self.swapped = swapped
        self.groups = groups
        self.total = jnp.zeros_like(self.mix)
        self.on = [jnp.zeros_like(self.mix) for _ in range(BITS)]
        self.off = [jnp.zeros_like(self.mix) for _ in range(BITS)]

    def add(self, j, dg):
        dg = to_selectors(dg)
        self.total = self.total + dg * self.r[j]
        dlog = self.r[j] * (self.mix * dg - ENTROPY_WEIGHT * (self.log_r[j] + 1.0))
        for b in range(BITS):
            if j >> b & 1:
                self.on[b] = self.on[b] + dlog
            else:
                self.off[b] = self.off[b] + dlog

    def result(self):
        mix, groups = self.mix, self.groups
        dalpha = mix * (self.total - to_selectors(over_selectors(mix * self.total, groups, jnp.add)))
        on, off = self.on[3], self.off[3]
        self.on[3], self.off[3] = jnp.where(self.swapped, off, on), jnp.where(self.swapped, on, off)
        dz = [STEP_SLOPE * (self.on[b] * self.sig_n[b] - self.off[b] * self.sig_p[b]) for b in range(BITS)]
        used = SEL * (BITS + 1) * groups
        pad = jnp.zeros(((-used) % GROWS, mix.shape[1]), F32)
        return jnp.concatenate(dz + [dalpha, pad], axis=0)


def t_dot(a, b):
    ah, al = split(a)
    left = jnp.concatenate([ah, al, ah], axis=0)
    return lax.dot_general(left, tall(b), (((0,), (0,)), ((), ())), preferred_element_type=F32)


def weave(count, first, middle, last, extra=(), after=None):
    extra = iter(extra)
    for step in range(count + 2):
        if step < count:
            first(step, step % 2)
        next(extra, None)
        if 0 <= step - 1 < count:
            middle(step - 1, (step - 1) % 2, 0)
        next(extra, None)
        if step >= 2:
            last(step - 2, step % 2)
        next(extra, None)
        if 0 <= step - 1 < count:
            middle(step - 1, (step - 1) % 2, 1)
            if after is not None:
                after(step - 1)
        next(extra, None)
    for _ in extra:
        pass


def halves(size):
    tiles = [slice(a, a + TILE) for a in range(0, size, TILE)]
    return tiles[: len(tiles) // 2], tiles[len(tiles) // 2 :]


def kernel(
    n,
    subs,
    small_rows,
    x_ref,
    fw_ref,
    gain_ref,
    gate_ref,
    win_ref,
    wout_ref,
    tin_ref,
    tout_ref,
    tbias_ref,
    labels_ref,
    ids_ref,
    table_ref,
    o_pred,
    o_ig,
    o_fw,
    o_gain,
    o_gate,
    o_in,
    o_out,
    o_tin,
    o_tout,
    o_bias,
    o_scale,
    kept,
    wt,
    w_in,
    w_out,
    a1,
    a2,
    d_in,
    d_out,
    gbuf,
    kbuf,
    kp,
    rd,
    xf,
    part,
    pre0,
    pre1,
    pre2,
    pre,
    inbox,
    outbox,
    u_t,
    u_n,
    s_t,
    s_n,
    bb,
    acc,
    wg,
    gt,
    gt0,
    cs,
    dgt,
    dg,
    gb,
    sm,
    smo,
    ti,
    tp,
    tw,
    dp,
    gain_row,
    columns,
    u_next,
    gt_next,
    cs_next,
    acc_b,
    dy_kept,
    tower_t,
    tower_n,
    out_cols,
    dcs,
    held,
    tm,
    sb,
    sr,
    so,
    sa,
    sg,
    send,
    recv,
    local,
    fetch_sem,
    ready,
    turns,
    rs_send,
    rs_recv,
    ag_send,
    ag_recv,
    store_sem,
    sr_send,
    sr_recv,
    sa_send,
    sa_recv,
):
    s = lax.axis_index("section")
    x = s // 2
    c = s % 2
    mate = s + 1 - 2 * c
    across = s + 2 - 4 * x
    diag = 3 - s
    R = part.shape[0] // 2
    mine = pl.ds(pl.multiple_of(c * R, R), R)
    theirs = pl.ds(pl.multiple_of((1 - c) * R, R), R)

    me = lax.axis_index("dp")
    odd = me % 2
    p = (1 - odd) * (me // 2) + odd * (n - 1 - me // 2)

    def ring_id(q):
        far = q // (n // 2)
        return (1 - far) * 2 * q + far * (2 * (n - 1 - q) + 1)

    nbr = [ring_id((p + 1) % n), ring_id((p + n - 1) % n)]

    barrier = pltpu.get_barrier_semaphore()
    for sec in (mate, across, diag):
        pl.semaphore_signal(barrier, inc=1, device_id={"section": sec}, device_id_type=MESH)

    def greet(i, carry):
        pl.semaphore_signal(barrier, inc=1, device_id={"dp": (me + i) % n}, device_id_type=MESH)
        return carry

    lax.fori_loop(1, n, greet, 0)
    fields = [pltpu.make_async_copy(x_ref.at[:, f], xf.at[f], local.at[2 + f]) for f in range(2)]
    for f in fields:
        f.start()
    own = pl.ds(0, HALF * H)
    swapped = c == 1
    own_in = pltpu.make_async_copy(win_ref, d_in.at[own], local.at[0])
    own_out = pltpu.make_async_copy(wout_ref, d_out.at[own], local.at[1])
    own_in.start()
    own_out.start()
    pl.semaphore_wait(barrier, 3 + n - 1)

    def copy(src, dst, k, sec, ks=None):
        return pltpu.make_async_remote_copy(
            src_ref=src,
            dst_ref=dst,
            send_sem=send.at[k if ks is None else ks],
            recv_sem=recv.at[k],
            device_id={"section": sec},
            device_id_type=MESH,
        )

    def expert(j, count=1):
        return pl.ds(pl.multiple_of(j * H, H), count * H)

    for f in fields:
        f.wait()
    part[...] = xf[0] * fw_ref[0, 0] + xf[1] * fw_ref[0, 1]
    to_mate = copy(part.at[theirs], pre0, K_P, mate)
    to_mate.start()
    def swap(e):
        return (
            copy(win_ref.at[expert(e)], d_in.at[expert(HALF + e)], K_W + e, mate),
            copy(wout_ref.at[expert(e)], d_out.at[expert(HALF + e)], K_W + HALF + e, mate),
        )

    for e in range(HALF):
        for move in swap(e):
            move.start()
    own_in.wait()
    own_out.wait()

    ids = ids_ref[...]
    mask = jnp.zeros(ids.shape, F32)
    for q in range(SOURCES):
        mask = mask + jnp.where(ids == q, table_ref[0, q].astype(F32), 0.0)
    smo[...] = jnp.zeros_like(smo)
    smo[0:1] = labels_ref[...]
    smo[1:2] = mask
    smo[2:3, :TOWER] = tout_ref[...]
    smo[3:4] = jnp.zeros((1, 2 * R), F32) + tbias_ref[0, 0]
    for k in range(2):

        @pl.when(s != 2 + k)
        def _():
            copy(smo, sm.at[s], K_SM + s, 2 + k, K_SM + k).start()
            copy(tin_ref, ti.at[s], K_TI + s, 2 + k, K_TI + k).start()

    to_mate.wait_recv()

    @pl.when(x == 1)
    def _():
        pre2[...] = part[mine] + pre0[...]
        copy(pre2, pre1, K_P + 1, across).start()
        sm[s] = smo[...]
        ti[s] = tin_ref[...]

    wg[...] = jnp.zeros_like(wg)

    @pl.when(x == 0)
    def _():
        def order(t, carry):
            for sel in range(SEL):
                for e in range(BITS + 1):
                    row = t * (SEL * (BITS + 1)) + sel * (BITS + 1) + e
                    wg[pl.ds((e * SEL + sel) * TASKS + t, 1)] = gate_ref[0, pl.ds(row, 1)]
            return carry

        lax.fori_loop(0, TASKS, order, 0)

    @pl.when(x == 1)
    def _():
        def order(t, carry):
            for sel in range(SEL):
                for e in range(BITS + 1):
                    row = t * (SEL * (BITS + 1)) + sel * (BITS + 1) + e
                    wg[pl.ds(t * GROWS + e * SEL + sel, 1)] = gate_ref[1, pl.ds(row, 1)]
            return carry

        lax.fori_loop(0, TASKS, order, 0)

    def keep_plain(e, carry):
        put(w_in.at[e], (slice(None),), d_in[expert(e)])
        put(w_out.at[e], (slice(None),), d_out[expert(e)])
        return carry

    def keep_flipped(e, carry):
        put(wt.at[e], (slice(None),), d_in[expert(e)].T)
        put(wt.at[E + e], (slice(None),), d_out[expert(e)].T)
        return carry

    def keep_both(e, carry):
        keep_plain(e, carry)
        return keep_flipped(e, carry)

    def arrived(prepare):
        def one(e, carry):
            for move in swap(e):
                move.wait_recv()
            return prepare(HALF + e, carry)

        return one

    def rows_of(size):
        return [slice(a, a + TILE) for a in range(0, size, TILE)]

    def shifted(tile, e):
        return slice(e * H + tile.start, e * H + tile.stop)

    chunk = HALF * H // n
    sub = chunk // subs
    lanes = [(d, k) for d in range(2) for k in range(subs)]

    def at(k, q):
        return pl.ds(pl.multiple_of(q * chunk + k * sub, 8), sub)

    def holds(d, step):
        return (p + n - step) % n if d == 0 else (p + step) % n

    def slot(d, k, step):
        return pl.ds(pl.multiple_of(((d * subs + k) * (n - 1) + step) * sub, 8), sub)

    def rs(d, k, step, src):
        return pltpu.make_async_remote_copy(
            src_ref=src,
            dst_ref=a1.at[slot(d, k, step)],
            send_sem=rs_send.at[d, k, step],
            recv_sem=rs_recv.at[d, k, step],
            device_id={"dp": nbr[d]},
            device_id_type=MESH,
        )

    results = (o_in, o_out)

    def landed(d, k, q):
        return a2.at[pl.ds(pl.multiple_of(d * HALF * H + q * chunk + k * sub, 8), sub)]

    def store(d, k, q, src, step):
        return pltpu.make_async_copy(src, results[d].at[at(k, q)], store_sem.at[d, k, step])

    def ag(d, k, step, src, q):
        return pltpu.make_async_remote_copy(
            src_ref=src,
            dst_ref=landed(d, k, q),
            send_sem=ag_send.at[d, k, step],
            recv_sem=ag_recv.at[d, k, step],
            device_id={"dp": nbr[d]},
            device_id_type=MESH,
        )

    def give(e):
        j = HALF + e
        return (
            copy(d_in.at[expert(j)], rd.at[0, expert(e)], K_DX + e, mate),
            copy(d_out.at[expert(j)], rd.at[1, expert(e)], K_DX + HALF + e, mate),
        )

    start_at = p * chunk // H

    def near(k):
        return (start_at + HALF + ((k + 1) // 2) * (1 - 2 * (k % 2))) % HALF

    def turn_of(i):
        own_turn = i % 2
        return (1 - own_turn) * HALF + near(i // 2)

    def fetch(i):
        at = pl.ds((i % (AHEAD + 1)) * 8, 2 * SPILL)
        return pltpu.make_async_copy(kept.at[turn_of(i)], wt.at[at], fetch_sem.at[i % (AHEAD + 1)])

    def fetch_start(i):
        for k in range(2 * SPILL):
            slab = (i % (AHEAD + 1)) * 8 + k
            pltpu.make_async_copy(
                kept.at[turn_of(i), k], wt.at[slab], fetch_sem.at[i % (AHEAD + 1)]
            ).start()

    def greet_ring():
        for dev in nbr:
            pl.semaphore_signal(ready, inc=1, device_id={"dp": dev}, device_id_type=MESH)

    def merge(k, carry):
        e = near(k)
        for move in give(e):
            move.wait_recv()
        rows = expert(e)
        rd[0, rows] = (rd[0, rows] + d_in[rows]).T
        rd[1, rows] += d_out[rows]
        return carry

    def ring_start():
        pl.semaphore_wait(ready, 2)
        for d, k in lanes:
            rs(d, k, 0, rd.at[d, at(k, holds(d, 0))]).start()

    def reduce_step(step, carry):
        for d, k in lanes:
            rs(d, k, step - 1, a1.at[slot(d, k, step - 1)]).wait_recv()
            a1[slot(d, k, step - 1)] += rd[d, at(k, holds(d, step))]
            rs(d, k, step, a1.at[slot(d, k, step - 1)]).start()
        return carry

    @pl.when(x == 0)
    def _():
        lax.fori_loop(0, HALF, keep_plain, 0)
        copy(pre2, pre1, K_P + 1, across).wait_recv()
        pre_rows = part[mine] + pre0[...] + pre1[...]
        pre[...] = pre_rows
        rho = lax.rsqrt(jnp.mean(pre_rows * pre_rows, axis=1, keepdims=True) + NORM_EPS)
        pooled = pre_rows * rho * gain_ref[...]
        acc[...] = pooled
        u_n[0] = tall(pooled)
        u_t[...] = tall(pooled.T)
        logits = mm(wide(wg[:FROWS]), u_t[...])
        cs[...] = logits
        gates = gate_forward(logits, TASKS, swapped)
        for j, g in enumerate(gates):
            gt0[j] = g

        def forward(base):
            def first(i, par):
                left = jnp.concatenate([u_n[0, :R], u_n[0, 2 * R :], u_n[0, :R]], axis=1)
                bb[par] = mm(left, stack(w_in[base + i]))

            def activate(i, par, part_no):
                for tile in halves(R)[part_no]:
                    value, slope = gelu_pair(bb[par, tile])
                    a1[shifted(tile, base + i)] = value
                    a2[shifted(tile, base + i)] = slope
                    put(gbuf, (base + i, tile), value)

            def finish(i, par):
                d_in[expert(base + i)] = mm(pair(gbuf[base + i]), stack(w_out[base + i]))

            weave(HALF, first, activate, finish)

        forward(0)
        lax.fori_loop(0, HALF, arrived(keep_plain), 0)
        forward(HALF)
        columns[...] = jnp.concatenate(gates, axis=0).T

        for t in range(TASKS):

            def mix(i, carry):
                tile = pl.ds(pl.multiple_of(i * TILE, TILE), TILE)
                cols = columns[tile]
                total = acc[tile]
                for j in range(E):
                    rows = pl.ds(pl.multiple_of(j * R + i * TILE, TILE), TILE)
                    total = total + cols[:, j * TASKS + t : j * TASKS + t + 1] * d_in[rows]
                outbox[t, tile] = total
                return carry

            lax.fori_loop(0, R // TILE, mix, 0)

            @pl.when(c == 0)
            def _():
                if t == 0:
                    copy(outbox.at[t], inbox.at[t], K_UP + t, across).start()

        first_up = copy(outbox.at[0], inbox.at[0], K_UP, across)

        @pl.when(c == 0)
        def _():
            first_up.wait_send()
            pl.semaphore_signal(turns, inc=1, device_id={"section": mate}, device_id_type=MESH)
            pl.semaphore_wait(turns, 1)

        @pl.when(c == 1)
        def _():
            pl.semaphore_wait(turns, 1)
            first_up.start()
            first_up.wait_send()
            pl.semaphore_signal(turns, inc=1, device_id={"section": mate}, device_id_type=MESH)

        for t in range(1, TASKS):
            copy(outbox.at[t], inbox.at[t], K_UP + t, across).start()

        def flip(j, carry):
            value = a1[expert(j)].T
            a1[expert(j)] = value
            put(gbuf.at[j], (slice(None),), value)
            a2[expert(j)] = a2[expert(j)].T
            d_in[expert(j)] = d_in[expert(j)].T
            return carry

        lax.fori_loop(0, E, flip, 0)
        greet_ring()
        d_out[...] = jnp.zeros_like(d_out)
        acc[...] = jnp.zeros_like(acc)

    @pl.when(x == 1)
    def _():
        for q in range(TASKS):

            @pl.when(s != q)
            def _():
                copy(smo, sm.at[q], K_SM + q, q).wait_recv()
                copy(tin_ref, ti.at[q], K_TI + q, q).wait_recv()

        for q in range(TASKS):
            tower_t[q] = wide(ti[q].T)
            tower_n[q] = wide(ti[q])
            out_cols[q] = jnp.broadcast_to(sm[q][:, :TOWER].T[:, 2:3], (TOWER, R))
        lax.fori_loop(0, HALF, keep_both, 0)
        lax.fori_loop(0, HALF, arrived(keep_both), 0)

        def keep(k, t):
            return pltpu.make_async_copy((gbuf, kbuf)[k], kept.at[:, k * SPILL + t], local.at[4 + k])

        def keep_start(k, t):
            def one(j, carry):
                pltpu.make_async_copy((gbuf, kbuf)[k].at[j], kept.at[j, k * SPILL + t], local.at[4 + k]).start()
                return carry

            @pl.when(t < SPILL)
            def _():
                lax.fori_loop(0, E, one, 0)

        def gate_rows(t):
            return pl.ds(pl.multiple_of(t * GROWS, GROWS), GROWS)

        def enter(t):
            for k in range(2):
                cols = slice(k * (R // 2), (k + 1) * (R // 2))
                flipped = inbox[t, cols].T
                hi, lo = split(flipped)
                u_next[:D, cols] = hi
                u_next[D : 2 * D, cols] = hi
                u_next[2 * D :, cols] = lo
                acc[:, cols] = flipped
                yield
            logits = mm(wide(wg[gate_rows(t)]), u_next[...])
            cs_next[...] = logits
            yield
            u_n[t] = tall(inbox[t])
            yield
            _, r, mix, _, _ = gate_state(logits, 1, swapped)
            yield
            for j in range(E):
                gt_next[j] = over_selectors(mix * r[j], 1, jnp.add)
                yield

        def turn():
            u_t[...] = u_next[...]
            gt[...] = gt_next[...]
            cs[:GROWS] = cs_next[...]

        def all_of(pieces):
            for _ in pieces:
                pass

        copy(outbox.at[0], inbox.at[0], K_UP, across).wait_recv()
        all_of(enter(0))
        turn()

        def task(t, carry):
            @pl.when(t > 0)
            def _():
                keep(0, 0).wait()

            def first(j, par):
                bb[par] = mm(pair(wt[j]), u_t[...])

            def activate(j, par, part_no):
                for tile in halves(H)[part_no]:
                    value, slope = gelu_pair(bb[par, tile])
                    a1[shifted(tile, j)] = value
                    a2[shifted(tile, j)] = slope
                    put(gbuf, (j, tile), value * gt[j])

            def finish(j, par):
                acc[...] += mm(pair(wt[E + j]), stack(gbuf[j]))

            weave(E, first, activate, finish)
            keep_start(0, t)

            second = acc[...]
            held[...] = second
            g, slope = gelu_pair(mm(tower_t[t], tall(second)))
            out_col = out_cols[t]
            here = sm[t, :, mine]
            logit = jnp.sum(g * out_col, axis=0, keepdims=True) + here[3:4]
            prob = jax.nn.sigmoid(logit)
            dlogit = here[1:2] * (prob - here[0:1])
            m = dlogit * out_col * slope
            dy = mm(tower_n[t], tall(m))
            s_t[...] = tall(dy)
            acc_b[...] = dy
            dy_kept[...] = dy
            tm[:TOWER] = m
            tm[TOWER:] = g * dlogit
            tp[t, TOWER : TOWER + 1] = prob
            tp[t, TOWER + 2 : TOWER + 3] = dlogit
            tp[t, TOWER + 3 :] = jnp.zeros((5, R), F32)

            @pl.when(t > 0)
            def _():
                keep(1, 0).wait()

            @pl.when(t == TASKS - 1)
            def _():
                for i in range(AHEAD):
                    fetch_start(i)

            after = jnp.minimum(t + 1, TASKS - 1)

            @pl.when(t < TASKS - 1)
            def _():
                copy(outbox.at[after], inbox.at[after], K_UP + after, across).wait_recv()

            def back(j, par):
                bb[par] = mm(pair(w_out[j]), s_t[...])

            def pull(j, par, part_no):
                total = jnp.zeros((8, R), F32)
                for tile in halves(H)[part_no]:
                    grad = bb[par, tile]
                    total = total + rows8(grad * a1[shifted(tile, j)])
                    put(kbuf, (j, tile), grad * a2[shifted(tile, j)] * gt[j])
                total = jnp.sum(total, axis=0, keepdims=True)
                if part_no == 0:
                    dgt[j, 0:1] = total
                else:
                    dgt[j, 0:1] += total

            def spread(j, par):
                acc_b[...] += mm(pair(w_in[j]), stack(kbuf[j]))

            def beside():
                s_n[t] = tall(dy_kept[...].T)
                yield
                yield from enter(after)
                flipped = tall(held[...].T)
                yield
                tp[t, :TOWER] = mm(wide(tm[:TOWER]), flipped)
                yield
                out_grad = jnp.sum(tm[TOWER:], axis=1, keepdims=True)
                out_row = jnp.broadcast_to(out_grad, (TOWER, TOWER)).T[0:1]
                tp[t, TOWER + 1 : TOWER + 2] = jnp.concatenate([out_row, jnp.zeros_like(out_row)], axis=1)
                yield

            gates_back = GateBackward(cs[:GROWS], 1, swapped)
            weave(E, back, pull, spread, beside(), lambda j: gates_back.add(j, dgt[j, 0:1]))
            dc = gates_back.result()
            outbox[t] = acc_b[...] + t_dot(wg[gate_rows(t)], dc)
            copy(outbox.at[t], inbox.at[t], K_DOWN + t, across).start()
            dcs[gate_rows(t)] = dc
            keep_start(1, t)
            turn()

            @pl.when(t != s)
            def _():
                copy(tp.at[t], tw.at[c], K_TW + c, t, K_TW + t).start()

            @pl.when(t == s)
            def _():
                tw[c] = tp[t]

            return carry

        lax.fori_loop(0, TASKS, task, 0)
        for q in range(TASKS):
            rows = slice(q * GROWS, (q + 1) * GROWS)
            dg[rows] = mm(wide(dcs[rows]), u_n[q])
        greet_ring()

    @pl.when(x == 1)
    def _():
        def one(i, carry):
            fetch(i).wait()

            @pl.when(i < E - AHEAD)
            def _():
                fetch_start(i + AHEAD)

            j = turn_of(i)
            slot_at = (i % (AHEAD + 1)) * 8
            for k, (grad, right, here) in enumerate(((d_out, s_n, gbuf), (d_in, u_n, kbuf))):
                left = [pair(wt[slot_at + k * SPILL + t]) for t in range(SPILL)] + [pair(here[j])]
                grad[expert(j)] = mm(jnp.concatenate(left, axis=1), right[...].reshape(3 * TASKS * R, D))

            @pl.when(i % 2 == 0)
            def _():
                for move in give(near(i // 2)):
                    move.start()

            @pl.when(i == 3)
            def _():
                merge(0, 0)
                ring_start()

            @pl.when((i % 2 == 1) & (i > 3))
            def _():
                merge((i - 3) // 2, 0)

            if n == HALF:

                @pl.when((i % 4 == 3) & (i > 3))
                def _():
                    reduce_step((i - 3) // 4, 0)

            return carry

        lax.fori_loop(0, E, one, 0)
        merge(HALF - 1, 0)
        if n != HALF:
            lax.fori_loop(1, 4, reduce_step, 0)

    @pl.when(x == 0)
    def _():
        def arrive(t, carry):
            copy(outbox.at[t], inbox.at[t], K_DOWN + t, across).wait_recv()
            acc[...] += inbox[t]

            def one(j, inner):
                gate = gt0[j, pl.ds(t, 1)]
                total = jnp.zeros((8, R), F32)
                for tile in rows_of(D):
                    dy = inbox[t, tile]
                    rows = pl.ds(pl.multiple_of(j * D + tile.start, TILE), TILE)
                    total = total + rows8(d_in[rows] * dy)
                    d_out[rows] += gate * dy
                dgt[j, pl.ds(t, 1)] = jnp.sum(total, axis=0, keepdims=True)
                return inner

            lax.fori_loop(0, E, one, 0)
            return carry

        lax.fori_loop(0, TASKS - 1, arrive, 0)
        last = TASKS - 1
        copy(outbox.at[last], inbox.at[last], K_DOWN + last, across).wait_recv()
        acc[...] += inbox[last]

        def one(i, inner):
            j = turn_of(i)
            gate = gt0[j, last : last + 1]
            total = jnp.zeros((8, R), F32)
            for tile in rows_of(D):
                dy = inbox[last, tile]
                rows = pl.ds(pl.multiple_of(j * D + tile.start, TILE), TILE)
                total = total + rows8(d_in[rows] * dy)
                put(kbuf.at[j], (tile,), d_out[rows] + gate * dy)
            dgt[j, last : last + 1] = jnp.sum(total, axis=0, keepdims=True)
            return inner

        def part_of(first, stop):
            lax.fori_loop(2 * first, 2 * stop, one, 0)

            def products(i, par):
                j = turn_of(2 * first + i)
                mixed = kbuf[j]
                bb[par] = mm(pair(w_out[j]), stack(mixed))
                right = jnp.concatenate([mixed[:, :R], mixed[:, :R], mixed[:, R:]], axis=1)
                d_out[expert(j)] = lax.dot_general(
                    pair(gbuf[j]), right, (((1,), (1,)), ((), ())), preferred_element_type=F32
                )

            def pull(i, par, part_no):
                j = turn_of(2 * first + i)
                for tile in halves(H)[part_no]:
                    kept_rows = pl.ds(pl.multiple_of(j * H + tile.start, TILE), TILE)
                    put(kp, (par, tile), bb[par, tile] * a2[kept_rows])

            def spread(i, par):
                j = turn_of(2 * first + i)
                acc[...] += mm(pair(w_in[j]), stack(kp[par]))
                d_in[expert(j)] = mm(pair(kp[par]), u_n[0])

            weave(2 * (stop - first), products, pull, spread)
            for k in range(first, stop):
                for move in give(near(k)):
                    move.start()

        part_of(0, 1)
        part_of(1, 2)
        merge(0, 0)
        ring_start()
        for k in range(2, HALF, 2):
            part_of(k, k + 2)
            lax.fori_loop(k - 1, k + 1, merge, 0)
            if n == HALF:
                reduce_step(k // 2, 0)
        merge(HALF - 1, 0)
        if n != HALF:
            lax.fori_loop(1, HALF // 2, reduce_step, 0)

    gates_own = pl.ds(pl.multiple_of(c * 2 * GROWS, 2 * GROWS), 2 * GROWS)
    gates_away = pl.ds(pl.multiple_of((1 - c) * 2 * GROWS, 2 * GROWS), 2 * GROWS)
    gain_row[...] = jnp.zeros_like(gain_row)

    @pl.when(x == 0)
    def _():
        gates_back = GateBackward(cs[...], TASKS, swapped)
        for j in range(E):
            gates_back.add(j, dgt[j, :TASKS])
        dc = gates_back.result()
        dpool = (acc[...] + t_dot(wg[:FROWS], dc)).T
        pre_rows = pre[...]
        rho = lax.rsqrt(jnp.mean(pre_rows * pre_rows, axis=1, keepdims=True) + NORM_EPS)
        scaled = dpool * gain_ref[...]
        dots = jnp.mean(scaled * pre_rows, axis=1, keepdims=True)
        dp[mine] = rho * scaled - pre_rows * (rho * rho * rho * dots)
        for k, sec in enumerate((mate, across, diag)):
            copy(dp.at[mine], dp.at[mine], K_DP + c, sec, K_DP + k).start()
        gain_row[0:1] = jnp.sum(dpool * pre_rows * rho, axis=0, keepdims=True)
        grad = mm(wide(dc), u_n[0])
        dg[: FROWS // 2] = grad[: FROWS // 2]
        dg[2 * GROWS : 2 * GROWS + FROWS // 2] = grad[FROWS // 2 :]

    gates_move = copy(dg.at[gates_away], gb, K_DG, mate)
    gates_move.start()

    lax.fori_loop(4, 6, reduce_step, 0)

    for half_no in range(2):

        @pl.when(s != half_no)
        def _():
            rows = pl.ds(half_no * R, R)
            copy(dp.at[rows], dp.at[rows], K_DP + half_no, half_no).wait_recv()

    for k in range(2):

        @pl.when(s != 2 + k)
        def _():
            copy(tp.at[0], tw.at[k], K_TW + k, s).wait_recv()

    gates_move.wait_recv()
    sb[:TOWER] = tw[0, :TOWER] + tw[1, :TOWER]
    sb[GATE_AT:MISC_AT] = dg[gates_own] + gb[...]
    sb[MISC_AT : MISC_AT + 1] = gain_row[0:1]
    sb[MISC_AT + 1 : MISC_AT + 3] = tw[0, TOWER + 1 : TOWER + 3] + tw[1, TOWER + 1 : TOWER + 3]
    for f in range(2):
        sb[MISC_AT + 3 + f : MISC_AT + 4 + f] = jnp.sum(xf[f] * dp[...], axis=0, keepdims=True)
    sb[MISC_AT + 5 : MISC_AT + 6] = smo[1:2, :R] + smo[1:2, R:]
    sb[MISC_AT + 6 :] = jnp.zeros((sb.shape[0] - MISC_AT - 6, D), F32)

    def block(q):
        return pl.ds(pl.multiple_of(q * small_rows, 8), small_rows)

    def scatter(i):
        to = (me + i) % n
        return pltpu.make_async_remote_copy(
            src_ref=sb.at[block(to)],
            dst_ref=sr.at[me],
            send_sem=sr_send.at[i],
            recv_sem=sr_recv.at[me],
            device_id={"dp": to},
            device_id_type=MESH,
        )

    def scattered(i):
        by = (me + i) % n
        return pltpu.make_async_remote_copy(
            src_ref=sb.at[block(me)],
            dst_ref=sr.at[by],
            send_sem=sr_send.at[i],
            recv_sem=sr_recv.at[by],
            device_id={"dp": by},
            device_id_type=MESH,
        )

    def spread_sum(i):
        return pltpu.make_async_remote_copy(
            src_ref=so,
            dst_ref=sa.at[block(me)],
            send_sem=sa_send.at[i],
            recv_sem=sa_recv.at[me],
            device_id={"dp": (me + i) % n},
            device_id_type=MESH,
        )

    def gathered(i):
        by = (me + i) % n
        return pltpu.make_async_remote_copy(
            src_ref=so,
            dst_ref=sa.at[block(by)],
            send_sem=sa_send.at[i],
            recv_sem=sa_recv.at[by],
            device_id={"dp": by},
            device_id_type=MESH,
        )

    def each(act):
        def one(i, carry):
            act(i)
            return carry

        lax.fori_loop(1, n, one, 0)

    each(lambda i: scatter(i).start())
    lax.fori_loop(6, n - 1, reduce_step, 0)
    last = n - 2
    for d, k in lanes:
        q = holds(d, n - 1)
        rs(d, k, last, a1.at[slot(d, k, last)]).wait_recv()
        a1[slot(d, k, last)] += rd[d, at(k, q)]
        ag(d, k, 0, a1.at[slot(d, k, last)], q).start()
        store(d, k, q, a1.at[slot(d, k, last)], 0).start()

    def gather_step(step, carry):
        for d, k in lanes:
            q = holds(d, step - 1)
            ag(d, k, step - 1, landed(d, k, q), q).wait_recv()
            ag(d, k, step, landed(d, k, q), q).start()
            store(d, k, q, landed(d, k, q), step).start()
        return carry

    so[...] = sb[block(me)]

    def take(i):
        scattered(i).wait_recv()
        so[...] += sr[(me + i) % n]

    each(take)
    sa[block(me)] = so[...]
    each(lambda i: spread_sum(i).start())
    lax.fori_loop(1, 3, gather_step, 0)
    each(lambda i: gathered(i).wait_recv())
    piece = sa.at[pl.ds(GATE_AT, KEPT)]
    for k, sec in enumerate((mate, across, diag)):
        copy(piece, sg.at[s], K_GO + s, sec, K_GO + k).start()
    sg[s] = sa[GATE_AT:SMALL]
    lax.fori_loop(3, 4, gather_step, 0)
    for sec in (mate, across, diag):
        copy(piece, sg.at[sec], K_GO + sec, sec).wait_recv()
    misc = KEPT - 8
    count = sum(sg[q, misc + 5 : misc + 6] for q in range(TASKS))
    scale = float(2 * R * n) / jnp.sum(count, axis=1, keepdims=True)

    o_scale[...] = jnp.broadcast_to(scale, o_scale.shape)

    for f in range(2):
        xf[f] = dp[...] * (scale * fw_ref[0, f])
        pltpu.make_async_copy(xf.at[f], o_ig.at[:, f], local.at[2 + f]).start()
    for k in range(2):
        o_pred[:, k * R : (k + 1) * R] = tw[k, TOWER : TOWER + 1]
    for f in range(2):
        o_fw[0, f] = jnp.sum(sa[MISC_AT + 3 + f : MISC_AT + 4 + f] * scale)
    o_bias[0, 0] = jnp.sum(sa[MISC_AT + 2 : MISC_AT + 3] * scale)
    o_gain[...] = (sg[0, misc : misc + 1] + sg[1, misc : misc + 1]) * scale
    o_tout[...] = sa[MISC_AT + 1 : MISC_AT + 2, :TOWER] * scale
    o_tin[...] = (sa[:TOWER] * scale).T

    def order(t, carry):
        for sel in range(SEL):
            for e in range(BITS + 1):
                row = t * (SEL * (BITS + 1)) + sel * (BITS + 1) + e
                at0 = (e * SEL + sel) * TASKS
                cut = FROWS // 2
                o_gate[0, pl.ds(row, 1)] = sg[at0 // cut, pl.ds(at0 % cut + t, 1)] * scale
                o_gate[1, pl.ds(row, 1)] = sg[2 + t // 2, pl.ds((t % 2) * GROWS + e * SEL + sel, 1)] * scale
        return carry

    lax.fori_loop(0, TASKS, order, 0)

    lax.fori_loop(4, n - 1, gather_step, 0)
    for d, k in lanes:
        q = holds(d, n - 2)
        ag(d, k, last, landed(d, k, q), q).wait_recv()
        store(d, k, q, landed(d, k, q), n - 1).start()

    def stored(step, carry):
        for d, k in lanes:
            store(d, k, 0, landed(d, k, 0), step).wait()
        return carry

    lax.fori_loop(0, n, stored, 0)

    def sent(step, carry):
        for d, k in lanes:
            rs(d, k, step, a1.at[slot(d, k, step)]).wait_send()
            ag(d, k, step, a1.at[slot(d, k, step)], 0).wait_send()
        return carry

    lax.fori_loop(0, n - 1, sent, 0)
    each(lambda i: scatter(i).wait_send())
    each(lambda i: spread_sum(i).wait_send())
    to_mate.wait_send()
    for e in range(HALF):
        for move in swap(e):
            move.wait_send()
    gates_move.wait_send()
    for e in range(HALF):
        for move in give(e):
            move.wait_send()
    for k in range(2):

        @pl.when(s != 2 + k)
        def _():
            copy(smo, sm.at[s], K_SM + s, 2 + k, K_SM + k).wait_send()
            copy(tin_ref, ti.at[s], K_TI + s, 2 + k, K_TI + k).wait_send()

    @pl.when(x == 0)
    def _():
        for t in range(1, TASKS):
            copy(outbox.at[t], inbox.at[t], K_UP + t, across).wait_send()
        for k, sec in enumerate((mate, across, diag)):
            copy(dp.at[mine], dp.at[mine], K_DP + c, sec, K_DP + k).wait_send()

    @pl.when(x == 1)
    def _():
        copy(pre2, pre1, K_P + 1, across).wait_send()
        for t in range(TASKS):
            copy(outbox.at[t], inbox.at[t], K_DOWN + t, across).wait_send()

            @pl.when(t != s)
            def _():
                copy(tp.at[t], tw.at[c], K_TW + c, t, K_TW + t).wait_send()

    for k, sec in enumerate((mate, across, diag)):
        copy(piece, sg.at[s], K_GO + s, sec, K_GO + k).wait_send()
    for f in range(2):
        pltpu.make_async_copy(xf.at[f], o_ig.at[:, f], local.at[2 + f]).wait()


def hand_over(count, scaled, scale_ref, *refs):
    held = refs[2 * count : 3 * count]
    sems = refs[-1]
    reads = [pltpu.make_async_copy(refs[k], held[k], sems.at[0, k]) for k in range(count)]
    writes = [pltpu.make_async_copy(held[k], refs[count + k], sems.at[1, k]) for k in range(count)]
    order = list(scaled) + [k for k in range(count) if k not in scaled]
    for k in order:
        reads[k].start()
    scale = scale_ref[0:1, 0:1]
    for k in order[len(scaled) :] + order[: len(scaled)]:
        reads[k].wait()
        if k in scaled:

            def one(i, carry):
                rows = pl.ds(pl.multiple_of(i * H, H), H)
                held[k][rows] = held[k][rows] * scale
                return carry

            lax.fori_loop(0, held[k].shape[0] // H, one, 0)
        writes[k].start()
    for move in writes:
        move.wait()


def body(
    field_inputs,
    field_weight,
    norm_gain,
    gate_weight,
    expert_in,
    expert_out,
    tower_in,
    tower_out,
    tower_bias,
    labels,
    source_ids,
    task_table,
):
    n = lax.axis_size("dp")
    rows = field_inputs.shape[0]
    half = rows // 2
    subs = 2
    small_rows = -(-SMALL // (8 * n)) * 8
    used = TASKS * SEL * (BITS + 1)

    vmem = pl.BlockSpec(memory_space=pltpu.VMEM)
    smem = pl.BlockSpec(memory_space=pltpu.SMEM)
    hbm = pl.BlockSpec(memory_space=pl.ANY)

    def bf(*shape):
        return pltpu.VMEM(shape, BF16)

    def f32(*shape):
        return pltpu.VMEM(shape, F32)

    def out(*shape):
        return jax.ShapeDtypeStruct(shape, F32)

    dma = pltpu.SemaphoreType.DMA
    *sums, scale, _ = pl.pallas_call(
        partial(kernel, n, subs, small_rows),
        out_shape=(
            out(1, rows),
            out(rows, 2, D),
            out(1, 2),
            out(1, D),
            out(2, used, D),
            out(HALF * H, D),
            out(HALF * H, D),
            out(D, TOWER),
            out(1, TOWER),
            out(1, 1),
            out(1, TOWER),
            jax.ShapeDtypeStruct((E, 2 * SPILL, H, 2 * half), BF16),
        ),
        in_specs=[hbm, smem, vmem, vmem, hbm, hbm, vmem, vmem, smem, vmem, vmem, smem],
        out_specs=(vmem, hbm, smem, vmem, vmem, hbm, hbm, vmem, vmem, smem, vmem, hbm),
        scratch_shapes=[
            bf(2 * E, H, 2 * D),
            bf(E, D, 2 * H),
            bf(E, H, 2 * D),
            f32(E * H, half),
            f32(E * H, half),
            f32(E * H, D),
            f32(E * H, D),
            bf(E, H, 2 * half),
            bf(E, H, 2 * half),
            bf(2, H, 2 * half),
            f32(2, HALF * H, D),
            f32(2, rows, D),
            f32(rows, D),
            f32(half, D),
            f32(half, D),
            f32(half, D),
            f32(half, D),
            f32(TASKS, D, half),
            f32(TASKS, D, half),
            bf(3 * D, half),
            bf(TASKS, 3 * half, D),
            bf(3 * D, half),
            bf(TASKS, 3 * half, D),
            f32(2, H, half),
            f32(D, half),
            f32(TASKS * GROWS, D),
            f32(E, 1, half),
            f32(E, TASKS, half),
            f32(FROWS, half),
            f32(E, TASKS, half),
            f32(TASKS * GROWS, D),
            f32(2 * GROWS, D),
            f32(TASKS, 8, rows),
            f32(8, rows),
            f32(TASKS, D, TOWER),
            f32(TASKS, TOWER + 8, D),
            f32(2, TOWER + 8, D),
            f32(rows, D),
            f32(8, D),
            f32(half, E * TASKS),
            bf(3 * D, half),
            f32(E, 1, half),
            f32(GROWS, half),
            f32(D, half),
            f32(D, half),
            bf(TASKS, TOWER, 3 * D),
            bf(TASKS, D, 3 * TOWER),
            f32(TASKS, TOWER, half),
            f32(TASKS * GROWS, half),
            f32(D, half),
            f32(2 * TOWER, half),
            f32(n * small_rows, D),
            f32(n, small_rows, D),
            f32(small_rows, D),
            f32(n * small_rows, D),
            f32(TASKS, KEPT, D),
            dma((K_COUNT,)),
            dma((K_COUNT,)),
            dma((6,)),
            dma((AHEAD + 1,)),
            pltpu.SemaphoreType.REGULAR,
            pltpu.SemaphoreType.REGULAR,
            dma((2, subs, n - 1)),
            dma((2, subs, n - 1)),
            dma((2, subs, n - 1)),
            dma((2, subs, n - 1)),
            dma((2, subs, n)),
            dma((n,)),
            dma((n,)),
            dma((n,)),
            dma((n,)),
        ],
        compiler_params=pltpu.CompilerParams(
            collective_id=0, has_side_effects=True, vmem_limit_bytes=64 * 1024 * 1024 - 65536
        ),
    )(
        field_inputs,
        field_weight.reshape(1, 2),
        norm_gain.reshape(1, D),
        gate_weight.swapaxes(1, 2),
        expert_in.reshape(HALF * H, D),
        expert_out.reshape(HALF * H, D),
        tower_in.reshape(D, TOWER),
        tower_out,
        tower_bias.reshape(1, 1),
        labels.reshape(1, rows),
        source_ids.reshape(1, rows),
        task_table.reshape(1, SOURCES),
    )
    pred, ig, fw, gain, gate, d_in, d_out, tin, tout, bias = pl.pallas_call(
        partial(hand_over, len(sums), (5, 6)),
        out_shape=tuple(jax.ShapeDtypeStruct(v.shape, v.dtype) for v in sums),
        in_specs=[vmem] + [hbm] * len(sums),
        out_specs=(hbm,) * len(sums),
        scratch_shapes=[pltpu.VMEM(v.shape, v.dtype) for v in sums] + [dma((2, len(sums)))],
        compiler_params=pltpu.CompilerParams(vmem_limit_bytes=64 * 1024 * 1024 - 65536),
    )(scale, *sums)
    return (
        pred.reshape(rows, 1),
        ig,
        fw.reshape(2),
        gain.reshape(D),
        gate.swapaxes(1, 2),
        d_in.reshape(HALF, D, H),
        d_out.reshape(HALF, H, D),
        tin.reshape(1, D, TOWER),
        tout,
        bias.reshape(1),
    )


def solution(mesh):
    in_specs = (
        P("dp", "section", None),
        P("section"),
        P(),
        P(),
        P("section", None, None),
        P("section", None, None),
        P("section", None, None),
        P("section", None),
        P("section"),
        P("dp", "section"),
        P("dp"),
        P(None, "section"),
    )
    out_specs = (
        P("dp", "section"),
        P("dp", "section", None),
        P("section"),
        P(),
        P(),
        P("section", None, None),
        P("section", None, None),
        P("section", None, None),
        P("section", None),
        P("section"),
    )
    return jax.shard_map(body, mesh=mesh, in_specs=in_specs, out_specs=out_specs, check_vma=False)
```

```python
from functools import partial

import jax
import jax.numpy as jnp
from jax import lax
from jax.experimental import pallas as pl
from jax.experimental.pallas import tpu as pltpu
from jax.sharding import PartitionSpec as P

D = 256
H = 256
E = 16
TASKS = 4
SEL = 4
BITS = 4
TOWER = 128
SOURCES = 32
HALF = E // 2
GROWS = 32
FROWS = 96

STEP_SLOPE = 0.6
ENTROPY_WEIGHT = 0.05
NORM_EPS = 1e-05
GELU_A = 0.7978845608028654
GELU_B = 0.044715

F32 = jnp.float32
BF16 = jnp.bfloat16
MESH = pl.DeviceIdType.MESH

K_W, K_P, K_SM, K_TI, K_UP, K_DOWN, K_TW, K_DG, K_DP, K_GO, K_DX = 0, 2, 4, 8, 12, 16, 20, 24, 25, 28, 32
K_COUNT = 48
TILE = 32
SPILL = TASKS - 1
AHEAD = 3

GATE_AT = TOWER
MISC_AT = GATE_AT + 2 * GROWS
SMALL = MISC_AT + 8
KEPT = SMALL - GATE_AT


def split(x):
    hi = x.astype(BF16)
    return hi, (x - hi.astype(F32)).astype(BF16)


def wide(x):
    hi, lo = split(x)
    return jnp.concatenate([hi, lo, hi], axis=1)


def tall(x):
    hi, lo = split(x)
    return jnp.concatenate([hi, hi, lo], axis=0)


def put(ref, at, x):
    k = x.shape[1]
    hi, lo = split(x)
    ref[*at, :k] = hi
    ref[*at, k:] = lo


def stack(x):
    k = x.shape[1] // 2
    return jnp.concatenate([x[:, :k], x[:, :k], x[:, k:]], axis=0)


def mm(a, b):
    return jnp.dot(a, b, preferred_element_type=F32)


def pair(x):
    k = x.shape[1] // 2
    return jnp.concatenate([x, x[:, :k]], axis=1)


def gelu_pair(x):
    x2 = x * x
    h = 0.5 + 0.5 * jnp.tanh(x * (GELU_A + (GELU_A * GELU_B) * x2))
    g = x * h
    slope = h + g * (1.0 - h) * (2.0 * GELU_A + (6.0 * GELU_A * GELU_B) * x2)
    return g, slope


def rows8(x):
    return jnp.sum(x.reshape(x.shape[0] // 8, 8, x.shape[1]), axis=0)


def over_selectors(v, groups, op):
    parts = [v[k * groups : (k + 1) * groups] for k in range(SEL)]
    return op(op(parts[0], parts[1]), op(parts[2], parts[3]))


def to_selectors(v):
    return jnp.concatenate([v] * SEL, axis=0)


def gate_state(c, groups):
    w = SEL * groups
    zs = [c[w * b : w * b + w] * STEP_SLOPE for b in range(BITS)]
    alpha = c[w * BITS : w * BITS + w]
    ups, downs, sig_p, sig_n = [], [], [], []
    for z in zs:
        e = jnp.exp(-jnp.abs(z))
        tail = jnp.log1p(e)
        ups.append(jnp.minimum(z, 0.0) - tail)
        downs.append(jnp.minimum(-z, 0.0) - tail)
        big = 1.0 / (1.0 + e)
        small = e * big
        sig_p.append(jnp.where(z >= 0.0, big, small))
        sig_n.append(jnp.where(z >= 0.0, small, big))
    low = [(ups[0] if k & 1 else downs[0]) + (ups[1] if k & 2 else downs[1]) for k in range(4)]
    high = [(ups[2] if k & 1 else downs[2]) + (ups[3] if k & 2 else downs[3]) for k in range(4)]
    log_r = [low[j & 3] + high[j >> 2] for j in range(E)]
    r = [jnp.exp(v) for v in log_r]
    top = jnp.exp(alpha - to_selectors(over_selectors(alpha, groups, jnp.maximum)))
    mix = top / to_selectors(over_selectors(top, groups, jnp.add))
    return log_r, r, mix, sig_p, sig_n


def gate_forward(c, groups):
    _, r, mix, _, _ = gate_state(c, groups)
    return [over_selectors(mix * v, groups, jnp.add) for v in r]


def gate_backward(c, dgate, groups, out):
    log_r, r, mix, sig_p, sig_n = gate_state(c, groups)
    yield
    total = jnp.zeros_like(mix)
    on = [jnp.zeros_like(mix) for _ in range(BITS)]
    off = [jnp.zeros_like(mix) for _ in range(BITS)]
    for j in range(E):
        dg = to_selectors(dgate(j))
        total = total + dg * r[j]
        dlog = r[j] * (mix * dg - ENTROPY_WEIGHT * (log_r[j] + 1.0))
        for b in range(BITS):
            if j >> b & 1:
                on[b] = on[b] + dlog
            else:
                off[b] = off[b] + dlog
        yield
    dalpha = mix * (total - to_selectors(over_selectors(mix * total, groups, jnp.add)))
    dz = [STEP_SLOPE * (on[b] * sig_n[b] - off[b] * sig_p[b]) for b in range(BITS)]
    used = SEL * (BITS + 1) * groups
    pad = jnp.zeros(((-used) % GROWS, c.shape[1]), F32)
    out.append(jnp.concatenate(dz + [dalpha, pad], axis=0))
    yield


def t_dot(a, b):
    ah, al = split(a)
    left = jnp.concatenate([ah, al, ah], axis=0)
    return lax.dot_general(left, tall(b), (((0,), (0,)), ((), ())), preferred_element_type=F32)


def weave(count, first, middle, last, extra=()):
    extra = iter(extra)
    for step in range(count + 2):
        if step < count:
            first(step, step % 2)
        next(extra, None)
        if 0 <= step - 1 < count:
            middle(step - 1, (step - 1) % 2, 0)
        next(extra, None)
        if step >= 2:
            last(step - 2, step % 2)
        next(extra, None)
        if 0 <= step - 1 < count:
            middle(step - 1, (step - 1) % 2, 1)
        next(extra, None)
    for _ in extra:
        pass


def halves(size):
    tiles = [slice(a, a + TILE) for a in range(0, size, TILE)]
    return tiles[: len(tiles) // 2], tiles[len(tiles) // 2 :]


def kernel(
    n,
    subs,
    small_rows,
    x_ref,
    fw_ref,
    gain_ref,
    gate_ref,
    win_ref,
    wout_ref,
    tin_ref,
    tout_ref,
    tbias_ref,
    labels_ref,
    ids_ref,
    table_ref,
    o_pred,
    o_ig,
    o_fw,
    o_gain,
    o_gate,
    o_in,
    o_out,
    o_tin,
    o_tout,
    o_bias,
    kept,
    wt,
    w_in,
    w_out,
    a1,
    a2,
    d_in,
    d_out,
    gbuf,
    kbuf,
    kp,
    rd,
    xf,
    part,
    pre0,
    pre1,
    pre2,
    pre,
    inbox,
    outbox,
    u_t,
    u_n,
    s_t,
    s_n,
    bb,
    acc,
    wg,
    gt,
    gt0,
    cs,
    dgt,
    dg,
    gb,
    sm,
    smo,
    ti,
    tp,
    tw,
    dp,
    gain_row,
    columns,
    u_next,
    gt_next,
    cs_next,
    acc_b,
    dy_kept,
    held,
    tm,
    sb,
    sr,
    so,
    sa,
    sg,
    send,
    recv,
    local,
    fetch_sem,
    ready,
    rs_send,
    rs_recv,
    ag_send,
    ag_recv,
    store_sem,
    sr_send,
    sr_recv,
    sa_send,
    sa_recv,
):
    s = lax.axis_index("section")
    x = s // 2
    c = s % 2
    mate = s + 1 - 2 * c
    across = s + 2 - 4 * x
    diag = 3 - s
    R = part.shape[0] // 2
    mine = pl.ds(pl.multiple_of(c * R, R), R)
    theirs = pl.ds(pl.multiple_of((1 - c) * R, R), R)

    me = lax.axis_index("dp")
    odd = me % 2
    p = (1 - odd) * (me // 2) + odd * (n - 1 - me // 2)

    def ring_id(q):
        far = q // (n // 2)
        return (1 - far) * 2 * q + far * (2 * (n - 1 - q) + 1)

    nbr = [ring_id((p + 1) % n), ring_id((p + n - 1) % n)]

    barrier = pltpu.get_barrier_semaphore()
    for sec in (mate, across, diag):
        pl.semaphore_signal(barrier, inc=1, device_id={"section": sec}, device_id_type=MESH)

    def greet(i, carry):
        pl.semaphore_signal(barrier, inc=1, device_id={"dp": (me + i) % n}, device_id_type=MESH)
        return carry

    lax.fori_loop(1, n, greet, 0)
    fields = [pltpu.make_async_copy(x_ref.at[:, f], xf.at[f], local.at[2 + f]) for f in range(2)]
    for f in fields:
        f.start()
    own = pl.ds(pl.multiple_of(c * HALF * H, HALF * H), HALF * H)
    own_in = pltpu.make_async_copy(win_ref, d_in.at[own], local.at[0])
    own_out = pltpu.make_async_copy(wout_ref, d_out.at[own], local.at[1])
    own_in.start()
    own_out.start()
    pl.semaphore_wait(barrier, 3 + n - 1)

    def copy(src, dst, k, sec, ks=None):
        return pltpu.make_async_remote_copy(
            src_ref=src,
            dst_ref=dst,
            send_sem=send.at[k if ks is None else ks],
            recv_sem=recv.at[k],
            device_id={"section": sec},
            device_id_type=MESH,
        )

    def expert(j, count=1):
        return pl.ds(pl.multiple_of(j * H, H), count * H)

    for f in fields:
        f.wait()
    part[...] = xf[0] * fw_ref[0, 0] + xf[1] * fw_ref[0, 1]
    to_mate = copy(part.at[theirs], pre0, K_P, mate)
    to_mate.start()
    swap_in = copy(d_in.at[own], d_in.at[own], K_W, mate)
    swap_out = copy(d_out.at[own], d_out.at[own], K_W + 1, mate)
    own_in.wait()
    swap_in.start()
    own_out.wait()
    swap_out.start()

    ids = ids_ref[...]
    mask = jnp.zeros(ids.shape, F32)
    for q in range(SOURCES):
        mask = mask + jnp.where(ids == q, table_ref[0, q].astype(F32), 0.0)
    smo[...] = jnp.zeros_like(smo)
    smo[0:1] = labels_ref[...]
    smo[1:2] = mask
    smo[2:3, :TOWER] = tout_ref[...]
    smo[3:4] = jnp.zeros((1, 2 * R), F32) + tbias_ref[0, 0]
    for k in range(2):

        @pl.when(s != 2 + k)
        def _():
            copy(smo, sm.at[s], K_SM + s, 2 + k, K_SM + k).start()
            copy(tin_ref, ti.at[s], K_TI + s, 2 + k, K_TI + k).start()

    to_mate.wait_recv()

    @pl.when(x == 1)
    def _():
        pre2[...] = part[mine] + pre0[...]
        copy(pre2, pre1, K_P + 1, across).start()
        sm[s] = smo[...]
        ti[s] = tin_ref[...]

    wg[...] = jnp.zeros_like(wg)

    @pl.when(x == 0)
    def _():
        def order(t, carry):
            for sel in range(SEL):
                for e in range(BITS + 1):
                    row = t * (SEL * (BITS + 1)) + sel * (BITS + 1) + e
                    wg[pl.ds((e * SEL + sel) * TASKS + t, 1)] = gate_ref[0, pl.ds(row, 1)]
            return carry

        lax.fori_loop(0, TASKS, order, 0)

    @pl.when(x == 1)
    def _():
        def order(t, carry):
            for sel in range(SEL):
                for e in range(BITS + 1):
                    row = t * (SEL * (BITS + 1)) + sel * (BITS + 1) + e
                    wg[pl.ds(t * GROWS + e * SEL + sel, 1)] = gate_ref[1, pl.ds(row, 1)]
            return carry

        lax.fori_loop(0, TASKS, order, 0)

    def keep_plain(e, carry):
        put(w_in.at[e], (slice(None),), d_in[expert(e)])
        put(w_out.at[e], (slice(None),), d_out[expert(e)])
        return carry

    def keep_flipped(e, carry):
        put(wt.at[e], (slice(None),), d_in[expert(e)].T)
        put(wt.at[E + e], (slice(None),), d_out[expert(e)].T)
        return carry

    lax.fori_loop(c * HALF, c * HALF + HALF, keep_plain, 0)
    swap_in.wait()
    swap_out.wait()
    lax.fori_loop((1 - c) * HALF, (1 - c) * HALF + HALF, keep_plain, 0)

    def rows_of(size):
        return [slice(a, a + TILE) for a in range(0, size, TILE)]

    def shifted(tile, e):
        return slice(e * H + tile.start, e * H + tile.stop)

    chunk = HALF * H // n
    sub = chunk // subs
    lanes = [(d, k) for d in range(2) for k in range(subs)]

    def at(k, q):
        return pl.ds(pl.multiple_of(q * chunk + k * sub, 8), sub)

    def holds(d, step):
        return (p + n - step) % n if d == 0 else (p + step) % n

    def slot(d, k, step):
        return pl.ds(pl.multiple_of(((d * subs + k) * (n - 1) + step) * sub, 8), sub)

    def rs(d, k, step, src):
        return pltpu.make_async_remote_copy(
            src_ref=src,
            dst_ref=a1.at[slot(d, k, step)],
            send_sem=rs_send.at[d, k, step],
            recv_sem=rs_recv.at[d, k, step],
            device_id={"dp": nbr[d]},
            device_id_type=MESH,
        )

    results = (o_in, o_out)

    def landed(d, k, q):
        return a2.at[pl.ds(pl.multiple_of(d * HALF * H + q * chunk + k * sub, 8), sub)]

    def store(d, k, q, src, step):
        return pltpu.make_async_copy(src, results[d].at[at(k, q)], store_sem.at[d, k, step])

    def ag(d, k, step, src, q):
        return pltpu.make_async_remote_copy(
            src_ref=src,
            dst_ref=landed(d, k, q),
            send_sem=ag_send.at[d, k, step],
            recv_sem=ag_recv.at[d, k, step],
            device_id={"dp": nbr[d]},
            device_id_type=MESH,
        )

    def give(e):
        j = (1 - c) * HALF + e
        return (
            copy(d_in.at[expert(j)], rd.at[0, expert(e)], K_DX + e, mate),
            copy(d_out.at[expert(j)], rd.at[1, expert(e)], K_DX + HALF + e, mate),
        )

    start_at = p * chunk // H

    def near(k):
        return (start_at + HALF + ((k + 1) // 2) * (1 - 2 * (k % 2))) % HALF

    def turn_of(i):
        own_turn = i % 2
        return ((1 - own_turn) * (1 - c) + own_turn * c) * HALF + near(i // 2)

    def fetch(i):
        at = pl.ds((i % (AHEAD + 1)) * 8, 2 * SPILL)
        return pltpu.make_async_copy(kept.at[turn_of(i)], wt.at[at], fetch_sem.at[i % (AHEAD + 1)])

    def fetch_start(i):
        for k in range(2 * SPILL):
            slab = (i % (AHEAD + 1)) * 8 + k
            pltpu.make_async_copy(
                kept.at[turn_of(i), k], wt.at[slab], fetch_sem.at[i % (AHEAD + 1)]
            ).start()

    def greet_ring():
        for dev in nbr:
            pl.semaphore_signal(ready, inc=1, device_id={"dp": dev}, device_id_type=MESH)

    def merge(k, carry):
        e = near(k)
        for move in give(e):
            move.wait_recv()
        rows = expert(e)
        rd[0, rows] = (rd[0, rows] + d_in[expert(c * HALF + e)]).T
        rd[1, rows] += d_out[expert(c * HALF + e)]
        return carry

    def ring_start():
        pl.semaphore_wait(ready, 2)
        for d, k in lanes:
            rs(d, k, 0, rd.at[d, at(k, holds(d, 0))]).start()

    def reduce_step(step, carry):
        for d, k in lanes:
            rs(d, k, step - 1, a1.at[slot(d, k, step - 1)]).wait_recv()
            a1[slot(d, k, step - 1)] += rd[d, at(k, holds(d, step))]
            rs(d, k, step, a1.at[slot(d, k, step - 1)]).start()
        return carry

    @pl.when(x == 0)
    def _():
        copy(pre2, pre1, K_P + 1, across).wait_recv()
        pre_rows = part[mine] + pre0[...] + pre1[...]
        pre[...] = pre_rows
        rho = lax.rsqrt(jnp.mean(pre_rows * pre_rows, axis=1, keepdims=True) + NORM_EPS)
        pooled = pre_rows * rho * gain_ref[...]
        acc[...] = pooled
        u_n[0] = tall(pooled)
        u_t[...] = tall(pooled.T)
        logits = mm(wide(wg[:FROWS]), u_t[...])
        cs[...] = logits
        gates = gate_forward(logits, TASKS)
        for j, g in enumerate(gates):
            gt0[j] = g

        def first(j, par):
            left = jnp.concatenate([u_n[0, :R], u_n[0, 2 * R :], u_n[0, :R]], axis=1)
            bb[par] = mm(left, stack(w_in[j]))

        def activate(j, par, part_no):
            for tile in halves(R)[part_no]:
                value, slope = gelu_pair(bb[par, tile])
                a1[shifted(tile, j)] = value
                a2[shifted(tile, j)] = slope
                put(gbuf, (j, tile), value)

        def finish(j, par):
            d_in[expert(j)] = mm(pair(gbuf[j]), stack(w_out[j]))

        weave(E, first, activate, finish)
        columns[...] = jnp.concatenate(gates, axis=0).T

        for t in range(TASKS):

            def mix(i, carry):
                tile = pl.ds(pl.multiple_of(i * TILE, TILE), TILE)
                cols = columns[tile]
                total = acc[tile]
                for j in range(E):
                    rows = pl.ds(pl.multiple_of(j * R + i * TILE, TILE), TILE)
                    total = total + cols[:, j * TASKS + t : j * TASKS + t + 1] * d_in[rows]
                outbox[t, tile] = total
                return carry

            lax.fori_loop(0, R // TILE, mix, 0)
            copy(outbox.at[t], inbox.at[t], K_UP + t, across).start()

        def flip(j, carry):
            put(gbuf.at[j], (slice(None),), a1[expert(j)].T)
            a2[expert(j)] = a2[expert(j)].T
            d_in[expert(j)] = d_in[expert(j)].T
            return carry

        lax.fori_loop(0, E, flip, 0)
        greet_ring()
        d_out[...] = jnp.zeros_like(d_out)
        acc[...] = jnp.zeros_like(acc)

    @pl.when(x == 1)
    def _():
        lax.fori_loop(0, E, keep_flipped, 0)
        for q in range(TASKS):

            @pl.when(s != q)
            def _():
                copy(smo, sm.at[q], K_SM + q, q).wait_recv()
                copy(tin_ref, ti.at[q], K_TI + q, q).wait_recv()

        def keep(k, t):
            return pltpu.make_async_copy((gbuf, kbuf)[k], kept.at[:, k * SPILL + t], local.at[4 + k])

        def keep_start(k, t):
            def one(j, carry):
                pltpu.make_async_copy((gbuf, kbuf)[k].at[j], kept.at[j, k * SPILL + t], local.at[4 + k]).start()
                return carry

            @pl.when(t < SPILL)
            def _():
                lax.fori_loop(0, E, one, 0)

        def gate_rows(t):
            return pl.ds(pl.multiple_of(t * GROWS, GROWS), GROWS)

        def enter(t):
            for k in range(2):
                cols = slice(k * (R // 2), (k + 1) * (R // 2))
                flipped = inbox[t, cols].T
                hi, lo = split(flipped)
                u_next[:D, cols] = hi
                u_next[D : 2 * D, cols] = hi
                u_next[2 * D :, cols] = lo
                acc[:, cols] = flipped
                yield
            logits = mm(wide(wg[gate_rows(t)]), u_next[...])
            cs_next[...] = logits
            yield
            u_n[t] = tall(inbox[t])
            yield
            _, r, mix, _, _ = gate_state(logits, 1)
            yield
            for j in range(E):
                gt_next[j] = over_selectors(mix * r[j], 1, jnp.add)
                yield

        def turn():
            u_t[...] = u_next[...]
            gt[...] = gt_next[...]
            cs[GROWS : 2 * GROWS] = cs[:GROWS]
            cs[:GROWS] = cs_next[...]

        def leave(t, at):
            out = []
            yield from gate_backward(cs[at : at + GROWS], lambda j: dgt[j, 0:1], 1, out)
            outbox[t] = acc_b[...] + t_dot(wg[gate_rows(t)], out[0])
            yield
            dg[gate_rows(t)] = mm(wide(out[0]), u_n[t])
            yield

        def all_of(pieces):
            for _ in pieces:
                pass

        cs[...] = jnp.zeros_like(cs)
        dgt[...] = jnp.zeros_like(dgt)
        acc_b[...] = jnp.zeros_like(acc_b)
        copy(outbox.at[0], inbox.at[0], K_UP, across).wait_recv()
        all_of(enter(0))
        turn()

        def task(t, carry):
            @pl.when(t > 0)
            def _():
                keep(0, 0).wait()

            def first(j, par):
                bb[par] = mm(pair(wt[j]), u_t[...])

            def activate(j, par, part_no):
                for tile in halves(H)[part_no]:
                    value, slope = gelu_pair(bb[par, tile])
                    a1[shifted(tile, j)] = value
                    a2[shifted(tile, j)] = slope
                    put(gbuf, (j, tile), value * gt[j])

            def finish(j, par):
                acc[...] += mm(pair(wt[E + j]), stack(gbuf[j]))

            before = (t + TASKS - 1) % TASKS
            weave(E, first, activate, finish, leave(before, GROWS))
            keep_start(0, t)

            @pl.when(t > 0)
            def _():
                copy(outbox.at[before], inbox.at[before], K_DOWN + before, across).start()

            second = acc[...]
            held[...] = second
            tower = ti[t]
            g, slope = gelu_pair(mm(wide(tower.T), tall(second)))
            info = sm[t]
            out_col = info[:, :TOWER].T[:, 2:3]
            here = sm[t, :, mine]
            logit = jnp.sum(g * out_col, axis=0, keepdims=True) + here[3:4]
            prob = jax.nn.sigmoid(logit)
            dlogit = here[1:2] * (prob - here[0:1])
            m = dlogit * out_col * slope
            dy = mm(wide(tower), tall(m))
            s_t[...] = tall(dy)
            acc_b[...] = dy
            dy_kept[...] = dy
            tm[:TOWER] = m
            tm[TOWER:] = g * dlogit
            tp[t, TOWER : TOWER + 1] = prob
            tp[t, TOWER + 2 : TOWER + 3] = dlogit
            tp[t, TOWER + 3 :] = jnp.zeros((5, R), F32)

            @pl.when(t > 0)
            def _():
                keep(1, 0).wait()

            @pl.when(t == TASKS - 1)
            def _():
                for i in range(AHEAD):
                    fetch_start(i)

            after = jnp.minimum(t + 1, TASKS - 1)

            @pl.when(t < TASKS - 1)
            def _():
                copy(outbox.at[after], inbox.at[after], K_UP + after, across).wait_recv()

            def back(j, par):
                bb[par] = mm(pair(w_out[j]), s_t[...])

            def pull(j, par, part_no):
                total = jnp.zeros((8, R), F32)
                for tile in halves(H)[part_no]:
                    grad = bb[par, tile]
                    total = total + rows8(grad * a1[shifted(tile, j)])
                    put(kbuf, (j, tile), grad * a2[shifted(tile, j)] * gt[j])
                total = jnp.sum(total, axis=0, keepdims=True)
                if part_no == 0:
                    dgt[j, 0:1] = total
                else:
                    dgt[j, 0:1] += total

            def spread(j, par):
                acc_b[...] += mm(pair(w_in[j]), stack(kbuf[j]))

            def beside():
                s_n[t] = tall(dy_kept[...].T)
                yield
                yield from enter(after)
                flipped = tall(held[...].T)
                yield
                tp[t, :TOWER] = mm(wide(tm[:TOWER]), flipped)
                yield
                out_grad = jnp.sum(tm[TOWER:], axis=1, keepdims=True)
                out_row = jnp.broadcast_to(out_grad, (TOWER, TOWER)).T[0:1]
                tp[t, TOWER + 1 : TOWER + 2] = jnp.concatenate([out_row, jnp.zeros_like(out_row)], axis=1)
                yield

            weave(E, back, pull, spread, beside())
            keep_start(1, t)
            turn()

            @pl.when(t != s)
            def _():
                copy(tp.at[t], tw.at[c], K_TW + c, t, K_TW + t).start()

            @pl.when(t == s)
            def _():
                tw[c] = tp[t]

            return carry

        lax.fori_loop(0, TASKS, task, 0)
        last_task = TASKS - 1
        all_of(leave(last_task, GROWS))
        copy(outbox.at[last_task], inbox.at[last_task], K_DOWN + last_task, across).start()
        greet_ring()

    @pl.when(x == 1)
    def _():
        def one(i, carry):
            fetch(i).wait()

            @pl.when(i < E - AHEAD)
            def _():
                fetch_start(i + AHEAD)

            j = turn_of(i)
            slot_at = (i % (AHEAD + 1)) * 8
            for k, (grad, right, here) in enumerate(((d_out, s_n, gbuf), (d_in, u_n, kbuf))):
                left = [pair(wt[slot_at + k * SPILL + t]) for t in range(SPILL)] + [pair(here[j])]
                grad[expert(j)] = mm(jnp.concatenate(left, axis=1), right[...].reshape(3 * TASKS * R, D))

            @pl.when(i % 2 == 0)
            def _():
                for move in give(near(i // 2)):
                    move.start()

            @pl.when(i == 3)
            def _():
                merge(0, 0)
                ring_start()

            @pl.when((i % 2 == 1) & (i > 3))
            def _():
                merge((i - 3) // 2, 0)

            if n == HALF:

                @pl.when((i % 4 == 3) & (i > 3))
                def _():
                    reduce_step((i - 3) // 4, 0)

            return carry

        lax.fori_loop(0, E, one, 0)
        merge(HALF - 1, 0)
        if n != HALF:
            lax.fori_loop(1, 4, reduce_step, 0)

    @pl.when(x == 0)
    def _():
        def arrive(t, carry):
            copy(outbox.at[t], inbox.at[t], K_DOWN + t, across).wait_recv()
            acc[...] += inbox[t]

            def one(j, inner):
                gate = gt0[j, pl.ds(t, 1)]
                total = jnp.zeros((8, R), F32)
                for tile in rows_of(D):
                    dy = inbox[t, tile]
                    rows = pl.ds(pl.multiple_of(j * D + tile.start, TILE), TILE)
                    total = total + rows8(d_in[rows] * dy)
                    d_out[rows] += gate * dy
                dgt[j, pl.ds(t, 1)] = jnp.sum(total, axis=0, keepdims=True)
                return inner

            lax.fori_loop(0, E, one, 0)
            return carry

        lax.fori_loop(0, TASKS - 1, arrive, 0)
        last = TASKS - 1
        copy(outbox.at[last], inbox.at[last], K_DOWN + last, across).wait_recv()
        acc[...] += inbox[last]

        def one(i, inner):
            j = turn_of(i)
            gate = gt0[j, last : last + 1]
            total = jnp.zeros((8, R), F32)
            for tile in rows_of(D):
                dy = inbox[last, tile]
                rows = pl.ds(pl.multiple_of(j * D + tile.start, TILE), TILE)
                total = total + rows8(d_in[rows] * dy)
                put(kbuf.at[j], (tile,), d_out[rows] + gate * dy)
            dgt[j, last : last + 1] = jnp.sum(total, axis=0, keepdims=True)
            return inner

        def part_of(first, stop):
            lax.fori_loop(2 * first, 2 * stop, one, 0)

            def products(i, par):
                j = turn_of(2 * first + i)
                mixed = kbuf[j]
                bb[par] = mm(pair(w_out[j]), stack(mixed))
                right = jnp.concatenate([mixed[:, :R], mixed[:, :R], mixed[:, R:]], axis=1)
                d_out[expert(j)] = lax.dot_general(
                    pair(gbuf[j]), right, (((1,), (1,)), ((), ())), preferred_element_type=F32
                )

            def pull(i, par, part_no):
                j = turn_of(2 * first + i)
                for tile in halves(H)[part_no]:
                    kept_rows = pl.ds(pl.multiple_of(j * H + tile.start, TILE), TILE)
                    put(kp, (par, tile), bb[par, tile] * a2[kept_rows])

            def spread(i, par):
                j = turn_of(2 * first + i)
                acc[...] += mm(pair(w_in[j]), stack(kp[par]))
                d_in[expert(j)] = mm(pair(kp[par]), u_n[0])

            weave(2 * (stop - first), products, pull, spread)
            for k in range(first, stop):
                for move in give(near(k)):
                    move.start()

        part_of(0, 1)
        part_of(1, 4)
        merge(0, 0)
        ring_start()
        part_of(4, HALF)
        lax.fori_loop(1, HALF, merge, 0)
        lax.fori_loop(1, 2, reduce_step, 0)

    gates_own = pl.ds(pl.multiple_of(c * 2 * GROWS, 2 * GROWS), 2 * GROWS)
    gates_away = pl.ds(pl.multiple_of((1 - c) * 2 * GROWS, 2 * GROWS), 2 * GROWS)
    gain_row[...] = jnp.zeros_like(gain_row)

    @pl.when(x == 0)
    def _():
        out = []
        for _ in gate_backward(cs[...], lambda j: dgt[j, :TASKS], TASKS, out):
            pass
        dc = out[0]
        dpool = (acc[...] + t_dot(wg[:FROWS], dc)).T
        pre_rows = pre[...]
        rho = lax.rsqrt(jnp.mean(pre_rows * pre_rows, axis=1, keepdims=True) + NORM_EPS)
        scaled = dpool * gain_ref[...]
        dots = jnp.mean(scaled * pre_rows, axis=1, keepdims=True)
        dp[mine] = rho * scaled - pre_rows * (rho * rho * rho * dots)
        for k, sec in enumerate((mate, across, diag)):
            copy(dp.at[mine], dp.at[mine], K_DP + c, sec, K_DP + k).start()
        gain_row[0:1] = jnp.sum(dpool * pre_rows * rho, axis=0, keepdims=True)
        grad = mm(wide(dc), u_n[0])
        dg[: FROWS // 2] = grad[: FROWS // 2]
        dg[2 * GROWS : 2 * GROWS + FROWS // 2] = grad[FROWS // 2 :]

    gates_move = copy(dg.at[gates_away], gb, K_DG, mate)
    gates_move.start()

    @pl.when(x == 0)
    def _():
        lax.fori_loop(2, 4, reduce_step, 0)

    for half_no in range(2):

        @pl.when(s != half_no)
        def _():
            rows = pl.ds(half_no * R, R)
            copy(dp.at[rows], dp.at[rows], K_DP + half_no, half_no).wait_recv()

    for k in range(2):

        @pl.when(s != 2 + k)
        def _():
            copy(tp.at[0], tw.at[k], K_TW + k, s).wait_recv()

    gates_move.wait_recv()
    sb[:TOWER] = tw[0, :TOWER] + tw[1, :TOWER]
    sb[GATE_AT:MISC_AT] = dg[gates_own] + gb[...]
    sb[MISC_AT : MISC_AT + 1] = gain_row[0:1]
    sb[MISC_AT + 1 : MISC_AT + 3] = tw[0, TOWER + 1 : TOWER + 3] + tw[1, TOWER + 1 : TOWER + 3]
    for f in range(2):
        sb[MISC_AT + 3 + f : MISC_AT + 4 + f] = jnp.sum(xf[f] * dp[...], axis=0, keepdims=True)
    sb[MISC_AT + 5 : MISC_AT + 6] = smo[1:2, :R] + smo[1:2, R:]
    sb[MISC_AT + 6 :] = jnp.zeros((sb.shape[0] - MISC_AT - 6, D), F32)

    def block(q):
        return pl.ds(pl.multiple_of(q * small_rows, 8), small_rows)

    def scatter(i):
        to = (me + i) % n
        return pltpu.make_async_remote_copy(
            src_ref=sb.at[block(to)],
            dst_ref=sr.at[me],
            send_sem=sr_send.at[i],
            recv_sem=sr_recv.at[me],
            device_id={"dp": to},
            device_id_type=MESH,
        )

    def scattered(i):
        by = (me + i) % n
        return pltpu.make_async_remote_copy(
            src_ref=sb.at[block(me)],
            dst_ref=sr.at[by],
            send_sem=sr_send.at[i],
            recv_sem=sr_recv.at[by],
            device_id={"dp": by},
            device_id_type=MESH,
        )

    def spread_sum(i):
        return pltpu.make_async_remote_copy(
            src_ref=so,
            dst_ref=sa.at[block(me)],
            send_sem=sa_send.at[i],
            recv_sem=sa_recv.at[me],
            device_id={"dp": (me + i) % n},
            device_id_type=MESH,
        )

    def gathered(i):
        by = (me + i) % n
        return pltpu.make_async_remote_copy(
            src_ref=so,
            dst_ref=sa.at[block(by)],
            send_sem=sa_send.at[i],
            recv_sem=sa_recv.at[by],
            device_id={"dp": by},
            device_id_type=MESH,
        )

    def each(act):
        def one(i, carry):
            act(i)
            return carry

        lax.fori_loop(1, n, one, 0)

    each(lambda i: scatter(i).start())
    lax.fori_loop(4, 5, reduce_step, 0)
    so[...] = sb[block(me)]

    def take(i):
        scattered(i).wait_recv()
        so[...] += sr[(me + i) % n]

    each(take)
    sa[block(me)] = so[...]
    each(lambda i: spread_sum(i).start())
    lax.fori_loop(5, 6, reduce_step, 0)
    each(lambda i: gathered(i).wait_recv())
    piece = sa.at[pl.ds(GATE_AT, KEPT)]
    for k, sec in enumerate((mate, across, diag)):
        copy(piece, sg.at[s], K_GO + s, sec, K_GO + k).start()
    sg[s] = sa[GATE_AT:SMALL]
    lax.fori_loop(6, n - 1, reduce_step, 0)
    for sec in (mate, across, diag):
        copy(piece, sg.at[sec], K_GO + sec, sec).wait_recv()
    misc = KEPT - 8
    count = sum(sg[q, misc + 5 : misc + 6] for q in range(TASKS))
    scale = float(2 * R * n) / jnp.sum(count, axis=1, keepdims=True)

    last = n - 2
    for d, k in lanes:
        q = holds(d, n - 1)
        rs(d, k, last, a1.at[slot(d, k, last)]).wait_recv()
        a1[slot(d, k, last)] = (a1[slot(d, k, last)] + rd[d, at(k, q)]) * scale
        ag(d, k, 0, a1.at[slot(d, k, last)], q).start()
        store(d, k, q, a1.at[slot(d, k, last)], 0).start()

    for f in range(2):
        xf[f] = dp[...] * (scale * fw_ref[0, f])
        pltpu.make_async_copy(xf.at[f], o_ig.at[:, f], local.at[2 + f]).start()
    for k in range(2):
        o_pred[:, k * R : (k + 1) * R] = tw[k, TOWER : TOWER + 1]
    for f in range(2):
        o_fw[0, f] = jnp.sum(sa[MISC_AT + 3 + f : MISC_AT + 4 + f] * scale)
    o_bias[0, 0] = jnp.sum(sa[MISC_AT + 2 : MISC_AT + 3] * scale)
    o_gain[...] = (sg[0, misc : misc + 1] + sg[1, misc : misc + 1]) * scale
    o_tout[...] = sa[MISC_AT + 1 : MISC_AT + 2, :TOWER] * scale
    o_tin[...] = (sa[:TOWER] * scale).T

    def order(t, carry):
        for sel in range(SEL):
            for e in range(BITS + 1):
                row = t * (SEL * (BITS + 1)) + sel * (BITS + 1) + e
                at0 = (e * SEL + sel) * TASKS
                cut = FROWS // 2
                o_gate[0, pl.ds(row, 1)] = sg[at0 // cut, pl.ds(at0 % cut + t, 1)] * scale
                o_gate[1, pl.ds(row, 1)] = sg[2 + t // 2, pl.ds((t % 2) * GROWS + e * SEL + sel, 1)] * scale
        return carry

    lax.fori_loop(0, TASKS, order, 0)

    def gather_step(step, carry):
        for d, k in lanes:
            q = holds(d, step - 1)
            ag(d, k, step - 1, landed(d, k, q), q).wait_recv()
            ag(d, k, step, landed(d, k, q), q).start()
            store(d, k, q, landed(d, k, q), step).start()
        return carry

    lax.fori_loop(1, n - 1, gather_step, 0)
    for d, k in lanes:
        q = holds(d, n - 2)
        ag(d, k, last, landed(d, k, q), q).wait_recv()
        store(d, k, q, landed(d, k, q), n - 1).start()

    def stored(step, carry):
        for d, k in lanes:
            store(d, k, 0, landed(d, k, 0), step).wait()
        return carry

    lax.fori_loop(0, n, stored, 0)

    def sent(step, carry):
        for d, k in lanes:
            rs(d, k, step, a1.at[slot(d, k, step)]).wait_send()
            ag(d, k, step, a1.at[slot(d, k, step)], 0).wait_send()
        return carry

    lax.fori_loop(0, n - 1, sent, 0)
    each(lambda i: scatter(i).wait_send())
    each(lambda i: spread_sum(i).wait_send())
    to_mate.wait_send()
    gates_move.wait_send()
    for e in range(HALF):
        for move in give(e):
            move.wait_send()
    for k in range(2):

        @pl.when(s != 2 + k)
        def _():
            copy(smo, sm.at[s], K_SM + s, 2 + k, K_SM + k).wait_send()
            copy(tin_ref, ti.at[s], K_TI + s, 2 + k, K_TI + k).wait_send()

    @pl.when(x == 0)
    def _():
        for t in range(TASKS):
            copy(outbox.at[t], inbox.at[t], K_UP + t, across).wait_send()
        for k, sec in enumerate((mate, across, diag)):
            copy(dp.at[mine], dp.at[mine], K_DP + c, sec, K_DP + k).wait_send()

    @pl.when(x == 1)
    def _():
        copy(pre2, pre1, K_P + 1, across).wait_send()
        for t in range(TASKS):
            copy(outbox.at[t], inbox.at[t], K_DOWN + t, across).wait_send()

            @pl.when(t != s)
            def _():
                copy(tp.at[t], tw.at[c], K_TW + c, t, K_TW + t).wait_send()

    for k, sec in enumerate((mate, across, diag)):
        copy(piece, sg.at[s], K_GO + s, sec, K_GO + k).wait_send()
    for f in range(2):
        pltpu.make_async_copy(xf.at[f], o_ig.at[:, f], local.at[2 + f]).wait()


def hand_over(count, *refs):
    held = refs[2 * count : 3 * count]
    sems = refs[-1]
    reads = [pltpu.make_async_copy(refs[k], held[k], sems.at[0, k]) for k in range(count)]
    writes = [pltpu.make_async_copy(held[k], refs[count + k], sems.at[1, k]) for k in range(count)]
    for move in reads:
        move.start()
    for read, write in zip(reads, writes):
        read.wait()
        write.start()
    for move in writes:
        move.wait()


def body(
    field_inputs,
    field_weight,
    norm_gain,
    gate_weight,
    expert_in,
    expert_out,
    tower_in,
    tower_out,
    tower_bias,
    labels,
    source_ids,
    task_table,
):
    n = lax.axis_size("dp")
    rows = field_inputs.shape[0]
    half = rows // 2
    subs = 2
    small_rows = -(-SMALL // (8 * n)) * 8
    used = TASKS * SEL * (BITS + 1)

    vmem = pl.BlockSpec(memory_space=pltpu.VMEM)
    smem = pl.BlockSpec(memory_space=pltpu.SMEM)
    hbm = pl.BlockSpec(memory_space=pl.ANY)

    def bf(*shape):
        return pltpu.VMEM(shape, BF16)

    def f32(*shape):
        return pltpu.VMEM(shape, F32)

    def out(*shape):
        return jax.ShapeDtypeStruct(shape, F32)

    dma = pltpu.SemaphoreType.DMA
    *sums, _ = pl.pallas_call(
        partial(kernel, n, subs, small_rows),
        out_shape=(
            out(1, rows),
            out(rows, 2, D),
            out(1, 2),
            out(1, D),
            out(2, used, D),
            out(HALF * H, D),
            out(HALF * H, D),
            out(D, TOWER),
            out(1, TOWER),
            out(1, 1),
            jax.ShapeDtypeStruct((E, 2 * SPILL, H, 2 * half), BF16),
        ),
        in_specs=[hbm, smem, vmem, vmem, hbm, hbm, vmem, vmem, smem, vmem, vmem, smem],
        out_specs=(vmem, hbm, smem, vmem, vmem, hbm, hbm, vmem, vmem, smem, hbm),
        scratch_shapes=[
            bf(2 * E, H, 2 * D),
            bf(E, D, 2 * H),
            bf(E, H, 2 * D),
            f32(E * H, half),
            f32(E * H, half),
            f32(E * H, D),
            f32(E * H, D),
            bf(E, H, 2 * half),
            bf(E, H, 2 * half),
            bf(2, H, 2 * half),
            f32(2, HALF * H, D),
            f32(2, rows, D),
            f32(rows, D),
            f32(half, D),
            f32(half, D),
            f32(half, D),
            f32(half, D),
            f32(TASKS, D, half),
            f32(TASKS, D, half),
            bf(3 * D, half),
            bf(TASKS, 3 * half, D),
            bf(3 * D, half),
            bf(TASKS, 3 * half, D),
            f32(2, H, half),
            f32(D, half),
            f32(TASKS * GROWS, D),
            f32(E, 1, half),
            f32(E, TASKS, half),
            f32(FROWS, half),
            f32(E, TASKS, half),
            f32(TASKS * GROWS, D),
            f32(2 * GROWS, D),
            f32(TASKS, 8, rows),
            f32(8, rows),
            f32(TASKS, D, TOWER),
            f32(TASKS, TOWER + 8, D),
            f32(2, TOWER + 8, D),
            f32(rows, D),
            f32(8, D),
            f32(half, E * TASKS),
            bf(3 * D, half),
            f32(E, 1, half),
            f32(GROWS, half),
            f32(D, half),
            f32(D, half),
            f32(D, half),
            f32(2 * TOWER, half),
            f32(n * small_rows, D),
            f32(n, small_rows, D),
            f32(small_rows, D),
            f32(n * small_rows, D),
            f32(TASKS, KEPT, D),
            dma((K_COUNT,)),
            dma((K_COUNT,)),
            dma((6,)),
            dma((AHEAD + 1,)),
            pltpu.SemaphoreType.REGULAR,
            dma((2, subs, n - 1)),
            dma((2, subs, n - 1)),
            dma((2, subs, n - 1)),
            dma((2, subs, n - 1)),
            dma((2, subs, n)),
            dma((n,)),
            dma((n,)),
            dma((n,)),
            dma((n,)),
        ],
        compiler_params=pltpu.CompilerParams(
            collective_id=0, has_side_effects=True, vmem_limit_bytes=64 * 1024 * 1024 - 65536
        ),
    )(
        field_inputs,
        field_weight.reshape(1, 2),
        norm_gain.reshape(1, D),
        gate_weight.swapaxes(1, 2),
        expert_in.reshape(HALF * H, D),
        expert_out.reshape(HALF * H, D),
        tower_in.reshape(D, TOWER),
        tower_out,
        tower_bias.reshape(1, 1),
        labels.reshape(1, rows),
        source_ids.reshape(1, rows),
        task_table.reshape(1, SOURCES),
    )
    pred, ig, fw, gain, gate, d_in, d_out, tin, tout, bias = pl.pallas_call(
        partial(hand_over, len(sums)),
        out_shape=tuple(jax.ShapeDtypeStruct(v.shape, v.dtype) for v in sums),
        in_specs=[hbm] * len(sums),
        out_specs=(hbm,) * len(sums),
        scratch_shapes=[pltpu.VMEM(v.shape, v.dtype) for v in sums] + [dma((2, len(sums)))],
        compiler_params=pltpu.CompilerParams(vmem_limit_bytes=64 * 1024 * 1024 - 65536),
    )(*sums)
    return (
        pred.reshape(rows, 1),
        ig,
        fw.reshape(2),
        gain.reshape(D),
        gate.swapaxes(1, 2),
        d_in.reshape(HALF, D, H),
        d_out.reshape(HALF, H, D),
        tin.reshape(1, D, TOWER),
        tout,
        bias.reshape(1),
    )


def solution(mesh):
    in_specs = (
        P("dp", "section", None),
        P("section"),
        P(),
        P(),
        P("section", None, None),
        P("section", None, None),
        P("section", None, None),
        P("section", None),
        P("section"),
        P("dp", "section"),
        P("dp"),
        P(None, "section"),
    )
    out_specs = (
        P("dp", "section"),
        P("dp", "section", None),
        P("section"),
        P(),
        P(),
        P("section", None, None),
        P("section", None, None),
        P("section", None, None),
        P("section", None),
        P("section"),
    )
    return jax.shard_map(body, mesh=mesh, in_specs=in_specs, out_specs=out_specs, check_vma=False)
```
